32 devices in a mesh: dp: 8 (over z, y), seq: 4 (over x, core).
Axes of the slice: x: 2, y: 2, z: 4, core: 2. Of those that a mesh axis runs over, the one named last changes fastest.
Arguments:
- tokens: bfloat16 [16, 584, 1024], P('dp', 'seq'), may hold values from -6 to 6
- cotangent: bfloat16 [16, 584, 1024], P('dp', 'seq'), may hold values from -6 to 6
- key_mask: int32 [16, 584], P('dp'), may hold values from 0 to 1, as said below
- attention_weights: float32 [1024, 4096], P('dp')
- expand_weights: float32 [1024, 4096], P('dp'), may hold values from -0.1875 to 0.1875
- shrink_weights: float32 [4096, 1024], P('dp'), may hold values from -0.09375 to 0.09375
- vector_params: float32 [12288], P('dp')
- attention_moment: float32 [1024, 4096], P('dp'), may hold values from -512 to 512
- attention_square: float32 [1024, 4096], P('dp'), may hold values from 3737.6 to 59801.6
- expand_moment: float32 [1024, 4096], P('dp'), may hold values from -320 to 320
- expand_square: float32 [1024, 4096], P('dp'), may hold values from 1681.92 to 27097.6
- shrink_moment: float32 [4096, 1024], P('dp'), may hold values from -256 to 256
- shrink_square: float32 [4096, 1024], P('dp'), may hold values from 1168 to 18688
- vector_moment: float32 [12288], P('dp'), may hold values from -512 to 512
- vector_square: float32 [12288], P('dp'), may hold values from 3737.6 to 59801.6
Outputs:
- block_output: bfloat16 [16, 584, 1024], P('dp', 'seq')
- token_gradient: bfloat16 [16, 584, 1024], P('dp', 'seq')
- attention_momentum: float32 [1024, 4096], P('dp')
- attention_variance: float32 [1024, 4096], P('dp')
- attention_updated: float32 [1024, 4096], P('dp')
- attention_rounded: bfloat16 [1024, 4096], P('dp')
- expand_momentum: float32 [1024, 4096], P('dp')
- expand_variance: float32 [1024, 4096], P('dp')
- expand_updated: float32 [1024, 4096], P('dp')
- expand_rounded: bfloat16 [1024, 4096], P('dp')
- shrink_momentum: float32 [4096, 1024], P('dp')
- shrink_variance: float32 [4096, 1024], P('dp')
- shrink_updated: float32 [4096, 1024], P('dp')
- shrink_rounded: bfloat16 [4096, 1024], P('dp')
- vector_momentum: float32 [12288], P('dp')
- vector_variance: float32 [12288], P('dp')
- vector_updated: float32 [12288], P('dp')
- vector_rounded: bfloat16 [12288], P('dp')
The draws below stay inside these ranges and needn't reach their ends.
Inputs may be any that keep to these rules, and one draw needn't show every extreme that they name: In image i, key_mask is 1 on the first L_i slots and 0 after, with 292 < L_i <= 577; in every aligned block of 2 images one image has L_i = 577.
All inputs are finite; a program needn't handle non-finite values.
Results may differ from the reference program's by a relative error of at most 0.018.
Values may be sent and summed in bfloat16 or wider, within the bound.
A program may use at most 256 MiB of HBM per device.

```python
import math
import jax
import jax.numpy as jnp
from jax import lax

D = 1024
HEADS = 16
HEAD_DIM = 64
FF = 4096
SEQ = 584
IMG_DEV = 2
STEP = 5
VALID = 577
IMAGES = 16
SMALL = 12288


def draw_key_mask(key, part):
    key = jax.random.fold_in(key, 7)
    first_key, second_key = jax.random.split(key)
    lengths = jax.random.randint(first_key, (IMAGES,), SEQ // 2 + 1, VALID + 1)
    chosen = jax.random.randint(second_key, (IMAGES // IMG_DEV,), 0, IMG_DEV)
    position = jnp.arange(IMAGES)
    longest = position % IMG_DEV == chosen[position // IMG_DEV]
    lengths = jnp.where(longest, VALID, lengths)
    return (jnp.arange(SEQ)[None, :] < lengths[:, None]).astype(jnp.int32)


def draw_attention_weights(key, part):
    key = jax.random.fold_in(key, 11)
    base = jnp.clip(jax.random.normal(key, (D, 4 * D), jnp.float32), -4.0, 4.0)
    column_block = jnp.arange(4 * D) // D
    out_scale = max(1.0, (VALID / 50.0) ** 0.5)
    scale = jnp.where(column_block < 2, 1.4, jnp.where(column_block == 2, 1.0, out_scale))
    return base * scale[None, :] * D ** (-0.5)


def draw_vector_params(key, part):
    key = jax.random.fold_in(key, 13)
    gain_key, shift_key, bias_key, hidden_key = jax.random.split(key, 4)
    gains = jax.random.uniform(gain_key, (2, D), jnp.float32, 0.6, 1.4)
    shifts = 0.3 * jnp.clip(jax.random.normal(shift_key, (2, D), jnp.float32), -4.0, 4.0)
    biases = 0.3 * jnp.clip(jax.random.normal(bias_key, (4, D), jnp.float32), -4.0, 4.0)
    hidden = 0.5 * jnp.clip(jax.random.normal(hidden_key, (FF,), jnp.float32), -4.0, 4.0)
    return jnp.concatenate([gains[0], shifts[0], gains[1], shifts[1], biases.reshape(-1), hidden])


def block_levels(own_key, shape, shards, low, high):
    loudness = 1.0
    for dim, shards_of in shards:
        steps = jax.random.uniform(jax.random.fold_in(jax.random.fold_in(own_key, 6), dim), (shards_of,), jnp.float32, low / len(shards), high / len(shards))
        loudness = loudness * jnp.repeat(jnp.exp(steps), shape[dim] // shards_of).reshape((-1,) + (1,) * (len(shape) - 1 - dim))
    return loudness


def bell_draw(stream_key, dims, deviation, bound, shards=(), dtype=jnp.bfloat16):
    loudness = block_levels(stream_key, dims, shards, -0.22, 0.18) if shards else 1.0
    drawn = jax.random.normal(stream_key, dims, jnp.float32) * deviation * loudness
    return jnp.minimum(jnp.maximum(drawn, -bound), bound).astype(dtype)


def setup_inputs(seed: int = 0) -> dict:
    seeds = jax.random.split(jax.random.key(seed), 16)
    tokens = bell_draw(seeds[0], (IMAGES, SEQ, D), 1.0, 6.0, ((0, 8), (1, 4)))
    cotangent = bell_draw(seeds[1], (IMAGES, SEQ, D), 1.0, 6.0, ((0, 8), (1, 4)))
    key_mask = draw_key_mask(jax.random.fold_in(seeds[15], 71), 0)
    attention_weights = draw_attention_weights(jax.random.fold_in(seeds[15], 71), 0)
    expand_weights = bell_draw(seeds[4], (D, FF), D ** -0.5, 0.1875, ((0, 8),), jnp.float32)
    shrink_weights = bell_draw(seeds[5], (FF, D), FF ** -0.5, 0.09375, ((0, 8),), jnp.float32)
    vector_params = draw_vector_params(jax.random.fold_in(seeds[15], 71), 0)
    attention_moment = bell_draw(seeds[7], (D, 4 * D), (0.9 * (IMAGES * SEQ) ** 0.5), 512.0, ((0, 8),), jnp.float32)
    attention_square = jnp.clip(jnp.exp(math.log(59801.6) - 2.7725887 * jax.random.uniform(seeds[8], (D, 4 * D), jnp.float32) ** block_levels(seeds[8], (D, 4 * D), ((0, 8),), -0.2, 0.2)), 3737.6, 59801.6)
    expand_moment = bell_draw(seeds[9], (D, FF), (0.6 * (IMAGES * SEQ) ** 0.5), 320.0, ((0, 8),), jnp.float32)
    expand_square = jnp.clip(jnp.exp(math.log(27097.6) - 2.779509 * jax.random.uniform(seeds[10], (D, FF), jnp.float32) ** block_levels(seeds[10], (D, FF), ((0, 8),), -0.2, 0.2)), 1681.92, 27097.6)
    shrink_moment = bell_draw(seeds[11], (FF, D), (0.5 * (IMAGES * SEQ) ** 0.5), 256.0, ((0, 8),), jnp.float32)
    shrink_square = jnp.clip(jnp.exp(math.log(18688.0) - 2.7725887 * jax.random.uniform(seeds[12], (FF, D), jnp.float32) ** block_levels(seeds[12], (FF, D), ((0, 8),), -0.2, 0.2)), 1168.0, 18688.0)
    vector_moment = bell_draw(seeds[13], (SMALL,), (0.9 * (IMAGES * SEQ) ** 0.5), 512.0, ((0, 8),), jnp.float32)
    vector_square = jnp.clip(jnp.exp(math.log(59801.6) - 2.7725887 * jax.random.uniform(seeds[14], (SMALL,), jnp.float32) ** block_levels(seeds[14], (SMALL,), ((0, 8),), -0.2, 0.2)), 3737.6, 59801.6)
    return {"tokens": tokens, "cotangent": cotangent, "key_mask": key_mask, "attention_weights": attention_weights, "expand_weights": expand_weights, "shrink_weights": shrink_weights, "vector_params": vector_params, "attention_moment": attention_moment, "attention_square": attention_square, "expand_moment": expand_moment, "expand_square": expand_square, "shrink_moment": shrink_moment, "shrink_square": shrink_square, "vector_moment": vector_moment, "vector_square": vector_square}


EPS_NORM = 1e-05
BETA_ONE = 0.5
BETA_TWO = 0.5
EPS_ADAM = 1e-08
RATE_MATRIX = 0.05
RATE_VECTOR = 0.2
DECAY_MATRIX = 0.1
SLOPE = 1.702

@jax.custom_vjp
def low(v):
    return lax.optimization_barrier(v.astype(jnp.bfloat16)).astype(jnp.float32)

@jax.custom_vjp
def low_back(v):
    return v

def low_keep(v):
    return (low(v), None)

def low_pass(kept, grad):
    return (grad,)

def back_keep(v):
    return (v, None)

def back_low(kept, grad):
    return (low(grad),)
low.defvjp(low_keep, low_pass)
low_back.defvjp(back_keep, back_low)

def product(left, right):
    return jnp.dot(left, right, precision=lax.Precision.HIGHEST, preferred_element_type=jnp.float32)

def layer_norm(values, gain, shift):
    centred = values - lax.optimization_barrier(jnp.mean(values, -1, keepdims=True))
    spread = lax.optimization_barrier(jnp.mean(centred * centred, -1, keepdims=True))
    return centred * lax.rsqrt(spread + EPS_NORM) * gain + shift

def attend_image(packed):
    queries, keys, values, keep = packed
    scores = jnp.einsum('shd,thd->hst', queries, keys, precision=lax.Precision.HIGHEST) * HEAD_DIM ** (-0.5)
    scores = low_back(scores)
    scores = jnp.where(keep[None, None, :] > 0, scores, -1e+30)
    highest = lax.optimization_barrier(jnp.max(scores, -1, keepdims=True))
    raised = jnp.exp(scores - highest)
    chance = raised / lax.optimization_barrier(jnp.sum(raised, -1, keepdims=True))
    return jnp.einsum('hst,thd->shd', low(chance), values, precision=lax.Precision.HIGHEST)

def block(params, inputs, keep):
    attention, expand, shrink, vector = [low(item) for item in params]
    gain_one = vector[0:D]
    shift_one = vector[D:2 * D]
    gain_two = vector[2 * D:3 * D]
    shift_two = vector[3 * D:4 * D]
    bias_query = vector[4 * D:5 * D]
    bias_value = vector[5 * D:6 * D]
    bias_attention = vector[6 * D:7 * D]
    bias_out = vector[7 * D:8 * D]
    bias_hidden = vector[8 * D:]
    images = inputs.shape[0]
    rows = inputs.reshape(-1, D)
    row_live = keep.reshape(-1, 1)
    normed_one = low(layer_norm(rows, gain_one, shift_one))
    qkv_bias = jnp.concatenate([bias_query, jnp.zeros_like(bias_query), bias_value])
    qkv = low(low_back(product(normed_one, attention[:, :3 * D]) + qkv_bias))
    shaped = qkv.reshape(images, SEQ, 3, HEADS, HEAD_DIM)
    attended = lax.map(jax.checkpoint(attend_image), (shaped[:, :, 0], shaped[:, :, 1], shaped[:, :, 2], keep))
    attended = low(low_back(attended.reshape(-1, D)))
    resid = rows + low_back(product(attended, attention[:, 3 * D:]) + bias_attention)
    normed_two = low(layer_norm(resid, gain_two, shift_two))
    hidden = low_back(product(normed_two, expand) + bias_hidden)
    active = low(hidden * jax.nn.sigmoid(SLOPE * hidden))
    branch = low_back(product(active, shrink) + bias_out)
    return (row_live * (resid + branch)).reshape(images, SEQ, D)

def adamw(grad, moment, square, weight, rate, decay):
    momentum = BETA_ONE * moment + (1.0 - BETA_ONE) * grad
    variance = BETA_TWO * square + (1.0 - BETA_TWO) * grad * grad
    first_fix = 1.0 - BETA_ONE ** STEP
    second_fix = 1.0 - BETA_TWO ** STEP
    direction = momentum / first_fix / (jnp.sqrt(variance / second_fix) + EPS_ADAM)
    updated = weight - rate * (direction + decay * weight)
    return (momentum, variance, updated, updated.astype(jnp.bfloat16))

def reference(tokens, cotangent, key_mask, attention_weights, expand_weights, shrink_weights, vector_params, attention_moment, attention_square, expand_moment, expand_square, shrink_moment, shrink_square, vector_moment, vector_square):
    groups = IMAGES // IMG_DEV
    inputs = tokens.astype(jnp.float32).reshape(groups, IMG_DEV, SEQ, D)
    back_in = cotangent.astype(jnp.float32).reshape(groups, IMG_DEV, SEQ, D)
    keeps = (key_mask > 0).astype(jnp.float32).reshape(groups, IMG_DEV, SEQ)
    params = (attention_weights, expand_weights, shrink_weights, vector_params)

    def one_group(totals, packed):
        group_in, group_back, group_keep = packed

        def forward(weights, values):
            return block(weights, values, group_keep)
        result, pullback = jax.vjp(forward, params, group_in)
        grad_params, grad_in = pullback(group_back)
        totals = jax.tree.map(jnp.add, totals, grad_params)
        return (totals, (result, grad_in))
    zeros = jax.tree.map(jnp.zeros_like, params)
    grads, (results, grad_inputs) = lax.scan(one_group, zeros, (inputs, back_in, keeps))
    block_output = results.reshape(IMAGES, SEQ, D).astype(jnp.bfloat16)
    token_gradient = grad_inputs.reshape(IMAGES, SEQ, D).astype(jnp.bfloat16)
    attention_out = adamw(grads[0], attention_moment, attention_square, attention_weights, RATE_MATRIX, DECAY_MATRIX)
    expand_out = adamw(grads[1], expand_moment, expand_square, expand_weights, RATE_MATRIX, DECAY_MATRIX)
    shrink_out = adamw(grads[2], shrink_moment, shrink_square, shrink_weights, RATE_MATRIX, DECAY_MATRIX)
    vector_out = adamw(grads[3], vector_moment, vector_square, vector_params, RATE_VECTOR, 0.0)
    return (block_output, token_gradient, attention_out[0], attention_out[1], attention_out[2], attention_out[3], expand_out[0], expand_out[1], expand_out[2], expand_out[3], shrink_out[0], shrink_out[1], shrink_out[2], shrink_out[3], vector_out[0], vector_out[1], vector_out[2], vector_out[3])
```

```python
import functools

import jax
import jax.numpy as jnp
from jax import lax
from jax.experimental import pallas as pl
from jax.experimental.pallas import tpu as pltpu
from jax.sharding import PartitionSpec as P

HEAD_DIM = 64
STEP = 5
EPS_NORM = 1e-05
BETA_ONE = 0.5
BETA_TWO = 0.5
EPS_ADAM = 1e-08
RATE_MATRIX = 0.05
RATE_VECTOR = 0.2
DECAY_MATRIX = 0.1
SLOPE = 1.702

BF16 = jnp.bfloat16
F32 = jnp.float32
MESH = pl.DeviceIdType.MESH

UNIT = 512
EDGE = 128
WINDOW = UNIT - EDGE
UNITS = 12
SLOTS = 8
PAIR = 128


def dot(a, b):
    return jnp.dot(a, b, preferred_element_type=F32)


def dot_rows(a, b):
    return lax.dot_general(a, b, (((0,), (0,)), ((), ())), preferred_element_type=F32)


def dot_cols(a, b):
    return lax.dot_general(a, b, (((1,), (1,)), ((), ())), preferred_element_type=F32)


def unit_rows(x):
    centred = x - jnp.mean(x, -1, keepdims=True)
    rstd = lax.rsqrt(jnp.mean(centred * centred, -1, keepdims=True) + EPS_NORM)
    return centred * rstd, rstd


def norm_back(grad_normed, unit, rstd, gain):
    g = grad_normed * gain
    return rstd * (g - jnp.mean(g, -1, keepdims=True) - unit * jnp.mean(g * unit, -1, keepdims=True))


def fold8(v):
    return jnp.sum(v.reshape(v.shape[0] // 8, 8, v.shape[1]), 0)


def layer_kernel(
    line, vec_len,
    tok, cot, kbias, live, p_att, p_exp, p_shr, p_vec,
    o_blk, o_tok, o_g, o_vec,
    w, w_oth, g, rx, ry, rz, s_own, s_oth, f_own,
    vec_all, vec, bias_h, vg, vr, vz,
    x_stage, tok_own, cot_own,
    n1, go, qkv, att, lse, resid, n2, act, fac, own_p, send_p, recv_p, recv_m,
    gb, gat, tr, dk_acc, dv_acc,
    ag, rs, sib, xe, vs, fill, credit,
):
    dp_n = 2 * line
    r = w.shape[3]
    block = tok.shape[1]
    own = 2 * block
    rows = 2 * own
    width = tok.shape[2]
    half = UNIT
    d = lax.axis_index("dp")
    s = lax.axis_index("seq")
    zi, yi = d // 2, d % 2
    x, c = s // 2, s % 2
    sibling = (d, x * 2 + 1 - c)
    x_neigh = (d, (1 - x) * 2 + c)
    y_neigh = (zi * 2 + 1 - yi, s)

    def z_peer(o):
        return (lax.rem(zi + o, line) * 2 + yi, s)

    my_rows = pl.ds(pl.multiple_of(c * own, own), own)
    oth_rows = pl.ds(pl.multiple_of((1 - c) * own, own), own)
    my_half = pl.ds(pl.multiple_of(c * half, half), half)
    oth_half = pl.ds(pl.multiple_of((1 - c) * half, half), half)
    win = pl.ds(pl.multiple_of(x * EDGE, EDGE), WINDOW)
    mine = pl.ds(pl.multiple_of(x * WINDOW, EDGE), EDGE)
    theirs = pl.ds(pl.multiple_of((1 - x) * WINDOW, EDGE), EDGE)
    my_block = pl.ds(pl.multiple_of(x * block, block), block)
    oth_block = pl.ds(pl.multiple_of((1 - x) * block, block), block)

    def remote(src, dst, send, recv, to):
        return pltpu.make_async_remote_copy(
            src_ref=src, dst_ref=dst, send_sem=send, recv_sem=recv, device_id=to, device_id_type=MESH
        )

    def wait_bytes(ref, sem):
        pltpu.make_async_copy(ref, ref, sem).wait()

    fills = [
        pltpu.make_async_copy(p, w.at[pl.ds(4 * n, 4), zi, yi], fill.at[n])
        for n, p in enumerate((p_att, p_exp, p_shr))
    ]
    for copy in fills:
        copy.start()
    vec_all[d] = p_vec[...]
    x_stage[0] = tok[1 - x]
    x_stage[1] = cot[1 - x]
    tok_own[my_block] = tok[x]
    cot_own[my_block] = cot[x]

    for copy in fills:
        copy.wait()
    barrier = pltpu.get_barrier_semaphore()

    def greet(o, carry):
        pl.semaphore_signal(barrier, inc=1, device_id=(lax.rem(d + o, dp_n), s), device_id_type=MESH)
        return carry

    lax.fori_loop(1, dp_n, greet, 0)
    pl.semaphore_signal(barrier, inc=1, device_id=sibling, device_id_type=MESH)
    pl.semaphore_signal(barrier, inc=1, device_id=x_neigh, device_id_type=MESH)
    pl.semaphore_wait(barrier, dp_n + 1)

    def send_vec(o, carry):
        remote(p_vec, vec_all.at[d], vs.at[0, 0], vs.at[1, 0], (lax.rem(d + o, dp_n), s)).start()
        return carry

    lax.fori_loop(1, dp_n, send_vec, 0)
    x_copies = [
        remote(x_stage.at[0], tok_own.at[my_block], xe.at[0, 0], xe.at[1, 0], x_neigh),
        remote(x_stage.at[1], cot_own.at[my_block], xe.at[0, 1], xe.at[1, 1], x_neigh),
    ]
    for copy in x_copies:
        copy.start()

    def ag_z(u):
        for o in range(1, line):
            part = w.at[u, zi, yi, :, win]
            remote(part, part, ag.at[0, u], ag.at[1, u], z_peer(o)).start()

    def ag_y_copy(u):
        part = w.at[u, :, yi, :, win]
        return remote(part, part, ag.at[2, u], ag.at[3, u], y_neigh)

    def ag_x_copy(u):
        part = w.at[u, :, :, :, mine]
        return remote(part, part, ag.at[4, u], ag.at[5, u], x_neigh)

    def z_bytes(u):
        return w.at[u, pl.ds(0, line - 1), yi, :, win]

    def ag_y(u):
        wait_bytes(z_bytes(u), ag.at[1, u])
        ag_y_copy(u).start()

    def ag_x(u):
        ag_y_copy(u).wait_recv()
        ag_x_copy(u).start()

    def ag_end(u):
        ag_x_copy(u).wait_recv()

    steps = []
    for t in range(UNITS + 2):
        def step(t=t):
            if t + 2 < UNITS:
                ag_z(t + 2)
            if t < UNITS:
                ag_y(t)
            if 0 <= t - 1 < UNITS:
                ag_x(t - 1)
            if 0 <= t - 2 < UNITS:
                ag_end(t - 2)
        steps.append(step)
    ag_z(0)
    ag_z(1)
    done = [0]

    def ag_until(u):
        while done[0] < min(u + 3, len(steps)):
            steps[done[0]]()
            done[0] += 1

    wait_bytes(vec_all.at[pl.ds(0, dp_n - 1)], vs.at[1, 0])
    grain = 128 if vec_len % 128 == 0 else 64

    def vec_lanes(first):
        parts = []
        for e in range(first, first + 128, grain):
            o = e % vec_len
            parts.append(vec_all[e // vec_len, o // 128 : o // 128 + 1, o % 128 : o % 128 + grain])
        return parts[0] if len(parts) == 1 else jnp.concatenate(parts, 1)

    for row in range(12):
        for lane in range(0, width, 128):
            vec[row : row + 1, lane : lane + 128] = vec_lanes(row * width + lane)

    def hidden_bias(core):
        parts = []
        for h in range(2):
            for shard in range(dp_n):
                n = shard * 4 * r + core * 2 * r + h * r
                parts.append(vec[8 + n // width : 9 + n // width, n % width : n % width + r])
        return jnp.concatenate(parts, 1)

    bias_h[...] = jnp.where(c == 0, hidden_bias(0), hidden_bias(1))

    x_copies[0].wait_recv()
    x_copies[1].wait_recv()

    chunk = 32
    gain_one, shift_one = vec[0:1, :], vec[1:2, :]

    def norm_one(i, carry):
        at = pl.ds(pl.multiple_of(i * chunk, chunk), chunk)
        to = pl.ds(pl.multiple_of(c * own + i * chunk, chunk), chunk)
        unit, _ = unit_rows(tok_own[at, :].astype(F32))
        n1[to, :] = (unit * gain_one + shift_one).astype(BF16)
        go[to, :] = (cot_own[at, :].astype(F32) * live[at, :]).astype(BF16)
        return carry

    lax.fori_loop(0, own // chunk, norm_one, 0)
    n1_copy = remote(n1.at[my_rows], n1.at[my_rows], sib.at[0, 0], sib.at[1, 0], sibling)
    n1_copy.start()
    go_copy = remote(go.at[my_rows], go.at[my_rows], sib.at[0, 1], sib.at[1, 1], sibling)
    go_copy.start()
    n1_copy.wait_recv()

    def unit_matrix(u):
        return w[u].reshape(dp_n * r, UNIT)

    for u in range(3):
        ag_until(u)
        out = dot(n1[...], unit_matrix(u))
        if u == 0:
            out = out + vec[4:5, my_half]
        if u == 2:
            out = out + vec[5:6, my_half]
        out = out.astype(BF16)
        if u == 0:
            out = out * jnp.asarray(HEAD_DIM**-0.5, BF16)
        qkv[:, u * UNIT : (u + 1) * UNIT] = out

    low_lane = lax.broadcasted_iota(jnp.int32, (PAIR, PAIR), 1) < HEAD_DIM
    low_row = lax.broadcasted_iota(jnp.int32, (PAIR, PAIR), 0) < HEAD_DIM
    q_chunks = rows // PAIR

    def two_heads(v):
        zero = jnp.zeros_like(v)
        return jnp.concatenate([jnp.where(low_lane, v, zero), jnp.where(low_lane, zero, v)], 0)

    def lanes(first, p):
        return pl.ds(pl.multiple_of(first + p * PAIR, PAIR), PAIR)

    def attend_forward(n, carry):
        p, j = n // q_chunks, n % q_chunks
        at = pl.ds(pl.multiple_of(j * PAIR, PAIR), PAIR)
        keys = qkv[:, lanes(UNIT, p)]
        values = qkv[:, lanes(2 * UNIT, p)]
        both = two_heads(qkv[at, lanes(0, p)])
        mask = kbias[...]
        scores = dot_cols(keys, both) + jnp.concatenate([mask, mask], 1)
        highest = jnp.max(scores, 0, keepdims=True)
        raised = jnp.exp(scores - highest)
        total = jnp.sum(raised, 0, keepdims=True)
        out = dot_rows(values, raised.astype(BF16)) / total
        out = jnp.where(low_row, out[:, :PAIR], out[:, PAIR:])
        att[at, lanes(c * half, p)] = out.T.astype(BF16)
        lse[pl.ds(n, 1), :] = highest + jnp.log(total)
        return carry

    lax.fori_loop(0, q_chunks * (UNIT // PAIR), attend_forward, 0)
    att_copy = remote(att.at[:, my_half], att.at[:, my_half], sib.at[0, 2], sib.at[1, 2], sibling)
    att_copy.start()

    ag_until(3)
    wo_copy = remote(w.at[3], w_oth, sib.at[0, 3], sib.at[1, 3], sibling)
    wo_copy.start()
    att_copy.wait_recv()

    bias_att = vec[6:7, :]
    mixed = att[my_rows, :]
    resid[:, my_half] = dot(mixed, unit_matrix(3))
    wo_copy.wait_recv()
    resid[:, oth_half] = dot(mixed, w_oth[...].reshape(dp_n * r, UNIT))
    gain_two, shift_two = vec[2:3, :], vec[3:4, :]

    def norm_two(i, carry):
        at = pl.ds(pl.multiple_of(i * chunk, chunk), chunk)
        to = pl.ds(pl.multiple_of(c * own + i * chunk, chunk), chunk)
        res = resid[at, :] + tok_own[at, :].astype(F32) + bias_att
        resid[at, :] = res
        unit, _ = unit_rows(res)
        n2[to, :] = (unit * gain_two + shift_two).astype(BF16)
        return carry

    lax.fori_loop(0, own // chunk, norm_two, 0)
    n2_copy = remote(n2.at[my_rows], n2.at[my_rows], sib.at[0, 4], sib.at[1, 4], sibling)
    n2_copy.start()
    n2_copy.wait_recv()

    tile = 256
    for u in range(4):
        ag_until(4 + u)

        def expand(i, carry, u=u):
            lane = pl.ds(pl.multiple_of(i * tile, tile), tile)
            to = pl.ds(pl.multiple_of(u * UNIT + i * tile, tile), tile)
            hidden = dot(n2[...], w[4 + u, :, :, :, lane].reshape(dp_n * r, tile)) + bias_h[:, to]
            gate = jax.nn.sigmoid(SLOPE * hidden)
            act[:, to] = (hidden * gate).astype(BF16)
            fac[:, to] = (gate + SLOPE * hidden * gate * (1.0 - gate)).astype(BF16)
            return carry

        lax.fori_loop(0, UNIT // tile, expand, 0)
    go_copy.wait_recv()

    def rs_x_copy(k, u):
        return remote(g.at[k, :, :, :, theirs], rx.at[k], rs.at[0, u], rs.at[1, u], x_neigh)

    def rs_y_copy(k, u):
        return remote(g.at[k, :, 1 - yi, :, win], ry.at[k], rs.at[2, u], rs.at[3, u], y_neigh)

    def rs_2_copy(k, u):
        return remote(s_own.at[k], s_oth.at[k], rs.at[6, u], rs.at[7, u], x_neigh)

    def rs_f_copy(k, u):
        return remote(f_own.at[k], o_g.at[u, c], rs.at[8, u], rs.at[9, u], sibling)

    def rs_l_copy(k, u):
        return pltpu.make_async_copy(f_own.at[k], o_g.at[u, c], rs.at[10, u])

    def rs_y(k, u):
        rs_x_copy(k, u).wait_recv()

        def add(z, carry):
            g[k, z, :, :, mine] = (g[k, z, :, :, mine].astype(F32) + rx[k, z].astype(F32)).astype(BF16)
            return carry

        lax.fori_loop(0, line, add, 0)
        rs_y_copy(k, u).start()

    def rs_z(k, u):
        rs_y_copy(k, u).wait_recv()

        def add(z, carry):
            g[k, z, yi, :, win] = (g[k, z, yi, :, win].astype(F32) + ry[k, z].astype(F32)).astype(BF16)
            return carry

        lax.fori_loop(0, line, add, 0)
        for o in range(1, line):
            z = lax.rem(zi + o, line)
            remote(g.at[k, z, yi, :, win], rz.at[k, o - 1], rs.at[4, u], rs.at[5, u], z_peer(o)).start()

    def rs_2(k, u):
        wait_bytes(rz.at[k], rs.at[5, u])
        total = g[k, zi, yi, :, win].astype(F32)
        for o in range(1, line):
            total = total + rz[k, o - 1].astype(F32)
        s_own[k] = total.astype(BF16)
        rs_2_copy(k, u).start()

    def rs_f(k, u):
        rs_2_copy(k, u).wait_recv()
        here, there = s_own[k], s_oth[k]
        first = jnp.where(x == 0, here, there)
        last = jnp.where(x == 0, there, here)
        f_own[k, :, :EDGE] = first[:, :EDGE]
        f_own[k, :, EDGE:WINDOW] = (first[:, EDGE:].astype(F32) + last[:, : WINDOW - EDGE].astype(F32)).astype(BF16)
        f_own[k, :, WINDOW:] = last[:, WINDOW - EDGE :]
        rs_f_copy(k, u).start()
        rs_l_copy(k, u).start()

    def rs_end(k, u):
        rs_x_copy(k, u).wait_send()
        rs_y_copy(k, u).wait_send()
        wait_bytes(rz.at[k], rs.at[4, u])
        rs_2_copy(k, u).wait_send()
        rs_f_copy(k, u).wait()
        rs_l_copy(k, u).wait()

    def grad_unit(k, u, left, right):
        g[k] = dot(left, right).reshape(g.shape[1:]).astype(BF16)
        rs_x_copy(k, u).start()

    stages = [rs_y, rs_z, rs_2, rs_f, rs_end]

    def rs_all(pairs):
        for t in range(len(pairs) + len(stages) - 1):
            for n, stage in enumerate(stages):
                if 0 <= t - n < len(pairs):
                    stage(*pairs[t - n])

    def transpose_into(src, lanes_at):
        def move(i, carry):
            at = pl.ds(pl.multiple_of(i * 128, 128), 128)
            tr[at, :] = src[:, pl.ds(pl.multiple_of(lanes_at + i * 128, 128), 128)].T
            return carry

        lax.fori_loop(0, width // 128, move, 0)

    for h in range(2):
        transpose_into(act, h * width)
        for j in range(2):
            k = 2 * j + h
            grad_unit(k, 8 + k, tr[...], go[:, j * UNIT : (j + 1) * UNIT])

    for u in range(4):
        ag_until(8 + u)

    span = max(1, tile // (2 * r))

    def hidden_back(n, carry):
        z = n * span
        for h in range(2):
            total = None
            for j in range(2):
                part = w[8 + 2 * j + h, pl.ds(z, span)].reshape(span * 2 * r, UNIT)
                term = dot_cols(go[:, j * UNIT : (j + 1) * UNIT], part)
                total = term if total is None else total + term
            to = pl.ds(pl.multiple_of(h * width + n * (span * 2 * r), span * 2 * r), span * 2 * r)
            low = (total * fac[:, to].astype(F32)).astype(BF16)
            fac[:, to] = low
            sums = jnp.sum(fold8(low.astype(F32)), 0, keepdims=True)
            at = pl.ds(pl.multiple_of(n * (span * 2 * r), span * 2 * r), span * 2 * r)
            vg[pl.ds(8 + 2 * c + h, 1), at] = sums
        return carry

    vg[...] = jnp.zeros_like(vg)
    lax.fori_loop(0, line // span, hidden_back, 0)

    def back_partial(src, n_units, first, rows_at, dst):
        def back(n, carry):
            total = None
            for u in range(n_units):
                part = w[first + u, pl.ds(n * span, span)].reshape(span * 2 * r, UNIT)
                term = dot_cols(src[rows_at, u * UNIT : (u + 1) * UNIT], part)
                total = term if total is None else total + term
            dst[:, pl.ds(pl.multiple_of(n * (span * 2 * r), span * 2 * r), span * 2 * r)] = total
            return carry

        lax.fori_loop(0, line // span, back, 0)

    back_partial(fac, 4, 4, oth_rows, send_p)
    p2_copy = remote(send_p, recv_p, sib.at[0, 5], sib.at[1, 5], sibling)
    p2_copy.start()
    back_partial(fac, 4, 4, my_rows, own_p)
    transpose_into(n2, 0)
    for u in range(4):
        grad_unit(4 + u, 4 + u, tr[...], fac[:, u * UNIT : (u + 1) * UNIT])
    p2_copy.wait()

    zeros8 = jnp.zeros((8, width), F32)

    def norm_two_back(i, carry):
        at = pl.ds(pl.multiple_of(i * chunk, chunk), chunk)
        to = pl.ds(pl.multiple_of(c * own + i * chunk, chunk), chunk)
        unit, rstd = unit_rows(resid[at, :])
        gn = own_p[at, :] + recv_p[at, :]
        grad_out = go[to, :].astype(F32)
        gr = grad_out + norm_back(gn, unit, rstd, gain_two)
        own_p[at, :] = gr
        low = gr.astype(BF16)
        gb[to, :] = low
        a, b, e, f = carry
        return (a + fold8(gn * unit), b + fold8(gn), e + fold8(low.astype(F32)), f + fold8(grad_out))

    sums = lax.fori_loop(0, own // chunk, norm_two_back, (zeros8,) * 4)
    for row, v in zip((2, 3, 6, 7), sums):
        vg[row : row + 1, :] = jnp.sum(v, 0, keepdims=True)
    gb_copy = remote(gb.at[my_rows], gb.at[my_rows], sib.at[0, 6], sib.at[1, 6], sibling)
    gb_copy.start()

    def branch(dst, rows_at, add):
        def out(n, carry):
            lane = pl.ds(pl.multiple_of(n * tile, tile), tile)
            for j in range(2):
                total = None
                for h in range(2):
                    part = w[8 + 2 * j + h, :, :, :, lane].reshape(dp_n * r, tile)
                    term = dot(act[rows_at, h * width : (h + 1) * width], part)
                    total = term if total is None else total + term
                to = pl.ds(pl.multiple_of(j * UNIT + n * tile, tile), tile)
                dst[:, to] = dst[:, to] + total if add else total
            return carry

        lax.fori_loop(0, UNIT // tile, out, 0)

    branch(send_p, oth_rows, False)
    m_copy = remote(send_p, recv_m, sib.at[0, 8], sib.at[1, 8], sibling)
    m_copy.start()
    branch(resid, my_rows, True)
    gb_copy.wait_recv()
    m_copy.wait()

    bias_out = vec[7:8, :]

    def finish_block(i, carry):
        at = pl.ds(pl.multiple_of(i * chunk, chunk), chunk)
        out = live[at, :] * (resid[at, :] + recv_m[at, :] + bias_out)
        cot_own[at, :] = out.astype(BF16)
        return carry

    lax.fori_loop(0, own // chunk, finish_block, 0)
    o_blk[x] = cot_own[my_block, :]
    blk_copy = remote(cot_own.at[oth_block], o_blk.at[x], xe.at[0, 2], xe.at[1, 2], x_neigh)
    blk_copy.start()

    head_rows = pl.ds(c * (line // 2), line // 2)
    gat[...] = (
        dot_cols(gb[:, my_half], w[3, head_rows].reshape(half, UNIT))
        + dot_cols(gb[:, oth_half], w_oth[head_rows].reshape(half, UNIT))
    ).astype(BF16)

    def attend_backward(p, carry):
        keys = qkv[:, lanes(UNIT, p)]
        values = qkv[:, lanes(2 * UNIT, p)]
        mask = kbias[...]
        mask2 = jnp.concatenate([mask, mask], 1)
        dk_acc[...] = jnp.zeros_like(dk_acc)
        dv_acc[...] = jnp.zeros_like(dv_acc)

        def queries(j, inner_carry):
            at = pl.ds(pl.multiple_of(j * PAIR, PAIR), PAIR)
            both = two_heads(qkv[at, lanes(0, p)])
            grads = two_heads(gat[at, lanes(0, p)])
            scores = dot_cols(keys, both) + mask2
            chance = jnp.exp(scores - lse[pl.ds(p * q_chunks + j, 1), :])
            dv_acc[...] += dot(chance.astype(BF16), grads)
            grad_chance = dot_cols(values, grads)
            inner = jnp.sum(chance * grad_chance, 0, keepdims=True)
            grad_scores = (chance * (grad_chance - inner)).astype(BF16)
            dk_acc[...] += dot(grad_scores, both)
            out = dot_rows(keys, grad_scores)
            out = jnp.where(low_row, out[:, :PAIR], out[:, PAIR:]) * HEAD_DIM**-0.5
            qkv[at, lanes(0, p)] = out.T.astype(BF16)
            return inner_carry

        lax.fori_loop(0, q_chunks, queries, 0)
        qkv[:, lanes(UNIT, p)] = dk_acc[...].astype(BF16)
        qkv[:, lanes(2 * UNIT, p)] = dv_acc[...].astype(BF16)
        return carry

    lax.fori_loop(0, UNIT // PAIR, attend_backward, 0)
    vg[4:5, my_half] = jnp.sum(fold8(qkv[:, 0:UNIT].astype(F32)), 0, keepdims=True)
    vg[5:6, my_half] = jnp.sum(fold8(qkv[:, 2 * UNIT : 3 * UNIT].astype(F32)), 0, keepdims=True)

    back_partial(qkv, 3, 0, oth_rows, send_p)
    p1_copy = remote(send_p, recv_p, sib.at[0, 7], sib.at[1, 7], sibling)
    p1_copy.start()
    back_partial(qkv, 3, 0, my_rows, resid)

    rs_all([(k, 8 + k) for k in range(4)])
    pl.semaphore_signal(credit.at[0], inc=1, device_id=x_neigh, device_id_type=MESH)
    pl.semaphore_signal(credit.at[1], inc=1, device_id=y_neigh, device_id_type=MESH)
    for o in range(1, line):
        pl.semaphore_signal(credit.at[2], inc=1, device_id=z_peer(o), device_id_type=MESH)
    rs_all([(4 + k, 4 + k) for k in range(4)])
    pl.semaphore_wait(credit.at[0], 1)
    pl.semaphore_wait(credit.at[1], 1)
    pl.semaphore_wait(credit.at[2], line - 1)
    transpose_into(att, 0)
    grad_unit(3, 3, tr[...], gb[:, my_half])
    transpose_into(n1, 0)
    for u in (2, 1, 0):
        grad_unit(u, u, tr[...], qkv[:, u * UNIT : (u + 1) * UNIT])
    p1_copy.wait()

    def norm_one_back(i, carry):
        at = pl.ds(pl.multiple_of(i * chunk, chunk), chunk)
        unit, rstd = unit_rows(tok_own[at, :].astype(F32))
        gn = resid[at, :] + recv_p[at, :]
        out = own_p[at, :] + norm_back(gn, unit, rstd, gain_one)
        tok_own[at, :] = out.astype(BF16)
        a, b = carry
        return (a + fold8(gn * unit), b + fold8(gn))

    sums = lax.fori_loop(0, own // chunk, norm_one_back, (zeros8,) * 2)
    for row, v in zip((0, 1), sums):
        vg[row : row + 1, :] = jnp.sum(v, 0, keepdims=True)
    o_tok[x] = tok_own[my_block, :]
    tok_copy = remote(tok_own.at[oth_block], o_tok.at[x], xe.at[0, 3], xe.at[1, 3], x_neigh)
    tok_copy.start()

    for n, to in enumerate((sibling, x_neigh, y_neigh)):
        copy = remote(vg, vr.at[n], vs.at[0, 1 + n], vs.at[1, 1 + n], to)
        copy.start()
        copy.wait()
        vg[...] += vr[n]

    def send_vz(o, carry):
        remote(vg, vz.at[zi], vs.at[0, 4], vs.at[1, 4], (lax.rem(zi + o, line) * 2 + yi, s)).start()
        return carry

    lax.fori_loop(1, line, send_vz, 0)
    vz[zi] = vg[...]
    wait_bytes(vz.at[pl.ds(0, line - 1)], vs.at[1, 4])
    wait_bytes(vz.at[pl.ds(0, line - 1)], vs.at[0, 4])
    o_vec[...] = lax.fori_loop(1, line, lambda i, t: t + vz[i], vz[0])

    rs_all([(u, u) for u in (3, 2, 1, 0)])

    blk_copy.wait()
    tok_copy.wait()
    wait_bytes(vec_all.at[pl.ds(0, dp_n - 1)], vs.at[0, 0])
    for copy in x_copies + [n1_copy, go_copy, att_copy, wo_copy, n2_copy, gb_copy]:
        copy.wait_send()
    for u in range(UNITS):
        wait_bytes(z_bytes(u), ag.at[0, u])
        ag_y_copy(u).wait_send()
        ag_x_copy(u).wait_send()


def adamw(grad, moment, square, weight, rate, decay):
    momentum = BETA_ONE * moment + (1.0 - BETA_ONE) * grad
    variance = BETA_TWO * square + (1.0 - BETA_TWO) * grad * grad
    first_fix = 1.0 - BETA_ONE**STEP
    second_fix = 1.0 - BETA_TWO**STEP
    direction = momentum / first_fix / (jnp.sqrt(variance / second_fix) + EPS_ADAM)
    updated = weight - rate * (direction + decay * weight)
    return (momentum, variance, updated, updated.astype(BF16))


def body(
    tokens, cotangent, key_mask,
    attention_weights, expand_weights, shrink_weights, vector_params,
    attention_moment, attention_square, expand_moment, expand_square,
    shrink_moment, shrink_square, vector_moment, vector_square,
):
    dp_n = lax.axis_size("dp")
    line = dp_n // 2
    d = lax.axis_index("dp")
    place = lax.axis_index("seq")
    x, c = place // 2, place % 2
    _, local_len, width = tokens.shape
    r = width // dp_n
    block = -(-local_len // 16) * 16
    own, rows = 2 * block, 4 * block
    pad = ((0, 0), (0, block - local_len), (0, 0))

    keep = lax.dynamic_index_in_dim(key_mask, x, 0, keepdims=False).reshape(2, 2, local_len)
    keep = jnp.pad(keep.transpose(1, 0, 2), ((0, 0), (0, 0), pad[1])).reshape(2, own)
    kbias = jnp.broadcast_to(jnp.where(keep > 0, 0.0, -1e30).astype(F32).reshape(rows, 1), (rows, PAIR))
    live = lax.dynamic_index_in_dim(keep, c, 0, keepdims=False).astype(F32).reshape(own, 1)

    def pick(v, axis):
        return lax.dynamic_index_in_dim(v, c, axis, keepdims=False)

    p_att = pick(attention_weights.reshape(r, 4, 2, UNIT), 2).astype(BF16).transpose(1, 0, 2)
    p_exp = pick(expand_weights.reshape(r, dp_n, 2, 2, r), 2).astype(BF16)
    p_exp = p_exp.transpose(2, 0, 1, 3).reshape(2, r, 2, UNIT).transpose(0, 2, 1, 3).reshape(4, r, UNIT)
    p_shr = pick(shrink_weights.reshape(2, 2, r, 2, UNIT), 0).astype(BF16)
    p_shr = p_shr.transpose(2, 0, 1, 3).reshape(4, r, UNIT)
    vec_len = vector_params.shape[0]
    vec_rows = -(-vec_len // 1024) * 8
    p_vec = jnp.pad(vector_params.astype(BF16).astype(F32), (0, vec_rows * 128 - vec_len)).reshape(vec_rows, 128)

    vmem = pl.BlockSpec(memory_space=pltpu.VMEM)
    hbm = pl.BlockSpec(memory_space=pl.ANY)
    padded = jax.ShapeDtypeStruct((2, block, width), BF16)
    o_blk, o_tok, o_g, o_vec = pl.pallas_call(
        functools.partial(layer_kernel, line, vec_len),
        out_shape=(
            padded,
            padded,
            jax.ShapeDtypeStruct((UNITS, 2, r, UNIT), BF16),
            jax.ShapeDtypeStruct((16, width), F32),
        ),
        in_specs=[vmem] * 4 + [hbm] * 3 + [vmem],
        out_specs=(vmem, vmem, hbm, vmem),
        scratch_shapes=[
            pltpu.VMEM((UNITS, line, 2, r, UNIT), BF16),
            pltpu.VMEM((line, 2, r, UNIT), BF16),
            pltpu.VMEM((SLOTS, line, 2, r, UNIT), BF16),
            pltpu.VMEM((SLOTS, line, 2, r, EDGE), BF16),
            pltpu.VMEM((SLOTS, line, r, WINDOW), BF16),
            pltpu.VMEM((SLOTS, line - 1, r, WINDOW), BF16),
            pltpu.VMEM((SLOTS, r, WINDOW), BF16),
            pltpu.VMEM((SLOTS, r, WINDOW), BF16),
            pltpu.VMEM((SLOTS, r, UNIT), BF16),
            pltpu.VMEM((dp_n, vec_rows, 128), F32),
            pltpu.VMEM((16, width), F32),
            pltpu.VMEM((1, 2 * width), F32),
            pltpu.VMEM((16, width), F32),
            pltpu.VMEM((3, 16, width), F32),
            pltpu.VMEM((line, 16, width), F32),
            pltpu.VMEM((2, block, width), BF16),
            pltpu.VMEM((own, width), BF16),
            pltpu.VMEM((own, width), BF16),
            pltpu.VMEM((rows, width), BF16),
            pltpu.VMEM((rows, width), BF16),
            pltpu.VMEM((rows, 3 * UNIT), BF16),
            pltpu.VMEM((rows, width), BF16),
            pltpu.VMEM(((rows // PAIR) * (UNIT // PAIR), 2 * PAIR), F32),
            pltpu.VMEM((own, width), F32),
            pltpu.VMEM((rows, width), BF16),
            pltpu.VMEM((rows, 2 * width), BF16),
            pltpu.VMEM((rows, 2 * width), BF16),
            pltpu.VMEM((own, width), F32),
            pltpu.VMEM((own, width), F32),
            pltpu.VMEM((own, width), F32),
            pltpu.VMEM((own, width), F32),
            pltpu.VMEM((rows, width), BF16),
            pltpu.VMEM((rows, UNIT), BF16),
            pltpu.VMEM((width, rows), BF16),
            pltpu.VMEM((rows, PAIR), F32),
            pltpu.VMEM((rows, PAIR), F32),
            pltpu.SemaphoreType.DMA((6, UNITS)),
            pltpu.SemaphoreType.DMA((11, UNITS)),
            pltpu.SemaphoreType.DMA((2, 9)),
            pltpu.SemaphoreType.DMA((2, 4)),
            pltpu.SemaphoreType.DMA((2, 5)),
            pltpu.SemaphoreType.DMA((3,)),
            pltpu.SemaphoreType.REGULAR((3,)),
        ],
        compiler_params=pltpu.CompilerParams(
            collective_id=0, has_side_effects=True, vmem_limit_bytes=VMEM_LIMIT
        ),
        name="layer",
    )(jnp.pad(tokens, pad), jnp.pad(cotangent, pad), kbias, live, p_att, p_exp, p_shr, p_vec)

    block_output = o_blk[:, :local_len]
    token_gradient = o_tok[:, :local_len]
    grad_attention = o_g[0:4].transpose(2, 0, 1, 3).reshape(r, 4 * width).astype(F32)
    grad_expand = o_g[4:8].transpose(2, 1, 0, 3).reshape(r, 2, 2, dp_n, r).transpose(0, 3, 1, 2, 4)
    grad_expand = grad_expand.reshape(r, 4 * width).astype(F32)
    grad_shrink = o_g[8:12].reshape(2, 2, 2, r, UNIT).transpose(2, 1, 3, 0, 4).reshape(4 * r, width).astype(F32)
    hidden_sums = o_vec[8:12].reshape(2, 2, dp_n, r).transpose(2, 0, 1, 3).reshape(4, width)
    grad_vector = jnp.concatenate([o_vec[0:8], hidden_sums], 0).reshape(dp_n, vec_len)
    grad_vector = lax.dynamic_index_in_dim(grad_vector, d, 0, keepdims=False)

    attention_out = adamw(
        grad_attention, attention_moment, attention_square, attention_weights, RATE_MATRIX, DECAY_MATRIX
    )
    expand_out = adamw(grad_expand, expand_moment, expand_square, expand_weights, RATE_MATRIX, DECAY_MATRIX)
    shrink_out = adamw(grad_shrink, shrink_moment, shrink_square, shrink_weights, RATE_MATRIX, DECAY_MATRIX)
    vector_out = adamw(grad_vector, vector_moment, vector_square, vector_params, RATE_VECTOR, 0.0)
    return (block_output, token_gradient, *attention_out, *expand_out, *shrink_out, *vector_out)


VMEM_LIMIT = 62 * 2**20


def solution(mesh):
    split = P("dp", "seq", None)
    rows = P("dp", None)
    flat = P("dp")
    return jax.shard_map(
        body,
        mesh=mesh,
        in_specs=(split, split, rows, rows, rows, rows, flat) + (rows,) * 6 + (flat, flat),
        out_specs=(split, split) + (rows,) * 12 + (flat,) * 4,
        check_vma=False,
    )
```

```python
import functools

import jax
import jax.numpy as jnp
from jax import lax
from jax.experimental import pallas as pl
from jax.experimental.pallas import tpu as pltpu
from jax.sharding import PartitionSpec as P

HEAD_DIM = 64
STEP = 5
EPS_NORM = 1e-05
BETA_ONE = 0.5
BETA_TWO = 0.5
EPS_ADAM = 1e-08
RATE_MATRIX = 0.05
RATE_VECTOR = 0.2
DECAY_MATRIX = 0.1
SLOPE = 1.702

BF16 = jnp.bfloat16
F32 = jnp.float32
MESH = pl.DeviceIdType.MESH

UNIT = 512
EDGE = 128
WINDOW = UNIT - EDGE
UNITS = 12
SLOTS = 8
PAIR = 128


def dot(a, b):
    return jnp.dot(a, b, preferred_element_type=F32)


def dot_rows(a, b):
    return lax.dot_general(a, b, (((0,), (0,)), ((), ())), preferred_element_type=F32)


def dot_cols(a, b):
    return lax.dot_general(a, b, (((1,), (1,)), ((), ())), preferred_element_type=F32)


def unit_rows(x):
    centred = x - jnp.mean(x, -1, keepdims=True)
    rstd = lax.rsqrt(jnp.mean(centred * centred, -1, keepdims=True) + EPS_NORM)
    return centred * rstd, rstd


def norm_back(grad_normed, unit, rstd, gain):
    g = grad_normed * gain
    return rstd * (g - jnp.mean(g, -1, keepdims=True) - unit * jnp.mean(g * unit, -1, keepdims=True))


def fold8(v):
    return jnp.sum(v.reshape(v.shape[0] // 8, 8, v.shape[1]), 0)


def layer_kernel(
    line, vec_len,
    tok, cot, kbias, p_vec, p_att, p_exp, p_shr,
    o_blk, o_tok, o_att, o_exp, o_shr, o_vec,
    w, w_oth, g, rx, ry, rz, s_own, s_oth, f_own,
    vec_all, vec, bias_h, vg, vr, vz,
    tok_own, cot_own,
    n1, go, qkv, att, lse, resid, n2, act, fac, own_p, send_p, recv_p, recv_m, dst_p,
    gb, tr, tr_att, dk_acc, dv_acc,
    ag, rs, sib, wo, xe, vs, fill, credit,
):
    dp_n = 2 * line
    r = w.shape[3]
    block = tok.shape[1]
    own = 2 * block
    rows = 2 * own
    width = tok.shape[2]
    half = UNIT
    d = lax.axis_index("dp")
    s = lax.axis_index("seq")
    zi, yi = d // 2, d % 2
    x, c = s // 2, s % 2
    sibling = (d, x * 2 + 1 - c)
    x_neigh = (d, (1 - x) * 2 + c)
    y_neigh = (zi * 2 + 1 - yi, s)

    def z_peer(o):
        return (lax.rem(zi + o, line) * 2 + yi, s)

    my_rows = pl.ds(pl.multiple_of(c * own, own), own)
    oth_rows = pl.ds(pl.multiple_of((1 - c) * own, own), own)
    my_half = pl.ds(pl.multiple_of(c * half, half), half)
    oth_half = pl.ds(pl.multiple_of((1 - c) * half, half), half)
    win = pl.ds(pl.multiple_of(x * EDGE, EDGE), WINDOW)
    mine = pl.ds(pl.multiple_of(x * WINDOW, EDGE), EDGE)
    theirs = pl.ds(pl.multiple_of((1 - x) * WINDOW, EDGE), EDGE)
    my_block = pl.ds(pl.multiple_of(x * block, block), block)
    oth_block = pl.ds(pl.multiple_of((1 - x) * block, block), block)

    def remote(src, dst, send, recv, to):
        return pltpu.make_async_remote_copy(
            src_ref=src, dst_ref=dst, send_sem=send, recv_sem=recv, device_id=to, device_id_type=MESH
        )

    def wait_bytes(ref, sem):
        pltpu.make_async_copy(ref, ref, sem).wait()

    wide = r % 128 == 0

    def unit_parts(u, core):
        if u < 4:
            return [((slice(None), pl.ds(pl.multiple_of(n * width + core * half + u * PAIR, PAIR), PAIR)), n * PAIR, PAIR)
                    for n in range(4)]
        if u < 8:
            if not wide:
                return None
            first = (u - 4) * UNIT
            return [((slice(None), pl.ds(pl.multiple_of((n % width // r) * 4 * r + core * 2 * r + n // width * r, r), r)), n - first, r)
                    for n in range(first, first + UNIT, r)]
        h, j = (u - 8) // 2, (u - 8) % 2
        return [((pl.ds(pl.multiple_of(core * 2 * r + h * r, r), r), slice(j * UNIT, (j + 1) * UNIT)), 0, UNIT)]

    def stage(u):
        n = u % 4
        return (own_p, send_p, recv_m)[u // 4].at[(n // 2) * r : (n // 2 + 1) * r, (n % 2) * UNIT : (n % 2 + 1) * UNIT]

    for u in range(UNITS):
        parts = unit_parts(u, c)
        source = (p_att, p_exp, p_shr)[u // 4]
        if parts is None:
            pltpu.make_async_copy(source.at[u - 4], stage(u), fill.at[u]).start()
        else:
            for at, first, size in parts:
                pltpu.make_async_copy(source.at[at], stage(u).at[:, first : first + size], fill.at[u]).start()

    vec_all[d] = p_vec[...]
    act[:block, :width] = tok[1 - x]
    act[:block, width:] = cot[1 - x]
    tok_own[my_block] = tok[x]
    cot_own[my_block] = cot[x]

    barrier = pltpu.get_barrier_semaphore()

    def greet(o, carry):
        pl.semaphore_signal(barrier, inc=1, device_id=(lax.rem(d + o, dp_n), s), device_id_type=MESH)
        return carry

    lax.fori_loop(1, dp_n, greet, 0)
    pl.semaphore_signal(barrier, inc=1, device_id=sibling, device_id_type=MESH)
    pl.semaphore_signal(barrier, inc=1, device_id=x_neigh, device_id_type=MESH)
    pl.semaphore_wait(barrier, dp_n + 1)

    def send_vec(o, carry):
        remote(p_vec, vec_all.at[d], vs.at[0, 0], vs.at[1, 0], (lax.rem(d + o, dp_n), s)).start()
        return carry

    lax.fori_loop(1, dp_n, send_vec, 0)
    x_copies = [
        remote(act.at[:block, :width], tok_own.at[my_block], xe.at[0, 0], xe.at[1, 0], x_neigh),
        remote(act.at[:block, width:], cot_own.at[my_block], xe.at[0, 1], xe.at[1, 1], x_neigh),
    ]
    for copy in x_copies:
        copy.start()

    def ag_z(u):
        wait_bytes(stage(u), fill.at[u])
        w[u, zi, yi, :, win] = stage(u)[:, win].astype(BF16)
        for o in range(1, line):
            part = w.at[u, zi, yi, :, win]
            remote(part, part, ag.at[0, u], ag.at[1, u], z_peer(o)).start()

    def ag_y_copy(u):
        part = w.at[u, :, yi, :, win]
        return remote(part, part, ag.at[2, u], ag.at[3, u], y_neigh)

    def ag_x_copy(u):
        part = w.at[u, :, :, :, mine]
        return remote(part, part, ag.at[4, u], ag.at[5, u], x_neigh)

    def z_bytes(u):
        return w.at[u, pl.ds(0, line - 1), yi, :, win]

    def ag_y(u):
        wait_bytes(z_bytes(u), ag.at[1, u])
        ag_y_copy(u).start()

    def ag_x(u):
        ag_y_copy(u).wait_recv()
        ag_x_copy(u).start()

    def ag_end(u):
        ag_x_copy(u).wait_recv()

    steps = []
    for t in range(UNITS + 2):
        def step(t=t):
            if t + 2 < UNITS:
                ag_z(t + 2)
            if t < UNITS:
                ag_y(t)
            if 0 <= t - 1 < UNITS:
                ag_x(t - 1)
            if 0 <= t - 2 < UNITS:
                ag_end(t - 2)
        steps.append(step)
    ag_z(0)
    ag_z(1)
    done = [0]

    def ag_step():
        if done[0] < len(steps):
            steps[done[0]]()
            done[0] += 1

    def ag_until(u):
        while done[0] < min(u + 3, len(steps)):
            ag_step()

    wait_bytes(vec_all.at[pl.ds(0, dp_n - 1)], vs.at[1, 0])
    grain = 128 if vec_len % 128 == 0 else 64

    def vec_lanes(first):
        parts = []
        for e in range(first, first + 128, grain):
            o = e % vec_len
            parts.append(vec_all[e // vec_len, o // 128 : o // 128 + 1, o % 128 : o % 128 + grain])
        return parts[0] if len(parts) == 1 else jnp.concatenate(parts, 1)

    for row in range(12):
        for lane in range(0, width, 128):
            vec[row : row + 1, lane : lane + 128] = vec_lanes(row * width + lane)

    def hidden_bias(core):
        parts = []
        for h in range(2):
            for shard in range(dp_n):
                n = shard * 4 * r + core * 2 * r + h * r
                parts.append(vec[8 + n // width : 9 + n // width, n % width : n % width + r])
        return jnp.concatenate(parts, 1)

    bias_h[...] = jnp.where(c == 0, hidden_bias(0), hidden_bias(1))

    x_copies[0].wait()
    x_copies[1].wait()

    def live(to):
        return jnp.where(kbias[to, 0:1] < 0, 0.0, 1.0)

    chunk = 32
    gain_one, shift_one = vec[0:1, :], vec[1:2, :]

    def norm_one(i, carry):
        at = pl.ds(pl.multiple_of(i * chunk, chunk), chunk)
        to = pl.ds(pl.multiple_of(c * own + i * chunk, chunk), chunk)
        unit, _ = unit_rows(tok_own[at, :].astype(F32))
        n1[to, :] = (unit * gain_one + shift_one).astype(BF16)
        go[to, :] = (cot_own[at, :].astype(F32) * live(to)).astype(BF16)
        return carry

    lax.fori_loop(0, own // chunk, norm_one, 0)
    n1_copy = remote(n1.at[my_rows], n1.at[my_rows], sib.at[0, 0], sib.at[1, 0], sibling)
    n1_copy.start()
    go_copy = remote(go.at[my_rows], go.at[my_rows], sib.at[0, 1], sib.at[1, 1], sibling)
    go_copy.start()
    n1_copy.wait_recv()

    low_lane = lax.broadcasted_iota(jnp.int32, (PAIR, PAIR), 1) < HEAD_DIM
    low_row = lax.broadcasted_iota(jnp.int32, (PAIR, PAIR), 0) < HEAD_DIM
    q_chunks = rows // PAIR

    def two_heads(v):
        zero = jnp.zeros_like(v)
        return jnp.concatenate([jnp.where(low_lane, v, zero), jnp.where(low_lane, zero, v)], 0)

    qkv_lanes = 3 * PAIR

    def pair_lanes(p):
        return tuple(slice(p * qkv_lanes + n * PAIR, p * qkv_lanes + (n + 1) * PAIR) for n in range(3))

    def att_lanes(p):
        return pl.ds(pl.multiple_of(c * half + p * PAIR, PAIR), PAIR)

    def wo_copy(p):
        part = slice(UNIT - PAIR, UNIT)
        return remote(
            w.at[p, :, :, :, part], w_oth.at[:, :, :, p * PAIR : (p + 1) * PAIR], wo.at[0, p], wo.at[1, p], sibling
        )

    def attend_forward(p):
        q_at, k_at, v_at = pair_lanes(p)
        out = dot(n1[...], w[p, :, :, :, :qkv_lanes].reshape(dp_n * r, qkv_lanes))
        queries = (out[:, :PAIR] + vec[4:5, att_lanes(p)]).astype(BF16)
        qkv[:, q_at] = queries * jnp.asarray(HEAD_DIM**-0.5, BF16)
        qkv[:, k_at] = out[:, PAIR : 2 * PAIR].astype(BF16)
        qkv[:, v_at] = (out[:, 2 * PAIR :] + vec[5:6, att_lanes(p)]).astype(BF16)

        def some(j, carry):
            at = pl.ds(pl.multiple_of(j * PAIR, PAIR), PAIR)
            mask = kbias[...]
            scores = dot_cols(qkv[:, k_at], two_heads(qkv[at, q_at])) + jnp.concatenate([mask, mask], 1)
            highest = jnp.max(scores, 0, keepdims=True)
            raised = jnp.exp(scores - highest)
            total = jnp.sum(raised, 0, keepdims=True)
            out = dot_rows(qkv[:, v_at], raised.astype(BF16)) / total
            out = jnp.where(low_row, out[:, :PAIR], out[:, PAIR:])
            att[at, att_lanes(p)] = out.T.astype(BF16)
            lse[pl.ds(p * q_chunks + j, 1), :] = highest + jnp.log(total)
            return carry

        lax.fori_loop(0, q_chunks, some, 0)

    for p in range(4):
        ag_until(p)
        wo_copy(p).start()
        attend_forward(p)
    att_copy = remote(att.at[:, my_half], att.at[:, my_half], sib.at[0, 2], sib.at[1, 2], sibling)
    att_copy.start()
    for p in range(4):
        wo_copy(p).wait_recv()
    att_copy.wait_recv()

    bias_att = vec[6:7, :]
    mixed = att[my_rows, :]

    def own_out(z):
        return jnp.concatenate([w[p, z, :, :, UNIT - PAIR :].reshape(-1, PAIR) for p in range(4)], 1)

    resid[:, my_half] = dot(mixed, own_out(slice(None)))
    resid[:, oth_half] = dot(mixed, w_oth[...].reshape(dp_n * r, UNIT))
    gain_two, shift_two = vec[2:3, :], vec[3:4, :]

    def norm_two(i, carry):
        at = pl.ds(pl.multiple_of(i * chunk, chunk), chunk)
        to = pl.ds(pl.multiple_of(c * own + i * chunk, chunk), chunk)
        res = resid[at, :] + tok_own[at, :].astype(F32) + bias_att
        resid[at, :] = res
        unit, _ = unit_rows(res)
        n2[to, :] = (unit * gain_two + shift_two).astype(BF16)
        return carry

    lax.fori_loop(0, own // chunk, norm_two, 0)
    n2_copy = remote(n2.at[my_rows], n2.at[my_rows], sib.at[0, 4], sib.at[1, 4], sibling)
    n2_copy.start()
    n2_copy.wait()

    tile = 256
    for u in range(4):
        ag_until(4 + u)

        def expand(i, carry, u=u):
            lane = pl.ds(pl.multiple_of(i * tile, tile), tile)
            to = pl.ds(pl.multiple_of(u * UNIT + i * tile, tile), tile)
            hidden = dot(n2[...], w[4 + u, :, :, :, lane].reshape(dp_n * r, tile)) + bias_h[:, to]
            gate = jax.nn.sigmoid(SLOPE * hidden)
            act[:, to] = (hidden * gate).astype(BF16)
            fac[:, to] = (gate + SLOPE * hidden * gate * (1.0 - gate)).astype(BF16)
            return carry

        lax.fori_loop(0, UNIT // tile, expand, 0)
    go_copy.wait_recv()

    def rs_x_copy(k, u):
        return remote(g.at[k, :, :, :, theirs], rx.at[k], rs.at[0, u], rs.at[1, u], x_neigh)

    def rs_y_copy(k, u):
        return remote(g.at[k, :, 1 - yi, :, win], ry.at[k], rs.at[2, u], rs.at[3, u], y_neigh)

    def rs_2_copy(k, u):
        return remote(s_own.at[k], s_oth.at[k], rs.at[6, u], rs.at[7, u], x_neigh)

    def rs_f_copies(k, u):
        parts = unit_parts(u, c)
        result = (o_att, o_exp, o_shr)[u // 4]
        if parts is None:
            pairs = [(f_own.at[k], result.at[u - 4, c])]
        else:
            pairs = [(f_own.at[k, :, first : first + size], result.at[at]) for at, first, size in parts]
        return [remote(a, b, rs.at[8, u], rs.at[9, u], sibling) for a, b in pairs] + [
            pltpu.make_async_copy(a, b, rs.at[10, u]) for a, b in pairs
        ]

    def rs_y(k, u):
        rs_x_copy(k, u).wait_recv()

        def add(z, carry):
            g[k, z, :, :, mine] = (g[k, z, :, :, mine].astype(F32) + rx[k, z].astype(F32)).astype(BF16)
            return carry

        lax.fori_loop(0, line, add, 0)
        rs_y_copy(k, u).start()

    def rs_z(k, u):
        rs_y_copy(k, u).wait_recv()

        def add(z, carry):
            g[k, z, yi, :, win] = (g[k, z, yi, :, win].astype(F32) + ry[k, z].astype(F32)).astype(BF16)
            return carry

        lax.fori_loop(0, line, add, 0)
        for o in range(1, line):
            z = lax.rem(zi + o, line)
            remote(g.at[k, z, yi, :, win], rz.at[k, o - 1], rs.at[4, u], rs.at[5, u], z_peer(o)).start()

    def rs_2(k, u):
        wait_bytes(rz.at[k], rs.at[5, u])
        total = g[k, zi, yi, :, win].astype(F32)
        for o in range(1, line):
            total = total + rz[k, o - 1].astype(F32)
        s_own[k] = total.astype(BF16)
        rs_2_copy(k, u).start()

    def rs_f(k, u):
        rs_2_copy(k, u).wait_recv()
        here, there = s_own[k], s_oth[k]
        first = jnp.where(x == 0, here, there)
        last = jnp.where(x == 0, there, here)
        f_own[k, :, :EDGE] = first[:, :EDGE]
        f_own[k, :, EDGE:WINDOW] = (first[:, EDGE:].astype(F32) + last[:, : WINDOW - EDGE].astype(F32)).astype(BF16)
        f_own[k, :, WINDOW:] = last[:, WINDOW - EDGE :]
        for copy in rs_f_copies(k, u):
            copy.start()

    def rs_end(k, u):
        rs_x_copy(k, u).wait_send()
        rs_y_copy(k, u).wait_send()
        wait_bytes(rz.at[k], rs.at[4, u])
        rs_2_copy(k, u).wait_send()
        for n in (8, 9, 10):
            wait_bytes(f_own.at[k], rs.at[n, u])

    flight = []

    def send_unit(k, u):
        rs_x_copy(k, u).start()
        flight.append([0, k, u])

    def grad_unit(k, u, left, right):
        g[k] = dot(left, right).reshape(g.shape[1:]).astype(BF16)
        send_unit(k, u)

    stages = [rs_y, rs_z, rs_2, rs_f, rs_end]

    def rs_tick():
        for item in list(flight):
            n, k, u = item
            stages[n](k, u)
            item[0] = n + 1
            if item[0] == len(stages):
                flight.remove(item)
                if u == UNITS - 1:
                    give_credit()

    def give_credit():
        pl.semaphore_signal(credit.at[0], inc=1, device_id=x_neigh, device_id_type=MESH)
        pl.semaphore_signal(credit.at[1], inc=1, device_id=y_neigh, device_id_type=MESH)
        for o in range(1, line):
            pl.semaphore_signal(credit.at[2], inc=1, device_id=z_peer(o), device_id_type=MESH)

    def take_credit():
        pl.semaphore_wait(credit.at[0], 1)
        pl.semaphore_wait(credit.at[1], 1)
        pl.semaphore_wait(credit.at[2], line - 1)

    def transpose_into(dst, src, lanes_at):
        def move(i, carry):
            at = pl.ds(pl.multiple_of(i * 128, 128), 128)
            dst[at, :] = src[:, pl.ds(pl.multiple_of(lanes_at + i * 128, 128), 128)].T
            return carry

        lax.fori_loop(0, width // 128, move, 0)

    for h in range(2):
        transpose_into(tr, act, h * width)
        for j in range(2):
            k = 2 * h + j
            ag_step()
            grad_unit(k, 8 + k, tr[...], go[:, j * UNIT : (j + 1) * UNIT])
            if k > 0:
                rs_tick()

    ag_until(UNITS - 1)

    span = max(1, tile // (2 * r))

    def hidden_back(n, carry):
        z = n * span
        for h in range(2):
            total = None
            for j in range(2):
                part = w[8 + 2 * h + j, pl.ds(z, span)].reshape(span * 2 * r, UNIT)
                term = dot_cols(go[:, j * UNIT : (j + 1) * UNIT], part)
                total = term if total is None else total + term
            to = pl.ds(pl.multiple_of(h * width + n * (span * 2 * r), span * 2 * r), span * 2 * r)
            low = (total * fac[:, to].astype(F32)).astype(BF16)
            fac[:, to] = low
            sums = jnp.sum(fold8(low.astype(F32)), 0, keepdims=True)
            at = pl.ds(pl.multiple_of(n * (span * 2 * r), span * 2 * r), span * 2 * r)
            vg[pl.ds(8 + 2 * c + h, 1), at] = sums
        return carry

    vg[...] = jnp.zeros_like(vg)
    lax.fori_loop(0, line // span, hidden_back, 0)
    rs_tick()

    def back_partial(src, lanes, first, rows_at, dst):
        def back(n, carry):
            total = None
            for u in range(4):
                part = w[first + u, pl.ds(n * span, span), :, :, :lanes].reshape(span * 2 * r, lanes)
                term = dot_cols(src[rows_at, u * lanes : (u + 1) * lanes], part)
                total = term if total is None else total + term
            dst[:, pl.ds(pl.multiple_of(n * (span * 2 * r), span * 2 * r), span * 2 * r)] = total
            return carry

        lax.fori_loop(0, line // span, back, 0)

    back_partial(fac, UNIT, 4, oth_rows, send_p)
    p2_copy = remote(send_p, recv_p, sib.at[0, 5], sib.at[1, 5], sibling)
    p2_copy.start()
    back_partial(fac, UNIT, 4, my_rows, own_p)
    rs_tick()
    transpose_into(tr, n2, 0)
    for u in range(2):
        grad_unit(4 + u, 4 + u, tr[...], fac[:, u * UNIT : (u + 1) * UNIT])
        rs_tick()
    p2_copy.wait()

    zeros8 = jnp.zeros((8, width), F32)

    def norm_two_back(i, carry):
        at = pl.ds(pl.multiple_of(i * chunk, chunk), chunk)
        to = pl.ds(pl.multiple_of(c * own + i * chunk, chunk), chunk)
        unit, rstd = unit_rows(resid[at, :])
        gn = own_p[at, :] + recv_p[at, :]
        grad_out = go[to, :].astype(F32)
        gr = grad_out + norm_back(gn, unit, rstd, gain_two)
        own_p[at, :] = gr
        low = gr.astype(BF16)
        gb[to, :] = low
        a, b, e, f = carry
        return (a + fold8(gn * unit), b + fold8(gn), e + fold8(low.astype(F32)), f + fold8(grad_out))

    sums = lax.fori_loop(0, own // chunk, norm_two_back, (zeros8,) * 4)
    for row, v in zip((2, 3, 6, 7), sums):
        vg[row : row + 1, :] = jnp.sum(v, 0, keepdims=True)
    gb_copy = remote(gb.at[my_rows], gb.at[my_rows], sib.at[0, 6], sib.at[1, 6], sibling)
    gb_copy.start()

    for u in range(2, 4):
        grad_unit(4 + u, 4 + u, tr[...], fac[:, u * UNIT : (u + 1) * UNIT])
        rs_tick()
    gb_copy.wait_recv()
    rs_tick()
    transpose_into(tr, n1, 0)
    transpose_into(tr_att, att, 0)

    head_rows = pl.ds(c * (line // 2), line // 2)
    n2[:, :UNIT] = (
        dot_cols(gb[:, my_half], own_out(head_rows)) + dot_cols(gb[:, oth_half], w_oth[head_rows].reshape(half, UNIT))
    ).astype(BF16)

    def attend_backward(p):
        q_at, k_at, v_at = pair_lanes(p)
        own_lanes = slice(p * PAIR, (p + 1) * PAIR)
        dk_acc[...] = jnp.zeros_like(dk_acc)
        dv_acc[...] = jnp.zeros_like(dv_acc)

        def some(j, carry):
            at = pl.ds(pl.multiple_of(j * PAIR, PAIR), PAIR)
            both = two_heads(qkv[at, q_at])
            grads = two_heads(n2[at, own_lanes])
            mask = kbias[...]
            scores = dot_cols(qkv[:, k_at], both) + jnp.concatenate([mask, mask], 1)
            chance = jnp.exp(scores - lse[pl.ds(p * q_chunks + j, 1), :])
            dv_acc[...] += dot(chance.astype(BF16), grads)
            grad_chance = dot_cols(qkv[:, v_at], grads)
            inner = jnp.sum(chance * grad_chance, 0, keepdims=True)
            grad_scores = (chance * (grad_chance - inner)).astype(BF16)
            dk_acc[...] += dot(grad_scores, both)
            out = dot_rows(qkv[:, k_at], grad_scores)
            out = jnp.where(low_row, out[:, :PAIR], out[:, PAIR:]) * HEAD_DIM**-0.5
            qkv[at, q_at] = out.T.astype(BF16)
            return carry

        lax.fori_loop(0, q_chunks, some, 0)
        qkv[:, k_at] = dk_acc[...].astype(BF16)
        qkv[:, v_at] = dv_acc[...].astype(BF16)
        vg[4:5, att_lanes(p)] = jnp.sum(fold8(qkv[:, q_at].astype(F32)), 0, keepdims=True)
        vg[5:6, att_lanes(p)] = jnp.sum(fold8(qkv[:, v_at].astype(F32)), 0, keepdims=True)

    for p in range(4):
        attend_backward(p)
        if p == 0:
            take_credit()
        g[p, :, :, :, :qkv_lanes] = (
            dot(tr[...], qkv[:, p * qkv_lanes : (p + 1) * qkv_lanes]).reshape(line, 2, r, qkv_lanes).astype(BF16)
        )
        g[p, :, :, :, qkv_lanes:] = dot(tr_att[...], gb[:, att_lanes(p)]).reshape(line, 2, r, PAIR).astype(BF16)
        send_unit(p, p)
        rs_tick()

    back_partial(qkv, qkv_lanes, 0, oth_rows, send_p)
    p1_copy = remote(send_p, recv_p, sib.at[0, 7], sib.at[1, 7], sibling)
    p1_copy.start()
    back_partial(qkv, qkv_lanes, 0, my_rows, dst_p)
    rs_tick()
    p1_copy.wait()

    def norm_one_back(i, carry):
        at = pl.ds(pl.multiple_of(i * chunk, chunk), chunk)
        unit, rstd = unit_rows(tok_own[at, :].astype(F32))
        gn = dst_p[at, :] + recv_p[at, :]
        out = own_p[at, :] + norm_back(gn, unit, rstd, gain_one)
        tok_own[at, :] = out.astype(BF16)
        a, b = carry
        return (a + fold8(gn * unit), b + fold8(gn))

    sums = lax.fori_loop(0, own // chunk, norm_one_back, (zeros8,) * 2)
    for row, v in zip((0, 1), sums):
        vg[row : row + 1, :] = jnp.sum(v, 0, keepdims=True)
    o_tok[x] = tok_own[my_block, :]
    tok_copy = remote(tok_own.at[oth_block], o_tok.at[x], xe.at[0, 3], xe.at[1, 3], x_neigh)
    tok_copy.start()
    rs_tick()

    def branch(dst, rows_at, add):
        def out(n, carry):
            lane = pl.ds(pl.multiple_of(n * tile, tile), tile)
            for j in range(2):
                total = None
                for h in range(2):
                    part = w[8 + 2 * h + j, :, :, :, lane].reshape(dp_n * r, tile)
                    term = dot(act[rows_at, h * width : (h + 1) * width], part)
                    total = term if total is None else total + term
                to = pl.ds(pl.multiple_of(j * UNIT + n * tile, tile), tile)
                dst[:, to] = dst[:, to] + total if add else total
            return carry

        lax.fori_loop(0, UNIT // tile, out, 0)

    branch(send_p, oth_rows, False)
    m_copy = remote(send_p, recv_m, sib.at[0, 8], sib.at[1, 8], sibling)
    m_copy.start()
    branch(resid, my_rows, True)
    m_copy.wait()

    bias_out = vec[7:8, :]

    def finish_block(i, carry):
        at = pl.ds(pl.multiple_of(i * chunk, chunk), chunk)
        out = live(pl.ds(pl.multiple_of(c * own + i * chunk, chunk), chunk)) * (resid[at, :] + recv_m[at, :] + bias_out)
        cot_own[at, :] = out.astype(BF16)
        return carry

    lax.fori_loop(0, own // chunk, finish_block, 0)
    o_blk[x] = cot_own[my_block, :]
    blk_copy = remote(cot_own.at[oth_block], o_blk.at[x], xe.at[0, 2], xe.at[1, 2], x_neigh)
    blk_copy.start()

    for n, to in enumerate((sibling, x_neigh, y_neigh)):
        copy = remote(vg, vr.at[n], vs.at[0, 1 + n], vs.at[1, 1 + n], to)
        copy.start()
        copy.wait()
        vg[...] += vr[n]
        rs_tick()

    def send_vz(o, carry):
        remote(vg, vz.at[zi], vs.at[0, 4], vs.at[1, 4], (lax.rem(zi + o, line) * 2 + yi, s)).start()
        return carry

    lax.fori_loop(1, line, send_vz, 0)
    vz[zi] = vg[...]
    wait_bytes(vz.at[pl.ds(0, line - 1)], vs.at[1, 4])
    wait_bytes(vz.at[pl.ds(0, line - 1)], vs.at[0, 4])
    o_vec[...] = lax.fori_loop(1, line, lambda i, t: t + vz[i], vz[0])

    while flight:
        rs_tick()

    blk_copy.wait()
    tok_copy.wait()
    wait_bytes(vec_all.at[pl.ds(0, dp_n - 1)], vs.at[0, 0])
    for copy in [n1_copy, go_copy, att_copy, gb_copy] + [wo_copy(p) for p in range(4)]:
        copy.wait_send()
    for u in range(UNITS):
        wait_bytes(z_bytes(u), ag.at[0, u])
        ag_y_copy(u).wait_send()
        ag_x_copy(u).wait_send()


def adamw(grad, moment, square, weight, rate, decay):
    momentum = BETA_ONE * moment + (1.0 - BETA_ONE) * grad
    variance = BETA_TWO * square + (1.0 - BETA_TWO) * grad * grad
    first_fix = 1.0 - BETA_ONE**STEP
    second_fix = 1.0 - BETA_TWO**STEP
    direction = momentum / first_fix / (jnp.sqrt(variance / second_fix) + EPS_ADAM)
    updated = weight - rate * (direction + decay * weight)
    return (momentum, variance, updated, updated.astype(BF16))


def body(
    tokens, cotangent, key_mask,
    attention_weights, expand_weights, shrink_weights, vector_params,
    attention_moment, attention_square, expand_moment, expand_square,
    shrink_moment, shrink_square, vector_moment, vector_square,
):
    dp_n = lax.axis_size("dp")
    line = dp_n // 2
    d = lax.axis_index("dp")
    place = lax.axis_index("seq")
    x, c = place // 2, place % 2
    _, local_len, width = tokens.shape
    r = width // dp_n
    block = -(-local_len // 16) * 16
    own, rows = 2 * block, 4 * block
    pad = ((0, 0), (0, block - local_len), (0, 0))

    keep = lax.dynamic_index_in_dim(key_mask, x, 0, keepdims=False).reshape(2, 2, local_len)
    keep = jnp.pad(keep.transpose(1, 0, 2), ((0, 0), (0, 0), pad[1])).reshape(2, own)
    kbias = jnp.broadcast_to(jnp.where(keep > 0, 0.0, -1e30).astype(F32).reshape(rows, 1), (rows, PAIR))
    p_exp = expand_weights
    if r % 128:
        p_exp = lax.dynamic_index_in_dim(expand_weights.reshape(r, dp_n, 2, 2, r), c, 2, keepdims=False)
        p_exp = p_exp.transpose(2, 0, 1, 3).reshape(2, r, 2, UNIT).transpose(0, 2, 1, 3).reshape(4, r, UNIT)
    vec_len = vector_params.shape[0]
    vec_rows = -(-vec_len // 1024) * 8
    p_vec = jnp.pad(vector_params.astype(BF16).astype(F32), (0, vec_rows * 128 - vec_len)).reshape(vec_rows, 128)

    vmem = pl.BlockSpec(memory_space=pltpu.VMEM)
    hbm = pl.BlockSpec(memory_space=pl.ANY)
    padded = jax.ShapeDtypeStruct((2, block, width), BF16)
    o_blk, o_tok, o_att, o_exp, o_shr, o_vec = pl.pallas_call(
        functools.partial(layer_kernel, line, vec_len),
        out_shape=(
            padded,
            padded,
            jax.ShapeDtypeStruct((r, 4 * width), BF16),
            jax.ShapeDtypeStruct((4, 2, r, UNIT) if r % 128 else (r, 4 * width), BF16),
            jax.ShapeDtypeStruct((4 * r, width), BF16),
            jax.ShapeDtypeStruct((16, width), F32),
        ),
        in_specs=[vmem] * 4 + [hbm] * 3,
        out_specs=(vmem, vmem, hbm, hbm, hbm, vmem),
        scratch_shapes=[
            pltpu.VMEM((UNITS, line, 2, r, UNIT), BF16),
            pltpu.VMEM((line, 2, r, UNIT), BF16),
            pltpu.VMEM((SLOTS, line, 2, r, UNIT), BF16),
            pltpu.VMEM((SLOTS, line, 2, r, EDGE), BF16),
            pltpu.VMEM((SLOTS, line, r, WINDOW), BF16),
            pltpu.VMEM((SLOTS, line - 1, r, WINDOW), BF16),
            pltpu.VMEM((SLOTS, r, WINDOW), BF16),
            pltpu.VMEM((SLOTS, r, WINDOW), BF16),
            pltpu.VMEM((SLOTS, r, UNIT), BF16),
            pltpu.VMEM((dp_n, vec_rows, 128), F32),
            pltpu.VMEM((16, width), F32),
            pltpu.VMEM((1, 2 * width), F32),
            pltpu.VMEM((16, width), F32),
            pltpu.VMEM((3, 16, width), F32),
            pltpu.VMEM((line, 16, width), F32),
            pltpu.VMEM((own, width), BF16),
            pltpu.VMEM((own, width), BF16),
            pltpu.VMEM((rows, width), BF16),
            pltpu.VMEM((rows, width), BF16),
            pltpu.VMEM((rows, 3 * UNIT), BF16),
            pltpu.VMEM((rows, width), BF16),
            pltpu.VMEM(((rows // PAIR) * (UNIT // PAIR), 2 * PAIR), F32),
            pltpu.VMEM((own, width), F32),
            pltpu.VMEM((rows, width), BF16),
            pltpu.VMEM((rows, 2 * width), BF16),
            pltpu.VMEM((rows, 2 * width), BF16),
            pltpu.VMEM((own, width), F32),
            pltpu.VMEM((own, width), F32),
            pltpu.VMEM((own, width), F32),
            pltpu.VMEM((own, width), F32),
            pltpu.VMEM((own, width), F32),
            pltpu.VMEM((rows, width), BF16),
            pltpu.VMEM((width, rows), BF16),
            pltpu.VMEM((width, rows), BF16),
            pltpu.VMEM((rows, PAIR), F32),
            pltpu.VMEM((rows, PAIR), F32),
            pltpu.SemaphoreType.DMA((6, UNITS)),
            pltpu.SemaphoreType.DMA((11, UNITS)),
            pltpu.SemaphoreType.DMA((2, 9)),
            pltpu.SemaphoreType.DMA((2, 4)),
            pltpu.SemaphoreType.DMA((2, 4)),
            pltpu.SemaphoreType.DMA((2, 5)),
            pltpu.SemaphoreType.DMA((UNITS,)),
            pltpu.SemaphoreType.REGULAR((3,)),
        ],
        compiler_params=pltpu.CompilerParams(
            collective_id=0, has_side_effects=True, vmem_limit_bytes=VMEM_LIMIT
        ),
        name="layer",
    )(jnp.pad(tokens, pad), jnp.pad(cotangent, pad), kbias, p_vec, attention_weights, p_exp, shrink_weights)

    block_output = o_blk[:, :local_len]
    token_gradient = o_tok[:, :local_len]
    grad_attention, grad_shrink = o_att.astype(F32), o_shr.astype(F32)
    if r % 128:
        o_exp = o_exp.transpose(2, 1, 0, 3).reshape(r, 2, 2, dp_n, r).transpose(0, 3, 1, 2, 4).reshape(r, 4 * width)
    grad_expand = o_exp.astype(F32)
    hidden_sums = o_vec[8:12].reshape(2, 2, dp_n, r).transpose(2, 0, 1, 3).reshape(4, width)
    grad_vector = jnp.concatenate([o_vec[0:8], hidden_sums], 0).reshape(dp_n, vec_len)
    grad_vector = lax.dynamic_index_in_dim(grad_vector, d, 0, keepdims=False)

    attention_out = adamw(
        grad_attention, attention_moment, attention_square, attention_weights, RATE_MATRIX, DECAY_MATRIX
    )
    expand_out = adamw(grad_expand, expand_moment, expand_square, expand_weights, RATE_MATRIX, DECAY_MATRIX)
    shrink_out = adamw(grad_shrink, shrink_moment, shrink_square, shrink_weights, RATE_MATRIX, DECAY_MATRIX)
    vector_out = adamw(grad_vector, vector_moment, vector_square, vector_params, RATE_VECTOR, 0.0)
    return (block_output, token_gradient, *attention_out, *expand_out, *shrink_out, *vector_out)


VMEM_LIMIT = 62 * 2**20


def solution(mesh):
    split = P("dp", "seq", None)
    rows = P("dp", None)
    flat = P("dp")
    return jax.shard_map(
        body,
        mesh=mesh,
        in_specs=(split, split, rows, rows, rows, rows, flat) + (rows,) * 6 + (flat, flat),
        out_specs=(split, split) + (rows,) * 12 + (flat,) * 4,
        check_vma=False,
    )
```

```python
import functools

import jax
import jax.numpy as jnp
from jax import lax
from jax.experimental import pallas as pl
from jax.experimental.pallas import tpu as pltpu
from jax.sharding import PartitionSpec as P

HEAD_DIM = 64
STEP = 5
EPS_NORM = 1e-05
BETA_ONE = 0.5
BETA_TWO = 0.5
EPS_ADAM = 1e-08
RATE_MATRIX = 0.05
RATE_VECTOR = 0.2
DECAY_MATRIX = 0.1
SLOPE = 1.702

BF16 = jnp.bfloat16
F32 = jnp.float32
MESH = pl.DeviceIdType.MESH

UNIT = 512
BLOCKS = 4
RS_EDGE = 1
RS_WINDOW = BLOCKS - RS_EDGE
UNITS = 12
SLOTS = 8
PAIR = 128


def dot(a, b):
    return jnp.dot(a, b, preferred_element_type=F32)


def dot_rows(a, b):
    return lax.dot_general(a, b, (((0,), (0,)), ((), ())), preferred_element_type=F32)


def dot_cols(a, b):
    return lax.dot_general(a, b, (((1,), (1,)), ((), ())), preferred_element_type=F32)


def unit_rows(x):
    centred = x - jnp.mean(x, -1, keepdims=True)
    rstd = lax.rsqrt(jnp.mean(centred * centred, -1, keepdims=True) + EPS_NORM)
    return centred * rstd, rstd


def norm_back(grad_normed, unit, rstd, gain):
    g = grad_normed * gain
    return rstd * (g - jnp.mean(g, -1, keepdims=True) - unit * jnp.mean(g * unit, -1, keepdims=True))


def fold8(v):
    return jnp.sum(v.reshape(v.shape[0] // 8, 8, v.shape[1]), 0)


def layer_kernel(
    line, vec_len,
    tok, cot, kbias, p_vec, p_att, p_exp, p_shr,
    o_blk, o_tok, o_att, o_exp, o_shr, o_vec,
    w, w_oth, g, rx, ry, rz, s_own, s_oth, f_own,
    vec_all, vec, bias_h, vg, vr, vz,
    tok_own, cot_own,
    n1, go, qkv, att, lse, resid, n2, act, fac, own_p, send_p, recv_p, recv_m, dst_p,
    gb, tr, tr_att, dk_acc, dv_acc,
    ag, rs, sib, wo, xe, vs, fill, credit,
):
    dp_n = 2 * line
    r = w.shape[4]
    block = tok.shape[1]
    own = 2 * block
    rows = 2 * own
    width = tok.shape[2]
    half = UNIT
    d = lax.axis_index("dp")
    s = lax.axis_index("seq")
    zi, yi = d // 2, d % 2
    x, c = s // 2, s % 2
    sibling = (d, x * 2 + 1 - c)
    x_neigh = (d, (1 - x) * 2 + c)
    y_neigh = (zi * 2 + 1 - yi, s)

    def z_peer(o):
        return (lax.rem(zi + o, line) * 2 + yi, s)

    my_rows = pl.ds(pl.multiple_of(c * own, own), own)
    oth_rows = pl.ds(pl.multiple_of((1 - c) * own, own), own)
    my_half = pl.ds(pl.multiple_of(c * half, half), half)
    oth_half = pl.ds(pl.multiple_of((1 - c) * half, half), half)

    def window(edge):
        return pl.ds(x * edge, BLOCKS - edge)

    def mine(edge):
        return pl.ds(x * (BLOCKS - edge), edge)

    def theirs(edge):
        return pl.ds((1 - x) * (BLOCKS - edge), edge)

    def ag_edge(u):
        return 2 if u % 3 == 2 else 1

    my_block = pl.ds(pl.multiple_of(x * block, block), block)
    oth_block = pl.ds(pl.multiple_of((1 - x) * block, block), block)

    def remote(src, dst, send, recv, to):
        return pltpu.make_async_remote_copy(
            src_ref=src, dst_ref=dst, send_sem=send, recv_sem=recv, device_id=to, device_id_type=MESH
        )

    def wait_bytes(ref, sem):
        pltpu.make_async_copy(ref, ref, sem).wait()

    wide = r % 128 == 0

    def unit_parts(u, core):
        if u < 4:
            return [
                (slice(None), pl.ds(pl.multiple_of(n * width + core * half + u * PAIR, PAIR), PAIR)) for n in range(BLOCKS)
            ]
        if u < 8:
            if not wide:
                return None
            parts = []
            for n in range((u - 4) * UNIT, (u - 3) * UNIT, PAIR):
                h, shard, rest = n // width, n % width // r, n % r
                at = shard * 4 * r + core * 2 * r + h * r + rest
                parts.append((slice(None), pl.ds(pl.multiple_of(at, PAIR), PAIR)))
            return parts
        h, j = (u - 8) // 2, (u - 8) % 2
        held = pl.ds(pl.multiple_of(core * 2 * r + h * r, r), r)
        return [(held, slice(j * UNIT + n * PAIR, j * UNIT + (n + 1) * PAIR)) for n in range(BLOCKS)]

    def stage(u):
        n = u % 4
        return (own_p, send_p, recv_m)[u // 4].at[(n // 2) * r : (n // 2 + 1) * r, (n % 2) * UNIT : (n % 2 + 1) * UNIT]

    for u in range(UNITS):
        parts = unit_parts(u, c)
        source = (p_att, p_exp, p_shr)[u // 4]
        for n in range(BLOCKS):
            part = source.at[parts[n]] if parts else source.at[u - 4, n]
            pltpu.make_async_copy(part, stage(u).at[:, n * PAIR : (n + 1) * PAIR], fill.at[u]).start()

    vec_all[d] = p_vec[...]
    act[:block, :width] = tok[1 - x]
    act[:block, width:] = cot[1 - x]
    tok_own[my_block] = tok[x]
    cot_own[my_block] = cot[x]

    barrier = pltpu.get_barrier_semaphore()

    def greet(o, carry):
        pl.semaphore_signal(barrier, inc=1, device_id=(lax.rem(d + o, dp_n), s), device_id_type=MESH)
        return carry

    lax.fori_loop(1, dp_n, greet, 0)
    pl.semaphore_signal(barrier, inc=1, device_id=sibling, device_id_type=MESH)
    pl.semaphore_signal(barrier, inc=1, device_id=x_neigh, device_id_type=MESH)
    pl.semaphore_wait(barrier, dp_n + 1)

    def send_vec(o, carry):
        remote(p_vec, vec_all.at[d], vs.at[0, 0], vs.at[1, 0], (lax.rem(d + o, dp_n), s)).start()
        return carry

    lax.fori_loop(1, dp_n, send_vec, 0)
    x_copies = [
        remote(act.at[:block, :width], tok_own.at[my_block], xe.at[0, 0], xe.at[1, 0], x_neigh),
        remote(act.at[:block, width:], cot_own.at[my_block], xe.at[0, 1], xe.at[1, 1], x_neigh),
    ]
    for copy in x_copies:
        copy.start()

    def ag_z(u):
        edge = ag_edge(u)
        wait_bytes(stage(u), fill.at[u])
        for n in range(BLOCKS - edge):
            b = x * edge + n
            w[u, b, zi, yi] = stage(u)[:, pl.ds(pl.multiple_of(b * PAIR, PAIR), PAIR)].astype(BF16)
        part = w.at[u, window(edge), zi, yi]
        for o in range(1, line):
            remote(part, part, ag.at[0, u], ag.at[1, u], z_peer(o)).start()

    def ag_y_copy(u):
        part = w.at[u, window(ag_edge(u)), :, yi]
        return remote(part, part, ag.at[2, u], ag.at[3, u], y_neigh)

    def ag_x_copy(u):
        part = w.at[u, mine(ag_edge(u))]
        return remote(part, part, ag.at[4, u], ag.at[5, u], x_neigh)

    def z_bytes(u):
        return w.at[u, window(ag_edge(u)), pl.ds(0, line - 1), yi]

    def ag_y(u):
        wait_bytes(z_bytes(u), ag.at[1, u])
        ag_y_copy(u).start()

    def ag_x(u):
        ag_y_copy(u).wait_recv()
        ag_x_copy(u).start()

    def ag_end(u):
        ag_x_copy(u).wait_recv()

    steps = []
    for t in range(UNITS + 2):
        def step(t=t):
            if t + 3 < UNITS:
                ag_z(t + 3)
            if t < UNITS:
                ag_y(t)
            if 0 <= t - 1 < UNITS:
                ag_x(t - 1)
            if 0 <= t - 2 < UNITS:
                ag_end(t - 2)
        steps.append(step)
    ag_z(0)
    ag_z(1)
    ag_z(2)
    done = [0]

    def ag_step():
        if done[0] < len(steps):
            steps[done[0]]()
            done[0] += 1

    def ag_until(u):
        while done[0] < min(u + 3, len(steps)):
            ag_step()

    wait_bytes(vec_all.at[pl.ds(0, dp_n - 1)], vs.at[1, 0])
    grain = 128 if vec_len % 128 == 0 else 64

    def vec_lanes(first):
        parts = []
        for e in range(first, first + 128, grain):
            o = e % vec_len
            parts.append(vec_all[e // vec_len, o // 128 : o // 128 + 1, o % 128 : o % 128 + grain])
        return parts[0] if len(parts) == 1 else jnp.concatenate(parts, 1)

    for row in range(12):
        for lane in range(0, width, 128):
            vec[row : row + 1, lane : lane + 128] = vec_lanes(row * width + lane)

    def hidden_bias(core):
        parts = []
        for h in range(2):
            for shard in range(dp_n):
                n = shard * 4 * r + core * 2 * r + h * r
                parts.append(vec[8 + n // width : 9 + n // width, n % width : n % width + r])
        return jnp.concatenate(parts, 1)

    bias_h[...] = jnp.where(c == 0, hidden_bias(0), hidden_bias(1))

    x_copies[0].wait()
    x_copies[1].wait()

    def live(to):
        return jnp.where(kbias[to, 0:1] < 0, 0.0, 1.0)

    chunk = 32
    gain_one, shift_one = vec[0:1, :], vec[1:2, :]

    def norm_one(i, carry):
        at = pl.ds(pl.multiple_of(i * chunk, chunk), chunk)
        to = pl.ds(pl.multiple_of(c * own + i * chunk, chunk), chunk)
        unit, _ = unit_rows(tok_own[at, :].astype(F32))
        n1[to, :] = (unit * gain_one + shift_one).astype(BF16)
        go[to, :] = (cot_own[at, :].astype(F32) * live(to)).astype(BF16)
        return carry

    lax.fori_loop(0, own // chunk, norm_one, 0)
    n1_copy = remote(n1.at[my_rows], n1.at[my_rows], sib.at[0, 0], sib.at[1, 0], sibling)
    n1_copy.start()
    go_copy = remote(go.at[my_rows], go.at[my_rows], sib.at[0, 1], sib.at[1, 1], sibling)
    go_copy.start()
    n1_copy.wait_recv()

    low_lane = lax.broadcasted_iota(jnp.int32, (PAIR, PAIR), 1) < HEAD_DIM
    low_row = lax.broadcasted_iota(jnp.int32, (PAIR, PAIR), 0) < HEAD_DIM
    q_chunks = rows // PAIR

    def two_heads(v):
        zero = jnp.zeros_like(v)
        return jnp.concatenate([jnp.where(low_lane, v, zero), jnp.where(low_lane, zero, v)], 0)

    qkv_lanes = 3 * PAIR

    def pair_lanes(p):
        return tuple(slice(p * qkv_lanes + n * PAIR, p * qkv_lanes + (n + 1) * PAIR) for n in range(3))

    def att_lanes(p):
        return pl.ds(pl.multiple_of(c * half + p * PAIR, PAIR), PAIR)

    def wo_copy(p):
        return remote(w.at[p, BLOCKS - 1], w_oth.at[p], wo.at[0, p], wo.at[1, p], sibling)

    def columns(blocks):
        return jnp.concatenate([v.reshape(-1, PAIR) for v in blocks], 1)

    def attend_forward(p):
        q_at, k_at, v_at = pair_lanes(p)
        out = dot(n1[...], columns([w[p, n] for n in range(3)]))
        queries = (out[:, :PAIR] + vec[4:5, att_lanes(p)]).astype(BF16)
        qkv[:, q_at] = queries * jnp.asarray(HEAD_DIM**-0.5, BF16)
        qkv[:, k_at] = out[:, PAIR : 2 * PAIR].astype(BF16)
        qkv[:, v_at] = (out[:, 2 * PAIR :] + vec[5:6, att_lanes(p)]).astype(BF16)

        def some(j, carry):
            at = pl.ds(pl.multiple_of(j * PAIR, PAIR), PAIR)
            mask = kbias[...]
            scores = dot_cols(qkv[:, k_at], two_heads(qkv[at, q_at])) + jnp.concatenate([mask, mask], 1)
            highest = jnp.max(scores, 0, keepdims=True)
            raised = jnp.exp(scores - highest)
            total = jnp.sum(raised, 0, keepdims=True)
            out = dot_rows(qkv[:, v_at], raised.astype(BF16)) / total
            out = jnp.where(low_row, out[:, :PAIR], out[:, PAIR:])
            att[at, att_lanes(p)] = out.T.astype(BF16)
            lse[pl.ds(p * q_chunks + j, 1), :] = highest + jnp.log(total)
            return carry

        lax.fori_loop(0, q_chunks, some, 0)

    for p in range(4):
        ag_until(p)
        wo_copy(p).start()
        attend_forward(p)
    att_copy = remote(att.at[:, my_half], att.at[:, my_half], sib.at[0, 2], sib.at[1, 2], sibling)
    att_copy.start()
    for p in range(4):
        wo_copy(p).wait_recv()
    att_copy.wait_recv()

    bias_att = vec[6:7, :]
    mixed = att[my_rows, :]

    def own_out(z):
        return columns([w[p, BLOCKS - 1, z] for p in range(4)])

    def oth_out(z):
        return columns([w_oth[p, z] for p in range(4)])

    resid[:, my_half] = dot(mixed, own_out(slice(None)))
    resid[:, oth_half] = dot(mixed, oth_out(slice(None)))
    gain_two, shift_two = vec[2:3, :], vec[3:4, :]

    def norm_two(i, carry):
        at = pl.ds(pl.multiple_of(i * chunk, chunk), chunk)
        to = pl.ds(pl.multiple_of(c * own + i * chunk, chunk), chunk)
        res = resid[at, :] + tok_own[at, :].astype(F32) + bias_att
        resid[at, :] = res
        unit, _ = unit_rows(res)
        n2[to, :] = (unit * gain_two + shift_two).astype(BF16)
        return carry

    lax.fori_loop(0, own // chunk, norm_two, 0)
    n2_copy = remote(n2.at[my_rows], n2.at[my_rows], sib.at[0, 4], sib.at[1, 4], sibling)
    n2_copy.start()
    n2_copy.wait()

    tile = 256
    for u in range(4):
        ag_until(4 + u)

        def expand(i, carry, u=u):
            to = pl.ds(pl.multiple_of(u * UNIT + i * tile, tile), tile)
            hidden = dot(n2[...], columns([w[4 + u, 2 * i], w[4 + u, 2 * i + 1]])) + bias_h[:, to]
            gate = jax.nn.sigmoid(SLOPE * hidden)
            act[:, to] = (hidden * gate).astype(BF16)
            fac[:, to] = (gate + SLOPE * hidden * gate * (1.0 - gate)).astype(BF16)
            return carry

        lax.fori_loop(0, UNIT // tile, expand, 0)
    go_copy.wait_recv()

    rs_win = window(RS_EDGE)

    def rs_x_copy(k, u):
        return remote(g.at[k, theirs(RS_EDGE)], rx.at[k], rs.at[0, u], rs.at[1, u], x_neigh)

    def rs_y_copy(k, u):
        return remote(g.at[k, rs_win, :, 1 - yi], ry.at[k], rs.at[2, u], rs.at[3, u], y_neigh)

    def rs_2_copy(k, u):
        return remote(s_own.at[k], s_oth.at[k], rs.at[6, u], rs.at[7, u], x_neigh)

    def rs_f_copies(k, u):
        parts = unit_parts(u, c)
        result = (o_att, o_exp, o_shr)[u // 4]
        pairs = [
            (f_own.at[k, n], result.at[parts[n]] if parts else result.at[u - 4, c, n]) for n in range(BLOCKS)
        ]
        return [remote(a, b, rs.at[8, u], rs.at[9, u], sibling) for a, b in pairs] + [
            pltpu.make_async_copy(a, b, rs.at[10, u]) for a, b in pairs
        ]

    def rs_y(k, u):
        rs_x_copy(k, u).wait_recv()

        def add(z, carry):
            for n in range(RS_EDGE):
                b = x * RS_WINDOW + n
                g[k, b, z] = (g[k, b, z].astype(F32) + rx[k, n, z].astype(F32)).astype(BF16)
            return carry

        lax.fori_loop(0, line, add, 0)
        rs_y_copy(k, u).start()

    def rs_z(k, u):
        rs_y_copy(k, u).wait_recv()

        def add(z, carry):
            for n in range(RS_WINDOW):
                b = x * RS_EDGE + n
                g[k, b, z, yi] = (g[k, b, z, yi].astype(F32) + ry[k, n, z].astype(F32)).astype(BF16)
            return carry

        lax.fori_loop(0, line, add, 0)
        for o in range(1, line):
            z = lax.rem(zi + o, line)
            remote(g.at[k, rs_win, z, yi], rz.at[k, o - 1], rs.at[4, u], rs.at[5, u], z_peer(o)).start()

    def rs_2(k, u):
        wait_bytes(rz.at[k], rs.at[5, u])
        for n in range(RS_WINDOW):
            total = g[k, x * RS_EDGE + n, zi, yi].astype(F32)
            for o in range(1, line):
                total = total + rz[k, o - 1, n].astype(F32)
            s_own[k, n] = total.astype(BF16)
        rs_2_copy(k, u).start()

    def rs_f(k, u):
        rs_2_copy(k, u).wait_recv()
        here, there = s_own[k], s_oth[k]
        first = jnp.where(x == 0, here, there)
        last = jnp.where(x == 0, there, here)
        f_own[k, 0] = first[0]
        for n in range(1, RS_WINDOW):
            f_own[k, n] = (first[n].astype(F32) + last[n - 1].astype(F32)).astype(BF16)
        f_own[k, RS_WINDOW] = last[RS_WINDOW - 1]
        for copy in rs_f_copies(k, u):
            copy.start()

    def rs_end(k, u):
        rs_x_copy(k, u).wait_send()
        rs_y_copy(k, u).wait_send()
        wait_bytes(rz.at[k], rs.at[4, u])
        rs_2_copy(k, u).wait_send()
        for n in (8, 9, 10):
            wait_bytes(f_own.at[k], rs.at[n, u])

    def put(k, first, value):
        for n in range(value.shape[1] // PAIR):
            part = value[:, n * PAIR : (n + 1) * PAIR].astype(BF16)
            g[k, first + n] = part.reshape(line, 2, r, PAIR)

    flight = []

    def send_unit(k, u):
        rs_x_copy(k, u).start()
        flight.append([0, k, u])

    def grad_unit(k, u, left, right):
        put(k, 0, dot(left, right))
        send_unit(k, u)

    stages = [rs_y, rs_z, rs_2, rs_f, rs_end]

    def rs_tick():
        for item in flight[::-1]:
            n, k, u = item
            stages[n](k, u)
            item[0] = n + 1
            if item[0] == len(stages):
                flight.remove(item)
                if u == UNITS - 1:
                    give_credit()

    def give_credit():
        pl.semaphore_signal(credit.at[0], inc=1, device_id=x_neigh, device_id_type=MESH)
        pl.semaphore_signal(credit.at[1], inc=1, device_id=y_neigh, device_id_type=MESH)
        for o in range(1, line):
            pl.semaphore_signal(credit.at[2], inc=1, device_id=z_peer(o), device_id_type=MESH)

    def take_credit():
        pl.semaphore_wait(credit.at[0], 1)
        pl.semaphore_wait(credit.at[1], 1)
        pl.semaphore_wait(credit.at[2], line - 1)

    def transpose_into(dst, src, lanes_at):
        def move(i, carry):
            at = pl.ds(pl.multiple_of(i * 128, 128), 128)
            dst[at, :] = src[:, pl.ds(pl.multiple_of(lanes_at + i * 128, 128), 128)].T
            return carry

        lax.fori_loop(0, width // 128, move, 0)

    for h in range(2):
        transpose_into(tr, act, h * width)
        for j in range(2):
            k = 2 * h + j
            ag_step()
            grad_unit(k, 8 + k, tr[...], go[:, j * UNIT : (j + 1) * UNIT])
            if k > 0:
                rs_tick()

    ag_until(UNITS - 1)

    span = max(1, tile // (2 * r))

    def hidden_back(n, carry):
        z = n * span
        for h in range(2):
            total = None
            for j in range(2):
                part = columns([w[8 + 2 * h + j, b, pl.ds(z, span)] for b in range(BLOCKS)])
                term = dot_cols(go[:, j * UNIT : (j + 1) * UNIT], part)
                total = term if total is None else total + term
            to = pl.ds(pl.multiple_of(h * width + n * (span * 2 * r), span * 2 * r), span * 2 * r)
            low = (total * fac[:, to].astype(F32)).astype(BF16)
            fac[:, to] = low
            sums = jnp.sum(fold8(low.astype(F32)), 0, keepdims=True)
            at = pl.ds(pl.multiple_of(n * (span * 2 * r), span * 2 * r), span * 2 * r)
            vg[pl.ds(8 + 2 * c + h, 1), at] = sums
        return carry

    vg[...] = jnp.zeros_like(vg)
    lax.fori_loop(0, line // span, hidden_back, 0)
    rs_tick()

    def back_partial(src, lanes, first, rows_at, dst):
        def back(n, carry):
            total = None
            for u in range(4):
                part = columns([w[first + u, b, pl.ds(n * span, span)] for b in range(lanes // PAIR)])
                term = dot_cols(src[rows_at, u * lanes : (u + 1) * lanes], part)
                total = term if total is None else total + term
            dst[:, pl.ds(pl.multiple_of(n * (span * 2 * r), span * 2 * r), span * 2 * r)] = total
            return carry

        lax.fori_loop(0, line // span, back, 0)

    back_partial(fac, UNIT, 4, oth_rows, send_p)
    p2_copy = remote(send_p, recv_p, sib.at[0, 5], sib.at[1, 5], sibling)
    p2_copy.start()
    back_partial(fac, UNIT, 4, my_rows, own_p)
    rs_tick()
    transpose_into(tr, n2, 0)
    for u in range(2):
        grad_unit(4 + u, 4 + u, tr[...], fac[:, u * UNIT : (u + 1) * UNIT])
        rs_tick()
    p2_copy.wait()

    zeros8 = jnp.zeros((8, width), F32)

    def norm_two_back(i, carry):
        at = pl.ds(pl.multiple_of(i * chunk, chunk), chunk)
        to = pl.ds(pl.multiple_of(c * own + i * chunk, chunk), chunk)
        unit, rstd = unit_rows(resid[at, :])
        gn = own_p[at, :] + recv_p[at, :]
        grad_out = go[to, :].astype(F32)
        gr = grad_out + norm_back(gn, unit, rstd, gain_two)
        own_p[at, :] = gr
        low = gr.astype(BF16)
        gb[to, :] = low
        a, b, e, f = carry
        return (a + fold8(gn * unit), b + fold8(gn), e + fold8(low.astype(F32)), f + fold8(grad_out))

    sums = lax.fori_loop(0, own // chunk, norm_two_back, (zeros8,) * 4)
    for row, v in zip((2, 3, 6, 7), sums):
        vg[row : row + 1, :] = jnp.sum(v, 0, keepdims=True)
    gb_copy = remote(gb.at[my_rows], gb.at[my_rows], sib.at[0, 6], sib.at[1, 6], sibling)
    gb_copy.start()

    for u in range(2, 4):
        grad_unit(4 + u, 4 + u, tr[...], fac[:, u * UNIT : (u + 1) * UNIT])
        rs_tick()
    gb_copy.wait_recv()
    rs_tick()
    transpose_into(tr, n1, 0)
    transpose_into(tr_att, att, 0)

    head_rows = pl.ds(c * (line // 2), line // 2)
    n2[:, :UNIT] = (
        dot_cols(gb[:, my_half], own_out(head_rows)) + dot_cols(gb[:, oth_half], oth_out(head_rows))
    ).astype(BF16)

    def attend_backward(p):
        q_at, k_at, v_at = pair_lanes(p)
        own_lanes = slice(p * PAIR, (p + 1) * PAIR)
        dk_acc[...] = jnp.zeros_like(dk_acc)
        dv_acc[...] = jnp.zeros_like(dv_acc)

        def some(j, carry):
            at = pl.ds(pl.multiple_of(j * PAIR, PAIR), PAIR)
            both = two_heads(qkv[at, q_at])
            grads = two_heads(n2[at, own_lanes])
            mask = kbias[...]
            scores = dot_cols(qkv[:, k_at], both) + jnp.concatenate([mask, mask], 1)
            chance = jnp.exp(scores - lse[pl.ds(p * q_chunks + j, 1), :])
            dv_acc[...] += dot(chance.astype(BF16), grads)
            grad_chance = dot_cols(qkv[:, v_at], grads)
            inner = jnp.sum(chance * grad_chance, 0, keepdims=True)
            grad_scores = (chance * (grad_chance - inner)).astype(BF16)
            dk_acc[...] += dot(grad_scores, both)
            out = dot_rows(qkv[:, k_at], grad_scores)
            out = jnp.where(low_row, out[:, :PAIR], out[:, PAIR:]) * HEAD_DIM**-0.5
            qkv[at, q_at] = out.T.astype(BF16)
            return carry

        lax.fori_loop(0, q_chunks, some, 0)
        qkv[:, k_at] = dk_acc[...].astype(BF16)
        qkv[:, v_at] = dv_acc[...].astype(BF16)
        vg[4:5, att_lanes(p)] = jnp.sum(fold8(qkv[:, q_at].astype(F32)), 0, keepdims=True)
        vg[5:6, att_lanes(p)] = jnp.sum(fold8(qkv[:, v_at].astype(F32)), 0, keepdims=True)

    for p in range(4):
        attend_backward(p)
        if p == 0:
            take_credit()
        put(p, 0, dot(tr[...], qkv[:, p * qkv_lanes : (p + 1) * qkv_lanes]))
        put(p, BLOCKS - 1, dot(tr_att[...], gb[:, att_lanes(p)]))
        send_unit(p, p)
        rs_tick()

    back_partial(qkv, qkv_lanes, 0, oth_rows, send_p)
    p1_copy = remote(send_p, recv_p, sib.at[0, 7], sib.at[1, 7], sibling)
    p1_copy.start()
    back_partial(qkv, qkv_lanes, 0, my_rows, dst_p)
    rs_tick()
    p1_copy.wait()

    def norm_one_back(i, carry):
        at = pl.ds(pl.multiple_of(i * chunk, chunk), chunk)
        unit, rstd = unit_rows(tok_own[at, :].astype(F32))
        gn = dst_p[at, :] + recv_p[at, :]
        out = own_p[at, :] + norm_back(gn, unit, rstd, gain_one)
        tok_own[at, :] = out.astype(BF16)
        a, b = carry
        return (a + fold8(gn * unit), b + fold8(gn))

    sums = lax.fori_loop(0, own // chunk, norm_one_back, (zeros8,) * 2)
    for row, v in zip((0, 1), sums):
        vg[row : row + 1, :] = jnp.sum(v, 0, keepdims=True)
    o_tok[x] = tok_own[my_block, :]
    tok_copy = remote(tok_own.at[oth_block], o_tok.at[x], xe.at[0, 3], xe.at[1, 3], x_neigh)
    tok_copy.start()
    rs_tick()

    def branch(dst, rows_at, add):
        def out(n, carry):
            for j in range(2):
                total = None
                for h in range(2):
                    part = columns([w[8 + 2 * h + j, 2 * n], w[8 + 2 * h + j, 2 * n + 1]])
                    term = dot(act[rows_at, h * width : (h + 1) * width], part)
                    total = term if total is None else total + term
                to = pl.ds(pl.multiple_of(j * UNIT + n * tile, tile), tile)
                dst[:, to] = dst[:, to] + total if add else total
            return carry

        lax.fori_loop(0, UNIT // tile, out, 0)

    branch(send_p, oth_rows, False)
    m_copy = remote(send_p, recv_m, sib.at[0, 8], sib.at[1, 8], sibling)
    m_copy.start()
    branch(resid, my_rows, True)
    m_copy.wait()

    bias_out = vec[7:8, :]

    def finish_block(i, carry):
        at = pl.ds(pl.multiple_of(i * chunk, chunk), chunk)
        out = live(pl.ds(pl.multiple_of(c * own + i * chunk, chunk), chunk)) * (resid[at, :] + recv_m[at, :] + bias_out)
        cot_own[at, :] = out.astype(BF16)
        return carry

    lax.fori_loop(0, own // chunk, finish_block, 0)
    o_blk[x] = cot_own[my_block, :]
    blk_copy = remote(cot_own.at[oth_block], o_blk.at[x], xe.at[0, 2], xe.at[1, 2], x_neigh)
    blk_copy.start()

    for n, to in enumerate((sibling, x_neigh, y_neigh)):
        copy = remote(vg, vr.at[n], vs.at[0, 1 + n], vs.at[1, 1 + n], to)
        copy.start()
        copy.wait()
        vg[...] += vr[n]
        rs_tick()

    def send_vz(o, carry):
        remote(vg, vz.at[zi], vs.at[0, 4], vs.at[1, 4], (lax.rem(zi + o, line) * 2 + yi, s)).start()
        return carry

    lax.fori_loop(1, line, send_vz, 0)
    vz[zi] = vg[...]
    wait_bytes(vz.at[pl.ds(0, line - 1)], vs.at[1, 4])
    wait_bytes(vz.at[pl.ds(0, line - 1)], vs.at[0, 4])
    o_vec[...] = lax.fori_loop(1, line, lambda i, t: t + vz[i], vz[0])

    while flight:
        rs_tick()

    blk_copy.wait()
    tok_copy.wait()
    wait_bytes(vec_all.at[pl.ds(0, dp_n - 1)], vs.at[0, 0])
    for copy in [n1_copy, go_copy, att_copy, gb_copy] + [wo_copy(p) for p in range(4)]:
        copy.wait_send()
    for u in range(UNITS):
        wait_bytes(z_bytes(u), ag.at[0, u])
        ag_y_copy(u).wait_send()
        ag_x_copy(u).wait_send()


def adamw(grad, moment, square, weight, rate, decay):
    momentum = BETA_ONE * moment + (1.0 - BETA_ONE) * grad
    variance = BETA_TWO * square + (1.0 - BETA_TWO) * grad * grad
    first_fix = 1.0 - BETA_ONE**STEP
    second_fix = 1.0 - BETA_TWO**STEP
    direction = momentum / first_fix / (jnp.sqrt(variance / second_fix) + EPS_ADAM)
    updated = weight - rate * (direction + decay * weight)
    return (momentum, variance, updated, updated.astype(BF16))


def body(
    tokens, cotangent, key_mask,
    attention_weights, expand_weights, shrink_weights, vector_params,
    attention_moment, attention_square, expand_moment, expand_square,
    shrink_moment, shrink_square, vector_moment, vector_square,
):
    dp_n = lax.axis_size("dp")
    line = dp_n // 2
    d = lax.axis_index("dp")
    place = lax.axis_index("seq")
    x, c = place // 2, place % 2
    _, local_len, width = tokens.shape
    r = width // dp_n
    block = -(-local_len // 16) * 16
    own, rows = 2 * block, 4 * block
    pad = ((0, 0), (0, block - local_len), (0, 0))

    keep = lax.dynamic_index_in_dim(key_mask, x, 0, keepdims=False).reshape(2, 2, local_len)
    keep = jnp.pad(keep.transpose(1, 0, 2), ((0, 0), (0, 0), pad[1])).reshape(2, own)
    kbias = jnp.broadcast_to(jnp.where(keep > 0, 0.0, -1e30).astype(F32).reshape(rows, 1), (rows, PAIR))
    p_exp = expand_weights
    if r % 128:
        p_exp = lax.dynamic_index_in_dim(expand_weights.reshape(r, dp_n, 2, 2, r), c, 2, keepdims=False)
        p_exp = p_exp.transpose(2, 0, 1, 3).reshape(2, r, 2 * BLOCKS, PAIR).transpose(0, 2, 1, 3).reshape(4, BLOCKS, r, PAIR)
    vec_len = vector_params.shape[0]
    vec_rows = -(-vec_len // 1024) * 8
    p_vec = jnp.pad(vector_params.astype(BF16).astype(F32), (0, vec_rows * 128 - vec_len)).reshape(vec_rows, 128)

    vmem = pl.BlockSpec(memory_space=pltpu.VMEM)
    hbm = pl.BlockSpec(memory_space=pl.ANY)
    padded = jax.ShapeDtypeStruct((2, block, width), BF16)
    o_blk, o_tok, o_att, o_exp, o_shr, o_vec = pl.pallas_call(
        functools.partial(layer_kernel, line, vec_len),
        out_shape=(
            padded,
            padded,
            jax.ShapeDtypeStruct((r, 4 * width), BF16),
            jax.ShapeDtypeStruct((4, 2, BLOCKS, r, PAIR) if r % 128 else (r, 4 * width), BF16),
            jax.ShapeDtypeStruct((4 * r, width), BF16),
            jax.ShapeDtypeStruct((16, width), F32),
        ),
        in_specs=[vmem] * 4 + [hbm] * 3,
        out_specs=(vmem, vmem, hbm, hbm, hbm, vmem),
        scratch_shapes=[
            pltpu.VMEM((UNITS, BLOCKS, line, 2, r, PAIR), BF16),
            pltpu.VMEM((4, line, 2, r, PAIR), BF16),
            pltpu.VMEM((SLOTS, BLOCKS, line, 2, r, PAIR), BF16),
            pltpu.VMEM((SLOTS, RS_EDGE, line, 2, r, PAIR), BF16),
            pltpu.VMEM((SLOTS, RS_WINDOW, line, r, PAIR), BF16),
            pltpu.VMEM((SLOTS, line - 1, RS_WINDOW, r, PAIR), BF16),
            pltpu.VMEM((SLOTS, RS_WINDOW, r, PAIR), BF16),
            pltpu.VMEM((SLOTS, RS_WINDOW, r, PAIR), BF16),
            pltpu.VMEM((SLOTS, BLOCKS, r, PAIR), BF16),
            pltpu.VMEM((dp_n, vec_rows, 128), F32),
            pltpu.VMEM((16, width), F32),
            pltpu.VMEM((1, 2 * width), F32),
            pltpu.VMEM((16, width), F32),
            pltpu.VMEM((3, 16, width), F32),
            pltpu.VMEM((line, 16, width), F32),
            pltpu.VMEM((own, width), BF16),
            pltpu.VMEM((own, width), BF16),
            pltpu.VMEM((rows, width), BF16),
            pltpu.VMEM((rows, width), BF16),
            pltpu.VMEM((rows, 3 * UNIT), BF16),
            pltpu.VMEM((rows, width), BF16),
            pltpu.VMEM(((rows // PAIR) * (UNIT // PAIR), 2 * PAIR), F32),
            pltpu.VMEM((own, width), F32),
            pltpu.VMEM((rows, width), BF16),
            pltpu.VMEM((rows, 2 * width), BF16),
            pltpu.VMEM((rows, 2 * width), BF16),
            pltpu.VMEM((own, width), F32),
            pltpu.VMEM((own, width), F32),
            pltpu.VMEM((own, width), F32),
            pltpu.VMEM((own, width), F32),
            pltpu.VMEM((own, width), F32),
            pltpu.VMEM((rows, width), BF16),
            pltpu.VMEM((width, rows), BF16),
            pltpu.VMEM((width, rows), BF16),
            pltpu.VMEM((rows, PAIR), F32),
            pltpu.VMEM((rows, PAIR), F32),
            pltpu.SemaphoreType.DMA((6, UNITS)),
            pltpu.SemaphoreType.DMA((11, UNITS)),
            pltpu.SemaphoreType.DMA((2, 9)),
            pltpu.SemaphoreType.DMA((2, 4)),
            pltpu.SemaphoreType.DMA((2, 4)),
            pltpu.SemaphoreType.DMA((2, 5)),
            pltpu.SemaphoreType.DMA((UNITS,)),
            pltpu.SemaphoreType.REGULAR((3,)),
        ],
        compiler_params=pltpu.CompilerParams(
            collective_id=0, has_side_effects=True, vmem_limit_bytes=VMEM_LIMIT
        ),
        name="layer",
    )(jnp.pad(tokens, pad), jnp.pad(cotangent, pad), kbias, p_vec, attention_weights, p_exp, shrink_weights)

    block_output = o_blk[:, :local_len]
    token_gradient = o_tok[:, :local_len]
    grad_attention, grad_shrink = o_att.astype(F32), o_shr.astype(F32)
    if r % 128:
        o_exp = o_exp.transpose(3, 1, 0, 2, 4).reshape(r, 2, 2, dp_n, r).transpose(0, 3, 1, 2, 4).reshape(r, 4 * width)
    grad_expand = o_exp.astype(F32)
    hidden_sums = o_vec[8:12].reshape(2, 2, dp_n, r).transpose(2, 0, 1, 3).reshape(4, width)
    grad_vector = jnp.concatenate([o_vec[0:8], hidden_sums], 0).reshape(dp_n, vec_len)
    grad_vector = lax.dynamic_index_in_dim(grad_vector, d, 0, keepdims=False)

    attention_out = adamw(
        grad_attention, attention_moment, attention_square, attention_weights, RATE_MATRIX, DECAY_MATRIX
    )
    expand_out = adamw(grad_expand, expand_moment, expand_square, expand_weights, RATE_MATRIX, DECAY_MATRIX)
    shrink_out = adamw(grad_shrink, shrink_moment, shrink_square, shrink_weights, RATE_MATRIX, DECAY_MATRIX)
    vector_out = adamw(grad_vector, vector_moment, vector_square, vector_params, RATE_VECTOR, 0.0)
    return (block_output, token_gradient, *attention_out, *expand_out, *shrink_out, *vector_out)


VMEM_LIMIT = 62 * 2**20


def solution(mesh):
    split = P("dp", "seq", None)
    rows = P("dp", None)
    flat = P("dp")
    return jax.shard_map(
        body,
        mesh=mesh,
        in_specs=(split, split, rows, rows, rows, rows, flat) + (rows,) * 6 + (flat, flat),
        out_specs=(split, split) + (rows,) * 12 + (flat,) * 4,
        check_vma=False,
    )
```

```python
import functools

import jax
import jax.numpy as jnp
from jax import lax
from jax.experimental import pallas as pl
from jax.experimental.pallas import tpu as pltpu
from jax.sharding import PartitionSpec as P

HEAD_DIM = 64
STEP = 5
EPS_NORM = 1e-05
BETA_ONE = 0.5
BETA_TWO = 0.5
EPS_ADAM = 1e-08
RATE_MATRIX = 0.05
RATE_VECTOR = 0.2
DECAY_MATRIX = 0.1
SLOPE = 1.702

BF16 = jnp.bfloat16
F32 = jnp.float32
MESH = pl.DeviceIdType.MESH

UNIT = 512
BLOCKS = 4
RS_EDGE = 1
RS_WINDOW = BLOCKS - RS_EDGE
UNITS = 12
SLOTS = 8
PAIR = 128


def dot(a, b):
    return jnp.dot(a, b, preferred_element_type=F32)


def dot_rows(a, b):
    return lax.dot_general(a, b, (((0,), (0,)), ((), ())), preferred_element_type=F32)


def dot_cols(a, b):
    return lax.dot_general(a, b, (((1,), (1,)), ((), ())), preferred_element_type=F32)


def unit_rows(x):
    centred = x - jnp.mean(x, -1, keepdims=True)
    rstd = lax.rsqrt(jnp.mean(centred * centred, -1, keepdims=True) + EPS_NORM)
    return centred * rstd, rstd


def norm_back(grad_normed, unit, rstd, gain):
    g = grad_normed * gain
    return rstd * (g - jnp.mean(g, -1, keepdims=True) - unit * jnp.mean(g * unit, -1, keepdims=True))


def fold8(v):
    return jnp.sum(v.reshape(v.shape[0] // 8, 8, v.shape[1]), 0)


def layer_kernel(
    line, vec_len,
    tok, cot, kbias, p_vec, p_att, p_exp, p_shr,
    o_blk, o_tok, o_att, o_exp, o_shr, o_vec,
    w, w_oth, g, rx, ry, rz, s_own, s_oth, f_own,
    vec_all, vec, bias_h, vg, vr, vz,
    tok_own, cot_own,
    n1, go, qkv, att, lse, resid, n2, act, fac, own_p, send_p, recv_p, recv_m, dst_p,
    gb, tr, tr_att, dk_acc, dv_acc,
    ag, rs, sib, wo, xe, vs, fill, credit,
):
    dp_n = 2 * line
    r = w.shape[4]
    block = tok.shape[1]
    own = 2 * block
    rows = 2 * own
    width = tok.shape[2]
    half = UNIT
    d = lax.axis_index("dp")
    s = lax.axis_index("seq")
    zi, yi = d // 2, d % 2
    x, c = s // 2, s % 2
    sibling = (d, x * 2 + 1 - c)
    x_neigh = (d, (1 - x) * 2 + c)
    y_neigh = (zi * 2 + 1 - yi, s)

    def z_peer(o):
        return (lax.rem(zi + o, line) * 2 + yi, s)

    my_rows = pl.ds(pl.multiple_of(c * own, own), own)
    oth_rows = pl.ds(pl.multiple_of((1 - c) * own, own), own)
    my_half = pl.ds(pl.multiple_of(c * half, half), half)
    oth_half = pl.ds(pl.multiple_of((1 - c) * half, half), half)

    def window(edge):
        return pl.ds(x * edge, BLOCKS - edge)

    def mine(edge):
        return pl.ds(x * (BLOCKS - edge), edge)

    def theirs(edge):
        return pl.ds((1 - x) * (BLOCKS - edge), edge)

    def ag_edge(u):
        return 2 if u % 3 == 2 else 1

    my_block = pl.ds(pl.multiple_of(x * block, block), block)
    oth_block = pl.ds(pl.multiple_of((1 - x) * block, block), block)

    def remote(src, dst, send, recv, to):
        return pltpu.make_async_remote_copy(
            src_ref=src, dst_ref=dst, send_sem=send, recv_sem=recv, device_id=to, device_id_type=MESH
        )

    def wait_bytes(ref, sem):
        pltpu.make_async_copy(ref, ref, sem).wait()

    wide = r % 128 == 0

    def unit_parts(u, core):
        if u < 4:
            return [
                (slice(None), pl.ds(pl.multiple_of(n * width + core * half + u * PAIR, PAIR), PAIR)) for n in range(BLOCKS)
            ]
        if u < 8:
            if not wide:
                return None
            parts = []
            for n in range((u - 4) * UNIT, (u - 3) * UNIT, PAIR):
                h, shard, rest = n // width, n % width // r, n % r
                at = shard * 4 * r + core * 2 * r + h * r + rest
                parts.append((slice(None), pl.ds(pl.multiple_of(at, PAIR), PAIR)))
            return parts
        h, j = (u - 8) // 2, (u - 8) % 2
        held = pl.ds(pl.multiple_of(core * 2 * r + h * r, r), r)
        return [(held, slice(j * UNIT + n * PAIR, j * UNIT + (n + 1) * PAIR)) for n in range(BLOCKS)]

    def stage(u):
        n = u % 4
        return (own_p, send_p, recv_m)[u // 4].at[(n // 2) * r : (n // 2 + 1) * r, (n % 2) * UNIT : (n % 2 + 1) * UNIT]

    for u in range(UNITS):
        parts = unit_parts(u, c)
        source = (p_att, p_exp, p_shr)[u // 4]
        for n in range(BLOCKS):
            part = source.at[parts[n]] if parts else source.at[u - 4, n]
            pltpu.make_async_copy(part, stage(u).at[:, n * PAIR : (n + 1) * PAIR], fill.at[u]).start()

    vec_all[d] = p_vec[...]
    act[:block, :width] = tok[1 - x]
    act[:block, width:] = cot[1 - x]
    tok_own[my_block] = tok[x]
    cot_own[my_block] = cot[x]

    barrier = pltpu.get_barrier_semaphore()

    def greet(o, carry):
        pl.semaphore_signal(barrier, inc=1, device_id=(lax.rem(d + o, dp_n), s), device_id_type=MESH)
        return carry

    lax.fori_loop(1, dp_n, greet, 0)
    pl.semaphore_signal(barrier, inc=1, device_id=sibling, device_id_type=MESH)
    pl.semaphore_signal(barrier, inc=1, device_id=x_neigh, device_id_type=MESH)
    pl.semaphore_wait(barrier, dp_n + 1)

    def send_vec(o, carry):
        remote(p_vec, vec_all.at[d], vs.at[0, 0], vs.at[1, 0], (lax.rem(d + o, dp_n), s)).start()
        return carry

    lax.fori_loop(1, dp_n, send_vec, 0)
    x_copies = [
        remote(act.at[:block, :width], tok_own.at[my_block], xe.at[0, 0], xe.at[1, 0], x_neigh),
        remote(act.at[:block, width:], cot_own.at[my_block], xe.at[0, 1], xe.at[1, 1], x_neigh),
    ]
    for copy in x_copies:
        copy.start()

    def ag_z(u):
        edge = ag_edge(u)
        wait_bytes(stage(u), fill.at[u])
        for n in range(BLOCKS - edge):
            b = x * edge + n
            w[u, b, zi, yi] = stage(u)[:, pl.ds(pl.multiple_of(b * PAIR, PAIR), PAIR)].astype(BF16)
        part = w.at[u, window(edge), zi, yi]
        for o in range(1, line):
            remote(part, part, ag.at[0, u], ag.at[1, u], z_peer(o)).start()

    def ag_y_copy(u):
        part = w.at[u, window(ag_edge(u)), :, yi]
        return remote(part, part, ag.at[2, u], ag.at[3, u], y_neigh)

    def ag_x_copy(u):
        part = w.at[u, mine(ag_edge(u))]
        return remote(part, part, ag.at[4, u], ag.at[5, u], x_neigh)

    def z_bytes(u):
        return w.at[u, window(ag_edge(u)), pl.ds(0, line - 1), yi]

    def ag_y(u):
        wait_bytes(z_bytes(u), ag.at[1, u])
        ag_y_copy(u).start()

    def ag_x(u):
        ag_y_copy(u).wait_recv()
        ag_x_copy(u).start()

    def ag_end(u):
        ag_x_copy(u).wait_recv()

    steps = []
    for t in range(UNITS + 2):
        def step(t=t):
            if t + 3 < UNITS:
                ag_z(t + 3)
            if t < UNITS:
                ag_y(t)
            if 0 <= t - 1 < UNITS:
                ag_x(t - 1)
            if 0 <= t - 2 < UNITS:
                ag_end(t - 2)
        steps.append(step)
    ag_z(0)
    ag_z(1)
    ag_z(2)
    done = [0]

    def ag_step():
        if done[0] < len(steps):
            steps[done[0]]()
            done[0] += 1

    def ag_until(u):
        while done[0] < min(u + 3, len(steps)):
            ag_step()

    wait_bytes(vec_all.at[pl.ds(0, dp_n - 1)], vs.at[1, 0])
    grain = 128 if vec_len % 128 == 0 else 64

    def vec_lanes(first):
        parts = []
        for e in range(first, first + 128, grain):
            o = e % vec_len
            parts.append(vec_all[e // vec_len, o // 128 : o // 128 + 1, o % 128 : o % 128 + grain])
        return parts[0] if len(parts) == 1 else jnp.concatenate(parts, 1)

    for row in range(12):
        for lane in range(0, width, 128):
            vec[row : row + 1, lane : lane + 128] = vec_lanes(row * width + lane)

    def hidden_bias(core):
        parts = []
        for h in range(2):
            for shard in range(dp_n):
                n = shard * 4 * r + core * 2 * r + h * r
                parts.append(vec[8 + n // width : 9 + n // width, n % width : n % width + r])
        return jnp.concatenate(parts, 1)

    ag_step()
    bias_h[...] = jnp.where(c == 0, hidden_bias(0), hidden_bias(1))

    x_copies[0].wait()
    x_copies[1].wait()

    def live(to):
        return jnp.where(kbias[to, 0:1] < 0, 0.0, 1.0)

    chunk = 32
    gain_one, shift_one = vec[0:1, :], vec[1:2, :]

    def norm_one(i, carry):
        at = pl.ds(pl.multiple_of(i * chunk, chunk), chunk)
        to = pl.ds(pl.multiple_of(c * own + i * chunk, chunk), chunk)
        unit, _ = unit_rows(tok_own[at, :].astype(F32))
        n1[to, :] = (unit * gain_one + shift_one).astype(BF16)
        go[to, :] = (cot_own[at, :].astype(F32) * live(to)).astype(BF16)
        return carry

    lax.fori_loop(0, own // chunk, norm_one, 0)
    ag_step()
    n1_copy = remote(n1.at[my_rows], n1.at[my_rows], sib.at[0, 0], sib.at[1, 0], sibling)
    n1_copy.start()
    go_copy = remote(go.at[my_rows], go.at[my_rows], sib.at[0, 1], sib.at[1, 1], sibling)
    go_copy.start()
    n1_copy.wait_recv()

    low_lane = lax.broadcasted_iota(jnp.int32, (PAIR, PAIR), 1) < HEAD_DIM
    low_row = lax.broadcasted_iota(jnp.int32, (PAIR, PAIR), 0) < HEAD_DIM
    q_chunks = rows // PAIR

    def two_heads(v):
        zero = jnp.zeros_like(v)
        return jnp.concatenate([jnp.where(low_lane, v, zero), jnp.where(low_lane, zero, v)], 0)

    qkv_lanes = 3 * PAIR

    def pair_lanes(p):
        return tuple(slice(p * qkv_lanes + n * PAIR, p * qkv_lanes + (n + 1) * PAIR) for n in range(3))

    def att_lanes(p):
        return pl.ds(pl.multiple_of(c * half + p * PAIR, PAIR), PAIR)

    def wo_copy(p):
        return remote(w.at[p, BLOCKS - 1], w_oth.at[p], wo.at[0, p], wo.at[1, p], sibling)

    def columns(blocks):
        return jnp.concatenate([v.reshape(-1, PAIR) for v in blocks], 1)

    def attend_forward(p):
        q_at, k_at, v_at = pair_lanes(p)
        out = dot(n1[...], columns([w[p, n] for n in range(3)]))
        queries = (out[:, :PAIR] + vec[4:5, att_lanes(p)]).astype(BF16)
        qkv[:, q_at] = queries * jnp.asarray(HEAD_DIM**-0.5, BF16)
        qkv[:, k_at] = out[:, PAIR : 2 * PAIR].astype(BF16)
        qkv[:, v_at] = (out[:, 2 * PAIR :] + vec[5:6, att_lanes(p)]).astype(BF16)

        def some(j, carry):
            at = pl.ds(pl.multiple_of(j * PAIR, PAIR), PAIR)
            mask = kbias[...]
            scores = dot_cols(qkv[:, k_at], two_heads(qkv[at, q_at])) + jnp.concatenate([mask, mask], 1)
            highest = jnp.max(scores, 0, keepdims=True)
            raised = jnp.exp(scores - highest)
            total = jnp.sum(raised, 0, keepdims=True)
            out = dot_rows(qkv[:, v_at], raised.astype(BF16)) / total
            out = jnp.where(low_row, out[:, :PAIR], out[:, PAIR:])
            att[at, att_lanes(p)] = out.T.astype(BF16)
            lse[pl.ds(p * q_chunks + j, 1), :] = highest + jnp.log(total)
            return carry

        lax.fori_loop(0, q_chunks, some, 0)

    for p in range(4):
        ag_until(p)
        wo_copy(p).start()
        attend_forward(p)
    att_copy = remote(att.at[:, my_half], att.at[:, my_half], sib.at[0, 2], sib.at[1, 2], sibling)
    att_copy.start()
    for p in range(4):
        wo_copy(p).wait_recv()
    att_copy.wait_recv()

    bias_att = vec[6:7, :]
    mixed = att[my_rows, :]

    def own_out(z):
        return columns([w[p, BLOCKS - 1, z] for p in range(4)])

    def oth_out(z):
        return columns([w_oth[p, z] for p in range(4)])

    resid[:, my_half] = dot(mixed, own_out(slice(None)))
    resid[:, oth_half] = dot(mixed, oth_out(slice(None)))
    gain_two, shift_two = vec[2:3, :], vec[3:4, :]

    def norm_two(i, carry):
        at = pl.ds(pl.multiple_of(i * chunk, chunk), chunk)
        to = pl.ds(pl.multiple_of(c * own + i * chunk, chunk), chunk)
        res = resid[at, :] + tok_own[at, :].astype(F32) + bias_att
        resid[at, :] = res
        unit, _ = unit_rows(res)
        n2[to, :] = (unit * gain_two + shift_two).astype(BF16)
        return carry

    lax.fori_loop(0, own // chunk, norm_two, 0)
    n2_copy = remote(n2.at[my_rows], n2.at[my_rows], sib.at[0, 4], sib.at[1, 4], sibling)
    n2_copy.start()
    n2_copy.wait()

    tile = 256
    for u in range(4):
        ag_until(4 + u)

        def expand(i, carry, u=u):
            to = pl.ds(pl.multiple_of(u * UNIT + i * tile, tile), tile)
            hidden = dot(n2[...], columns([w[4 + u, 2 * i], w[4 + u, 2 * i + 1]])) + bias_h[:, to]
            gate = jax.nn.sigmoid(SLOPE * hidden)
            act[:, to] = (hidden * gate).astype(BF16)
            fac[:, to] = (gate + SLOPE * hidden * gate * (1.0 - gate)).astype(BF16)
            return carry

        lax.fori_loop(0, UNIT // tile, expand, 0)
    go_copy.wait_recv()

    rs_win = window(RS_EDGE)

    def rs_x_copy(k, u):
        return remote(g.at[k, theirs(RS_EDGE)], rx.at[k], rs.at[0, u], rs.at[1, u], x_neigh)

    def rs_y_copy(k, u):
        return remote(g.at[k, rs_win, :, 1 - yi], ry.at[k], rs.at[2, u], rs.at[3, u], y_neigh)

    def rs_2_copy(k, u):
        return remote(s_own.at[k], s_oth.at[k], rs.at[6, u], rs.at[7, u], x_neigh)

    def rs_f_copies(k, u):
        parts = unit_parts(u, c)
        result = (o_att, o_exp, o_shr)[u // 4]
        pairs = [
            (f_own.at[k, n], result.at[parts[n]] if parts else result.at[u - 4, c, n]) for n in range(BLOCKS)
        ]
        return [remote(a, b, rs.at[8, u], rs.at[9, u], sibling) for a, b in pairs] + [
            pltpu.make_async_copy(a, b, rs.at[10, u]) for a, b in pairs
        ]

    def rs_y(k, u):
        rs_x_copy(k, u).wait_recv()

        def add(z, carry):
            for n in range(RS_EDGE):
                b = x * RS_WINDOW + n
                g[k, b, z] = (g[k, b, z].astype(F32) + rx[k, n, z].astype(F32)).astype(BF16)
            return carry

        lax.fori_loop(0, line, add, 0)
        rs_y_copy(k, u).start()

    def rs_z(k, u):
        rs_y_copy(k, u).wait_recv()

        def add(z, carry):
            for n in range(RS_WINDOW):
                b = x * RS_EDGE + n
                g[k, b, z, yi] = (g[k, b, z, yi].astype(F32) + ry[k, n, z].astype(F32)).astype(BF16)
            return carry

        lax.fori_loop(0, line, add, 0)
        for o in range(1, line):
            z = lax.rem(zi + o, line)
            remote(g.at[k, rs_win, z, yi], rz.at[k, o - 1], rs.at[4, u], rs.at[5, u], z_peer(o)).start()

    def rs_2(k, u):
        wait_bytes(rz.at[k], rs.at[5, u])
        for n in range(RS_WINDOW):
            total = g[k, x * RS_EDGE + n, zi, yi].astype(F32)
            for o in range(1, line):
                total = total + rz[k, o - 1, n].astype(F32)
            s_own[k, n] = total.astype(BF16)
        rs_2_copy(k, u).start()

    def rs_f(k, u):
        rs_2_copy(k, u).wait_recv()
        here, there = s_own[k], s_oth[k]
        first = jnp.where(x == 0, here, there)
        last = jnp.where(x == 0, there, here)
        f_own[k, 0] = first[0]
        for n in range(1, RS_WINDOW):
            f_own[k, n] = (first[n].astype(F32) + last[n - 1].astype(F32)).astype(BF16)
        f_own[k, RS_WINDOW] = last[RS_WINDOW - 1]
        for copy in rs_f_copies(k, u):
            copy.start()

    def rs_end(k, u):
        rs_x_copy(k, u).wait_send()
        rs_y_copy(k, u).wait_send()
        wait_bytes(rz.at[k], rs.at[4, u])
        rs_2_copy(k, u).wait_send()
        for n in (8, 9, 10):
            wait_bytes(f_own.at[k], rs.at[n, u])

    def put(k, first, value):
        for n in range(value.shape[1] // PAIR):
            part = value[:, n * PAIR : (n + 1) * PAIR].astype(BF16)
            g[k, first + n] = part.reshape(line, 2, r, PAIR)

    flight, queue = [], []

    def inject():
        if queue:
            k, u = queue.pop(0)
            if u < 4:
                take_credit(k)
            rs_x_copy(k, u).start()
            flight.append([0, k, u])

    def grad_unit(k, u, left, right):
        put(k, 0, dot(left, right))
        queue.append((k, u))

    stages = [rs_y, rs_z, rs_2, rs_f, rs_end]

    def rs_tick():
        for item in list(flight):
            n, k, u = item
            stages[n](k, u)
            item[0] = n + 1
            if item[0] == len(stages):
                flight.remove(item)
                if u >= 8:
                    give_credit(k)
        inject()

    def give_credit(k):
        pl.semaphore_signal(credit.at[0, k], inc=1, device_id=x_neigh, device_id_type=MESH)
        pl.semaphore_signal(credit.at[1, k], inc=1, device_id=y_neigh, device_id_type=MESH)
        for o in range(1, line):
            pl.semaphore_signal(credit.at[2, k], inc=1, device_id=z_peer(o), device_id_type=MESH)

    def take_credit(k):
        pl.semaphore_wait(credit.at[0, k], 1)
        pl.semaphore_wait(credit.at[1, k], 1)
        pl.semaphore_wait(credit.at[2, k], line - 1)

    def transpose_into(dst, src, lanes_at):
        def move(i, carry):
            at = pl.ds(pl.multiple_of(i * 128, 128), 128)
            dst[at, :] = src[:, pl.ds(pl.multiple_of(lanes_at + i * 128, 128), 128)].T
            return carry

        lax.fori_loop(0, width // 128, move, 0)

    for h in range(2):
        transpose_into(tr, act, h * width)
        for j in range(2):
            k = 2 * h + j
            grad_unit(k, 8 + k, tr[...], go[:, j * UNIT : (j + 1) * UNIT])
            rs_tick()
            ag_step()
    transpose_into(tr, n2, 0)
    transpose_into(tr_att, att, 0)
    ag_until(UNITS - 1)

    span = max(1, tile // (2 * r))

    def hidden_back(n, carry):
        z = n * span
        for h in range(2):
            total = None
            for j in range(2):
                part = columns([w[8 + 2 * h + j, b, pl.ds(z, span)] for b in range(BLOCKS)])
                term = dot_cols(go[:, j * UNIT : (j + 1) * UNIT], part)
                total = term if total is None else total + term
            to = pl.ds(pl.multiple_of(h * width + n * (span * 2 * r), span * 2 * r), span * 2 * r)
            low = (total * fac[:, to].astype(F32)).astype(BF16)
            fac[:, to] = low
            sums = jnp.sum(fold8(low.astype(F32)), 0, keepdims=True)
            at = pl.ds(pl.multiple_of(n * (span * 2 * r), span * 2 * r), span * 2 * r)
            vg[pl.ds(8 + 2 * c + h, 1), at] = sums
        return carry

    vg[...] = jnp.zeros_like(vg)
    lax.fori_loop(0, line // span, hidden_back, 0)

    def expand_grad(u):
        grad_unit(4 + u, 4 + u, tr[...], fac[:, u * UNIT : (u + 1) * UNIT])

    expand_grad(0)
    rs_tick()

    def back_partial(src, lanes, first, rows_at, dst):
        def back(n, carry):
            total = None
            for u in range(4):
                part = columns([w[first + u, b, pl.ds(n * span, span)] for b in range(lanes // PAIR)])
                term = dot_cols(src[rows_at, u * lanes : (u + 1) * lanes], part)
                total = term if total is None else total + term
            dst[:, pl.ds(pl.multiple_of(n * (span * 2 * r), span * 2 * r), span * 2 * r)] = total
            return carry

        lax.fori_loop(0, line // span, back, 0)

    back_partial(fac, UNIT, 4, oth_rows, send_p)
    p2_copy = remote(send_p, recv_p, sib.at[0, 5], sib.at[1, 5], sibling)
    p2_copy.start()
    expand_grad(1)
    back_partial(fac, UNIT, 4, my_rows, own_p)
    rs_tick()
    p2_copy.wait()

    zeros8 = jnp.zeros((8, width), F32)

    def norm_two_back(i, carry):
        at = pl.ds(pl.multiple_of(i * chunk, chunk), chunk)
        to = pl.ds(pl.multiple_of(c * own + i * chunk, chunk), chunk)
        unit, rstd = unit_rows(resid[at, :])
        gn = own_p[at, :] + recv_p[at, :]
        grad_out = go[to, :].astype(F32)
        gr = grad_out + norm_back(gn, unit, rstd, gain_two)
        own_p[at, :] = gr
        low = gr.astype(BF16)
        gb[to, :] = low
        a, b, e, f = carry
        return (a + fold8(gn * unit), b + fold8(gn), e + fold8(low.astype(F32)), f + fold8(grad_out))

    sums = lax.fori_loop(0, own // chunk, norm_two_back, (zeros8,) * 4)
    for row, v in zip((2, 3, 6, 7), sums):
        vg[row : row + 1, :] = jnp.sum(v, 0, keepdims=True)
    gb_copy = remote(gb.at[my_rows], gb.at[my_rows], sib.at[0, 6], sib.at[1, 6], sibling)
    gb_copy.start()

    expand_grad(2)
    rs_tick()
    expand_grad(3)
    transpose_into(tr, n1, 0)
    gb_copy.wait_recv()

    head_rows = pl.ds(c * (line // 2), line // 2)
    n2[:, :UNIT] = (
        dot_cols(gb[:, my_half], own_out(head_rows)) + dot_cols(gb[:, oth_half], oth_out(head_rows))
    ).astype(BF16)
    rs_tick()

    def attend_backward(p):
        q_at, k_at, v_at = pair_lanes(p)
        own_lanes = slice(p * PAIR, (p + 1) * PAIR)
        dk_acc[...] = jnp.zeros_like(dk_acc)
        dv_acc[...] = jnp.zeros_like(dv_acc)

        def some(j, carry):
            at = pl.ds(pl.multiple_of(j * PAIR, PAIR), PAIR)
            both = two_heads(qkv[at, q_at])
            grads = two_heads(n2[at, own_lanes])
            mask = kbias[...]
            scores = dot_cols(qkv[:, k_at], both) + jnp.concatenate([mask, mask], 1)
            chance = jnp.exp(scores - lse[pl.ds(p * q_chunks + j, 1), :])
            dv_acc[...] += dot(chance.astype(BF16), grads)
            grad_chance = dot_cols(qkv[:, v_at], grads)
            inner = jnp.sum(chance * grad_chance, 0, keepdims=True)
            grad_scores = (chance * (grad_chance - inner)).astype(BF16)
            dk_acc[...] += dot(grad_scores, both)
            out = dot_rows(qkv[:, k_at], grad_scores)
            out = jnp.where(low_row, out[:, :PAIR], out[:, PAIR:]) * HEAD_DIM**-0.5
            qkv[at, q_at] = out.T.astype(BF16)
            return carry

        lax.fori_loop(0, q_chunks, some, 0)
        qkv[:, k_at] = dk_acc[...].astype(BF16)
        qkv[:, v_at] = dv_acc[...].astype(BF16)
        vg[4:5, att_lanes(p)] = jnp.sum(fold8(qkv[:, q_at].astype(F32)), 0, keepdims=True)
        vg[5:6, att_lanes(p)] = jnp.sum(fold8(qkv[:, v_at].astype(F32)), 0, keepdims=True)

    for p in range(4):
        attend_backward(p)
        put(p, 0, dot(tr[...], qkv[:, p * qkv_lanes : (p + 1) * qkv_lanes]))
        put(p, BLOCKS - 1, dot(tr_att[...], gb[:, att_lanes(p)]))
        queue.append((p, p))
        rs_tick()

    back_partial(qkv, qkv_lanes, 0, oth_rows, send_p)
    p1_copy = remote(send_p, recv_p, sib.at[0, 7], sib.at[1, 7], sibling)
    p1_copy.start()
    back_partial(qkv, qkv_lanes, 0, my_rows, dst_p)
    rs_tick()
    p1_copy.wait()

    def norm_one_back(i, carry):
        at = pl.ds(pl.multiple_of(i * chunk, chunk), chunk)
        unit, rstd = unit_rows(tok_own[at, :].astype(F32))
        gn = dst_p[at, :] + recv_p[at, :]
        out = own_p[at, :] + norm_back(gn, unit, rstd, gain_one)
        tok_own[at, :] = out.astype(BF16)
        a, b = carry
        return (a + fold8(gn * unit), b + fold8(gn))

    sums = lax.fori_loop(0, own // chunk, norm_one_back, (zeros8,) * 2)
    for row, v in zip((0, 1), sums):
        vg[row : row + 1, :] = jnp.sum(v, 0, keepdims=True)
    o_tok[x] = tok_own[my_block, :]
    tok_copy = remote(tok_own.at[oth_block], o_tok.at[x], xe.at[0, 3], xe.at[1, 3], x_neigh)
    tok_copy.start()
    rs_tick()

    def branch(dst, rows_at, add):
        def out(n, carry):
            for j in range(2):
                total = None
                for h in range(2):
                    part = columns([w[8 + 2 * h + j, 2 * n], w[8 + 2 * h + j, 2 * n + 1]])
                    term = dot(act[rows_at, h * width : (h + 1) * width], part)
                    total = term if total is None else total + term
                to = pl.ds(pl.multiple_of(j * UNIT + n * tile, tile), tile)
                dst[:, to] = dst[:, to] + total if add else total
            return carry

        lax.fori_loop(0, UNIT // tile, out, 0)

    branch(send_p, oth_rows, False)
    m_copy = remote(send_p, recv_m, sib.at[0, 8], sib.at[1, 8], sibling)
    m_copy.start()
    branch(resid, my_rows, True)
    rs_tick()
    m_copy.wait()

    bias_out = vec[7:8, :]

    def finish_block(i, carry):
        at = pl.ds(pl.multiple_of(i * chunk, chunk), chunk)
        out = live(pl.ds(pl.multiple_of(c * own + i * chunk, chunk), chunk)) * (resid[at, :] + recv_m[at, :] + bias_out)
        cot_own[at, :] = out.astype(BF16)
        return carry

    lax.fori_loop(0, own // chunk, finish_block, 0)
    o_blk[x] = cot_own[my_block, :]
    blk_copy = remote(cot_own.at[oth_block], o_blk.at[x], xe.at[0, 2], xe.at[1, 2], x_neigh)
    blk_copy.start()

    for n, to in enumerate((sibling, x_neigh, y_neigh)):
        copy = remote(vg, vr.at[n], vs.at[0, 1 + n], vs.at[1, 1 + n], to)
        copy.start()
        copy.wait()
        vg[...] += vr[n]
        rs_tick()

    def send_vz(o, carry):
        remote(vg, vz.at[zi], vs.at[0, 4], vs.at[1, 4], (lax.rem(zi + o, line) * 2 + yi, s)).start()
        return carry

    lax.fori_loop(1, line, send_vz, 0)
    vz[zi] = vg[...]
    wait_bytes(vz.at[pl.ds(0, line - 1)], vs.at[1, 4])
    wait_bytes(vz.at[pl.ds(0, line - 1)], vs.at[0, 4])
    o_vec[...] = lax.fori_loop(1, line, lambda i, t: t + vz[i], vz[0])

    while flight or queue:
        rs_tick()

    blk_copy.wait()
    tok_copy.wait()
    wait_bytes(vec_all.at[pl.ds(0, dp_n - 1)], vs.at[0, 0])
    for copy in [n1_copy, go_copy, att_copy, gb_copy] + [wo_copy(p) for p in range(4)]:
        copy.wait_send()
    for u in range(UNITS):
        wait_bytes(z_bytes(u), ag.at[0, u])
        ag_y_copy(u).wait_send()
        ag_x_copy(u).wait_send()


def adamw(grad, moment, square, weight, rate, decay):
    momentum = BETA_ONE * moment + (1.0 - BETA_ONE) * grad
    variance = BETA_TWO * square + (1.0 - BETA_TWO) * grad * grad
    first_fix = 1.0 - BETA_ONE**STEP
    second_fix = 1.0 - BETA_TWO**STEP
    direction = momentum / first_fix / (jnp.sqrt(variance / second_fix) + EPS_ADAM)
    updated = weight - rate * (direction + decay * weight)
    return (momentum, variance, updated, updated.astype(BF16))


def body(
    tokens, cotangent, key_mask,
    attention_weights, expand_weights, shrink_weights, vector_params,
    attention_moment, attention_square, expand_moment, expand_square,
    shrink_moment, shrink_square, vector_moment, vector_square,
):
    dp_n = lax.axis_size("dp")
    line = dp_n // 2
    d = lax.axis_index("dp")
    place = lax.axis_index("seq")
    x, c = place // 2, place % 2
    _, local_len, width = tokens.shape
    r = width // dp_n
    block = -(-local_len // 16) * 16
    own, rows = 2 * block, 4 * block
    pad = ((0, 0), (0, block - local_len), (0, 0))

    keep = lax.dynamic_index_in_dim(key_mask, x, 0, keepdims=False).reshape(2, 2, local_len)
    keep = jnp.pad(keep.transpose(1, 0, 2), ((0, 0), (0, 0), pad[1])).reshape(2, own)
    kbias = jnp.broadcast_to(jnp.where(keep > 0, 0.0, -1e30).astype(F32).reshape(rows, 1), (rows, PAIR))
    p_exp = expand_weights
    if r % 128:
        p_exp = lax.dynamic_index_in_dim(expand_weights.reshape(r, dp_n, 2, 2, r), c, 2, keepdims=False)
        p_exp = p_exp.transpose(2, 0, 1, 3).reshape(2, r, 2 * BLOCKS, PAIR).transpose(0, 2, 1, 3).reshape(4, BLOCKS, r, PAIR)
    vec_len = vector_params.shape[0]
    vec_rows = -(-vec_len // 1024) * 8
    p_vec = jnp.pad(vector_params.astype(BF16).astype(F32), (0, vec_rows * 128 - vec_len)).reshape(vec_rows, 128)

    vmem = pl.BlockSpec(memory_space=pltpu.VMEM)
    hbm = pl.BlockSpec(memory_space=pl.ANY)
    padded = jax.ShapeDtypeStruct((2, block, width), BF16)
    o_blk, o_tok, o_att, o_exp, o_shr, o_vec = pl.pallas_call(
        functools.partial(layer_kernel, line, vec_len),
        out_shape=(
            padded,
            padded,
            jax.ShapeDtypeStruct((r, 4 * width), BF16),
            jax.ShapeDtypeStruct((4, 2, BLOCKS, r, PAIR) if r % 128 else (r, 4 * width), BF16),
            jax.ShapeDtypeStruct((4 * r, width), BF16),
            jax.ShapeDtypeStruct((16, width), F32),
        ),
        in_specs=[vmem] * 4 + [hbm] * 3,
        out_specs=(vmem, vmem, hbm, hbm, hbm, vmem),
        scratch_shapes=[
            pltpu.VMEM((UNITS, BLOCKS, line, 2, r, PAIR), BF16),
            pltpu.VMEM((4, line, 2, r, PAIR), BF16),
            pltpu.VMEM((SLOTS, BLOCKS, line, 2, r, PAIR), BF16),
            pltpu.VMEM((SLOTS, RS_EDGE, line, 2, r, PAIR), BF16),
            pltpu.VMEM((SLOTS, RS_WINDOW, line, r, PAIR), BF16),
            pltpu.VMEM((SLOTS, line - 1, RS_WINDOW, r, PAIR), BF16),
            pltpu.VMEM((SLOTS, RS_WINDOW, r, PAIR), BF16),
            pltpu.VMEM((SLOTS, RS_WINDOW, r, PAIR), BF16),
            pltpu.VMEM((SLOTS, BLOCKS, r, PAIR), BF16),
            pltpu.VMEM((dp_n, vec_rows, 128), F32),
            pltpu.VMEM((16, width), F32),
            pltpu.VMEM((1, 2 * width), F32),
            pltpu.VMEM((16, width), F32),
            pltpu.VMEM((3, 16, width), F32),
            pltpu.VMEM((line, 16, width), F32),
            pltpu.VMEM((own, width), BF16),
            pltpu.VMEM((own, width), BF16),
            pltpu.VMEM((rows, width), BF16),
            pltpu.VMEM((rows, width), BF16),
            pltpu.VMEM((rows, 3 * UNIT), BF16),
            pltpu.VMEM((rows, width), BF16),
            pltpu.VMEM(((rows // PAIR) * (UNIT // PAIR), 2 * PAIR), F32),
            pltpu.VMEM((own, width), F32),
            pltpu.VMEM((rows, width), BF16),
            pltpu.VMEM((rows, 2 * width), BF16),
            pltpu.VMEM((rows, 2 * width), BF16),
            pltpu.VMEM((own, width), F32),
            pltpu.VMEM((own, width), F32),
            pltpu.VMEM((own, width), F32),
            pltpu.VMEM((own, width), F32),
            pltpu.VMEM((own, width), F32),
            pltpu.VMEM((rows, width), BF16),
            pltpu.VMEM((width, rows), BF16),
            pltpu.VMEM((width, rows), BF16),
            pltpu.VMEM((rows, PAIR), F32),
            pltpu.VMEM((rows, PAIR), F32),
            pltpu.SemaphoreType.DMA((6, UNITS)),
            pltpu.SemaphoreType.DMA((11, UNITS)),
            pltpu.SemaphoreType.DMA((2, 9)),
            pltpu.SemaphoreType.DMA((2, 4)),
            pltpu.SemaphoreType.DMA((2, 4)),
            pltpu.SemaphoreType.DMA((2, 5)),
            pltpu.SemaphoreType.DMA((UNITS,)),
            pltpu.SemaphoreType.REGULAR((3, 4)),
        ],
        compiler_params=pltpu.CompilerParams(
            collective_id=0, has_side_effects=True, vmem_limit_bytes=VMEM_LIMIT
        ),
        name="layer",
    )(jnp.pad(tokens, pad), jnp.pad(cotangent, pad), kbias, p_vec, attention_weights, p_exp, shrink_weights)

    block_output = o_blk[:, :local_len]
    token_gradient = o_tok[:, :local_len]
    grad_attention, grad_shrink = o_att.astype(F32), o_shr.astype(F32)
    if r % 128:
        o_exp = o_exp.transpose(3, 1, 0, 2, 4).reshape(r, 2, 2, dp_n, r).transpose(0, 3, 1, 2, 4).reshape(r, 4 * width)
    grad_expand = o_exp.astype(F32)
    hidden_sums = o_vec[8:12].reshape(2, 2, dp_n, r).transpose(2, 0, 1, 3).reshape(4, width)
    grad_vector = jnp.concatenate([o_vec[0:8], hidden_sums], 0).reshape(dp_n, vec_len)
    grad_vector = lax.dynamic_index_in_dim(grad_vector, d, 0, keepdims=False)

    attention_out = adamw(
        grad_attention, attention_moment, attention_square, attention_weights, RATE_MATRIX, DECAY_MATRIX
    )
    expand_out = adamw(grad_expand, expand_moment, expand_square, expand_weights, RATE_MATRIX, DECAY_MATRIX)
    shrink_out = adamw(grad_shrink, shrink_moment, shrink_square, shrink_weights, RATE_MATRIX, DECAY_MATRIX)
    vector_out = adamw(grad_vector, vector_moment, vector_square, vector_params, RATE_VECTOR, 0.0)
    return (block_output, token_gradient, *attention_out, *expand_out, *shrink_out, *vector_out)


VMEM_LIMIT = 62 * 2**20


def solution(mesh):
    split = P("dp", "seq", None)
    rows = P("dp", None)
    flat = P("dp")
    return jax.shard_map(
        body,
        mesh=mesh,
        in_specs=(split, split, rows, rows, rows, rows, flat) + (rows,) * 6 + (flat, flat),
        out_specs=(split, split) + (rows,) * 12 + (flat,) * 4,
        check_vma=False,
    )
```

```python
import functools

import jax
import jax.numpy as jnp
from jax import lax
from jax.experimental import pallas as pl
from jax.experimental.pallas import tpu as pltpu
from jax.sharding import PartitionSpec as P

HEAD_DIM = 64
STEP = 5
EPS_NORM = 1e-05
BETA_ONE = 0.5
BETA_TWO = 0.5
EPS_ADAM = 1e-08
RATE_MATRIX = 0.05
RATE_VECTOR = 0.2
DECAY_MATRIX = 0.1
SLOPE = 1.702

BF16 = jnp.bfloat16
F32 = jnp.float32
MESH = pl.DeviceIdType.MESH

UNIT = 512
BLOCKS = 4
RS_EDGE = 1
RS_WINDOW = BLOCKS - RS_EDGE
HALF = 2
UNITS = 8
ITEMS = 12
PAIR = 128


def dot(a, b):
    return jnp.dot(a, b, preferred_element_type=F32)


def dot_rows(a, b):
    return lax.dot_general(a, b, (((0,), (0,)), ((), ())), preferred_element_type=F32)


def dot_cols(a, b):
    return lax.dot_general(a, b, (((1,), (1,)), ((), ())), preferred_element_type=F32)


def unit_rows(x):
    centred = x - jnp.mean(x, -1, keepdims=True)
    rstd = lax.rsqrt(jnp.mean(centred * centred, -1, keepdims=True) + EPS_NORM)
    return centred * rstd, rstd


def norm_back(grad_normed, unit, rstd, gain):
    g = grad_normed * gain
    return rstd * (g - jnp.mean(g, -1, keepdims=True) - unit * jnp.mean(g * unit, -1, keepdims=True))


def fold8(v):
    return jnp.sum(v.reshape(v.shape[0] // 8, 8, v.shape[1]), 0)


def layer_kernel(
    line, vec_len,
    tok, cot, kbias, p_vec, p_att, p_exp, p_shr,
    o_blk, o_tok, o_att, o_exp, o_shr, o_vec,
    w, w_oth, g, rx, ry, rz, ry_f, rz_f, s_own, s_oth, f_own, f_oth,
    vec_all, vec, bias_h, vg, vr, vz,
    tok_own, cot_own,
    n1, go, qkv, att, lse, resid, n2, act, fac,
    own_p, keep_p, send_a, send_b, recv_a, recv_b, recv_m,
    gb, tr, dk_acc, dv_acc,
    ag, rs, sib, wo, xe, vs, fill, loc,
):
    dp_n = 2 * line
    r = w.shape[4]
    block = tok.shape[1]
    own = 2 * block
    rows = 2 * own
    width = tok.shape[2]
    half = UNIT
    d = lax.axis_index("dp")
    s = lax.axis_index("seq")
    zi, yi = d // 2, d % 2
    x, c = s // 2, s % 2
    sibling = (d, x * 2 + 1 - c)
    x_neigh = (d, (1 - x) * 2 + c)
    y_neigh = (zi * 2 + 1 - yi, s)

    def z_peer(o):
        return (lax.rem(zi + o, line) * 2 + yi, s)

    def own_rows(core):
        return pl.ds(pl.multiple_of(core * own, own), own)

    def ff_rows(chip, core):
        return pl.ds(pl.multiple_of(chip * rows + core * own, own), own)

    my_rows = own_rows(c)
    my_half = pl.ds(pl.multiple_of(c * half, half), half)
    oth_half = pl.ds(pl.multiple_of((1 - c) * half, half), half)
    my_block = pl.ds(pl.multiple_of(x * block, block), block)
    oth_block = pl.ds(pl.multiple_of((1 - x) * block, block), block)

    def window(edge):
        return pl.ds(x * edge, BLOCKS - edge)

    def mine(edge):
        return pl.ds(x * (BLOCKS - edge), edge)

    def theirs(edge):
        return pl.ds((1 - x) * (BLOCKS - edge), edge)

    def ag_edge(u):
        return 2 if u == 2 else 1

    def unit_of(i):
        return (i, None) if i < 4 else (4 + (i - 4) // 2, (i - 4) % 2 * HALF)

    def remote(src, dst, send, recv, to):
        return pltpu.make_async_remote_copy(
            src_ref=src, dst_ref=dst, send_sem=send, recv_sem=recv, device_id=to, device_id_type=MESH
        )

    def wait_bytes(ref, sem):
        pltpu.make_async_copy(ref, ref, sem).wait()

    wide = r % 128 == 0

    def unit_parts(u, place):
        if u < 4:
            core = place % 2
            return [
                (slice(None), pl.ds(pl.multiple_of(n * width + core * half + u * PAIR, PAIR), PAIR)) for n in range(BLOCKS)
            ]
        if u < 6:
            if not wide:
                return None
            parts = []
            for n in range((u - 4) * UNIT, (u - 3) * UNIT, PAIR):
                at = n // r * 4 * r + place * r + n % r
                parts.append((slice(None), pl.ds(pl.multiple_of(at, PAIR), PAIR)))
            return parts
        first = (u - 6) * UNIT
        held = pl.ds(pl.multiple_of(place * r, r), r)
        return [(held, slice(first + n * PAIR, first + (n + 1) * PAIR)) for n in range(BLOCKS)]

    def stage(u):
        n = u % 4 if u < 4 else u % 2
        hold = own_p if u < 4 else send_a if u < 6 else send_b
        return hold.at[(n // 2) * r : (n // 2 + 1) * r, (n % 2) * UNIT : (n % 2 + 1) * UNIT]

    def matrix(u, refs):
        return refs[0 if u < 4 else 1 if u < 6 else 2]

    for u in range(UNITS):
        parts = unit_parts(u, s)
        source = matrix(u, (p_att, p_exp, p_shr))
        for n in range(BLOCKS):
            part = source.at[parts[n]] if parts else source.at[u - 4, n]
            pltpu.make_async_copy(part, stage(u).at[:, n * PAIR : (n + 1) * PAIR], fill.at[u, n // HALF if u >= 4 else 0]).start()

    vec_all[d] = p_vec[...]
    own_copies = [
        pltpu.make_async_copy(tok.at[x], tok_own.at[my_block], loc.at[0]),
        pltpu.make_async_copy(cot.at[x], cot_own.at[my_block], loc.at[1]),
    ]
    for copy in own_copies:
        copy.start()

    barrier = pltpu.get_barrier_semaphore()

    def greet(o, carry):
        pl.semaphore_signal(barrier, inc=1, device_id=(lax.rem(d + o, dp_n), s), device_id_type=MESH)
        return carry

    lax.fori_loop(1, dp_n, greet, 0)
    pl.semaphore_signal(barrier, inc=1, device_id=sibling, device_id_type=MESH)
    pl.semaphore_signal(barrier, inc=1, device_id=x_neigh, device_id_type=MESH)
    pl.semaphore_wait(barrier, dp_n + 1)

    def send_vec(o, carry):
        remote(p_vec, vec_all.at[d], vs.at[0, 0], vs.at[1, 0], (lax.rem(d + o, dp_n), s)).start()
        return carry

    lax.fori_loop(1, dp_n, send_vec, 0)
    x_copies = [
        remote(tok.at[1 - x], tok_own.at[my_block], xe.at[0, 0], xe.at[1, 0], x_neigh),
        remote(cot.at[1 - x], cot_own.at[my_block], xe.at[0, 1], xe.at[1, 1], x_neigh),
    ]
    for copy in x_copies:
        copy.start()

    def ag_blocks(i):
        u, first = unit_of(i)
        return window(ag_edge(u)) if first is None else pl.ds(first, HALF)

    def ag_z(i):
        u, first = unit_of(i)
        count = BLOCKS - ag_edge(u) if first is None else HALF
        if first is None:
            wait_bytes(stage(u), fill.at[u, 0])
        else:
            wait_bytes(stage(u).at[:, first * PAIR : (first + HALF) * PAIR], fill.at[u, first // HALF])
        for n in range(count):
            b = x * ag_edge(u) + n if first is None else first + n
            w[u, b, zi, yi] = stage(u)[:, pl.ds(pl.multiple_of(b * PAIR, PAIR), PAIR)].astype(BF16)
        part = w.at[u, ag_blocks(i), zi, yi]
        for o in range(1, line):
            remote(part, part, ag.at[0, i], ag.at[1, i], z_peer(o)).start()

    def ag_y_copy(i):
        part = w.at[unit_of(i)[0], ag_blocks(i), :, yi]
        return remote(part, part, ag.at[2, i], ag.at[3, i], y_neigh)

    def ag_x_copy(i):
        part = w.at[i, mine(ag_edge(i))]
        return remote(part, part, ag.at[4, i], ag.at[5, i], x_neigh)

    def z_bytes(i):
        return w.at[unit_of(i)[0], ag_blocks(i), pl.ds(0, line - 1), yi]

    def ag_y(i):
        wait_bytes(z_bytes(i), ag.at[1, i])
        ag_y_copy(i).start()

    def ag_x(i):
        ag_y_copy(i).wait_recv()
        if i < 4:
            ag_x_copy(i).start()

    def ag_end(i):
        if i < 4:
            ag_x_copy(i).wait_recv()

    steps = []
    for t in range(ITEMS + 2):
        def step(t=t):
            if t + 3 < ITEMS:
                ag_z(t + 3)
            if t < ITEMS:
                ag_y(t)
            if 0 <= t - 1 < ITEMS:
                ag_x(t - 1)
            if 0 <= t - 2 < ITEMS:
                ag_end(t - 2)
        steps.append(step)
    ag_z(0)
    ag_z(1)
    ag_z(2)
    done = [0]

    def ag_step():
        if done[0] < len(steps):
            steps[done[0]]()
            done[0] += 1

    def ag_until(i):
        while done[0] < i + (3 if i < 4 else 2):
            ag_step()

    wait_bytes(vec_all.at[pl.ds(0, dp_n - 1)], vs.at[1, 0])
    grain = 128 if vec_len % 128 == 0 else 64

    def vec_lanes(first):
        parts = []
        for e in range(first, first + 128, grain):
            o = e % vec_len
            parts.append(vec_all[e // vec_len, o // 128 : o // 128 + 1, o % 128 : o % 128 + grain])
        return parts[0] if len(parts) == 1 else jnp.concatenate(parts, 1)

    for row in range(12):
        for lane in range(0, width, 128):
            vec[row : row + 1, lane : lane + 128] = vec_lanes(row * width + lane)

    def hidden_bias(place):
        parts = []
        for shard in range(dp_n):
            n = shard * 4 * r + place * r
            parts.append(vec[8 + n // width : 9 + n // width, n % width : n % width + r])
        return jnp.concatenate(parts, 1)

    ag_step()
    low_half = jnp.where(s == 0, hidden_bias(0), hidden_bias(1))
    bias_h[...] = jnp.where(s < 2, low_half, jnp.where(s == 2, hidden_bias(2), hidden_bias(3)))

    for copy in x_copies + own_copies:
        copy.wait()

    def live(to):
        return jnp.where(kbias[to, 0:1] < 0, 0.0, 1.0)

    chunk = block // 2

    def chunks(first, i):
        return pl.ds(pl.multiple_of(first + i * chunk, chunk), chunk)

    gain_one, shift_one = vec[0:1, :], vec[1:2, :]

    def norm_one(i, carry):
        at, to = chunks(0, i), chunks(c * own, i)
        unit, _ = unit_rows(tok_own[at, :].astype(F32))
        n1[to, :] = (unit * gain_one + shift_one).astype(BF16)
        go[chunks(x * rows + c * own, i), :] = (cot_own[at, :].astype(F32) * live(to)).astype(BF16)
        return carry

    lax.fori_loop(0, own // chunk, norm_one, 0)

    def rows_copies(ref, n):
        here, there = ref.at[ff_rows(x, c)], ref.at[ff_rows(1 - x, c)]
        return (
            remote(here, here, sib.at[0, n], sib.at[1, n], sibling),
            remote(here, here, xe.at[0, n], xe.at[1, n], x_neigh),
            remote(there, there, sib.at[0, n + 1], sib.at[1, n + 1], sibling),
        )

    n1_copy = remote(n1.at[my_rows], n1.at[my_rows], sib.at[0, 0], sib.at[1, 0], sibling)
    n1_copy.start()
    go_copies = rows_copies(go, 4)
    go_copies[1].start()
    go_copies[0].start()
    ag_step()
    n1_copy.wait_recv()

    low_lane = lax.broadcasted_iota(jnp.int32, (PAIR, PAIR), 1) < HEAD_DIM
    low_row = lax.broadcasted_iota(jnp.int32, (PAIR, PAIR), 0) < HEAD_DIM
    q_chunks = rows // PAIR

    def two_heads(v):
        zero = jnp.zeros_like(v)
        return jnp.concatenate([jnp.where(low_lane, v, zero), jnp.where(low_lane, zero, v)], 0)

    qkv_lanes = 3 * PAIR

    def pair_lanes(p):
        return tuple(slice(p * qkv_lanes + n * PAIR, p * qkv_lanes + (n + 1) * PAIR) for n in range(3))

    def att_lanes(p):
        return pl.ds(pl.multiple_of(c * half + p * PAIR, PAIR), PAIR)

    def wo_copy(p):
        return remote(w.at[p, BLOCKS - 1], w_oth.at[p], wo.at[0, p], wo.at[1, p], sibling)

    def columns(blocks):
        return jnp.concatenate([v.reshape(-1, PAIR) for v in blocks], 1)

    def attend_forward(p):
        q_at, k_at, v_at = pair_lanes(p)
        out = dot(n1[...], columns([w[p, n] for n in range(3)]))
        queries = (out[:, :PAIR] + vec[4:5, att_lanes(p)]).astype(BF16)
        qkv[:, q_at] = queries * jnp.asarray(HEAD_DIM**-0.5, BF16)
        qkv[:, k_at] = out[:, PAIR : 2 * PAIR].astype(BF16)
        qkv[:, v_at] = (out[:, 2 * PAIR :] + vec[5:6, att_lanes(p)]).astype(BF16)

        def some(j, carry):
            at = pl.ds(pl.multiple_of(j * PAIR, PAIR), PAIR)
            mask = kbias[...]
            scores = dot_cols(qkv[:, k_at], two_heads(qkv[at, q_at])) + jnp.concatenate([mask, mask], 1)
            highest = jnp.max(scores, 0, keepdims=True)
            raised = jnp.exp(scores - highest)
            total = jnp.sum(raised, 0, keepdims=True)
            out = dot_rows(qkv[:, v_at], raised.astype(BF16)) / total
            out = jnp.where(low_row, out[:, :PAIR], out[:, PAIR:])
            att[at, att_lanes(p)] = out.T.astype(BF16)
            lse[pl.ds(p * q_chunks + j, 1), :] = highest + jnp.log(total)
            return carry

        lax.fori_loop(0, q_chunks, some, 0)

    for p in range(4):
        ag_until(p)
        wo_copy(p).start()
        attend_forward(p)
        if p == 1:
            go_copies[1].wait_recv()
            go_copies[2].start()
    att_copy = remote(att.at[:, my_half], att.at[:, my_half], sib.at[0, 1], sib.at[1, 1], sibling)
    att_copy.start()
    ag_step()
    for p in range(4):
        wo_copy(p).wait_recv()
    att_copy.wait_recv()

    bias_att = vec[6:7, :]
    mixed = att[my_rows, :]

    def own_out(z):
        return columns([w[p, BLOCKS - 1, z] for p in range(4)])

    def oth_out(z):
        return columns([w_oth[p, z] for p in range(4)])

    resid[:, my_half] = dot(mixed, own_out(slice(None)))
    resid[:, oth_half] = dot(mixed, oth_out(slice(None)))
    gain_two, shift_two = vec[2:3, :], vec[3:4, :]

    def norm_two(i, carry):
        at = chunks(0, i)
        res = resid[at, :] + tok_own[at, :].astype(F32) + bias_att
        resid[at, :] = res
        unit, _ = unit_rows(res)
        n2[chunks(x * rows + c * own, i), :] = (unit * gain_two + shift_two).astype(BF16)
        return carry

    lax.fori_loop(0, own // chunk, norm_two, 0)
    n2_copies = rows_copies(n2, 6)
    n2_copies[1].start()
    n2_copies[0].start()
    ag_step()
    n2_copies[0].wait_recv()

    tile = HALF * PAIR

    def expand(n, chip):
        u, first = unit_of(4 + n)
        at = pl.ds(pl.multiple_of(chip * rows, rows), rows)
        to = slice(n * tile, (n + 1) * tile)
        hidden = dot(n2[at, :], columns([w[u, first], w[u, first + 1]])) + bias_h[:, to]
        gate = jax.nn.sigmoid(SLOPE * hidden)
        act[at, to] = (hidden * gate).astype(BF16)
        fac[at, to] = (gate + SLOPE * hidden * gate * (1.0 - gate)).astype(BF16)

    for n in range(4):
        ag_until(4 + n)
        expand(n, x)
    n2_copies[1].wait_recv()
    n2_copies[2].start()
    go_copies[0].wait_recv()
    go_copies[2].wait_recv()
    n2_copies[2].wait_recv()
    for n in range(4):
        expand(n, 1 - x)

    rs_win = window(RS_EDGE)

    def rs_x_copy(i):
        return remote(g.at[i, theirs(RS_EDGE)], rx.at[i], rs.at[0, i], rs.at[1, i], x_neigh)

    def rs_y_copy(i):
        u, first = unit_of(i)
        if first is None:
            return remote(g.at[u, rs_win, :, 1 - yi], ry.at[i], rs.at[2, i], rs.at[3, i], y_neigh)
        return remote(g.at[u, pl.ds(first, HALF), :, 1 - yi], ry_f.at[i - 4], rs.at[2, i], rs.at[3, i], y_neigh)

    def rs_2_copy(i):
        if i < 4:
            return remote(s_own.at[i], s_oth.at[i], rs.at[6, i], rs.at[7, i], x_neigh)
        u, first = unit_of(i)
        return remote(f_own.at[u, pl.ds(first, HALF)], f_oth.at[i - 4], rs.at[6, i], rs.at[7, i], x_neigh)

    def to_result(i, n, place):
        u, first = unit_of(i)
        result = matrix(u, (o_att, o_exp, o_shr))
        parts = unit_parts(u, place)
        n = n + (first or 0)
        return result.at[parts[n]] if parts else result.at[u - 4, place, n]

    def rs_share(i, source, count, place, sems):
        for n in range(count):
            to = to_result(i, n, place)
            remote(source.at[n], to, rs.at[sems, i], rs.at[sems + 1, i], sibling).start()
            pltpu.make_async_copy(source.at[n], to, rs.at[sems + 2, i]).start()

    def rs_x_add(i):
        rs_x_copy(i).wait_recv()

        def add(z, carry):
            for n in range(RS_EDGE):
                b = x * RS_WINDOW + n
                g[i, b, z] = (g[i, b, z].astype(F32) + rx[i, n, z].astype(F32)).astype(BF16)
            return carry

        lax.fori_loop(0, line, add, 0)
        rs_y_copy(i).start()

    def rs_y_add(i):
        rs_y_copy(i).wait_recv()
        u, first = unit_of(i)
        count, base, got = (RS_WINDOW, x * RS_EDGE, ry.at[i]) if first is None else (HALF, first, ry_f.at[i - 4])

        def add(z, carry):
            for n in range(count):
                g[u, base + n, z, yi] = (g[u, base + n, z, yi].astype(F32) + got[n, z].astype(F32)).astype(BF16)
            return carry

        lax.fori_loop(0, line, add, 0)
        got = rz.at[i] if first is None else rz_f.at[i - 4]
        for o in range(1, line):
            z = lax.rem(zi + o, line)
            remote(g.at[u, pl.ds(base, count), z, yi], got.at[o - 1], rs.at[4, i], rs.at[5, i], z_peer(o)).start()

    def rs_z_add(i):
        u, first = unit_of(i)
        count, base, got = (RS_WINDOW, x * RS_EDGE, rz.at[i]) if first is None else (HALF, first, rz_f.at[i - 4])
        wait_bytes(got, rs.at[5, i])
        for n in range(count):
            total = g[u, base + n, zi, yi].astype(F32)
            for o in range(1, line):
                total = total + got[o - 1, n].astype(F32)
            if first is None:
                s_own[i, n] = total.astype(BF16)
            else:
                f_own[u, first + n] = total.astype(BF16)
        rs_2_copy(i).start()
        if first is not None:
            rs_share(i, f_own.at[u, pl.ds(first, HALF)], HALF, s, 8)

    def rs_join(i):
        rs_2_copy(i).wait_recv()
        if i >= 4:
            rs_share(i, f_oth.at[i - 4], HALF, (1 - x) * 2 + c, 11)
            return
        here, there = s_own[i], s_oth[i]
        first = jnp.where(x == 0, here, there)
        last = jnp.where(x == 0, there, here)
        f_own[i, 0] = first[0]
        for n in range(1, RS_WINDOW):
            f_own[i, n] = (first[n].astype(F32) + last[n - 1].astype(F32)).astype(BF16)
        f_own[i, RS_WINDOW] = last[RS_WINDOW - 1]
        rs_share(i, f_own.at[i], BLOCKS, s, 8)

    def rs_end(i):
        u, first = unit_of(i)
        if first is None:
            rs_x_copy(i).wait_send()
        rs_y_copy(i).wait_send()
        wait_bytes(rz.at[i] if first is None else rz_f.at[i - 4], rs.at[4, i])
        rs_2_copy(i).wait_send()
        sent = f_own.at[i] if first is None else f_oth.at[i - 4]
        for n in range(8, 11 if first is None else 14):
            wait_bytes(sent, rs.at[n, i])

    def put(u, first, value):
        for n in range(value.shape[1] // PAIR):
            part = value[:, n * PAIR : (n + 1) * PAIR].astype(BF16)
            g[u, first + n] = part.reshape(line, 2, r, PAIR)

    flight, queue = [], []

    def inject():
        if queue:
            i = queue.pop(0)
            if i < 4:
                rs_x_copy(i).start()
                flight.append([i, [rs_x_add, rs_y_add, rs_z_add, rs_join, rs_end]])
            else:
                rs_y_copy(i).start()
                flight.append([i, [rs_y_add, rs_z_add, rs_join, rs_end]])

    def rs_tick():
        for item in list(flight):
            item[1].pop(0)(item[0])
            if not item[1]:
                flight.remove(item)
        inject()

    def transpose_into(first, src, size):
        def move(i, carry):
            at = pl.ds(pl.multiple_of(i * 128, 128), 128)
            tr[at, first : first + size] = src[:, at].T
            return carry

        lax.fori_loop(0, width // 128, move, 0)

    transpose_into(0, act, 2 * rows)
    for n in range(4):
        u, first = unit_of(8 + n)
        put(u, first, dot(tr[...], go[:, n * tile : (n + 1) * tile]))
        queue.append(8 + n)
        rs_tick()
        ag_step()
    ag_until(ITEMS - 1)

    span = max(1, tile // (2 * r))
    part_rows = span * 2 * r

    def hidden_back(n, carry):
        z = pl.ds(n * span, span)
        to = pl.ds(pl.multiple_of(n * part_rows, part_rows), part_rows)
        sums = None
        for at in (slice(0, rows), slice(rows, 2 * rows)):
            total = None
            for j in range(2):
                part = columns([w[6 + j, b, z] for b in range(BLOCKS)])
                term = dot_cols(go[at, j * UNIT : (j + 1) * UNIT], part)
                total = term if total is None else total + term
            low = (total * fac[at, to].astype(F32)).astype(BF16)
            fac[at, to] = low
            folded = fold8(low.astype(F32))
            sums = folded if sums is None else sums + folded
        vg[pl.ds(8 + s, 1), to] = jnp.sum(sums, 0, keepdims=True)
        return carry

    vg[...] = jnp.zeros_like(vg)
    lax.fori_loop(0, line // span, hidden_back, 0)
    rs_tick()

    def back_partial(src, rows_at, units, blocks, dst):
        lanes = blocks * PAIR

        def back(n, carry):
            total = None
            for k, u in enumerate(units):
                part = columns([w[u, b, pl.ds(n * span, span)] for b in range(blocks)])
                term = dot_cols(src[rows_at, k * lanes : (k + 1) * lanes], part)
                total = term if total is None else total + term
            dst[:, pl.ds(pl.multiple_of(n * part_rows, part_rows), part_rows)] = total
            return carry

        lax.fori_loop(0, line // span, back, 0)

    def expand_grad(n):
        u, first = unit_of(4 + n)
        put(u, first, dot(tr[...], fac[:, n * tile : (n + 1) * tile]))
        queue.append(4 + n)

    def to_x(i, carry):
        at = chunks(0, i)
        cot_own[at, :] = (keep_p[at, :] + recv_b[at, :]).astype(BF16)
        return carry

    ff = (4, 5)
    back_partial(fac, ff_rows(1 - x, 1 - c), ff, BLOCKS, send_b)
    b_copy = remote(send_b, recv_b, sib.at[0, 8], sib.at[1, 8], sibling)
    b_copy.start()
    back_partial(fac, ff_rows(1 - x, c), ff, BLOCKS, keep_p)
    b_copy.wait()
    lax.fori_loop(0, own // chunk, to_x, 0)
    x_back = [
        remote(cot_own.at[pl.ds(n * block, block)], o_blk.at[n], xe.at[0, 7 + n], xe.at[1, 7 + n], x_neigh) for n in range(2)
    ]
    for copy in x_back:
        copy.start()
    back_partial(fac, ff_rows(x, 1 - c), ff, BLOCKS, send_a)
    a_copy = remote(send_a, recv_a, sib.at[0, 9], sib.at[1, 9], sibling)
    a_copy.start()
    rs_tick()
    back_partial(fac, ff_rows(x, c), ff, BLOCKS, own_p)
    transpose_into(0, n2, 2 * rows)
    expand_grad(0)
    rs_tick()
    expand_grad(1)
    a_copy.wait()
    for copy in x_back:
        copy.wait()

    zeros8 = jnp.zeros((8, width), F32)

    def norm_two_back(i, carry):
        at = chunks(0, i)
        unit, rstd = unit_rows(resid[at, :])
        gn = own_p[at, :] + recv_a[at, :] + o_blk[i // 2, pl.ds(pl.multiple_of(i % 2 * chunk, chunk), chunk)].astype(F32)
        grad_out = go[chunks(x * rows + c * own, i), :].astype(F32)
        gr = grad_out + norm_back(gn, unit, rstd, gain_two)
        own_p[at, :] = gr
        low = gr.astype(BF16)
        gb[chunks(c * own, i), :] = low
        a, b, e, f = carry
        return (a + fold8(gn * unit), b + fold8(gn), e + fold8(low.astype(F32)), f + fold8(grad_out))

    sums = lax.fori_loop(0, own // chunk, norm_two_back, (zeros8,) * 4)
    for row, v in zip((2, 3, 6, 7), sums):
        vg[row : row + 1, :] = jnp.sum(v, 0, keepdims=True)
    gb_copy = remote(gb.at[my_rows], gb.at[my_rows], sib.at[0, 2], sib.at[1, 2], sibling)
    gb_copy.start()
    rs_tick()
    expand_grad(2)
    expand_grad(3)
    transpose_into(0, n1, rows)
    transpose_into(rows, att, rows)
    for copy in n2_copies:
        copy.wait_send()
    gb_copy.wait_recv()
    rs_tick()

    quarter = line // 4
    for n in range(2):
        head_rows = pl.ds(c * (line // 2) + n * quarter, quarter)
        part = dot_cols(gb[:, my_half], own_out(head_rows)) + dot_cols(gb[:, oth_half], oth_out(head_rows))
        n2[:rows, n * tile : (n + 1) * tile] = part.astype(BF16)

    def attend_backward(p):
        q_at, k_at, v_at = pair_lanes(p)
        own_lanes = slice(p * PAIR, (p + 1) * PAIR)
        dk_acc[...] = jnp.zeros_like(dk_acc)
        dv_acc[...] = jnp.zeros_like(dv_acc)

        def some(j, carry):
            at = pl.ds(pl.multiple_of(j * PAIR, PAIR), PAIR)
            both = two_heads(qkv[at, q_at])
            grads = two_heads(n2[at, own_lanes])
            mask = kbias[...]
            scores = dot_cols(qkv[:, k_at], both) + jnp.concatenate([mask, mask], 1)
            chance = jnp.exp(scores - lse[pl.ds(p * q_chunks + j, 1), :])
            dv_acc[...] += dot(chance.astype(BF16), grads)
            grad_chance = dot_cols(qkv[:, v_at], grads)
            inner = jnp.sum(chance * grad_chance, 0, keepdims=True)
            grad_scores = (chance * (grad_chance - inner)).astype(BF16)
            dk_acc[...] += dot(grad_scores, both)
            out = dot_rows(qkv[:, k_at], grad_scores)
            out = jnp.where(low_row, out[:, :PAIR], out[:, PAIR:]) * HEAD_DIM**-0.5
            qkv[at, q_at] = out.T.astype(BF16)
            return carry

        lax.fori_loop(0, q_chunks, some, 0)
        qkv[:, k_at] = dk_acc[...].astype(BF16)
        qkv[:, v_at] = dv_acc[...].astype(BF16)
        vg[4:5, att_lanes(p)] = jnp.sum(fold8(qkv[:, q_at].astype(F32)), 0, keepdims=True)
        vg[5:6, att_lanes(p)] = jnp.sum(fold8(qkv[:, v_at].astype(F32)), 0, keepdims=True)

    for p in range(4):
        attend_backward(p)
        put(p, 0, dot(tr[:, :rows], qkv[:, p * qkv_lanes : (p + 1) * qkv_lanes]))
        put(p, BLOCKS - 1, dot(tr[:, rows:], gb[:, att_lanes(p)]))
        queue.append(p)
        rs_tick()

    heads = (0, 1, 2, 3)
    back_partial(qkv, own_rows(1 - c), heads, 3, send_a)
    p1_copy = remote(send_a, recv_a, sib.at[0, 3], sib.at[1, 3], sibling)
    p1_copy.start()
    back_partial(qkv, my_rows, heads, 3, keep_p)
    rs_tick()
    p1_copy.wait()

    def norm_one_back(i, carry):
        at = chunks(0, i)
        unit, rstd = unit_rows(tok_own[at, :].astype(F32))
        gn = keep_p[at, :] + recv_a[at, :]
        out = own_p[at, :] + norm_back(gn, unit, rstd, gain_one)
        tok_own[at, :] = out.astype(BF16)
        a, b = carry
        return (a + fold8(gn * unit), b + fold8(gn))

    sums = lax.fori_loop(0, own // chunk, norm_one_back, (zeros8,) * 2)
    for row, v in zip((0, 1), sums):
        vg[row : row + 1, :] = jnp.sum(v, 0, keepdims=True)
    o_tok[x] = tok_own[my_block, :]
    tok_copy = remote(tok_own.at[oth_block], o_tok.at[x], xe.at[0, 3], xe.at[1, 3], x_neigh)
    tok_copy.start()
    rs_tick()

    def branch(dst, rows_at, add):
        def out(n, carry):
            for j in range(2):
                part = columns([w[6 + j, 2 * n], w[6 + j, 2 * n + 1]])
                to = pl.ds(pl.multiple_of(j * UNIT + n * tile, tile), tile)
                total = dot(act[rows_at, :], part)
                dst[:, to] = dst[:, to] + total if add else total
            return carry

        lax.fori_loop(0, UNIT // tile, out, 0)

    branch(send_b, ff_rows(1 - x, 1 - c), False)
    bm_copy = remote(send_b, recv_b, sib.at[0, 10], sib.at[1, 10], sibling)
    bm_copy.start()
    branch(keep_p, ff_rows(1 - x, c), False)
    bm_copy.wait()
    lax.fori_loop(0, own // chunk, to_x, 0)
    xm_copy = remote(cot_own, n2.at[rows : rows + own], xe.at[0, 9], xe.at[1, 9], x_neigh)
    xm_copy.start()
    rs_tick()
    branch(send_a, ff_rows(x, 1 - c), False)
    am_copy = remote(send_a, recv_m, sib.at[0, 11], sib.at[1, 11], sibling)
    am_copy.start()
    branch(resid, ff_rows(x, c), True)
    rs_tick()

    for n, to in enumerate((sibling, x_neigh, y_neigh)):
        copy = remote(vg, vr.at[n], vs.at[0, 1 + n], vs.at[1, 1 + n], to)
        copy.start()
        copy.wait()
        vg[...] += vr[n]
        rs_tick()

    def send_vz(o, carry):
        remote(vg, vz.at[zi], vs.at[0, 4], vs.at[1, 4], (lax.rem(zi + o, line) * 2 + yi, s)).start()
        return carry

    lax.fori_loop(1, line, send_vz, 0)
    vz[zi] = vg[...]
    am_copy.wait()
    xm_copy.wait()
    bias_out = vec[7:8, :]

    def finish_block(i, carry):
        at = chunks(0, i)
        out = resid[at, :] + recv_m[at, :] + n2[chunks(rows, i), :].astype(F32) + bias_out
        cot_own[at, :] = (live(chunks(c * own, i)) * out).astype(BF16)
        return carry

    lax.fori_loop(0, own // chunk, finish_block, 0)
    o_blk[x] = cot_own[my_block, :]
    blk_copy = remote(cot_own.at[oth_block], o_blk.at[x], xe.at[0, 2], xe.at[1, 2], x_neigh)
    blk_copy.start()
    rs_tick()
    wait_bytes(vz.at[pl.ds(0, line - 1)], vs.at[1, 4])
    wait_bytes(vz.at[pl.ds(0, line - 1)], vs.at[0, 4])
    o_vec[...] = lax.fori_loop(1, line, lambda i, t: t + vz[i], vz[0])

    while flight or queue:
        rs_tick()

    blk_copy.wait()
    tok_copy.wait()
    wait_bytes(vec_all.at[pl.ds(0, dp_n - 1)], vs.at[0, 0])
    for copy in [n1_copy, att_copy, gb_copy, *go_copies] + [wo_copy(p) for p in range(4)]:
        copy.wait_send()
    for i in range(ITEMS):
        wait_bytes(z_bytes(i), ag.at[0, i])
        ag_y_copy(i).wait_send()
        if i < 4:
            ag_x_copy(i).wait_send()


def adamw(grad, moment, square, weight, rate, decay):
    momentum = BETA_ONE * moment + (1.0 - BETA_ONE) * grad
    variance = BETA_TWO * square + (1.0 - BETA_TWO) * grad * grad
    first_fix = 1.0 - BETA_ONE**STEP
    second_fix = 1.0 - BETA_TWO**STEP
    direction = momentum / first_fix / (jnp.sqrt(variance / second_fix) + EPS_ADAM)
    updated = weight - rate * (direction + decay * weight)
    return (momentum, variance, updated, updated.astype(BF16))


def body(
    tokens, cotangent, key_mask,
    attention_weights, expand_weights, shrink_weights, vector_params,
    attention_moment, attention_square, expand_moment, expand_square,
    shrink_moment, shrink_square, vector_moment, vector_square,
):
    dp_n = lax.axis_size("dp")
    line = dp_n // 2
    d = lax.axis_index("dp")
    place = lax.axis_index("seq")
    x, c = place // 2, place % 2
    _, local_len, width = tokens.shape
    r = width // dp_n
    block = -(-local_len // 16) * 16
    own, rows = 2 * block, 4 * block
    pad = ((0, 0), (0, block - local_len), (0, 0))

    keep = lax.dynamic_index_in_dim(key_mask, x, 0, keepdims=False).reshape(2, 2, local_len)
    keep = jnp.pad(keep.transpose(1, 0, 2), ((0, 0), (0, 0), pad[1])).reshape(2, own)
    kbias = jnp.broadcast_to(jnp.where(keep > 0, 0.0, -1e30).astype(F32).reshape(rows, 1), (rows, PAIR))
    p_exp = expand_weights
    if r % 128:
        p_exp = lax.dynamic_index_in_dim(expand_weights.reshape(r, dp_n, 4, r), place, 2, keepdims=False)
        p_exp = p_exp.reshape(r, 2, BLOCKS, PAIR).transpose(1, 2, 0, 3)
    vec_len = vector_params.shape[0]
    vec_rows = -(-vec_len // 1024) * 8
    p_vec = jnp.pad(vector_params.astype(BF16).astype(F32), (0, vec_rows * 128 - vec_len)).reshape(vec_rows, 128)

    vmem = pl.BlockSpec(memory_space=pltpu.VMEM)
    hbm = pl.BlockSpec(memory_space=pl.ANY)
    padded = jax.ShapeDtypeStruct((2, block, width), BF16)
    o_blk, o_tok, o_att, o_exp, o_shr, o_vec = pl.pallas_call(
        functools.partial(layer_kernel, line, vec_len),
        out_shape=(
            padded,
            padded,
            jax.ShapeDtypeStruct((r, 4 * width), BF16),
            jax.ShapeDtypeStruct((2, 4, BLOCKS, r, PAIR) if r % 128 else (r, 4 * width), BF16),
            jax.ShapeDtypeStruct((4 * r, width), BF16),
            jax.ShapeDtypeStruct((16, width), F32),
        ),
        in_specs=[hbm, hbm, vmem, vmem, hbm, hbm, hbm],
        out_specs=(vmem, vmem, hbm, hbm, hbm, vmem),
        scratch_shapes=[
            pltpu.VMEM((UNITS, BLOCKS, line, 2, r, PAIR), BF16),
            pltpu.VMEM((4, line, 2, r, PAIR), BF16),
            pltpu.VMEM((UNITS, BLOCKS, line, 2, r, PAIR), BF16),
            pltpu.VMEM((4, RS_EDGE, line, 2, r, PAIR), BF16),
            pltpu.VMEM((4, RS_WINDOW, line, r, PAIR), BF16),
            pltpu.VMEM((4, line - 1, RS_WINDOW, r, PAIR), BF16),
            pltpu.VMEM((8, HALF, line, r, PAIR), BF16),
            pltpu.VMEM((8, line - 1, HALF, r, PAIR), BF16),
            pltpu.VMEM((4, RS_WINDOW, r, PAIR), BF16),
            pltpu.VMEM((4, RS_WINDOW, r, PAIR), BF16),
            pltpu.VMEM((UNITS, BLOCKS, r, PAIR), BF16),
            pltpu.VMEM((8, HALF, r, PAIR), BF16),
            pltpu.VMEM((dp_n, vec_rows, 128), F32),
            pltpu.VMEM((16, width), F32),
            pltpu.VMEM((1, width), F32),
            pltpu.VMEM((16, width), F32),
            pltpu.VMEM((3, 16, width), F32),
            pltpu.VMEM((line, 16, width), F32),
            pltpu.VMEM((own, width), BF16),
            pltpu.VMEM((own, width), BF16),
            pltpu.VMEM((rows, width), BF16),
            pltpu.VMEM((2 * rows, width), BF16),
            pltpu.VMEM((rows, 3 * UNIT), BF16),
            pltpu.VMEM((rows, width), BF16),
            pltpu.VMEM(((rows // PAIR) * (UNIT // PAIR), 2 * PAIR), F32),
            pltpu.VMEM((own, width), F32),
            pltpu.VMEM((2 * rows, width), BF16),
            pltpu.VMEM((2 * rows, width), BF16),
            pltpu.VMEM((2 * rows, width), BF16),
        ]
        + [pltpu.VMEM((own, width), F32)] * 7
        + [
            pltpu.VMEM((rows, width), BF16),
            pltpu.VMEM((width, 2 * rows), BF16),
            pltpu.VMEM((rows, PAIR), F32),
            pltpu.VMEM((rows, PAIR), F32),
            pltpu.SemaphoreType.DMA((6, ITEMS)),
            pltpu.SemaphoreType.DMA((14, ITEMS)),
            pltpu.SemaphoreType.DMA((2, 12)),
            pltpu.SemaphoreType.DMA((2, 4)),
            pltpu.SemaphoreType.DMA((2, 10)),
            pltpu.SemaphoreType.DMA((2, 5)),
            pltpu.SemaphoreType.DMA((UNITS, 2)),
            pltpu.SemaphoreType.DMA((2,)),
        ],
        compiler_params=pltpu.CompilerParams(
            collective_id=0, has_side_effects=True, vmem_limit_bytes=VMEM_LIMIT
        ),
        name="layer",
    )(jnp.pad(tokens, pad), jnp.pad(cotangent, pad), kbias, p_vec, attention_weights, p_exp, shrink_weights)

    block_output = o_blk[:, :local_len]
    token_gradient = o_tok[:, :local_len]
    grad_attention, grad_shrink = o_att.astype(F32), o_shr.astype(F32)
    if r % 128:
        o_exp = o_exp.transpose(3, 1, 0, 2, 4).reshape(r, 4, dp_n, r).transpose(0, 2, 1, 3).reshape(r, 4 * width)
    grad_expand = o_exp.astype(F32)
    hidden_sums = o_vec[8:12].reshape(4, dp_n, r).transpose(1, 0, 2).reshape(4, width)
    grad_vector = jnp.concatenate([o_vec[0:8], hidden_sums], 0).reshape(dp_n, vec_len)
    grad_vector = lax.dynamic_index_in_dim(grad_vector, d, 0, keepdims=False)

    attention_out = adamw(
        grad_attention, attention_moment, attention_square, attention_weights, RATE_MATRIX, DECAY_MATRIX
    )
    expand_out = adamw(grad_expand, expand_moment, expand_square, expand_weights, RATE_MATRIX, DECAY_MATRIX)
    shrink_out = adamw(grad_shrink, shrink_moment, shrink_square, shrink_weights, RATE_MATRIX, DECAY_MATRIX)
    vector_out = adamw(grad_vector, vector_moment, vector_square, vector_params, RATE_VECTOR, 0.0)
    return (block_output, token_gradient, *attention_out, *expand_out, *shrink_out, *vector_out)


VMEM_LIMIT = 63 * 2**20


def solution(mesh):
    split = P("dp", "seq", None)
    rows = P("dp", None)
    flat = P("dp")
    return jax.shard_map(
        body,
        mesh=mesh,
        in_specs=(split, split, rows, rows, rows, rows, flat) + (rows,) * 6 + (flat, flat),
        out_specs=(split, split) + (rows,) * 12 + (flat,) * 4,
        check_vma=False,
    )
```

```python
import functools

import jax
import jax.numpy as jnp
from jax import lax
from jax.experimental import pallas as pl
from jax.experimental.pallas import tpu as pltpu
from jax.sharding import PartitionSpec as P

HEAD_DIM = 64
STEP = 5
EPS_NORM = 1e-05
BETA_ONE = 0.5
BETA_TWO = 0.5
EPS_ADAM = 1e-08
RATE_MATRIX = 0.05
RATE_VECTOR = 0.2
DECAY_MATRIX = 0.1
SLOPE = 1.702

BF16 = jnp.bfloat16
F32 = jnp.float32
MESH = pl.DeviceIdType.MESH

UNIT = 512
BLOCKS = 4
RS_EDGE = 1
RS_WINDOW = BLOCKS - RS_EDGE
HALF = 2
UNITS = 8
ITEMS = 12
PAIR = 128


def dot(a, b):
    return jnp.dot(a, b, preferred_element_type=F32)


def dot_rows(a, b):
    return lax.dot_general(a, b, (((0,), (0,)), ((), ())), preferred_element_type=F32)


def dot_cols(a, b):
    return lax.dot_general(a, b, (((1,), (1,)), ((), ())), preferred_element_type=F32)


def unit_rows(x):
    centred = x - jnp.mean(x, -1, keepdims=True)
    rstd = lax.rsqrt(jnp.mean(centred * centred, -1, keepdims=True) + EPS_NORM)
    return centred * rstd, rstd


def norm_back(grad_normed, unit, rstd, gain):
    g = grad_normed * gain
    return rstd * (g - jnp.mean(g, -1, keepdims=True) - unit * jnp.mean(g * unit, -1, keepdims=True))


def fold8(v):
    return jnp.sum(v.reshape(v.shape[0] // 8, 8, v.shape[1]), 0)


def layer_kernel(
    line, vec_len,
    tok, cot, kbias, p_vec, p_att, p_exp, p_shr,
    o_blk, o_tok, o_att, o_exp, o_shr, o_vec,
    w, w_oth, g, rx, ry, rz, ry_f, rz_f, s_own, s_oth, f_own, f_oth,
    vec_all, vec, bias_h, vg, vr, vz,
    tok_own, cot_own,
    n1, go, qkv, att, lse, resid, n2, act, fac,
    own_p, keep_p, send_a, send_b, recv_a, recv_b, recv_m,
    gb, tr, dk_acc, dv_acc,
    ag, rs, sib, wo, xe, vs, fill, loc,
):
    dp_n = 2 * line
    r = w.shape[4]
    block = tok.shape[1]
    own = 2 * block
    rows = 2 * own
    width = tok.shape[2]
    half = UNIT
    d = lax.axis_index("dp")
    s = lax.axis_index("seq")
    zi, yi = d // 2, d % 2
    x, c = s // 2, s % 2
    sibling = (d, x * 2 + 1 - c)
    x_neigh = (d, (1 - x) * 2 + c)
    y_neigh = (zi * 2 + 1 - yi, s)

    def z_peer(o):
        return (lax.rem(zi + o, line) * 2 + yi, s)

    def own_rows(core):
        return pl.ds(pl.multiple_of(core * own, own), own)

    def ff_rows(chip, core):
        return pl.ds(pl.multiple_of(chip * rows + core * own, own), own)

    my_rows = own_rows(c)
    my_half = pl.ds(pl.multiple_of(c * half, half), half)
    oth_half = pl.ds(pl.multiple_of((1 - c) * half, half), half)
    my_block = pl.ds(pl.multiple_of(x * block, block), block)
    oth_block = pl.ds(pl.multiple_of((1 - x) * block, block), block)

    def window(edge):
        return pl.ds(x * edge, BLOCKS - edge)

    def mine(edge):
        return pl.ds(x * (BLOCKS - edge), edge)

    def theirs(edge):
        return pl.ds((1 - x) * (BLOCKS - edge), edge)

    def ag_edge(u):
        return EDGES[u]

    def unit_of(i):
        return (i, None) if i < 4 else (4 + (i - 4) // 2, (i - 4) % 2 * HALF)

    def remote(src, dst, send, recv, to):
        return pltpu.make_async_remote_copy(
            src_ref=src, dst_ref=dst, send_sem=send, recv_sem=recv, device_id=to, device_id_type=MESH
        )

    def wait_bytes(ref, sem):
        pltpu.make_async_copy(ref, ref, sem).wait()

    wide = r % 128 == 0

    def unit_parts(u, place):
        if u < 4:
            core = place % 2
            return [
                (slice(None), pl.ds(pl.multiple_of(n * width + core * half + u * PAIR, PAIR), PAIR)) for n in range(BLOCKS)
            ]
        if u < 6:
            if not wide:
                return None
            parts = []
            for n in range((u - 4) * UNIT, (u - 3) * UNIT, PAIR):
                at = n // r * 4 * r + place * r + n % r
                parts.append((slice(None), pl.ds(pl.multiple_of(at, PAIR), PAIR)))
            return parts
        first = (u - 6) * UNIT
        held = pl.ds(pl.multiple_of(place * r, r), r)
        return [(held, slice(first + n * PAIR, first + (n + 1) * PAIR)) for n in range(BLOCKS)]

    def stage(u):
        n = u % 4 if u < 4 else u % 2
        hold = own_p if u < 4 else send_a if u < 6 else send_b
        return hold.at[(n // 2) * r : (n // 2 + 1) * r, (n % 2) * UNIT : (n % 2 + 1) * UNIT]

    def matrix(u, refs):
        return refs[0 if u < 4 else 1 if u < 6 else 2]

    for u in range(UNITS):
        parts = unit_parts(u, s)
        source = matrix(u, (p_att, p_exp, p_shr))
        for n in range(BLOCKS):
            part = source.at[parts[n]] if parts else source.at[u - 4, n]
            pltpu.make_async_copy(part, stage(u).at[:, n * PAIR : (n + 1) * PAIR], fill.at[u, n // HALF if u >= 4 else 0]).start()

    vec_all[d] = p_vec[...]
    own_copies = [
        pltpu.make_async_copy(tok.at[x], tok_own.at[my_block], loc.at[0]),
        pltpu.make_async_copy(cot.at[x], cot_own.at[my_block], loc.at[1]),
    ]
    for copy in own_copies:
        copy.start()

    barrier = pltpu.get_barrier_semaphore()

    def greet(o, carry):
        pl.semaphore_signal(barrier, inc=1, device_id=(lax.rem(d + o, dp_n), s), device_id_type=MESH)
        return carry

    lax.fori_loop(1, dp_n, greet, 0)
    pl.semaphore_signal(barrier, inc=1, device_id=sibling, device_id_type=MESH)
    pl.semaphore_signal(barrier, inc=1, device_id=x_neigh, device_id_type=MESH)
    pl.semaphore_wait(barrier, dp_n + 1)

    def send_vec(o, carry):
        remote(p_vec, vec_all.at[d], vs.at[0, 0], vs.at[1, 0], (lax.rem(d + o, dp_n), s)).start()
        return carry

    lax.fori_loop(1, dp_n, send_vec, 0)
    x_copies = [
        remote(tok.at[1 - x], tok_own.at[my_block], xe.at[0, 0], xe.at[1, 0], x_neigh),
        remote(cot.at[1 - x], cot_own.at[my_block], xe.at[0, 1], xe.at[1, 1], x_neigh),
    ]
    for copy in x_copies:
        copy.start()

    def ag_blocks(i):
        u, first = unit_of(i)
        return window(ag_edge(u)) if first is None else pl.ds(first, HALF)

    def ag_z(i):
        u, first = unit_of(i)
        count = BLOCKS - ag_edge(u) if first is None else HALF
        if first is None:
            wait_bytes(stage(u), fill.at[u, 0])
        else:
            wait_bytes(stage(u).at[:, first * PAIR : (first + HALF) * PAIR], fill.at[u, first // HALF])
        for n in range(count):
            b = x * ag_edge(u) + n if first is None else first + n
            w[u, b, zi, yi] = stage(u)[:, pl.ds(pl.multiple_of(b * PAIR, PAIR), PAIR)].astype(BF16)
        part = w.at[u, ag_blocks(i), zi, yi]
        for o in range(1, line):
            remote(part, part, ag.at[0, i], ag.at[1, i], z_peer(o)).start()

    def ag_y_copy(i):
        part = w.at[unit_of(i)[0], ag_blocks(i), :, yi]
        return remote(part, part, ag.at[2, i], ag.at[3, i], y_neigh)

    def ag_x_copy(i):
        part = w.at[i, mine(ag_edge(i))]
        return remote(part, part, ag.at[4, i], ag.at[5, i], x_neigh)

    def z_bytes(i):
        return w.at[unit_of(i)[0], ag_blocks(i), pl.ds(0, line - 1), yi]

    def ag_y(i):
        wait_bytes(z_bytes(i), ag.at[1, i])
        ag_y_copy(i).start()

    def ag_x(i):
        ag_y_copy(i).wait_recv()
        if i < 4:
            ag_x_copy(i).start()

    def ag_end(i):
        if i < 4:
            ag_x_copy(i).wait_recv()

    gather_stages = [ag_z, ag_y, ag_x, ag_end]

    grain = 128 if vec_len % 128 == 0 else 64

    def vec_lanes(first):
        parts = []
        for e in range(first, first + 128, grain):
            o = e % vec_len
            parts.append(vec_all[e // vec_len, o // 128 : o // 128 + 1, o % 128 : o % 128 + grain])
        return parts[0] if len(parts) == 1 else jnp.concatenate(parts, 1)

    def hidden_bias(place):
        parts = []
        for shard in range(dp_n):
            n = shard * 4 * r + place * r
            parts.append(vec[8 + n // width : 9 + n // width, n % width : n % width + r])
        return jnp.concatenate(parts, 1)

    def vector():
        for row in range(12):
            for lane in range(0, width, 128):
                vec[row : row + 1, lane : lane + 128] = vec_lanes(row * width + lane)
        low_half = jnp.where(s == 0, hidden_bias(0), hidden_bias(1))
        bias_h[...] = jnp.where(s < 2, low_half, jnp.where(s == 2, hidden_bias(2), hidden_bias(3)))

    def live(to):
        return jnp.where(kbias[to, 0:1] < 0, 0.0, 1.0)

    chunk = block // 2

    def chunks(first, i):
        return pl.ds(pl.multiple_of(first + i * chunk, chunk), chunk)

    def first_norm():
        def some(i, carry):
            unit, _ = unit_rows(tok_own[chunks(0, i), :].astype(F32))
            n1[chunks(c * own, i), :] = (unit * vec[0:1, :] + vec[1:2, :]).astype(BF16)
            return carry

        lax.fori_loop(0, own // chunk, some, 0)
        n1_copy.start()

    def grad_output():
        def some(i, carry):
            to = chunks(c * own, i)
            go[chunks(x * rows + c * own, i), :] = (cot_own[chunks(0, i), :].astype(F32) * live(to)).astype(BF16)
            return carry

        lax.fori_loop(0, own // chunk, some, 0)
        go_copies[1].start()
        go_copies[0].start()

    def rows_copies(ref, n):
        here, there = ref.at[ff_rows(x, c)], ref.at[ff_rows(1 - x, c)]
        return (
            remote(here, here, sib.at[0, n], sib.at[1, n], sibling),
            remote(here, here, xe.at[0, n], xe.at[1, n], x_neigh),
            remote(there, there, sib.at[0, n + 1], sib.at[1, n + 1], sibling),
        )

    n1_copy = remote(n1.at[my_rows], n1.at[my_rows], sib.at[0, 0], sib.at[1, 0], sibling)
    att_copy = remote(att.at[:, my_half], att.at[:, my_half], sib.at[0, 1], sib.at[1, 1], sibling)
    gb_copy = remote(gb.at[my_rows], gb.at[my_rows], sib.at[0, 2], sib.at[1, 2], sibling)
    p1_copy = remote(send_a, recv_a, sib.at[0, 3], sib.at[1, 3], sibling)
    go_copies = rows_copies(go, 4)
    n2_copies = rows_copies(n2, 6)
    b_copy = remote(send_b, recv_b, sib.at[0, 8], sib.at[1, 8], sibling)
    a_copy = remote(send_a, recv_a, sib.at[0, 9], sib.at[1, 9], sibling)
    bm_copy = remote(send_b, recv_b, sib.at[0, 10], sib.at[1, 10], sibling)
    am_copy = remote(send_a, recv_m, sib.at[0, 11], sib.at[1, 11], sibling)
    x_back = [
        remote(cot_own.at[pl.ds(n * block, block)], o_blk.at[n], xe.at[0, 7 + n], xe.at[1, 7 + n], x_neigh) for n in range(2)
    ]
    xm_copy = remote(cot_own, n2.at[rows : rows + own], xe.at[0, 9], xe.at[1, 9], x_neigh)
    tok_copy = remote(tok_own.at[oth_block], o_tok.at[x], xe.at[0, 3], xe.at[1, 3], x_neigh)
    blk_copy = remote(cot_own.at[oth_block], o_blk.at[x], xe.at[0, 2], xe.at[1, 2], x_neigh)

    low_lane = lax.broadcasted_iota(jnp.int32, (PAIR, PAIR), 1) < HEAD_DIM
    low_row = lax.broadcasted_iota(jnp.int32, (PAIR, PAIR), 0) < HEAD_DIM
    q_chunks = rows // PAIR

    def two_heads(v):
        zero = jnp.zeros_like(v)
        return jnp.concatenate([jnp.where(low_lane, v, zero), jnp.where(low_lane, zero, v)], 0)

    qkv_lanes = 3 * PAIR

    def pair_lanes(p):
        return tuple(slice(p * qkv_lanes + n * PAIR, p * qkv_lanes + (n + 1) * PAIR) for n in range(3))

    def att_lanes(p):
        return pl.ds(pl.multiple_of(c * half + p * PAIR, PAIR), PAIR)

    def wo_copy(p):
        return remote(w.at[p, BLOCKS - 1], w_oth.at[p], wo.at[0, p], wo.at[1, p], sibling)

    def columns(blocks):
        return jnp.concatenate([v.reshape(-1, PAIR) for v in blocks], 1)

    def project(p):
        wo_copy(p).start()
        q_at, k_at, v_at = pair_lanes(p)
        out = dot(n1[...], columns([w[p, n] for n in range(3)]))
        queries = (out[:, :PAIR] + vec[4:5, att_lanes(p)]).astype(BF16)
        qkv[:, q_at] = queries * jnp.asarray(HEAD_DIM**-0.5, BF16)
        qkv[:, k_at] = out[:, PAIR : 2 * PAIR].astype(BF16)
        qkv[:, v_at] = (out[:, 2 * PAIR :] + vec[5:6, att_lanes(p)]).astype(BF16)

    def attend_forward(p, first, last):
        q_at, k_at, v_at = pair_lanes(p)

        def some(j, carry):
            at = pl.ds(pl.multiple_of(j * PAIR, PAIR), PAIR)
            mask = kbias[...]
            scores = dot_cols(qkv[:, k_at], two_heads(qkv[at, q_at])) + jnp.concatenate([mask, mask], 1)
            highest = jnp.max(scores, 0, keepdims=True)
            raised = jnp.exp(scores - highest)
            total = jnp.sum(raised, 0, keepdims=True)
            out = dot_rows(qkv[:, v_at], raised.astype(BF16)) / total
            out = jnp.where(low_row, out[:, :PAIR], out[:, PAIR:])
            att[at, att_lanes(p)] = out.T.astype(BF16)
            lse[pl.ds(p * q_chunks + j, 1), :] = highest + jnp.log(total)
            return carry

        lax.fori_loop(first, last, some, 0)
        if p == 3 and last == q_chunks:
            att_copy.start()

    def own_out(z):
        return columns([w[p, BLOCKS - 1, z] for p in range(4)])

    def oth_out(z):
        return columns([w_oth[p, z] for p in range(4)])

    def output_projection():
        mixed = att[my_rows, :]
        resid[:, my_half] = dot(mixed, own_out(slice(None)))
        resid[:, oth_half] = dot(mixed, oth_out(slice(None)))

    def second_norm():
        def some(i, carry):
            at = chunks(0, i)
            res = resid[at, :] + tok_own[at, :].astype(F32) + vec[6:7, :]
            resid[at, :] = res
            unit, _ = unit_rows(res)
            n2[chunks(x * rows + c * own, i), :] = (unit * vec[2:3, :] + vec[3:4, :]).astype(BF16)
            return carry

        lax.fori_loop(0, own // chunk, some, 0)
        n2_copies[1].start()
        n2_copies[0].start()

    tile = HALF * PAIR

    def expand(n, chip):
        u, first = unit_of(4 + n)
        at = pl.ds(pl.multiple_of(chip * rows, rows), rows)
        to = slice(n * tile, (n + 1) * tile)
        hidden = dot(n2[at, :], columns([w[u, first], w[u, first + 1]])) + bias_h[:, to]
        gate = jax.nn.sigmoid(SLOPE * hidden)
        act[at, to] = (hidden * gate).astype(BF16)
        fac[at, to] = (gate + SLOPE * hidden * gate * (1.0 - gate)).astype(BF16)

    rs_win = window(RS_EDGE)

    def rs_x_copy(i):
        return remote(g.at[i, theirs(RS_EDGE)], rx.at[i], rs.at[0, i], rs.at[1, i], x_neigh)

    def rs_y_copy(i):
        u, first = unit_of(i)
        if first is None:
            return remote(g.at[u, rs_win, :, 1 - yi], ry.at[i], rs.at[2, i], rs.at[3, i], y_neigh)
        return remote(g.at[u, pl.ds(first, HALF), :, 1 - yi], ry_f.at[i - 4], rs.at[2, i], rs.at[3, i], y_neigh)

    def rs_2_copy(i):
        if i < 4:
            return remote(s_own.at[i], s_oth.at[i], rs.at[6, i], rs.at[7, i], x_neigh)
        u, first = unit_of(i)
        return remote(f_own.at[u, pl.ds(first, HALF)], f_oth.at[i - 4], rs.at[6, i], rs.at[7, i], x_neigh)

    def to_result(i, n, place):
        u, first = unit_of(i)
        result = matrix(u, (o_att, o_exp, o_shr))
        parts = unit_parts(u, place)
        n = n + (first or 0)
        return result.at[parts[n]] if parts else result.at[u - 4, place, n]

    def rs_share(i, source, count, place, sems):
        for n in range(count):
            to = to_result(i, n, place)
            remote(source.at[n], to, rs.at[sems, i], rs.at[sems + 1, i], sibling).start()
            pltpu.make_async_copy(source.at[n], to, rs.at[sems + 2, i]).start()

    def rs_x_add(i):
        rs_x_copy(i).wait_recv()

        def add(z, carry):
            for n in range(RS_EDGE):
                b = x * RS_WINDOW + n
                g[i, b, z] = (g[i, b, z].astype(F32) + rx[i, n, z].astype(F32)).astype(BF16)
            return carry

        lax.fori_loop(0, line, add, 0)
        rs_y_copy(i).start()

    def rs_y_add(i):
        rs_y_copy(i).wait_recv()
        u, first = unit_of(i)
        count, base, got = (RS_WINDOW, x * RS_EDGE, ry.at[i]) if first is None else (HALF, first, ry_f.at[i - 4])

        def add(z, carry):
            for n in range(count):
                g[u, base + n, z, yi] = (g[u, base + n, z, yi].astype(F32) + got[n, z].astype(F32)).astype(BF16)
            return carry

        lax.fori_loop(0, line, add, 0)
        got = rz.at[i] if first is None else rz_f.at[i - 4]
        for o in range(1, line):
            z = lax.rem(zi + o, line)
            remote(g.at[u, pl.ds(base, count), z, yi], got.at[o - 1], rs.at[4, i], rs.at[5, i], z_peer(o)).start()

    def rs_z_add(i):
        u, first = unit_of(i)
        count, base, got = (RS_WINDOW, x * RS_EDGE, rz.at[i]) if first is None else (HALF, first, rz_f.at[i - 4])
        wait_bytes(got, rs.at[5, i])
        for n in range(count):
            total = g[u, base + n, zi, yi].astype(F32)
            for o in range(1, line):
                total = total + got[o - 1, n].astype(F32)
            if first is None:
                s_own[i, n] = total.astype(BF16)
            else:
                f_own[u, first + n] = total.astype(BF16)
        rs_2_copy(i).start()
        if first is not None:
            rs_share(i, f_own.at[u, pl.ds(first, HALF)], HALF, s, 8)

    def rs_join(i):
        rs_2_copy(i).wait_recv()
        if i >= 4:
            rs_share(i, f_oth.at[i - 4], HALF, (1 - x) * 2 + c, 11)
            return
        here, there = s_own[i], s_oth[i]
        first = jnp.where(x == 0, here, there)
        last = jnp.where(x == 0, there, here)
        f_own[i, 0] = first[0]
        for n in range(1, RS_WINDOW):
            f_own[i, n] = (first[n].astype(F32) + last[n - 1].astype(F32)).astype(BF16)
        f_own[i, RS_WINDOW] = last[RS_WINDOW - 1]
        rs_share(i, f_own.at[i], BLOCKS, s, 8)

    def rs_end(i):
        u, first = unit_of(i)
        if first is None:
            rs_x_copy(i).wait_send()
        rs_y_copy(i).wait_send()
        wait_bytes(rz.at[i] if first is None else rz_f.at[i - 4], rs.at[4, i])
        rs_2_copy(i).wait_send()
        sent = f_own.at[i] if first is None else f_oth.at[i - 4]
        for n in range(8, 11 if first is None else 14):
            wait_bytes(sent, rs.at[n, i])

    def put(u, first, value):
        for n in range(value.shape[1] // PAIR):
            part = value[:, n * PAIR : (n + 1) * PAIR].astype(BF16)
            g[u, first + n] = part.reshape(line, 2, r, PAIR)

    def rs_start(i):
        (rs_x_copy(i) if i < 4 else rs_y_copy(i)).start()

    def rs_stage(i, k):
        stages = [rs_x_add, rs_y_add, rs_z_add, rs_join, rs_end]
        (stages if i < 4 else stages[1:])[k](i)

    def transpose_into(first, src, size):
        def move(i, carry):
            at = pl.ds(pl.multiple_of(i * 128, 128), 128)
            tr[at, first : first + size] = src[:, at].T
            return carry

        lax.fori_loop(0, width // 128, move, 0)

    def shrink_grad(n):
        u, first = unit_of(8 + n)
        put(u, first, dot(tr[...], go[:, n * tile : (n + 1) * tile]))

    span = max(1, tile // (2 * r))
    part_rows = span * 2 * r

    def hidden_back(n):
        if n == 0:
            vg[...] = jnp.zeros_like(vg)

        def some(m, carry):
            hidden_part(m)
            return carry

        count = line // span // 4
        lax.fori_loop(n * count, (n + 1) * count, some, 0)

    def hidden_part(n):
        z = pl.ds(n * span, span)
        to = pl.ds(pl.multiple_of(n * part_rows, part_rows), part_rows)
        sums = None
        for at in (slice(0, rows), slice(rows, 2 * rows)):
            total = None
            for j in range(2):
                part = columns([w[6 + j, b, z] for b in range(BLOCKS)])
                term = dot_cols(go[at, j * UNIT : (j + 1) * UNIT], part)
                total = term if total is None else total + term
            low = (total * fac[at, to].astype(F32)).astype(BF16)
            fac[at, to] = low
            folded = fold8(low.astype(F32))
            sums = folded if sums is None else sums + folded
        vg[pl.ds(8 + s, 1), to] = jnp.sum(sums, 0, keepdims=True)

    def back_partial(src, rows_at, units, blocks, dst):
        lanes = blocks * PAIR

        def back(n, carry):
            total = None
            for k, u in enumerate(units):
                part = columns([w[u, b, pl.ds(n * span, span)] for b in range(blocks)])
                term = dot_cols(src[rows_at, k * lanes : (k + 1) * lanes], part)
                total = term if total is None else total + term
            dst[:, pl.ds(pl.multiple_of(n * part_rows, part_rows), part_rows)] = total
            return carry

        lax.fori_loop(0, line // span, back, 0)

    def expand_grad(n):
        u, first = unit_of(4 + n)
        put(u, first, dot(tr[...], fac[:, n * tile : (n + 1) * tile]))

    def to_x():
        def some(i, carry):
            at = chunks(0, i)
            cot_own[at, :] = (keep_p[at, :] + recv_b[at, :]).astype(BF16)
            return carry

        lax.fori_loop(0, own // chunk, some, 0)

    ff = (4, 5)

    def hidden_partial(n):
        at = ff_rows(*((1 - x, 1 - c), (1 - x, c), (x, 1 - c), (x, c))[n])
        back_partial(fac, at, ff, BLOCKS, (send_b, keep_p, send_a, own_p)[n])
        if n == 0:
            b_copy.start()
        if n == 2:
            a_copy.start()

    def partial_over_x():
        to_x()
        for copy in x_back:
            copy.start()

    zeros8 = jnp.zeros((8, width), F32)

    def second_norm_back():
        def some(i, carry):
            at = chunks(0, i)
            unit, rstd = unit_rows(resid[at, :])
            came = o_blk[i // 2, pl.ds(pl.multiple_of(i % 2 * chunk, chunk), chunk)].astype(F32)
            gn = own_p[at, :] + recv_a[at, :] + came
            grad_out = go[chunks(x * rows + c * own, i), :].astype(F32)
            gr = grad_out + norm_back(gn, unit, rstd, vec[2:3, :])
            own_p[at, :] = gr
            low = gr.astype(BF16)
            gb[chunks(c * own, i), :] = low
            a, b, e, f = carry
            return (a + fold8(gn * unit), b + fold8(gn), e + fold8(low.astype(F32)), f + fold8(grad_out))

        sums = lax.fori_loop(0, own // chunk, some, (zeros8,) * 4)
        for row, v in zip((2, 3, 6, 7), sums):
            vg[row : row + 1, :] = jnp.sum(v, 0, keepdims=True)
        gb_copy.start()

    def grad_attended(n):
        if n == 0:
            for copy in n2_copies:
                copy.wait_send()
        quarter = line // 4
        head_rows = pl.ds(c * (line // 2) + n * quarter, quarter)
        part = dot_cols(gb[:, my_half], own_out(head_rows)) + dot_cols(gb[:, oth_half], oth_out(head_rows))
        n2[:rows, n * tile : (n + 1) * tile] = part.astype(BF16)

    def attend_backward(p, first, last):
        q_at, k_at, v_at = pair_lanes(p)
        own_lanes = slice(p * PAIR, (p + 1) * PAIR)
        if first == 0:
            dk_acc[...] = jnp.zeros_like(dk_acc)
            dv_acc[...] = jnp.zeros_like(dv_acc)

        def some(j, carry):
            at = pl.ds(pl.multiple_of(j * PAIR, PAIR), PAIR)
            both = two_heads(qkv[at, q_at])
            grads = two_heads(n2[at, own_lanes])
            mask = kbias[...]
            scores = dot_cols(qkv[:, k_at], both) + jnp.concatenate([mask, mask], 1)
            chance = jnp.exp(scores - lse[pl.ds(p * q_chunks + j, 1), :])
            dv_acc[...] += dot(chance.astype(BF16), grads)
            grad_chance = dot_cols(qkv[:, v_at], grads)
            inner = jnp.sum(chance * grad_chance, 0, keepdims=True)
            grad_scores = (chance * (grad_chance - inner)).astype(BF16)
            dk_acc[...] += dot(grad_scores, both)
            out = dot_rows(qkv[:, k_at], grad_scores)
            out = jnp.where(low_row, out[:, :PAIR], out[:, PAIR:]) * HEAD_DIM**-0.5
            qkv[at, q_at] = out.T.astype(BF16)
            return carry

        lax.fori_loop(first, last, some, 0)
        if last < q_chunks:
            return
        qkv[:, k_at] = dk_acc[...].astype(BF16)
        qkv[:, v_at] = dv_acc[...].astype(BF16)
        vg[4:5, att_lanes(p)] = jnp.sum(fold8(qkv[:, q_at].astype(F32)), 0, keepdims=True)
        vg[5:6, att_lanes(p)] = jnp.sum(fold8(qkv[:, v_at].astype(F32)), 0, keepdims=True)

    def attention_grad(p):
        put(p, 0, dot(tr[:, :rows], qkv[:, p * qkv_lanes : (p + 1) * qkv_lanes]))
        put(p, BLOCKS - 1, dot(tr[:, rows:], gb[:, att_lanes(p)]))

    def input_partial(n):
        back_partial(qkv, own_rows(c if n else 1 - c), (0, 1, 2, 3), 3, keep_p if n else send_a)
        if n == 0:
            p1_copy.start()

    def first_norm_back():
        def some(i, carry):
            at = chunks(0, i)
            unit, rstd = unit_rows(tok_own[at, :].astype(F32))
            gn = keep_p[at, :] + recv_a[at, :]
            out = own_p[at, :] + norm_back(gn, unit, rstd, vec[0:1, :])
            tok_own[at, :] = out.astype(BF16)
            a, b = carry
            return (a + fold8(gn * unit), b + fold8(gn))

        sums = lax.fori_loop(0, own // chunk, some, (zeros8,) * 2)
        for row, v in zip((0, 1), sums):
            vg[row : row + 1, :] = jnp.sum(v, 0, keepdims=True)
        o_tok[x] = tok_own[my_block, :]
        tok_copy.start()

    def branch(dst, rows_at, add):
        def out(n, carry):
            for j in range(2):
                part = columns([w[6 + j, 2 * n], w[6 + j, 2 * n + 1]])
                to = pl.ds(pl.multiple_of(j * UNIT + n * tile, tile), tile)
                total = dot(act[rows_at, :], part)
                dst[:, to] = dst[:, to] + total if add else total
            return carry

        lax.fori_loop(0, UNIT // tile, out, 0)

    def output_partial(n):
        at = ff_rows(*((1 - x, 1 - c), (1 - x, c), (x, 1 - c), (x, c))[n])
        branch((send_b, keep_p, send_a, resid)[n], at, n == 3)
        if n == 0:
            bm_copy.start()
        if n == 2:
            am_copy.start()

    def output_over_x():
        to_x()
        xm_copy.start()

    def finish_block():
        def some(i, carry):
            at = chunks(0, i)
            out = resid[at, :] + recv_m[at, :] + n2[chunks(rows, i), :].astype(F32) + vec[7:8, :]
            cot_own[at, :] = (live(chunks(c * own, i)) * out).astype(BF16)
            return carry

        lax.fori_loop(0, own // chunk, some, 0)
        o_blk[x] = cot_own[my_block, :]
        blk_copy.start()

    v_copies = [
        remote(vg, vr.at[n], vs.at[0, 1 + n], vs.at[1, 1 + n], to) for n, to in enumerate((sibling, x_neigh, y_neigh))
    ]

    def vector_hop(n):
        if n < 3:
            v_copies[n].start()
            return

        def send(o, carry):
            remote(vg, vz.at[zi], vs.at[0, 4], vs.at[1, 4], (lax.rem(zi + o, line) * 2 + yi, s)).start()
            return carry

        lax.fori_loop(1, line, send, 0)
        vz[zi] = vg[...]

    def vector_add(n):
        if n < 3:
            v_copies[n].wait()
            vg[...] += vr[n]
            return
        wait_bytes(vz.at[pl.ds(0, line - 1)], vs.at[1, 4])
        wait_bytes(vz.at[pl.ds(0, line - 1)], vs.at[0, 4])

    def vector_out():
        o_vec[...] = lax.fori_loop(1, line, lambda i, t: t + vz[i], vz[0])

    def both(*copies):
        for copy in copies:
            copy.wait()

    def received(*copies):
        for copy in copies:
            copy.wait_recv()

    def relay(copies):
        copies[1].wait_recv()
        copies[2].start()

    waits = dict(
        vec=lambda: wait_bytes(vec_all.at[pl.ds(0, dp_n - 1)], vs.at[1, 0]),
        tok=lambda: both(x_copies[0], own_copies[0]),
        cot=lambda: both(x_copies[1], own_copies[1]),
        n1=lambda: received(n1_copy),
        gox=lambda: relay(go_copies),
        att=lambda: received(*[wo_copy(p) for p in range(4)], att_copy),
        n2=lambda: received(n2_copies[0]),
        n2x=lambda: relay(n2_copies),
        n2r=lambda: received(go_copies[0], go_copies[2], n2_copies[2]),
        b=lambda: both(b_copy),
        a=lambda: both(a_copy),
        xb=lambda: both(*x_back),
        gb=lambda: received(gb_copy),
        p1=lambda: both(p1_copy),
        bm=lambda: both(bm_copy),
        am=lambda: both(am_copy),
        xm=lambda: both(xm_copy),
        v0=lambda: vector_add(0),
        v1=lambda: vector_add(1),
        v2=lambda: vector_add(2),
        v3=lambda: vector_add(3),
    )
    split = 3
    work = dict(
        vec=lambda n: vector(),
        ln1=lambda n: first_norm(),
        go=lambda n: grad_output(),
        qkv=project,
        afa=lambda p: attend_forward(p, 0, split),
        afb=lambda p: attend_forward(p, split, q_chunks),
        out=lambda n: output_projection(),
        ln2=lambda n: second_norm(),
        eo=lambda n: expand(n, x),
        ex=lambda n: expand(n, 1 - x),
        tra=lambda n: transpose_into(0, act, 2 * rows),
        gs=shrink_grad,
        hb=hidden_back,
        bp0=lambda n: hidden_partial(0),
        bp1=lambda n: hidden_partial(1),
        tox=lambda n: partial_over_x(),
        bp2=lambda n: hidden_partial(2),
        bp3=lambda n: hidden_partial(3),
        trn=lambda n: transpose_into(0, n2, 2 * rows),
        gx=expand_grad,
        ln2b=lambda n: second_norm_back(),
        trb=lambda n: (transpose_into(0, n1, rows), transpose_into(rows, att, rows)),
        gat=grad_attended,
        aba=lambda p: attend_backward(p, 0, split),
        abb=lambda p: attend_backward(p, split, q_chunks),
        ga=attention_grad,
        b1o=lambda n: input_partial(0),
        b1m=lambda n: input_partial(1),
        ln1b=lambda n: first_norm_back(),
        br0=lambda n: output_partial(0),
        br1=lambda n: output_partial(1),
        tox2=lambda n: output_over_x(),
        br2=lambda n: output_partial(2),
        br3=lambda n: output_partial(3),
        v0=lambda n: vector_hop(0),
        v1=lambda n: vector_hop(1),
        v2=lambda n: vector_hop(2),
        v3=lambda n: vector_hop(3),
        fin=lambda n: finish_block(),
        ov=lambda n: vector_out(),
    )
    for kind, name, n in ORDER:
        if kind == "C":
            work[name](n)
        elif kind == "W":
            waits[name]()
        elif kind == "A":
            gather_stages[n](name)
        elif kind == "I":
            rs_start(name)
        else:
            rs_stage(name, n)

    blk_copy.wait()
    tok_copy.wait()
    wait_bytes(vec_all.at[pl.ds(0, dp_n - 1)], vs.at[0, 0])
    for copy in [n1_copy, att_copy, gb_copy, *go_copies] + [wo_copy(p) for p in range(4)]:
        copy.wait_send()
    for i in range(ITEMS):
        wait_bytes(z_bytes(i), ag.at[0, i])
        ag_y_copy(i).wait_send()
        if i < 4:
            ag_x_copy(i).wait_send()


def adamw(grad, moment, square, weight, rate, decay):
    momentum = BETA_ONE * moment + (1.0 - BETA_ONE) * grad
    variance = BETA_TWO * square + (1.0 - BETA_TWO) * grad * grad
    first_fix = 1.0 - BETA_ONE**STEP
    second_fix = 1.0 - BETA_TWO**STEP
    direction = momentum / first_fix / (jnp.sqrt(variance / second_fix) + EPS_ADAM)
    updated = weight - rate * (direction + decay * weight)
    return (momentum, variance, updated, updated.astype(BF16))


def body(
    tokens, cotangent, key_mask,
    attention_weights, expand_weights, shrink_weights, vector_params,
    attention_moment, attention_square, expand_moment, expand_square,
    shrink_moment, shrink_square, vector_moment, vector_square,
):
    dp_n = lax.axis_size("dp")
    line = dp_n // 2
    d = lax.axis_index("dp")
    place = lax.axis_index("seq")
    x, c = place // 2, place % 2
    _, local_len, width = tokens.shape
    r = width // dp_n
    block = -(-local_len // 16) * 16
    own, rows = 2 * block, 4 * block
    pad = ((0, 0), (0, block - local_len), (0, 0))

    keep = lax.dynamic_index_in_dim(key_mask, x, 0, keepdims=False).reshape(2, 2, local_len)
    keep = jnp.pad(keep.transpose(1, 0, 2), ((0, 0), (0, 0), pad[1])).reshape(2, own)
    kbias = jnp.broadcast_to(jnp.where(keep > 0, 0.0, -1e30).astype(F32).reshape(rows, 1), (rows, PAIR))
    p_exp = expand_weights
    if r % 128:
        p_exp = lax.dynamic_index_in_dim(expand_weights.reshape(r, dp_n, 4, r), place, 2, keepdims=False)
        p_exp = p_exp.reshape(r, 2, BLOCKS, PAIR).transpose(1, 2, 0, 3)
    vec_len = vector_params.shape[0]
    vec_rows = -(-vec_len // 1024) * 8
    p_vec = jnp.pad(vector_params.astype(BF16).astype(F32), (0, vec_rows * 128 - vec_len)).reshape(vec_rows, 128)

    vmem = pl.BlockSpec(memory_space=pltpu.VMEM)
    hbm = pl.BlockSpec(memory_space=pl.ANY)
    padded = jax.ShapeDtypeStruct((2, block, width), BF16)
    o_blk, o_tok, o_att, o_exp, o_shr, o_vec = pl.pallas_call(
        functools.partial(layer_kernel, line, vec_len),
        out_shape=(
            padded,
            padded,
            jax.ShapeDtypeStruct((r, 4 * width), BF16),
            jax.ShapeDtypeStruct((2, 4, BLOCKS, r, PAIR) if r % 128 else (r, 4 * width), BF16),
            jax.ShapeDtypeStruct((4 * r, width), BF16),
            jax.ShapeDtypeStruct((16, width), F32),
        ),
        in_specs=[hbm, hbm, vmem, vmem, hbm, hbm, hbm],
        out_specs=(vmem, vmem, hbm, hbm, hbm, vmem),
        scratch_shapes=[
            pltpu.VMEM((UNITS, BLOCKS, line, 2, r, PAIR), BF16),
            pltpu.VMEM((4, line, 2, r, PAIR), BF16),
            pltpu.VMEM((UNITS, BLOCKS, line, 2, r, PAIR), BF16),
            pltpu.VMEM((4, RS_EDGE, line, 2, r, PAIR), BF16),
            pltpu.VMEM((4, RS_WINDOW, line, r, PAIR), BF16),
            pltpu.VMEM((4, line - 1, RS_WINDOW, r, PAIR), BF16),
            pltpu.VMEM((8, HALF, line, r, PAIR), BF16),
            pltpu.VMEM((8, line - 1, HALF, r, PAIR), BF16),
            pltpu.VMEM((4, RS_WINDOW, r, PAIR), BF16),
            pltpu.VMEM((4, RS_WINDOW, r, PAIR), BF16),
            pltpu.VMEM((UNITS, BLOCKS, r, PAIR), BF16),
            pltpu.VMEM((8, HALF, r, PAIR), BF16),
            pltpu.VMEM((dp_n, vec_rows, 128), F32),
            pltpu.VMEM((16, width), F32),
            pltpu.VMEM((1, width), F32),
            pltpu.VMEM((16, width), F32),
            pltpu.VMEM((3, 16, width), F32),
            pltpu.VMEM((line, 16, width), F32),
            pltpu.VMEM((own, width), BF16),
            pltpu.VMEM((own, width), BF16),
            pltpu.VMEM((rows, width), BF16),
            pltpu.VMEM((2 * rows, width), BF16),
            pltpu.VMEM((rows, 3 * UNIT), BF16),
            pltpu.VMEM((rows, width), BF16),
            pltpu.VMEM(((rows // PAIR) * (UNIT // PAIR), 2 * PAIR), F32),
            pltpu.VMEM((own, width), F32),
            pltpu.VMEM((2 * rows, width), BF16),
            pltpu.VMEM((2 * rows, width), BF16),
            pltpu.VMEM((2 * rows, width), BF16),
        ]
        + [pltpu.VMEM((own, width), F32)] * 7
        + [
            pltpu.VMEM((rows, width), BF16),
            pltpu.VMEM((width, 2 * rows), BF16),
            pltpu.VMEM((rows, PAIR), F32),
            pltpu.VMEM((rows, PAIR), F32),
            pltpu.SemaphoreType.DMA((6, ITEMS)),
            pltpu.SemaphoreType.DMA((14, ITEMS)),
            pltpu.SemaphoreType.DMA((2, 12)),
            pltpu.SemaphoreType.DMA((2, 4)),
            pltpu.SemaphoreType.DMA((2, 10)),
            pltpu.SemaphoreType.DMA((2, 5)),
            pltpu.SemaphoreType.DMA((UNITS, 2)),
            pltpu.SemaphoreType.DMA((2,)),
        ],
        compiler_params=pltpu.CompilerParams(
            collective_id=0, has_side_effects=True, vmem_limit_bytes=VMEM_LIMIT
        ),
        name="layer",
    )(jnp.pad(tokens, pad), jnp.pad(cotangent, pad), kbias, p_vec, attention_weights, p_exp, shrink_weights)

    block_output = o_blk[:, :local_len]
    token_gradient = o_tok[:, :local_len]
    grad_attention, grad_shrink = o_att.astype(F32), o_shr.astype(F32)
    if r % 128:
        o_exp = o_exp.transpose(3, 1, 0, 2, 4).reshape(r, 4, dp_n, r).transpose(0, 2, 1, 3).reshape(r, 4 * width)
    grad_expand = o_exp.astype(F32)
    hidden_sums = o_vec[8:12].reshape(4, dp_n, r).transpose(1, 0, 2).reshape(4, width)
    grad_vector = jnp.concatenate([o_vec[0:8], hidden_sums], 0).reshape(dp_n, vec_len)
    grad_vector = lax.dynamic_index_in_dim(grad_vector, d, 0, keepdims=False)

    attention_out = adamw(
        grad_attention, attention_moment, attention_square, attention_weights, RATE_MATRIX, DECAY_MATRIX
    )
    expand_out = adamw(grad_expand, expand_moment, expand_square, expand_weights, RATE_MATRIX, DECAY_MATRIX)
    shrink_out = adamw(grad_shrink, shrink_moment, shrink_square, shrink_weights, RATE_MATRIX, DECAY_MATRIX)
    vector_out = adamw(grad_vector, vector_moment, vector_square, vector_params, RATE_VECTOR, 0.0)
    return (block_output, token_gradient, *attention_out, *expand_out, *shrink_out, *vector_out)


VMEM_LIMIT = 63 * 2**20

EDGES = (1, 1, 1, 1)

ORDER = (
    ("A", 0, 0), ("A", 1, 0), ("A", 2, 0), ("A", 3, 0), ("W", "vec", 0), ("C", "vec", 0), ("W", "tok", 0),
    ("C", "ln1", 0), ("A", 0, 1), ("A", 4, 0), ("W", "cot", 0), ("C", "go", 0), ("W", "n1", 0), ("A", 1, 1),
    ("A", 5, 0), ("A", 0, 2), ("A", 2, 1), ("A", 6, 0), ("A", 1, 2), ("A", 3, 1), ("A", 7, 0), ("A", 0, 3),
    ("C", "qkv", 0), ("C", "afa", 0), ("A", 2, 2), ("C", "afb", 0), ("A", 4, 1), ("A", 8, 0), ("A", 1, 3),
    ("C", "qkv", 1), ("C", "afa", 1), ("C", "afb", 1), ("W", "gox", 0), ("A", 3, 2), ("A", 5, 1), ("A", 9, 0),
    ("A", 2, 3), ("C", "qkv", 2), ("C", "afa", 2), ("C", "afb", 2), ("A", 4, 2), ("A", 6, 1), ("A", 10, 0),
    ("A", 3, 3), ("C", "qkv", 3), ("C", "afa", 3), ("C", "afb", 3), ("A", 5, 2), ("A", 7, 1), ("A", 11, 0),
    ("W", "att", 0), ("C", "out", 0), ("C", "ln2", 0), ("A", 6, 2), ("A", 8, 1), ("W", "n2", 0), ("C", "eo", 0),
    ("C", "eo", 1), ("C", "eo", 2), ("A", 7, 2), ("C", "eo", 3), ("A", 9, 1), ("A", 8, 2), ("A", 10, 1),
    ("W", "n2x", 0), ("W", "n2r", 0), ("C", "ex", 0), ("A", 9, 2), ("C", "ex", 1), ("A", 11, 1), ("C", "ex", 2),
    ("C", "ex", 3), ("C", "tra", 0), ("C", "gs", 0), ("A", 10, 2), ("I", 8, 0), ("C", "gs", 1), ("I", 9, 0),
    ("C", "gs", 2), ("C", "gs", 3), ("A", 11, 2), ("C", "hb", 0), ("C", "hb", 1), ("C", "hb", 2), ("C", "hb", 3),
    ("C", "bp0", 0), ("R", 8, 0), ("I", 10, 0), ("C", "bp1", 0), ("W", "b", 0), ("C", "tox", 0), ("C", "bp2", 0),
    ("R", 9, 0), ("I", 11, 0), ("C", "bp3", 0), ("C", "trn", 0), ("R", 8, 1), ("C", "gx", 0), ("C", "gx", 1),
    ("R", 10, 0), ("I", 4, 0), ("C", "gx", 2), ("C", "gx", 3), ("R", 9, 1), ("W", "a", 0), ("R", 11, 0), ("I", 5, 0),
    ("R", 10, 1), ("W", "xb", 0), ("C", "ln2b", 0), ("R", 4, 0), ("R", 8, 2), ("I", 6, 0), ("C", "trb", 0),
    ("R", 9, 2), ("W", "gb", 0), ("C", "gat", 0), ("R", 10, 2), ("R", 8, 3), ("R", 11, 1), ("C", "gat", 1),
    ("C", "aba", 0), ("R", 9, 3), ("R", 10, 3), ("R", 5, 0), ("I", 7, 0), ("C", "abb", 0), ("R", 11, 2),
    ("C", "ga", 0), ("R", 4, 1), ("C", "aba", 1), ("R", 11, 3), ("R", 6, 0), ("I", 0, 0), ("C", "abb", 1),
    ("R", 4, 2), ("R", 5, 1), ("C", "ga", 1), ("C", "aba", 2), ("R", 4, 3), ("R", 7, 0), ("I", 1, 0), ("C", "abb", 2),
    ("C", "ga", 2), ("R", 6, 1), ("R", 0, 0), ("R", 5, 2), ("I", 2, 0), ("C", "aba", 3), ("C", "abb", 3), ("R", 5, 3),
    ("C", "ga", 3), ("R", 7, 1), ("R", 1, 0), ("I", 3, 0), ("C", "b1o", 0), ("R", 6, 2), ("C", "b1m", 0), ("R", 0, 1),
    ("W", "p1", 0), ("C", "ln1b", 0), ("R", 6, 3), ("R", 2, 0), ("R", 7, 2), ("C", "v0", 0), ("C", "br0", 0),
    ("W", "v0", 0), ("C", "v1", 0), ("C", "br1", 0), ("R", 7, 3), ("R", 1, 1), ("R", 3, 0), ("W", "bm", 0),
    ("C", "tox2", 0), ("C", "br2", 0), ("R", 0, 2), ("R", 2, 1), ("W", "v1", 0), ("C", "v2", 0), ("C", "br3", 0),
    ("R", 1, 2), ("R", 3, 1), ("W", "v2", 0), ("C", "v3", 0), ("W", "am", 0), ("R", 2, 2), ("W", "xm", 0),
    ("C", "fin", 0), ("R", 0, 3), ("R", 1, 3), ("R", 0, 4), ("R", 3, 2), ("R", 2, 3), ("R", 1, 4), ("R", 2, 4),
    ("W", "v3", 0), ("C", "ov", 0), ("R", 3, 3), ("R", 3, 4),
)


def solution(mesh):
    split = P("dp", "seq", None)
    rows = P("dp", None)
    flat = P("dp")
    return jax.shard_map(
        body,
        mesh=mesh,
        in_specs=(split, split, rows, rows, rows, rows, flat) + (rows,) * 6 + (flat, flat),
        out_specs=(split, split) + (rows,) * 12 + (flat,) * 4,
        check_vma=False,
    )
```

```python
import functools

import jax
import jax.numpy as jnp
from jax import lax
from jax.experimental import pallas as pl
from jax.experimental.pallas import tpu as pltpu
from jax.sharding import PartitionSpec as P

HEAD_DIM = 64
STEP = 5
EPS_NORM = 1e-05
BETA_ONE = 0.5
BETA_TWO = 0.5
EPS_ADAM = 1e-08
RATE_MATRIX = 0.05
RATE_VECTOR = 0.2
DECAY_MATRIX = 0.1
SLOPE = 1.702

BF16 = jnp.bfloat16
F32 = jnp.float32
MESH = pl.DeviceIdType.MESH

UNIT = 512
BLOCKS = 4
EDGE = BLOCKS - 1
HALF = 2
UNITS = 8
ITEMS = 16
FIRST_EDGE = 12
PAIR = 128


def dot(a, b):
    return jnp.dot(a, b, preferred_element_type=F32)


def dot_rows(a, b):
    return lax.dot_general(a, b, (((0,), (0,)), ((), ())), preferred_element_type=F32)


def dot_cols(a, b):
    return lax.dot_general(a, b, (((1,), (1,)), ((), ())), preferred_element_type=F32)


def unit_rows(x):
    centred = x - jnp.mean(x, -1, keepdims=True)
    rstd = lax.rsqrt(jnp.mean(centred * centred, -1, keepdims=True) + EPS_NORM)
    return centred * rstd, rstd


def norm_back(grad_normed, unit, rstd, gain):
    g = grad_normed * gain
    return rstd * (g - jnp.mean(g, -1, keepdims=True) - unit * jnp.mean(g * unit, -1, keepdims=True))


def fold8(v):
    return jnp.sum(v.reshape(v.shape[0] // 8, 8, v.shape[1]), 0)


def layer_kernel(
    line, vec_len,
    tok, cot, kbias, p_vec, p_att, p_exp, p_shr,
    o_blk, o_tok, o_att, o_exp, o_shr, o_vec,
    w, w_oth, g, rx, ry, rz, ry_e, rz_e, s_own, s_oth, f_own, f_oth,
    vec_all, vec, bias_h, vg, vr, vz, hidden_sums,
    tok_own, cot_own,
    n1, go, qkv, att, lse, resid, n2, act, fac,
    own_p, keep_p, send_a, send_b, recv_a, recv_b, recv_m, x_recv_m,
    gb, tr, dk_acc, dv_acc,
    ag, rs, sib, wo, xe, vs, fill, loc,
):
    dp_n = 2 * line
    r = w.shape[4]
    block = tok.shape[1]
    own = 2 * block
    rows = 2 * own
    width = tok.shape[2]
    half = UNIT
    d = lax.axis_index("dp")
    s = lax.axis_index("seq")
    zi, yi = d // 2, d % 2
    x, c = s // 2, s % 2
    sibling = (d, x * 2 + 1 - c)
    x_neigh = (d, (1 - x) * 2 + c)
    y_neigh = (zi * 2 + 1 - yi, s)

    def z_peer(o):
        return (lax.rem(zi + o, line) * 2 + yi, s)

    def own_rows(core):
        return pl.ds(pl.multiple_of(core * own, own), own)

    def ff_rows(chip, core):
        return pl.ds(pl.multiple_of(chip * rows + core * own, own), own)

    my_rows = own_rows(c)
    my_half = pl.ds(pl.multiple_of(c * half, half), half)
    oth_half = pl.ds(pl.multiple_of((1 - c) * half, half), half)
    my_block = pl.ds(pl.multiple_of(x * block, block), block)
    oth_block = pl.ds(pl.multiple_of((1 - x) * block, block), block)

    mine, theirs = x * EDGE, (1 - x) * EDGE

    def blocks_of(i):
        if i < 4:
            return i, 1, HALF
        if i < FIRST_EDGE:
            return 4 + (i - 4) // 2, (i - 4) % 2 * HALF, HALF
        return i - FIRST_EDGE, mine, 1

    def item(ref, i):
        u, first, count = blocks_of(i)
        return ref.at[u, pl.ds(first, count)]

    def remote(src, dst, send, recv, to):
        return pltpu.make_async_remote_copy(
            src_ref=src, dst_ref=dst, send_sem=send, recv_sem=recv, device_id=to, device_id_type=MESH
        )

    def wait_bytes(ref, sem):
        pltpu.make_async_copy(ref, ref, sem).wait()

    wide = r % 128 == 0

    def unit_parts(u, place):
        if u < 4:
            core = place % 2
            return [
                (slice(None), pl.ds(pl.multiple_of(n * width + core * half + u * PAIR, PAIR), PAIR)) for n in range(BLOCKS)
            ]
        if u < 6:
            if not wide:
                return None
            parts = []
            for n in range((u - 4) * UNIT, (u - 3) * UNIT, PAIR):
                at = n // r * 4 * r + place * r + n % r
                parts.append((slice(None), pl.ds(pl.multiple_of(at, PAIR), PAIR)))
            return parts
        first = (u - 6) * UNIT
        held = pl.ds(pl.multiple_of(place * r, r), r)
        return [(held, slice(first + n * PAIR, first + (n + 1) * PAIR)) for n in range(BLOCKS)]

    def stage(u):
        n = u % 4 if u < 4 else u % 2
        hold = own_p if u < 4 else send_a if u < 6 else send_b
        return hold.at[(n // 2) * r : (n // 2 + 1) * r, (n % 2) * UNIT : (n % 2 + 1) * UNIT]

    def matrix(u, refs):
        return refs[0 if u < 4 else 1 if u < 6 else 2]

    for u in range(UNITS):
        parts = unit_parts(u, s)
        source = matrix(u, (p_att, p_exp, p_shr))
        for n in range(BLOCKS):
            part = source.at[parts[n]] if parts else source.at[u - 4, n]
            pltpu.make_async_copy(part, stage(u).at[:, n * PAIR : (n + 1) * PAIR], fill.at[u, n // HALF if u >= 4 else int(n in (0, EDGE))]).start()

    vec_all[d] = p_vec[...]
    tok_copy_in = pltpu.make_async_copy(tok.at[x], tok_own.at[my_block], loc.at[0])
    tok_copy_in.start()

    def go_rows(chip, place):
        return pl.ds(pl.multiple_of(chip * rows + place % 2 * own + place // 2 * block, block), block)

    go_local = [pltpu.make_async_copy(cot.at[n], go.at[go_rows(n, s)], loc.at[1]) for n in range(2)]
    for copy in go_local:
        copy.start()

    barrier = pltpu.get_barrier_semaphore()

    def greet(o, carry):
        pl.semaphore_signal(barrier, inc=1, device_id=(lax.rem(d + o, dp_n), s), device_id_type=MESH)
        return carry

    lax.fori_loop(1, dp_n, greet, 0)
    pl.semaphore_signal(barrier, inc=1, device_id=sibling, device_id_type=MESH)
    pl.semaphore_signal(barrier, inc=1, device_id=x_neigh, device_id_type=MESH)
    pl.semaphore_wait(barrier, dp_n + 1)

    def send_vec(o, carry):
        remote(p_vec, vec_all.at[d], vs.at[0, 0], vs.at[1, 0], (lax.rem(d + o, dp_n), s)).start()
        return carry

    lax.fori_loop(1, dp_n, send_vec, 0)
    tok_copy_x = remote(tok.at[1 - x], tok_own.at[my_block], xe.at[0, 0], xe.at[1, 0], x_neigh)
    tok_copy_x.start()
    other = (1 - x) * 2 + c
    go_copies = [
        [remote(cot.at[n], go.at[go_rows(n, s)], sib.at[0, 4], sib.at[1, 4], sibling) for n in range(2)],
        [remote(cot.at[n], go.at[go_rows(n, s)], xe.at[0, 4], xe.at[1, 4], x_neigh) for n in range(2)],
        [remote(go.at[go_rows(n, other)], go.at[go_rows(n, other)], sib.at[0, 5], sib.at[1, 5], sibling) for n in range(2)],
    ]
    go_bytes = go.at[:own]

    def ag_z(i):
        u, first, count = blocks_of(i)
        group = first // HALF if 4 <= i < FIRST_EDGE else int(i >= FIRST_EDGE)
        wait_bytes(stage(u).at[:, : HALF * PAIR], fill.at[u, group])
        for n in range(count):
            w[u, first + n, zi, yi] = stage(u)[:, pl.ds(pl.multiple_of((first + n) * PAIR, PAIR), PAIR)].astype(BF16)
        part = item(w, i).at[:, zi, yi]
        for o in range(1, line):
            remote(part, part, ag.at[0, i], ag.at[1, i], z_peer(o)).start()

    def ag_y_copy(i):
        part = item(w, i).at[:, :, yi]
        return remote(part, part, ag.at[2, i], ag.at[3, i], y_neigh)

    def ag_x_copy(i):
        return remote(item(w, i), item(w, i), ag.at[4, i], ag.at[5, i], x_neigh)

    def z_bytes(i):
        return item(w, i).at[:, pl.ds(0, line - 1), yi]

    def ag_y(i):
        wait_bytes(z_bytes(i), ag.at[1, i])
        ag_y_copy(i).start()

    def ag_x(i):
        ag_y_copy(i).wait_recv()
        if i >= FIRST_EDGE:
            ag_x_copy(i).start()

    def ag_end(i):
        ag_x_copy(i).wait_recv()

    gather_stages = [ag_z, ag_y, ag_x, ag_end]

    grain = 128 if vec_len % 128 == 0 else 64

    def vec_lanes(first):
        parts = []
        for e in range(first, first + 128, grain):
            o = e % vec_len
            parts.append(vec_all[e // vec_len, o // 128 : o // 128 + 1, o % 128 : o % 128 + grain])
        return parts[0] if len(parts) == 1 else jnp.concatenate(parts, 1)

    def hidden_bias(place):
        parts = []
        for shard in range(dp_n):
            n = shard * 4 * r + place * r
            parts.append(vec[8 + n // width : 9 + n // width, n % width : n % width + r])
        return jnp.concatenate(parts, 1)

    def vector():
        for row in range(12):
            for lane in range(0, width, 128):
                vec[row : row + 1, lane : lane + 128] = vec_lanes(row * width + lane)
        low_half = jnp.where(s == 0, hidden_bias(0), hidden_bias(1))
        bias_h[...] = jnp.where(s < 2, low_half, jnp.where(s == 2, hidden_bias(2), hidden_bias(3)))

    def live(to):
        return jnp.where(kbias[to, 0:1] < 0, 0.0, 1.0)

    chunk = block // 2

    def chunks(first, i):
        return pl.ds(pl.multiple_of(first + i * chunk, chunk), chunk)

    def first_norm():
        def some(i, carry):
            unit, _ = unit_rows(tok_own[chunks(0, i), :].astype(F32))
            n1[chunks(c * own, i), :] = (unit * vec[0:1, :] + vec[1:2, :]).astype(BF16)
            return carry

        lax.fori_loop(0, own // chunk, some, 0)
        n1_copy.start()

    def grad_output():
        for copy in go_copies[1] + go_copies[0]:
            copy.start()

    def rows_copies(ref, n):
        here, there = ref.at[ff_rows(x, c)], ref.at[ff_rows(1 - x, c)]
        return (
            remote(here, here, sib.at[0, n], sib.at[1, n], sibling),
            remote(here, here, xe.at[0, n], xe.at[1, n], x_neigh),
            remote(there, there, sib.at[0, n + 1], sib.at[1, n + 1], sibling),
        )

    n1_copy = remote(n1.at[my_rows], n1.at[my_rows], sib.at[0, 0], sib.at[1, 0], sibling)
    att_copy = remote(att.at[:, my_half], att.at[:, my_half], sib.at[0, 1], sib.at[1, 1], sibling)
    gb_copy = remote(gb.at[my_rows], gb.at[my_rows], sib.at[0, 2], sib.at[1, 2], sibling)
    p1_copy = remote(send_a, recv_a, sib.at[0, 3], sib.at[1, 3], sibling)
    n2_copies = rows_copies(n2, 6)
    b_copy = remote(send_b, recv_b, sib.at[0, 8], sib.at[1, 8], sibling)
    a_copy = remote(send_a, recv_a, sib.at[0, 9], sib.at[1, 9], sibling)
    bm_copy = remote(send_b, recv_m, sib.at[0, 10], sib.at[1, 10], sibling)
    am_copy = remote(send_a, recv_b, sib.at[0, 11], sib.at[1, 11], sibling)
    x_back = [
        remote(cot_own.at[pl.ds(n * block, block)], o_blk.at[n], xe.at[0, 7 + n], xe.at[1, 7 + n], x_neigh) for n in range(2)
    ]
    xm_copy = remote(cot_own, x_recv_m, xe.at[0, 9], xe.at[1, 9], x_neigh)
    tok_copy = remote(tok_own.at[oth_block], o_tok.at[x], xe.at[0, 3], xe.at[1, 3], x_neigh)
    blk_copy = remote(cot_own.at[oth_block], o_blk.at[x], xe.at[0, 2], xe.at[1, 2], x_neigh)

    low_lane = lax.broadcasted_iota(jnp.int32, (PAIR, PAIR), 1) < HEAD_DIM
    low_row = lax.broadcasted_iota(jnp.int32, (PAIR, PAIR), 0) < HEAD_DIM
    q_chunks = rows // PAIR

    def two_heads(v):
        zero = jnp.zeros_like(v)
        return jnp.concatenate([jnp.where(low_lane, v, zero), jnp.where(low_lane, zero, v)], 0)

    qkv_lanes = 3 * PAIR

    def pair_lanes(p):
        return tuple(slice(p * qkv_lanes + n * PAIR, p * qkv_lanes + (n + 1) * PAIR) for n in range(3))

    def att_lanes(p):
        return pl.ds(pl.multiple_of(c * half + p * PAIR, PAIR), PAIR)

    def wo_copy(p):
        return remote(w.at[p, BLOCKS - 1], w_oth.at[p], wo.at[0, p], wo.at[1, p], sibling)

    def columns(blocks):
        return jnp.concatenate([v.reshape(-1, PAIR) for v in blocks], 1)

    def project(p):
        wo_copy(p).start()
        q_at, k_at, v_at = pair_lanes(p)
        out = dot(n1[...], columns([w[p, n] for n in range(3)]))
        queries = (out[:, :PAIR] + vec[4:5, att_lanes(p)]).astype(BF16)
        qkv[:, q_at] = queries * jnp.asarray(HEAD_DIM**-0.5, BF16)
        qkv[:, k_at] = out[:, PAIR : 2 * PAIR].astype(BF16)
        qkv[:, v_at] = (out[:, 2 * PAIR :] + vec[5:6, att_lanes(p)]).astype(BF16)

    def attend_forward(p, first, last):
        q_at, k_at, v_at = pair_lanes(p)

        def some(j, carry):
            at = pl.ds(pl.multiple_of(j * PAIR, PAIR), PAIR)
            mask = kbias[...]
            scores = dot_cols(qkv[:, k_at], two_heads(qkv[at, q_at])) + jnp.concatenate([mask, mask], 1)
            highest = jnp.max(scores, 0, keepdims=True)
            raised = jnp.exp(scores - highest)
            total = jnp.sum(raised, 0, keepdims=True)
            out = dot_rows(qkv[:, v_at], raised.astype(BF16)) / total
            out = jnp.where(low_row, out[:, :PAIR], out[:, PAIR:])
            att[at, att_lanes(p)] = out.T.astype(BF16)
            lse[pl.ds(p * q_chunks + j, 1), :] = highest + jnp.log(total)
            return carry

        lax.fori_loop(first, last, some, 0)
        if p == 3 and last == q_chunks:
            att_copy.start()

    def own_out(z):
        return columns([w[p, BLOCKS - 1, z] for p in range(4)])

    def oth_out(z):
        return columns([w_oth[p, z] for p in range(4)])

    def output_projection():
        mixed = att[my_rows, :]
        resid[:, my_half] = dot(mixed, own_out(slice(None)))
        resid[:, oth_half] = dot(mixed, oth_out(slice(None)))

    def second_norm():
        def some(i, carry):
            at = chunks(0, i)
            res = resid[at, :] + tok_own[at, :].astype(F32) + vec[6:7, :]
            resid[at, :] = res
            unit, _ = unit_rows(res)
            n2[chunks(x * rows + c * own, i), :] = (unit * vec[2:3, :] + vec[3:4, :]).astype(BF16)
            return carry

        lax.fori_loop(0, own // chunk, some, 0)
        n2_copies[1].start()
        n2_copies[0].start()

    tile = HALF * PAIR

    def expand(n, chip):
        u, first, _ = blocks_of(4 + n)
        at = pl.ds(pl.multiple_of(chip * rows, rows), rows)
        to = slice(n * tile, (n + 1) * tile)
        hidden = dot(n2[at, :], columns([w[u, first], w[u, first + 1]])) + bias_h[:, to]
        gate = jax.nn.sigmoid(SLOPE * hidden)
        act[at, to] = (hidden * gate).astype(BF16)
        fac[at, to] = (gate + SLOPE * hidden * gate * (1.0 - gate)).astype(BF16)

    def rs_x_copy(i):
        u = i - FIRST_EDGE
        return remote(g.at[u, theirs], rx.at[u], rs.at[0, i], rs.at[1, i], x_neigh)

    def y_place(i):
        return ry.at[i] if i < FIRST_EDGE else ry_e.at[i - FIRST_EDGE]

    def z_place(i):
        return rz.at[i] if i < FIRST_EDGE else rz_e.at[i - FIRST_EDGE]

    def rs_y_copy(i):
        return remote(item(g, i).at[:, :, 1 - yi], y_place(i), rs.at[2, i], rs.at[3, i], y_neigh)

    def done_blocks(i):
        u, first, count = blocks_of(i)
        return f_own.at[u, pl.ds(first, count)]

    def rs_2_copy(i):
        if i < 4:
            return remote(s_own.at[i], s_oth.at[i], rs.at[6, i], rs.at[7, i], x_neigh)
        to = f_oth.at[i - 4] if i < FIRST_EDGE else f_own.at[i - FIRST_EDGE, pl.ds(mine, 1)]
        return remote(done_blocks(i), to, rs.at[6, i], rs.at[7, i], x_neigh)

    def to_result(u, n, place):
        result = matrix(u, (o_att, o_exp, o_shr))
        if u < 4:
            first = n * width + place % 2 * half + u * PAIR
            return result.at[:, pl.ds(pl.multiple_of(first, PAIR), PAIR)]
        parts = unit_parts(u, place)
        return result.at[parts[n]] if parts else result.at[u - 4, place, n]

    def rs_share(i, source, first, count, place, sems):
        u = blocks_of(i)[0]
        for n in range(count):
            to = to_result(u, first + n, place)
            remote(source.at[n], to, rs.at[sems, i], rs.at[sems + 1, i], sibling).start()
            pltpu.make_async_copy(source.at[n], to, rs.at[sems + 2, i]).start()

    def rs_x_add(i):
        rs_x_copy(i).wait_recv()
        u = i - FIRST_EDGE

        def add(z, carry):
            g[u, mine, z] = (g[u, mine, z].astype(F32) + rx[u, z].astype(F32)).astype(BF16)
            return carry

        lax.fori_loop(0, line, add, 0)
        rs_y_copy(i).start()

    def rs_y_add(i):
        rs_y_copy(i).wait_recv()
        u, first, count = blocks_of(i)
        got = y_place(i)

        def add(z, carry):
            for n in range(count):
                g[u, first + n, z, yi] = (g[u, first + n, z, yi].astype(F32) + got[n, z].astype(F32)).astype(BF16)
            return carry

        lax.fori_loop(0, line, add, 0)
        for o in range(1, line):
            z = lax.rem(zi + o, line)
            remote(item(g, i).at[:, z, yi], z_place(i).at[o - 1], rs.at[4, i], rs.at[5, i], z_peer(o)).start()

    def rs_z_add(i):
        u, first, count = blocks_of(i)
        got = z_place(i)
        wait_bytes(got, rs.at[5, i])
        for n in range(count):
            total = g[u, first + n, zi, yi].astype(F32)
            for o in range(1, line):
                total = total + got[o - 1, n].astype(F32)
            if i < 4:
                s_own[i, n] = total.astype(BF16)
            else:
                f_own[u, first + n] = total.astype(BF16)
        rs_2_copy(i).start()
        if i >= 4:
            rs_share(i, done_blocks(i), first, count, s, 8)

    def rs_join(i):
        rs_2_copy(i).wait_recv()
        u, first, count = blocks_of(i)
        if i < 4:
            for n in range(count):
                f_own[u, first + n] = (s_own[i, n].astype(F32) + s_oth[i, n].astype(F32)).astype(BF16)
            rs_share(i, done_blocks(i), first, count, s, 8)
        elif i < FIRST_EDGE:
            rs_share(i, f_oth.at[i - 4], first, count, other, 11)
        else:
            rs_share(i, f_own.at[u, pl.ds(theirs, 1)], theirs, count, other, 11)

    def rs_end(i):
        if i >= FIRST_EDGE:
            rs_x_copy(i).wait_send()
        rs_y_copy(i).wait_send()
        wait_bytes(z_place(i), rs.at[4, i])
        rs_2_copy(i).wait_send()
        for n in range(8, 11 if i < 4 else 14):
            wait_bytes(done_blocks(i), rs.at[n, i])

    def put(u, first, value):
        for n in range(value.shape[1] // PAIR):
            part = value[:, n * PAIR : (n + 1) * PAIR].astype(BF16)
            g[u, first + n] = part.reshape(line, 2, r, PAIR)

    def rs_start(i):
        (rs_y_copy(i) if i < FIRST_EDGE else rs_x_copy(i)).start()

    def rs_stage(i, k):
        stages = [rs_x_add, rs_y_add, rs_z_add, rs_join, rs_end]
        (stages[1:] if i < FIRST_EDGE else stages)[k](i)

    def transpose_into(first, src, size):
        def move(i, carry):
            at = pl.ds(pl.multiple_of(i * 128, 128), 128)
            tr[at, first : first + size] = src[:, at].T
            return carry

        lax.fori_loop(0, width // 128, move, 0)

    def shrink_grad(n):
        u, first, _ = blocks_of(8 + n)
        put(u, first, dot(tr[...], go[:, n * tile : (n + 1) * tile]))

    span = max(1, tile // (2 * r))
    part_rows = span * 2 * r

    def hidden_back(n, chip, clear):
        at = pl.ds(pl.multiple_of(chip * rows, rows), rows)
        if clear:
            hidden_sums[...] = jnp.zeros_like(hidden_sums)

        def some(m, carry):
            to = pl.ds(pl.multiple_of(m * part_rows, part_rows), part_rows)
            total = None
            for j in range(2):
                part = columns([w[6 + j, b, pl.ds(m * span, span)] for b in range(BLOCKS)])
                term = dot_cols(go[at, j * UNIT : (j + 1) * UNIT], part)
                total = term if total is None else total + term
            low = (total * fac[at, to].astype(F32)).astype(BF16)
            fac[at, to] = low
            hidden_sums[:, to] += fold8(low.astype(F32))
            return carry

        count = line // span // 4
        lax.fori_loop(n * count, (n + 1) * count, some, 0)

    def back_partial(src, rows_at, units, blocks, dst):
        lanes = blocks * PAIR

        def back(n, carry):
            total = None
            for k, u in enumerate(units):
                part = columns([w[u, b, pl.ds(n * span, span)] for b in range(blocks)])
                term = dot_cols(src[rows_at, k * lanes : (k + 1) * lanes], part)
                total = term if total is None else total + term
            dst[:, pl.ds(pl.multiple_of(n * part_rows, part_rows), part_rows)] = total
            return carry

        lax.fori_loop(0, line // span, back, 0)

    def expand_grad(n):
        u, first, _ = blocks_of(4 + n)
        put(u, first, dot(tr[...], fac[:, n * tile : (n + 1) * tile]))

    def to_x(came):
        def some(i, carry):
            at = chunks(0, i)
            cot_own[at, :] = (keep_p[at, :] + came[at, :]).astype(BF16)
            return carry

        lax.fori_loop(0, own // chunk, some, 0)

    ff = (4, 5)

    def hidden_partial(n):
        at = ff_rows(*((1 - x, 1 - c), (1 - x, c), (x, 1 - c), (x, c))[n])
        back_partial(fac, at, ff, BLOCKS, (send_b, keep_p, send_a, own_p)[n])
        if n == 0:
            b_copy.start()
        if n == 2:
            a_copy.start()

    def partial_over_x():
        to_x(recv_b)
        for copy in x_back:
            copy.start()

    zeros8 = jnp.zeros((8, width), F32)

    def second_norm_back():
        def some(i, carry):
            at = chunks(0, i)
            unit, rstd = unit_rows(resid[at, :])
            came = o_blk[i // 2, pl.ds(pl.multiple_of(i % 2 * chunk, chunk), chunk)].astype(F32)
            gn = own_p[at, :] + recv_a[at, :] + came
            grad_out = go[chunks(x * rows + c * own, i), :].astype(F32)
            gr = grad_out + norm_back(gn, unit, rstd, vec[2:3, :])
            own_p[at, :] = gr
            low = gr.astype(BF16)
            gb[chunks(c * own, i), :] = low
            a, b, e, f = carry
            return (a + fold8(gn * unit), b + fold8(gn), e + fold8(low.astype(F32)), f + fold8(grad_out))

        vg[...] = jnp.zeros_like(vg)
        vg[pl.ds(8 + s, 1), :] = jnp.sum(hidden_sums[...], 0, keepdims=True)
        sums = lax.fori_loop(0, own // chunk, some, (zeros8,) * 4)
        for row, v in zip((2, 3, 6, 7), sums):
            vg[row : row + 1, :] = jnp.sum(v, 0, keepdims=True)
        gb_copy.start()

    def grad_attended(n):
        if n == 0:
            for copy in n2_copies:
                copy.wait_send()
        quarter = line // 4
        head_rows = pl.ds(c * (line // 2) + n * quarter, quarter)
        part = dot_cols(gb[:, my_half], own_out(head_rows)) + dot_cols(gb[:, oth_half], oth_out(head_rows))
        n2[:rows, n * tile : (n + 1) * tile] = part.astype(BF16)

    def attend_backward(p, first, last):
        q_at, k_at, v_at = pair_lanes(p)
        own_lanes = slice(p * PAIR, (p + 1) * PAIR)
        if first == 0:
            dk_acc[...] = jnp.zeros_like(dk_acc)
            dv_acc[...] = jnp.zeros_like(dv_acc)

        def some(j, carry):
            at = pl.ds(pl.multiple_of(j * PAIR, PAIR), PAIR)
            both = two_heads(qkv[at, q_at])
            grads = two_heads(n2[at, own_lanes])
            mask = kbias[...]
            scores = dot_cols(qkv[:, k_at], both) + jnp.concatenate([mask, mask], 1)
            chance = jnp.exp(scores - lse[pl.ds(p * q_chunks + j, 1), :])
            dv_acc[...] += dot(chance.astype(BF16), grads)
            grad_chance = dot_cols(qkv[:, v_at], grads)
            inner = jnp.sum(chance * grad_chance, 0, keepdims=True)
            grad_scores = (chance * (grad_chance - inner)).astype(BF16)
            dk_acc[...] += dot(grad_scores, both)
            out = dot_rows(qkv[:, k_at], grad_scores)
            out = jnp.where(low_row, out[:, :PAIR], out[:, PAIR:]) * HEAD_DIM**-0.5
            qkv[at, q_at] = out.T.astype(BF16)
            return carry

        lax.fori_loop(first, last, some, 0)
        if last < q_chunks:
            return
        qkv[:, k_at] = dk_acc[...].astype(BF16)
        qkv[:, v_at] = dv_acc[...].astype(BF16)
        vg[4:5, att_lanes(p)] = jnp.sum(fold8(qkv[:, q_at].astype(F32)), 0, keepdims=True)
        vg[5:6, att_lanes(p)] = jnp.sum(fold8(qkv[:, v_at].astype(F32)), 0, keepdims=True)

    def attention_grad(p):
        put(p, 0, dot(tr[:, :rows], qkv[:, p * qkv_lanes : (p + 1) * qkv_lanes]))
        put(p, BLOCKS - 1, dot(tr[:, rows:], gb[:, att_lanes(p)]))

    def input_partial(n):
        back_partial(qkv, own_rows(c if n else 1 - c), (0, 1, 2, 3), 3, keep_p if n else send_a)
        if n == 0:
            p1_copy.start()

    def first_norm_back():
        def some(i, carry):
            at = chunks(0, i)
            unit, rstd = unit_rows(tok_own[at, :].astype(F32))
            gn = keep_p[at, :] + recv_a[at, :]
            out = own_p[at, :] + norm_back(gn, unit, rstd, vec[0:1, :])
            tok_own[at, :] = out.astype(BF16)
            a, b = carry
            return (a + fold8(gn * unit), b + fold8(gn))

        sums = lax.fori_loop(0, own // chunk, some, (zeros8,) * 2)
        for row, v in zip((0, 1), sums):
            vg[row : row + 1, :] = jnp.sum(v, 0, keepdims=True)
        o_tok[x] = tok_own[my_block, :]
        tok_copy.start()

    def branch(dst, rows_at, add):
        def out(n, carry):
            for j in range(2):
                part = columns([w[6 + j, 2 * n], w[6 + j, 2 * n + 1]])
                to = pl.ds(pl.multiple_of(j * UNIT + n * tile, tile), tile)
                total = dot(act[rows_at, :], part)
                dst[:, to] = dst[:, to] + total if add else total
            return carry

        lax.fori_loop(0, UNIT // tile, out, 0)

    def output_partial(n):
        at = ff_rows(*((1 - x, 1 - c), (1 - x, c), (x, 1 - c), (x, c))[n])
        branch((send_b, keep_p, send_a, resid)[n], at, n == 3)
        if n == 0:
            bm_copy.start()
        if n == 2:
            am_copy.start()

    def output_over_x():
        to_x(recv_m)
        xm_copy.start()

    def finish_block():
        def some(i, carry):
            at = chunks(0, i)
            out = resid[at, :] + recv_b[at, :] + x_recv_m[at, :].astype(F32) + vec[7:8, :]
            cot_own[at, :] = (live(chunks(c * own, i)) * out).astype(BF16)
            return carry

        lax.fori_loop(0, own // chunk, some, 0)
        o_blk[x] = cot_own[my_block, :]
        blk_copy.start()

    v_copies = [
        remote(vg, vr.at[n], vs.at[0, 1 + n], vs.at[1, 1 + n], to) for n, to in enumerate((sibling, x_neigh, y_neigh))
    ]

    def vector_hop(n):
        if n < 3:
            v_copies[n].start()
            return

        def send(o, carry):
            remote(vg, vz.at[zi], vs.at[0, 4], vs.at[1, 4], (lax.rem(zi + o, line) * 2 + yi, s)).start()
            return carry

        lax.fori_loop(1, line, send, 0)
        vz[zi] = vg[...]

    def vector_add(n):
        if n < 3:
            v_copies[n].wait()
            vg[...] += vr[n]
            return
        wait_bytes(vz.at[pl.ds(0, line - 1)], vs.at[1, 4])
        wait_bytes(vz.at[pl.ds(0, line - 1)], vs.at[0, 4])

    def vector_out():
        o_vec[...] = lax.fori_loop(1, line, lambda i, t: t + vz[i], vz[0])

    def both(*copies):
        for copy in copies:
            copy.wait()

    def received(*copies):
        for copy in copies:
            copy.wait_recv()

    def relay(copies):
        copies[1].wait_recv()
        copies[2].start()

    def relay_go():
        wait_bytes(go_bytes, xe.at[1, 4])
        for copy in go_copies[2]:
            copy.start()

    def all_rows():
        received(n2_copies[2])
        wait_bytes(go_bytes, loc.at[1])
        wait_bytes(go_bytes, sib.at[1, 4])
        wait_bytes(go_bytes, sib.at[1, 5])

    waits = dict(
        vec=lambda: wait_bytes(vec_all.at[pl.ds(0, dp_n - 1)], vs.at[1, 0]),
        tok=lambda: both(tok_copy_x, tok_copy_in),
        cot=lambda: None,
        n1=lambda: received(n1_copy),
        gox=relay_go,
        att=lambda: received(*[wo_copy(p) for p in range(4)], att_copy),
        n2=lambda: received(n2_copies[0]),
        n2x=lambda: relay(n2_copies),
        n2r=all_rows,
        b=lambda: both(b_copy),
        a=lambda: both(a_copy),
        xb=lambda: both(*x_back),
        gb=lambda: received(gb_copy),
        p1=lambda: both(p1_copy),
        bm=lambda: both(bm_copy),
        am=lambda: both(am_copy),
        xm=lambda: both(xm_copy),
        v0=lambda: vector_add(0),
        v1=lambda: vector_add(1),
        v2=lambda: vector_add(2),
        v3=lambda: vector_add(3),
    )
    split = 3
    work = dict(
        vec=lambda n: vector(),
        ln1=lambda n: first_norm(),
        go=lambda n: grad_output(),
        qkv=project,
        afa=lambda p: attend_forward(p, 0, split),
        afb=lambda p: attend_forward(p, split, q_chunks),
        out=lambda n: output_projection(),
        ln2=lambda n: second_norm(),
        eo=lambda n: expand(n, x),
        ex=lambda n: expand(n, 1 - x),
        tra=lambda n: transpose_into(0, act, 2 * rows),
        gs=shrink_grad,
        hx=lambda n: hidden_back(n, 1 - x, n == 0),
        hb=lambda n: hidden_back(n, x, False),
        bp0=lambda n: hidden_partial(0),
        bp1=lambda n: hidden_partial(1),
        tox=lambda n: partial_over_x(),
        bp2=lambda n: hidden_partial(2),
        bp3=lambda n: hidden_partial(3),
        trn=lambda n: transpose_into(0, n2, 2 * rows),
        gx=expand_grad,
        ln2b=lambda n: second_norm_back(),
        trb=lambda n: (transpose_into(0, n1, rows), transpose_into(rows, att, rows)),
        gat=grad_attended,
        aba=lambda p: attend_backward(p, 0, split),
        abb=lambda p: attend_backward(p, split, q_chunks),
        ga=attention_grad,
        b1o=lambda n: input_partial(0),
        b1m=lambda n: input_partial(1),
        ln1b=lambda n: first_norm_back(),
        br0=lambda n: output_partial(0),
        br1=lambda n: output_partial(1),
        tox2=lambda n: output_over_x(),
        br2=lambda n: output_partial(2),
        br3=lambda n: output_partial(3),
        v0=lambda n: vector_hop(0),
        v1=lambda n: vector_hop(1),
        v2=lambda n: vector_hop(2),
        v3=lambda n: vector_hop(3),
        fin=lambda n: finish_block(),
        ov=lambda n: vector_out(),
    )
    for kind, name, n in ORDER:
        if kind == "C":
            work[name](n)
        elif kind == "W":
            waits[name]()
        elif kind == "A":
            gather_stages[n](name)
        elif kind == "I":
            rs_start(name)
        else:
            rs_stage(name, n)

    blk_copy.wait()
    tok_copy.wait()
    wait_bytes(vec_all.at[pl.ds(0, dp_n - 1)], vs.at[0, 0])
    for sem in (sib.at[0, 4], sib.at[0, 5], xe.at[0, 4]):
        wait_bytes(go_bytes, sem)
    for copy in [n1_copy, att_copy, gb_copy] + [wo_copy(p) for p in range(4)]:
        copy.wait_send()
    for i in range(ITEMS):
        wait_bytes(z_bytes(i), ag.at[0, i])
        ag_y_copy(i).wait_send()
        if i >= FIRST_EDGE:
            ag_x_copy(i).wait_send()


def adamw(grad, moment, square, weight, rate, decay):
    momentum = BETA_ONE * moment + (1.0 - BETA_ONE) * grad
    variance = BETA_TWO * square + (1.0 - BETA_TWO) * grad * grad
    first_fix = 1.0 - BETA_ONE**STEP
    second_fix = 1.0 - BETA_TWO**STEP
    direction = momentum / first_fix / (jnp.sqrt(variance / second_fix) + EPS_ADAM)
    updated = weight - rate * (direction + decay * weight)
    return (momentum, variance, updated, updated.astype(BF16))


def body(
    tokens, cotangent, key_mask,
    attention_weights, expand_weights, shrink_weights, vector_params,
    attention_moment, attention_square, expand_moment, expand_square,
    shrink_moment, shrink_square, vector_moment, vector_square,
):
    dp_n = lax.axis_size("dp")
    line = dp_n // 2
    d = lax.axis_index("dp")
    place = lax.axis_index("seq")
    x, c = place // 2, place % 2
    _, local_len, width = tokens.shape
    r = width // dp_n
    block = -(-local_len // 16) * 16
    own, rows = 2 * block, 4 * block
    pad = ((0, 0), (0, block - local_len), (0, 0))

    keep = lax.dynamic_index_in_dim(key_mask, x, 0, keepdims=False).reshape(2, 2, local_len)
    keep = jnp.pad(keep.transpose(1, 0, 2), ((0, 0), (0, 0), pad[1])).reshape(2, own)
    kbias = jnp.broadcast_to(jnp.where(keep > 0, 0.0, -1e30).astype(F32).reshape(rows, 1), (rows, PAIR))
    p_exp = expand_weights
    if r % 128:
        p_exp = lax.dynamic_index_in_dim(expand_weights.reshape(r, dp_n, 4, r), place, 2, keepdims=False)
        p_exp = p_exp.reshape(r, 2, BLOCKS, PAIR).transpose(1, 2, 0, 3)
    vec_len = vector_params.shape[0]
    here = lax.dynamic_slice_in_dim(key_mask, place * local_len, local_len, 1)
    grad_out = jnp.where(here[:, :, None] > 0, cotangent, jnp.zeros_like(cotangent))
    vec_rows = -(-vec_len // 1024) * 8
    p_vec = jnp.pad(vector_params.astype(BF16).astype(F32), (0, vec_rows * 128 - vec_len)).reshape(vec_rows, 128)

    vmem = pl.BlockSpec(memory_space=pltpu.VMEM)
    hbm = pl.BlockSpec(memory_space=pl.ANY)
    padded = jax.ShapeDtypeStruct((2, block, width), BF16)
    o_blk, o_tok, o_att, o_exp, o_shr, o_vec = pl.pallas_call(
        functools.partial(layer_kernel, line, vec_len),
        out_shape=(
            padded,
            padded,
            jax.ShapeDtypeStruct((r, 4 * width), BF16),
            jax.ShapeDtypeStruct((2, 4, BLOCKS, r, PAIR) if r % 128 else (r, 4 * width), BF16),
            jax.ShapeDtypeStruct((4 * r, width), BF16),
            jax.ShapeDtypeStruct((16, width), F32),
        ),
        in_specs=[hbm, hbm, vmem, vmem, hbm, hbm, hbm],
        out_specs=(vmem, vmem, hbm, hbm, hbm, vmem),
        scratch_shapes=[
            pltpu.VMEM((UNITS, BLOCKS, line, 2, r, PAIR), BF16),
            pltpu.VMEM((4, line, 2, r, PAIR), BF16),
            pltpu.VMEM((UNITS, BLOCKS, line, 2, r, PAIR), BF16),
            pltpu.VMEM((4, line, 2, r, PAIR), BF16),
            pltpu.VMEM((FIRST_EDGE, HALF, line, r, PAIR), BF16),
            pltpu.VMEM((FIRST_EDGE, line - 1, HALF, r, PAIR), BF16),
            pltpu.VMEM((4, 1, line, r, PAIR), BF16),
            pltpu.VMEM((4, line - 1, 1, r, PAIR), BF16),
            pltpu.VMEM((4, HALF, r, PAIR), BF16),
            pltpu.VMEM((4, HALF, r, PAIR), BF16),
            pltpu.VMEM((UNITS, BLOCKS, r, PAIR), BF16),
            pltpu.VMEM((8, HALF, r, PAIR), BF16),
            pltpu.VMEM((dp_n, vec_rows, 128), F32),
            pltpu.VMEM((16, width), F32),
            pltpu.VMEM((1, width), F32),
            pltpu.VMEM((16, width), F32),
            pltpu.VMEM((3, 16, width), F32),
            pltpu.VMEM((line, 16, width), F32),
            pltpu.VMEM((8, width), F32),
            pltpu.VMEM((own, width), BF16),
            pltpu.VMEM((own, width), BF16),
            pltpu.VMEM((rows, width), BF16),
            pltpu.VMEM((2 * rows, width), BF16),
            pltpu.VMEM((rows, 3 * UNIT), BF16),
            pltpu.VMEM((rows, width), BF16),
            pltpu.VMEM(((rows // PAIR) * (UNIT // PAIR), 2 * PAIR), F32),
            pltpu.VMEM((own, width), F32),
            pltpu.VMEM((2 * rows, width), BF16),
            pltpu.VMEM((2 * rows, width), BF16),
            pltpu.VMEM((2 * rows, width), BF16),
        ]
        + [pltpu.VMEM((own, width), F32)] * 7
        + [
            pltpu.VMEM((own, width), BF16),
            pltpu.VMEM((rows, width), BF16),
            pltpu.VMEM((width, 2 * rows), BF16),
            pltpu.VMEM((rows, PAIR), F32),
            pltpu.VMEM((rows, PAIR), F32),
            pltpu.SemaphoreType.DMA((6, ITEMS)),
            pltpu.SemaphoreType.DMA((14, ITEMS)),
            pltpu.SemaphoreType.DMA((2, 12)),
            pltpu.SemaphoreType.DMA((2, 4)),
            pltpu.SemaphoreType.DMA((2, 10)),
            pltpu.SemaphoreType.DMA((2, 5)),
            pltpu.SemaphoreType.DMA((UNITS, 2)),
            pltpu.SemaphoreType.DMA((2,)),
        ],
        compiler_params=pltpu.CompilerParams(
            collective_id=0, has_side_effects=True, vmem_limit_bytes=VMEM_LIMIT
        ),
        name="layer",
    )(jnp.pad(tokens, pad), jnp.pad(grad_out, pad), kbias, p_vec, attention_weights, p_exp, shrink_weights)

    block_output = o_blk[:, :local_len]
    token_gradient = o_tok[:, :local_len]
    grad_attention, grad_shrink = o_att.astype(F32), o_shr.astype(F32)
    if r % 128:
        o_exp = o_exp.transpose(3, 1, 0, 2, 4).reshape(r, 4, dp_n, r).transpose(0, 2, 1, 3).reshape(r, 4 * width)
    grad_expand = o_exp.astype(F32)
    hidden_sums = o_vec[8:12].reshape(4, dp_n, r).transpose(1, 0, 2).reshape(4, width)
    grad_vector = jnp.concatenate([o_vec[0:8], hidden_sums], 0).reshape(dp_n, vec_len)
    grad_vector = lax.dynamic_index_in_dim(grad_vector, d, 0, keepdims=False)

    attention_out = adamw(
        grad_attention, attention_moment, attention_square, attention_weights, RATE_MATRIX, DECAY_MATRIX
    )
    grad_expand, attention_out = lax.optimization_barrier((grad_expand, attention_out))
    expand_out = adamw(grad_expand, expand_moment, expand_square, expand_weights, RATE_MATRIX, DECAY_MATRIX)
    shrink_out = adamw(grad_shrink, shrink_moment, shrink_square, shrink_weights, RATE_MATRIX, DECAY_MATRIX)
    vector_out = adamw(grad_vector, vector_moment, vector_square, vector_params, RATE_VECTOR, 0.0)
    return (block_output, token_gradient, *attention_out, *expand_out, *shrink_out, *vector_out)


VMEM_LIMIT = 63 * 2**20

ORDER = (
    ("A", 12, 0), ("A", 0, 0), ("A", 13, 0), ("A", 1, 0), ("A", 14, 0), ("A", 2, 0), ("W", "cot", 0), ("C", "go", 0),
    ("W", "vec", 0), ("C", "vec", 0), ("A", 12, 1), ("W", "tok", 0), ("C", "ln1", 0), ("A", 12, 2), ("A", 0, 1),
    ("A", 15, 0), ("A", 3, 0), ("W", "n1", 0), ("A", 13, 1), ("A", 0, 2), ("A", 1, 1), ("A", 4, 0), ("A", 13, 2),
    ("A", 14, 1), ("A", 5, 0), ("A", 1, 2), ("A", 2, 1), ("A", 6, 0), ("A", 12, 3), ("C", "qkv", 0), ("A", 14, 2),
    ("C", "afa", 0), ("A", 15, 1), ("C", "afb", 0), ("A", 13, 3), ("C", "qkv", 1), ("A", 2, 2), ("C", "afa", 1),
    ("A", 3, 1), ("A", 7, 0), ("C", "afb", 1), ("W", "gox", 0), ("A", 15, 2), ("A", 14, 3), ("C", "qkv", 2),
    ("C", "afa", 2), ("A", 4, 1), ("A", 8, 0), ("C", "afb", 2), ("A", 3, 2), ("A", 15, 3), ("C", "qkv", 3),
    ("C", "afa", 3), ("A", 5, 1), ("A", 9, 0), ("C", "afb", 3), ("A", 4, 2), ("W", "att", 0), ("C", "out", 0),
    ("C", "ln2", 0), ("A", 6, 1), ("A", 10, 0), ("A", 5, 2), ("W", "n2", 0), ("C", "eo", 0), ("C", "eo", 1),
    ("A", 7, 1), ("A", 11, 0), ("A", 6, 2), ("C", "eo", 2), ("A", 8, 1), ("A", 7, 2), ("C", "eo", 3), ("W", "n2x", 0),
    ("A", 9, 1), ("W", "n2r", 0), ("C", "ex", 0), ("A", 8, 2), ("C", "ex", 1), ("C", "ex", 2), ("C", "ex", 3),
    ("A", 10, 1), ("C", "tra", 0), ("C", "gs", 0), ("C", "gs", 1), ("A", 9, 2), ("C", "gs", 2), ("A", 11, 1),
    ("I", 8, 0), ("I", 9, 0), ("I", 10, 0), ("C", "gs", 3), ("A", 10, 2), ("A", 11, 2), ("C", "hx", 0),
    ("C", "hx", 1), ("C", "hx", 2), ("C", "hx", 3), ("C", "bp0", 0), ("C", "bp1", 0), ("C", "hb", 0), ("R", 8, 0),
    ("I", 11, 0), ("C", "hb", 1), ("W", "b", 0), ("C", "tox", 0), ("C", "hb", 2), ("C", "hb", 3), ("C", "bp2", 0),
    ("C", "bp3", 0), ("R", 9, 0), ("C", "trn", 0), ("R", 8, 1), ("C", "gx", 0), ("I", 4, 0), ("C", "gx", 1),
    ("R", 10, 0), ("I", 5, 0), ("C", "br0", 0), ("C", "br1", 0), ("C", "gx", 2), ("R", 9, 1), ("C", "gx", 3),
    ("R", 11, 0), ("I", 6, 0), ("C", "trb", 0), ("W", "a", 0), ("W", "xb", 0), ("C", "ln2b", 0), ("R", 8, 2),
    ("R", 10, 1), ("W", "bm", 0), ("C", "tox2", 0), ("R", 9, 2), ("R", 4, 0), ("I", 7, 0), ("W", "gb", 0),
    ("C", "gat", 0), ("C", "gat", 1), ("R", 8, 3), ("C", "aba", 0), ("R", 9, 3), ("R", 10, 2), ("R", 11, 1),
    ("C", "abb", 0), ("R", 5, 0), ("C", "ga", 0), ("R", 10, 3), ("I", 12, 0), ("I", 0, 0), ("C", "aba", 1),
    ("R", 4, 1), ("C", "abb", 1), ("R", 6, 0), ("C", "ga", 1), ("I", 13, 0), ("I", 1, 0), ("C", "br2", 0),
    ("C", "br3", 0), ("R", 5, 1), ("C", "aba", 2), ("R", 11, 2), ("R", 7, 0), ("C", "abb", 2), ("C", "ga", 2),
    ("R", 11, 3), ("R", 6, 1), ("I", 14, 0), ("I", 2, 0), ("C", "aba", 3), ("R", 12, 0), ("R", 0, 0), ("C", "abb", 3),
    ("R", 4, 2), ("C", "ga", 3), ("R", 7, 1), ("I", 15, 0), ("R", 1, 0), ("I", 3, 0), ("R", 4, 3), ("W", "am", 0),
    ("C", "b1o", 0), ("C", "b1m", 0), ("R", 5, 2), ("R", 0, 1), ("R", 13, 0), ("R", 6, 2), ("R", 2, 0),
    ("W", "p1", 0), ("C", "ln1b", 0), ("R", 5, 3), ("R", 6, 3), ("C", "v0", 0), ("W", "xm", 0), ("C", "fin", 0),
    ("R", 12, 1), ("R", 1, 1), ("W", "v0", 0), ("C", "v1", 0), ("R", 14, 0), ("R", 7, 2), ("R", 3, 0), ("W", "v1", 0),
    ("C", "v2", 0), ("R", 7, 3), ("R", 2, 1), ("R", 13, 1), ("R", 15, 0), ("R", 12, 2), ("W", "v2", 0),
    ("C", "v3", 0), ("R", 0, 2), ("R", 14, 1), ("R", 0, 3), ("R", 15, 1), ("R", 3, 1), ("R", 13, 2), ("R", 14, 2),
    ("W", "v3", 0), ("C", "ov", 0), ("R", 15, 2), ("R", 1, 2), ("R", 2, 2), ("R", 12, 3), ("R", 1, 3), ("R", 3, 2),
    ("R", 2, 3), ("R", 13, 3), ("R", 12, 4), ("R", 14, 3), ("R", 15, 3), ("R", 3, 3), ("R", 13, 4), ("R", 14, 4),
    ("R", 15, 4),
)


def solution(mesh):
    split = P("dp", "seq", None)
    rows = P("dp", None)
    flat = P("dp")
    return jax.shard_map(
        body,
        mesh=mesh,
        in_specs=(split, split, rows, rows, rows, rows, flat) + (rows,) * 6 + (flat, flat),
        out_specs=(split, split) + (rows,) * 12 + (flat,) * 4,
        check_vma=False,
    )
```

```python
import functools

import jax
import jax.numpy as jnp
from jax import lax
from jax.experimental import pallas as pl
from jax.experimental.pallas import tpu as pltpu
from jax.sharding import PartitionSpec as P

HEAD_DIM = 64
STEP = 5
EPS_NORM = 1e-05
BETA_ONE = 0.5
BETA_TWO = 0.5
EPS_ADAM = 1e-08
RATE_MATRIX = 0.05
RATE_VECTOR = 0.2
DECAY_MATRIX = 0.1
SLOPE = 1.702

BF16 = jnp.bfloat16
F32 = jnp.float32
MESH = pl.DeviceIdType.MESH

UNIT = 512
BLOCKS = 4
EDGE = BLOCKS - 1
HALF = 2
UNITS = 8
ITEMS = 16
FIRST_EDGE = 12
PAIR = 128


def dot(a, b):
    return jnp.dot(a, b, preferred_element_type=F32)


def dot_rows(a, b):
    return lax.dot_general(a, b, (((0,), (0,)), ((), ())), preferred_element_type=F32)


def dot_cols(a, b):
    return lax.dot_general(a, b, (((1,), (1,)), ((), ())), preferred_element_type=F32)


def unit_rows(x):
    centred = x - jnp.mean(x, -1, keepdims=True)
    rstd = lax.rsqrt(jnp.mean(centred * centred, -1, keepdims=True) + EPS_NORM)
    return centred * rstd, rstd


def norm_back(grad_normed, unit, rstd, gain):
    g = grad_normed * gain
    return rstd * (g - jnp.mean(g, -1, keepdims=True) - unit * jnp.mean(g * unit, -1, keepdims=True))


def fold8(v):
    return jnp.sum(v.reshape(v.shape[0] // 8, 8, v.shape[1]), 0)


def layer_kernel(
    line, vec_len,
    tok, cot, kbias, p_vec, p_att, p_exp, p_shr,
    o_blk, o_tok, o_att, o_exp, o_shr, o_vec,
    w, w_oth, g, rx, ry, rz, ry_e, rz_e, s_own, s_oth, f_own, f_oth,
    vec_all, vec, bias_h, vg, vr, vz, hidden_sums,
    tok_own, cot_own,
    n1, go, qkv, att, lse, resid, n2, act, fac,
    own_p, keep_p, send_a, send_b, recv_a, recv_b, recv_m, x_recv_m,
    gb, tr, dk_acc, dv_acc,
    ag, rs, sib, wo, xe, vs, fill, loc,
):
    dp_n = 2 * line
    r = w.shape[4]
    block = tok.shape[1]
    own = 2 * block
    rows = 2 * own
    width = tok.shape[2]
    half = UNIT
    d = lax.axis_index("dp")
    s = lax.axis_index("seq")
    zi, yi = d // 2, d % 2
    x, c = s // 2, s % 2
    sibling = (d, x * 2 + 1 - c)
    x_neigh = (d, (1 - x) * 2 + c)
    y_neigh = (zi * 2 + 1 - yi, s)

    def z_peer(o):
        return (lax.rem(zi + o, line) * 2 + yi, s)

    def own_rows(core):
        return pl.ds(pl.multiple_of(core * own, own), own)

    def ff_rows(chip, core):
        return pl.ds(pl.multiple_of(chip * rows + core * own, own), own)

    my_rows = own_rows(c)
    my_half = pl.ds(pl.multiple_of(c * half, half), half)
    oth_half = pl.ds(pl.multiple_of((1 - c) * half, half), half)
    my_block = pl.ds(pl.multiple_of(x * block, block), block)
    oth_block = pl.ds(pl.multiple_of((1 - x) * block, block), block)

    mine, theirs = x * EDGE, (1 - x) * EDGE

    def blocks_of(i):
        if i < 4:
            return i, 1, HALF
        if i < FIRST_EDGE:
            return 4 + (i - 4) // 2, (i - 4) % 2 * HALF, HALF
        return i - FIRST_EDGE, mine, 1

    def item(ref, i):
        u, first, count = blocks_of(i)
        return ref.at[u, pl.ds(first, count)]

    def remote(src, dst, send, recv, to):
        return pltpu.make_async_remote_copy(
            src_ref=src, dst_ref=dst, send_sem=send, recv_sem=recv, device_id=to, device_id_type=MESH
        )

    def wait_bytes(ref, sem):
        pltpu.make_async_copy(ref, ref, sem).wait()

    wide = r % 128 == 0

    def unit_parts(u, place):
        if u < 4:
            core = place % 2
            return [
                (slice(None), pl.ds(pl.multiple_of(n * width + core * half + u * PAIR, PAIR), PAIR)) for n in range(BLOCKS)
            ]
        if u < 6:
            if not wide:
                return None
            parts = []
            for n in range((u - 4) * UNIT, (u - 3) * UNIT, PAIR):
                at = n // r * 4 * r + place * r + n % r
                parts.append((slice(None), pl.ds(pl.multiple_of(at, PAIR), PAIR)))
            return parts
        first = (u - 6) * UNIT
        held = pl.ds(pl.multiple_of(place * r, r), r)
        return [(held, slice(first + n * PAIR, first + (n + 1) * PAIR)) for n in range(BLOCKS)]

    def stage(u):
        n = u % 4 if u < 4 else u % 2
        hold = own_p if u < 4 else send_a if u < 6 else send_b
        return hold.at[(n // 2) * r : (n // 2 + 1) * r, (n % 2) * UNIT : (n % 2 + 1) * UNIT]

    def matrix(u, refs):
        return refs[0 if u < 4 else 1 if u < 6 else 2]

    for u in range(UNITS):
        parts = unit_parts(u, s)
        source = matrix(u, (p_att, p_exp, p_shr))
        for n in range(BLOCKS):
            part = source.at[parts[n]] if parts else source.at[u - 4, n]
            pltpu.make_async_copy(part, stage(u).at[:, n * PAIR : (n + 1) * PAIR], fill.at[u, n // HALF if u >= 4 else int(n in (0, EDGE))]).start()

    vec_all[d] = p_vec[...]
    tok_copy_in = pltpu.make_async_copy(tok.at[x], tok_own.at[my_block], loc.at[0])
    tok_copy_in.start()

    def go_rows(chip, place):
        return pl.ds(pl.multiple_of(chip * rows + place % 2 * own + place // 2 * block, block), block)

    go_local = [pltpu.make_async_copy(cot.at[n], go.at[go_rows(n, s)], loc.at[1]) for n in range(2)]
    for copy in go_local:
        copy.start()

    barrier = pltpu.get_barrier_semaphore()

    def greet(o, carry):
        pl.semaphore_signal(barrier, inc=1, device_id=(lax.rem(d + o, dp_n), s), device_id_type=MESH)
        return carry

    lax.fori_loop(1, dp_n, greet, 0)
    pl.semaphore_signal(barrier, inc=1, device_id=sibling, device_id_type=MESH)
    pl.semaphore_signal(barrier, inc=1, device_id=x_neigh, device_id_type=MESH)
    pl.semaphore_wait(barrier, dp_n + 1)

    def send_vec(o, carry):
        remote(p_vec, vec_all.at[d], vs.at[0, 0], vs.at[1, 0], (lax.rem(d + o, dp_n), s)).start()
        return carry

    lax.fori_loop(1, dp_n, send_vec, 0)
    tok_copy_x = remote(tok.at[1 - x], tok_own.at[my_block], xe.at[0, 0], xe.at[1, 0], x_neigh)
    tok_copy_x.start()
    other = (1 - x) * 2 + c
    go_copies = [
        [remote(cot.at[n], go.at[go_rows(n, s)], sib.at[0, 4], sib.at[1, 4], sibling) for n in range(2)],
        [remote(cot.at[n], go.at[go_rows(n, s)], xe.at[0, 4], xe.at[1, 4], x_neigh) for n in range(2)],
        [remote(go.at[go_rows(n, other)], go.at[go_rows(n, other)], sib.at[0, 5], sib.at[1, 5], sibling) for n in range(2)],
    ]
    go_bytes = go.at[:own]

    def ag_z(i):
        u, first, count = blocks_of(i)
        group = first // HALF if 4 <= i < FIRST_EDGE else int(i >= FIRST_EDGE)
        wait_bytes(stage(u).at[:, : HALF * PAIR], fill.at[u, group])
        for n in range(count):
            w[u, first + n, zi, yi] = stage(u)[:, pl.ds(pl.multiple_of((first + n) * PAIR, PAIR), PAIR)].astype(BF16)
        part = item(w, i).at[:, zi, yi]
        for o in range(1, line):
            remote(part, part, ag.at[0, i], ag.at[1, i], z_peer(o)).start()

    def ag_y_copy(i):
        part = item(w, i).at[:, :, yi]
        return remote(part, part, ag.at[2, i], ag.at[3, i], y_neigh)

    def ag_x_copy(i):
        return remote(item(w, i), item(w, i), ag.at[4, i], ag.at[5, i], x_neigh)

    def z_bytes(i):
        return item(w, i).at[:, pl.ds(0, line - 1), yi]

    def ag_y(i):
        wait_bytes(z_bytes(i), ag.at[1, i])
        ag_y_copy(i).start()

    def ag_x(i):
        ag_y_copy(i).wait_recv()
        if i >= FIRST_EDGE:
            ag_x_copy(i).start()

    def ag_end(i):
        ag_x_copy(i).wait_recv()

    gather_stages = [ag_z, ag_y, ag_x, ag_end]

    grain = 128 if vec_len % 128 == 0 else 64

    def vec_lanes(first):
        parts = []
        for e in range(first, first + 128, grain):
            o = e % vec_len
            parts.append(vec_all[e // vec_len, o // 128 : o // 128 + 1, o % 128 : o % 128 + grain])
        return parts[0] if len(parts) == 1 else jnp.concatenate(parts, 1)

    def hidden_bias(place):
        parts = []
        for shard in range(dp_n):
            n = shard * 4 * r + place * r
            parts.append(vec[8 + n // width : 9 + n // width, n % width : n % width + r])
        return jnp.concatenate(parts, 1)

    def vector():
        for row in range(12):
            for lane in range(0, width, 128):
                vec[row : row + 1, lane : lane + 128] = vec_lanes(row * width + lane)
        low_half = jnp.where(s == 0, hidden_bias(0), hidden_bias(1))
        bias_h[...] = jnp.where(s < 2, low_half, jnp.where(s == 2, hidden_bias(2), hidden_bias(3)))

    def live(to):
        return jnp.where(kbias[to, 0:1] < 0, 0.0, 1.0)

    chunk = block // 2

    def chunks(first, i):
        return pl.ds(pl.multiple_of(first + i * chunk, chunk), chunk)

    def first_norm():
        def some(i, carry):
            unit, _ = unit_rows(tok_own[chunks(0, i), :].astype(F32))
            n1[chunks(c * own, i), :] = (unit * vec[0:1, :] + vec[1:2, :]).astype(BF16)
            return carry

        lax.fori_loop(0, own // chunk, some, 0)
        n1_copy.start()

    def grad_output():
        for copy in go_copies[1] + go_copies[0]:
            copy.start()

    def rows_copies(ref, n):
        here, there = ref.at[ff_rows(x, c)], ref.at[ff_rows(1 - x, c)]
        return (
            remote(here, here, sib.at[0, n], sib.at[1, n], sibling),
            remote(here, here, xe.at[0, n], xe.at[1, n], x_neigh),
            remote(there, there, sib.at[0, n + 1], sib.at[1, n + 1], sibling),
        )

    n1_copy = remote(n1.at[my_rows], n1.at[my_rows], sib.at[0, 0], sib.at[1, 0], sibling)
    att_copy = remote(att.at[:, my_half], att.at[:, my_half], sib.at[0, 1], sib.at[1, 1], sibling)
    gb_copy = remote(gb.at[my_rows], gb.at[my_rows], sib.at[0, 2], sib.at[1, 2], sibling)
    p1_copy = remote(send_a, recv_a, sib.at[0, 3], sib.at[1, 3], sibling)
    n2_copies = rows_copies(n2, 6)
    b_copy = remote(send_b, recv_b, sib.at[0, 8], sib.at[1, 8], sibling)
    a_copy = remote(send_a, recv_a, sib.at[0, 9], sib.at[1, 9], sibling)
    bm_copy = remote(send_b, recv_m, sib.at[0, 10], sib.at[1, 10], sibling)
    am_copy = remote(send_a, recv_b, sib.at[0, 11], sib.at[1, 11], sibling)
    x_back = [
        remote(cot_own.at[pl.ds(n * block, block)], o_blk.at[n], xe.at[0, 7 + n], xe.at[1, 7 + n], x_neigh) for n in range(2)
    ]
    xm_copy = remote(cot_own, x_recv_m, xe.at[0, 9], xe.at[1, 9], x_neigh)
    tok_copy = remote(tok_own.at[oth_block], o_tok.at[x], xe.at[0, 3], xe.at[1, 3], x_neigh)
    blk_copy = remote(cot_own.at[oth_block], o_blk.at[x], xe.at[0, 2], xe.at[1, 2], x_neigh)

    low_lane = lax.broadcasted_iota(jnp.int32, (PAIR, PAIR), 1) < HEAD_DIM
    low_row = lax.broadcasted_iota(jnp.int32, (PAIR, PAIR), 0) < HEAD_DIM
    q_chunks = rows // PAIR

    def two_heads(v):
        zero = jnp.zeros_like(v)
        return jnp.concatenate([jnp.where(low_lane, v, zero), jnp.where(low_lane, zero, v)], 0)

    qkv_lanes = 3 * PAIR

    def pair_lanes(p):
        return tuple(slice(p * qkv_lanes + n * PAIR, p * qkv_lanes + (n + 1) * PAIR) for n in range(3))

    def att_lanes(p):
        return pl.ds(pl.multiple_of(c * half + p * PAIR, PAIR), PAIR)

    def wo_copy(p):
        return remote(w.at[p, BLOCKS - 1], w_oth.at[p], wo.at[0, p], wo.at[1, p], sibling)

    def columns(blocks):
        return jnp.concatenate([v.reshape(-1, PAIR) for v in blocks], 1)

    def project(p):
        wo_copy(p).start()
        q_at, k_at, v_at = pair_lanes(p)
        out = dot(n1[...], columns([w[p, n] for n in range(3)]))
        queries = (out[:, :PAIR] + vec[4:5, att_lanes(p)]).astype(BF16)
        qkv[:, q_at] = queries * jnp.asarray(HEAD_DIM**-0.5, BF16)
        qkv[:, k_at] = out[:, PAIR : 2 * PAIR].astype(BF16)
        qkv[:, v_at] = (out[:, 2 * PAIR :] + vec[5:6, att_lanes(p)]).astype(BF16)

    def attend_forward(p, first, last):
        q_at, k_at, v_at = pair_lanes(p)

        def some(j, carry):
            at = pl.ds(pl.multiple_of(j * PAIR, PAIR), PAIR)
            mask = kbias[...]
            scores = dot_cols(qkv[:, k_at], two_heads(qkv[at, q_at])) + jnp.concatenate([mask, mask], 1)
            highest = jnp.max(scores, 0, keepdims=True)
            raised = jnp.exp(scores - highest)
            total = jnp.sum(raised, 0, keepdims=True)
            out = dot_rows(qkv[:, v_at], raised.astype(BF16)) / total
            out = jnp.where(low_row, out[:, :PAIR], out[:, PAIR:])
            att[at, att_lanes(p)] = out.T.astype(BF16)
            lse[pl.ds(p * q_chunks + j, 1), :] = highest + jnp.log(total)
            return carry

        lax.fori_loop(first, last, some, 0)
        if p == 3 and last == q_chunks:
            att_copy.start()

    def own_out(z):
        return columns([w[p, BLOCKS - 1, z] for p in range(4)])

    def oth_out(z):
        return columns([w_oth[p, z] for p in range(4)])

    def output_projection():
        mixed = att[my_rows, :]
        resid[:, my_half] = dot(mixed, own_out(slice(None)))
        resid[:, oth_half] = dot(mixed, oth_out(slice(None)))

    def second_norm():
        def some(i, carry):
            at = chunks(0, i)
            res = resid[at, :] + tok_own[at, :].astype(F32) + vec[6:7, :]
            resid[at, :] = res
            unit, _ = unit_rows(res)
            n2[chunks(x * rows + c * own, i), :] = (unit * vec[2:3, :] + vec[3:4, :]).astype(BF16)
            return carry

        lax.fori_loop(0, own // chunk, some, 0)
        n2_copies[1].start()
        n2_copies[0].start()

    tile = HALF * PAIR

    def expand(n, chip):
        u, first, _ = blocks_of(4 + n)
        at = pl.ds(pl.multiple_of(chip * rows, rows), rows)
        to = slice(n * tile, (n + 1) * tile)
        hidden = dot(n2[at, :], columns([w[u, first], w[u, first + 1]])) + bias_h[:, to]
        gate = jax.nn.sigmoid(SLOPE * hidden)
        act[at, to] = (hidden * gate).astype(BF16)
        fac[at, to] = (gate + SLOPE * hidden * gate * (1.0 - gate)).astype(BF16)

    def rs_x_copy(i):
        u = i - FIRST_EDGE
        return remote(g.at[u, theirs], rx.at[u], rs.at[0, i], rs.at[1, i], x_neigh)

    def y_place(i):
        return ry.at[i] if i < FIRST_EDGE else ry_e.at[i - FIRST_EDGE]

    def z_place(i):
        return rz.at[i] if i < FIRST_EDGE else rz_e.at[i - FIRST_EDGE]

    def rs_y_copy(i):
        return remote(item(g, i).at[:, :, 1 - yi], y_place(i), rs.at[2, i], rs.at[3, i], y_neigh)

    def done_blocks(i):
        u, first, count = blocks_of(i)
        return f_own.at[u, pl.ds(first, count)]

    def rs_2_copy(i):
        if i < 4:
            return remote(s_own.at[i], s_oth.at[i], rs.at[6, i], rs.at[7, i], x_neigh)
        to = f_oth.at[i - 4] if i < FIRST_EDGE else f_own.at[i - FIRST_EDGE, pl.ds(mine, 1)]
        return remote(done_blocks(i), to, rs.at[6, i], rs.at[7, i], x_neigh)

    def to_result(u, n, place):
        result = matrix(u, (o_att, o_exp, o_shr))
        if u < 4:
            first = n * width + place % 2 * half + u * PAIR
            return result.at[:, pl.ds(pl.multiple_of(first, PAIR), PAIR)]
        parts = unit_parts(u, place)
        return result.at[parts[n]] if parts else result.at[u - 4, place, n]

    def rs_share(i, source, first, count, place, sems):
        u = blocks_of(i)[0]
        for n in range(count):
            to = to_result(u, first + n, place)
            remote(source.at[n], to, rs.at[sems, i], rs.at[sems + 1, i], sibling).start()
            pltpu.make_async_copy(source.at[n], to, rs.at[sems + 2, i]).start()

    def rs_x_add(i):
        rs_x_copy(i).wait_recv()
        u = i - FIRST_EDGE

        def add(z, carry):
            g[u, mine, z] = (g[u, mine, z].astype(F32) + rx[u, z].astype(F32)).astype(BF16)
            return carry

        lax.fori_loop(0, line, add, 0)
        rs_y_copy(i).start()

    def rs_y_add(i):
        rs_y_copy(i).wait_recv()
        u, first, count = blocks_of(i)
        got = y_place(i)

        def add(z, carry):
            for n in range(count):
                g[u, first + n, z, yi] = (g[u, first + n, z, yi].astype(F32) + got[n, z].astype(F32)).astype(BF16)
            return carry

        lax.fori_loop(0, line, add, 0)
        for o in range(1, line):
            z = lax.rem(zi + o, line)
            remote(item(g, i).at[:, z, yi], z_place(i).at[o - 1], rs.at[4, i], rs.at[5, i], z_peer(o)).start()

    def rs_z_add(i):
        u, first, count = blocks_of(i)
        got = z_place(i)
        wait_bytes(got, rs.at[5, i])
        for n in range(count):
            total = g[u, first + n, zi, yi].astype(F32)
            for o in range(1, line):
                total = total + got[o - 1, n].astype(F32)
            if i < 4:
                s_own[i, n] = total.astype(BF16)
            else:
                f_own[u, first + n] = total.astype(BF16)
        rs_2_copy(i).start()
        if i >= 4:
            rs_share(i, done_blocks(i), first, count, s, 8)

    def rs_join(i):
        rs_2_copy(i).wait_recv()
        u, first, count = blocks_of(i)
        if i < 4:
            for n in range(count):
                f_own[u, first + n] = (s_own[i, n].astype(F32) + s_oth[i, n].astype(F32)).astype(BF16)
            rs_share(i, done_blocks(i), first, count, s, 8)
        elif i < FIRST_EDGE:
            rs_share(i, f_oth.at[i - 4], first, count, other, 11)
        else:
            rs_share(i, f_own.at[u, pl.ds(theirs, 1)], theirs, count, other, 11)

    def rs_end(i):
        if i >= FIRST_EDGE:
            rs_x_copy(i).wait_send()
        rs_y_copy(i).wait_send()
        wait_bytes(z_place(i), rs.at[4, i])
        rs_2_copy(i).wait_send()
        for n in range(8, 11 if i < 4 else 14):
            wait_bytes(done_blocks(i), rs.at[n, i])

    def put(u, first, value):
        for n in range(value.shape[1] // PAIR):
            part = value[:, n * PAIR : (n + 1) * PAIR].astype(BF16)
            g[u, first + n] = part.reshape(line, 2, r, PAIR)

    def rs_start(i):
        (rs_y_copy(i) if i < FIRST_EDGE else rs_x_copy(i)).start()

    def rs_stage(i, k):
        stages = [rs_x_add, rs_y_add, rs_z_add, rs_join, rs_end]
        (stages[1:] if i < FIRST_EDGE else stages)[k](i)

    def transpose_into(first, src, size):
        def move(i, carry):
            at = pl.ds(pl.multiple_of(i * 128, 128), 128)
            tr[at, first : first + size] = src[:, at].T
            return carry

        lax.fori_loop(0, width // 128, move, 0)

    def shrink_grad(n):
        u, first, _ = blocks_of(8 + n)
        put(u, first, dot(tr[...], go[:, n * tile : (n + 1) * tile]))

    span = max(1, tile // (2 * r))
    part_rows = span * 2 * r

    def hidden_back(n, chip, clear):
        at = pl.ds(pl.multiple_of(chip * rows, rows), rows)
        if clear:
            hidden_sums[...] = jnp.zeros_like(hidden_sums)

        def some(m, carry):
            to = pl.ds(pl.multiple_of(m * part_rows, part_rows), part_rows)
            total = None
            for j in range(2):
                part = columns([w[6 + j, b, pl.ds(m * span, span)] for b in range(BLOCKS)])
                term = dot_cols(go[at, j * UNIT : (j + 1) * UNIT], part)
                total = term if total is None else total + term
            low = (total * fac[at, to].astype(F32)).astype(BF16)
            fac[at, to] = low
            hidden_sums[:, to] += fold8(low.astype(F32))
            return carry

        count = line // span // 4
        lax.fori_loop(n * count, (n + 1) * count, some, 0)

    def back_partial(src, rows_at, units, blocks, dst):
        lanes = blocks * PAIR

        def back(n, carry):
            total = None
            for k, u in enumerate(units):
                part = columns([w[u, b, pl.ds(n * span, span)] for b in range(blocks)])
                term = dot_cols(src[rows_at, k * lanes : (k + 1) * lanes], part)
                total = term if total is None else total + term
            dst[:, pl.ds(pl.multiple_of(n * part_rows, part_rows), part_rows)] = total
            return carry

        lax.fori_loop(0, line // span, back, 0)

    def expand_grad(n):
        u, first, _ = blocks_of(4 + n)
        put(u, first, dot(tr[...], fac[:, n * tile : (n + 1) * tile]))

    def to_x(came):
        def some(i, carry):
            at = chunks(0, i)
            cot_own[at, :] = (keep_p[at, :] + came[at, :]).astype(BF16)
            return carry

        lax.fori_loop(0, own // chunk, some, 0)

    ff = (4, 5)

    def hidden_partial(n):
        at = ff_rows(*((1 - x, 1 - c), (1 - x, c), (x, 1 - c), (x, c))[n])
        back_partial(fac, at, ff, BLOCKS, (send_b, keep_p, send_a, own_p)[n])
        if n == 0:
            b_copy.start()
        if n == 2:
            a_copy.start()

    def partial_over_x():
        to_x(recv_b)
        for copy in x_back:
            copy.start()

    zeros8 = jnp.zeros((8, width), F32)

    def second_norm_back():
        def some(i, carry):
            at = chunks(0, i)
            unit, rstd = unit_rows(resid[at, :])
            came = o_blk[i // 2, pl.ds(pl.multiple_of(i % 2 * chunk, chunk), chunk)].astype(F32)
            gn = own_p[at, :] + recv_a[at, :] + came
            grad_out = go[chunks(x * rows + c * own, i), :].astype(F32)
            gr = grad_out + norm_back(gn, unit, rstd, vec[2:3, :])
            own_p[at, :] = gr
            low = gr.astype(BF16)
            gb[chunks(c * own, i), :] = low
            a, b, e, f = carry
            return (a + fold8(gn * unit), b + fold8(gn), e + fold8(low.astype(F32)), f + fold8(grad_out))

        vg[...] = jnp.zeros_like(vg)
        vg[pl.ds(8 + s, 1), :] = jnp.sum(hidden_sums[...], 0, keepdims=True)
        sums = lax.fori_loop(0, own // chunk, some, (zeros8,) * 4)
        for row, v in zip((2, 3, 6, 7), sums):
            vg[row : row + 1, :] = jnp.sum(v, 0, keepdims=True)
        gb_copy.start()

    def grad_attended(n):
        if n == 0:
            for copy in n2_copies:
                copy.wait_send()
        quarter = line // 4
        head_rows = pl.ds(c * (line // 2) + n * quarter, quarter)
        part = dot_cols(gb[:, my_half], own_out(head_rows)) + dot_cols(gb[:, oth_half], oth_out(head_rows))
        n2[:rows, n * tile : (n + 1) * tile] = part.astype(BF16)

    def attend_backward(p, first, last):
        q_at, k_at, v_at = pair_lanes(p)
        own_lanes = slice(p * PAIR, (p + 1) * PAIR)
        if first == 0:
            dk_acc[...] = jnp.zeros_like(dk_acc)
            dv_acc[...] = jnp.zeros_like(dv_acc)

        def some(j, carry):
            at = pl.ds(pl.multiple_of(j * PAIR, PAIR), PAIR)
            both = two_heads(qkv[at, q_at])
            grads = two_heads(n2[at, own_lanes])
            mask = kbias[...]
            scores = dot_cols(qkv[:, k_at], both) + jnp.concatenate([mask, mask], 1)
            chance = jnp.exp(scores - lse[pl.ds(p * q_chunks + j, 1), :])
            dv_acc[...] += dot(chance.astype(BF16), grads)
            grad_chance = dot_cols(qkv[:, v_at], grads)
            inner = jnp.sum(chance * grad_chance, 0, keepdims=True)
            grad_scores = (chance * (grad_chance - inner)).astype(BF16)
            dk_acc[...] += dot(grad_scores, both)
            out = dot_rows(qkv[:, k_at], grad_scores)
            out = jnp.where(low_row, out[:, :PAIR], out[:, PAIR:]) * HEAD_DIM**-0.5
            qkv[at, q_at] = out.T.astype(BF16)
            return carry

        lax.fori_loop(first, last, some, 0)
        if last < q_chunks:
            return
        qkv[:, k_at] = dk_acc[...].astype(BF16)
        qkv[:, v_at] = dv_acc[...].astype(BF16)
        vg[4:5, att_lanes(p)] = jnp.sum(fold8(qkv[:, q_at].astype(F32)), 0, keepdims=True)
        vg[5:6, att_lanes(p)] = jnp.sum(fold8(qkv[:, v_at].astype(F32)), 0, keepdims=True)

    def attention_grad(p):
        put(p, 0, dot(tr[:, :rows], qkv[:, p * qkv_lanes : (p + 1) * qkv_lanes]))
        put(p, BLOCKS - 1, dot(tr[:, rows:], gb[:, att_lanes(p)]))

    def input_partial(n):
        back_partial(qkv, own_rows(c if n else 1 - c), (0, 1, 2, 3), 3, keep_p if n else send_a)
        if n == 0:
            p1_copy.start()

    def first_norm_back():
        def some(i, carry):
            at = chunks(0, i)
            unit, rstd = unit_rows(tok_own[at, :].astype(F32))
            gn = keep_p[at, :] + recv_a[at, :]
            out = own_p[at, :] + norm_back(gn, unit, rstd, vec[0:1, :])
            tok_own[at, :] = out.astype(BF16)
            a, b = carry
            return (a + fold8(gn * unit), b + fold8(gn))

        sums = lax.fori_loop(0, own // chunk, some, (zeros8,) * 2)
        for row, v in zip((0, 1), sums):
            vg[row : row + 1, :] = jnp.sum(v, 0, keepdims=True)
        o_tok[x] = tok_own[my_block, :]
        tok_copy.start()

    def branch(dst, rows_at, add):
        def out(n, carry):
            for j in range(2):
                part = columns([w[6 + j, 2 * n], w[6 + j, 2 * n + 1]])
                to = pl.ds(pl.multiple_of(j * UNIT + n * tile, tile), tile)
                total = dot(act[rows_at, :], part)
                dst[:, to] = dst[:, to] + total if add else total
            return carry

        lax.fori_loop(0, UNIT // tile, out, 0)

    def output_partial(n):
        at = ff_rows(*((1 - x, 1 - c), (1 - x, c), (x, 1 - c), (x, c))[n])
        branch((send_b, keep_p, send_a, resid)[n], at, n == 3)
        if n == 0:
            bm_copy.start()
        if n == 2:
            am_copy.start()

    def output_over_x():
        to_x(recv_m)
        xm_copy.start()

    def finish_block():
        def some(i, carry):
            at = chunks(0, i)
            out = resid[at, :] + recv_b[at, :] + x_recv_m[at, :].astype(F32) + vec[7:8, :]
            cot_own[at, :] = (live(chunks(c * own, i)) * out).astype(BF16)
            return carry

        lax.fori_loop(0, own // chunk, some, 0)
        o_blk[x] = cot_own[my_block, :]
        blk_copy.start()

    v_copies = [
        remote(vg, vr.at[n], vs.at[0, 1 + n], vs.at[1, 1 + n], to) for n, to in enumerate((sibling, x_neigh, y_neigh))
    ]

    def vector_hop(n):
        if n < 3:
            v_copies[n].start()
            return

        def send(o, carry):
            remote(vg, vz.at[zi], vs.at[0, 4], vs.at[1, 4], (lax.rem(zi + o, line) * 2 + yi, s)).start()
            return carry

        lax.fori_loop(1, line, send, 0)
        vz[zi] = vg[...]

    def vector_add(n):
        if n < 3:
            v_copies[n].wait()
            vg[...] += vr[n]
            return
        wait_bytes(vz.at[pl.ds(0, line - 1)], vs.at[1, 4])
        wait_bytes(vz.at[pl.ds(0, line - 1)], vs.at[0, 4])

    def vector_out():
        o_vec[...] = lax.fori_loop(1, line, lambda i, t: t + vz[i], vz[0])

    def both(*copies):
        for copy in copies:
            copy.wait()

    def received(*copies):
        for copy in copies:
            copy.wait_recv()

    def relay(copies):
        copies[1].wait_recv()
        copies[2].start()

    def relay_go():
        wait_bytes(go_bytes, xe.at[1, 4])
        for copy in go_copies[2]:
            copy.start()

    def all_rows():
        received(n2_copies[2])
        wait_bytes(go_bytes, loc.at[1])
        wait_bytes(go_bytes, sib.at[1, 4])
        wait_bytes(go_bytes, sib.at[1, 5])

    waits = dict(
        vec=lambda: wait_bytes(vec_all.at[pl.ds(0, dp_n - 1)], vs.at[1, 0]),
        tok=lambda: both(tok_copy_x, tok_copy_in),
        cot=lambda: None,
        n1=lambda: received(n1_copy),
        gox=relay_go,
        att=lambda: received(*[wo_copy(p) for p in range(4)], att_copy),
        n2=lambda: received(n2_copies[0]),
        n2x=lambda: relay(n2_copies),
        n2r=all_rows,
        b=lambda: both(b_copy),
        a=lambda: both(a_copy),
        xb=lambda: both(*x_back),
        gb=lambda: received(gb_copy),
        p1=lambda: both(p1_copy),
        bm=lambda: both(bm_copy),
        am=lambda: both(am_copy),
        xm=lambda: both(xm_copy),
        v0=lambda: vector_add(0),
        v1=lambda: vector_add(1),
        v2=lambda: vector_add(2),
        v3=lambda: vector_add(3),
    )
    split = 3
    work = dict(
        vec=lambda n: vector(),
        ln1=lambda n: first_norm(),
        go=lambda n: grad_output(),
        qkv=project,
        afa=lambda p: attend_forward(p, 0, split),
        afb=lambda p: attend_forward(p, split, q_chunks),
        out=lambda n: output_projection(),
        ln2=lambda n: second_norm(),
        eo=lambda n: expand(n, x),
        ex=lambda n: expand(n, 1 - x),
        tra=lambda n: transpose_into(0, act, 2 * rows),
        gs=shrink_grad,
        hx=lambda n: hidden_back(n, 1 - x, n == 0),
        hb=lambda n: hidden_back(n, x, False),
        bp0=lambda n: hidden_partial(0),
        bp1=lambda n: hidden_partial(1),
        tox=lambda n: partial_over_x(),
        bp2=lambda n: hidden_partial(2),
        bp3=lambda n: hidden_partial(3),
        trn=lambda n: transpose_into(0, n2, 2 * rows),
        gx=expand_grad,
        ln2b=lambda n: second_norm_back(),
        trb=lambda n: (transpose_into(0, n1, rows), transpose_into(rows, att, rows)),
        gat=grad_attended,
        aba=lambda p: attend_backward(p, 0, split),
        abb=lambda p: attend_backward(p, split, q_chunks),
        ga=attention_grad,
        b1o=lambda n: input_partial(0),
        b1m=lambda n: input_partial(1),
        ln1b=lambda n: first_norm_back(),
        br0=lambda n: output_partial(0),
        br1=lambda n: output_partial(1),
        tox2=lambda n: output_over_x(),
        br2=lambda n: output_partial(2),
        br3=lambda n: output_partial(3),
        v0=lambda n: vector_hop(0),
        v1=lambda n: vector_hop(1),
        v2=lambda n: vector_hop(2),
        v3=lambda n: vector_hop(3),
        fin=lambda n: finish_block(),
        ov=lambda n: vector_out(),
    )
    for kind, name, n in ORDER:
        if kind == "C":
            work[name](n)
        elif kind == "W":
            waits[name]()
        elif kind == "A":
            gather_stages[n](name)
        elif kind == "I":
            rs_start(name)
        else:
            rs_stage(name, n)

    blk_copy.wait()
    tok_copy.wait()
    wait_bytes(vec_all.at[pl.ds(0, dp_n - 1)], vs.at[0, 0])
    for sem in (sib.at[0, 4], sib.at[0, 5], xe.at[0, 4]):
        wait_bytes(go_bytes, sem)
    for copy in [n1_copy, att_copy, gb_copy] + [wo_copy(p) for p in range(4)]:
        copy.wait_send()
    for i in range(ITEMS):
        wait_bytes(z_bytes(i), ag.at[0, i])
        ag_y_copy(i).wait_send()
        if i >= FIRST_EDGE:
            ag_x_copy(i).wait_send()


def adamw(grad, moment, square, weight, rate, decay):
    momentum = BETA_ONE * moment + (1.0 - BETA_ONE) * grad
    variance = BETA_TWO * square + (1.0 - BETA_TWO) * grad * grad
    first_fix = 1.0 - BETA_ONE**STEP
    second_fix = 1.0 - BETA_TWO**STEP
    direction = momentum / first_fix / (jnp.sqrt(variance / second_fix) + EPS_ADAM)
    updated = weight - rate * (direction + decay * weight)
    return (momentum, variance, updated, updated.astype(BF16))


def body(
    tokens, cotangent, key_mask,
    attention_weights, expand_weights, shrink_weights, vector_params,
    attention_moment, attention_square, expand_moment, expand_square,
    shrink_moment, shrink_square, vector_moment, vector_square,
):
    dp_n = lax.axis_size("dp")
    line = dp_n // 2
    d = lax.axis_index("dp")
    place = lax.axis_index("seq")
    x, c = place // 2, place % 2
    _, local_len, width = tokens.shape
    r = width // dp_n
    block = -(-local_len // 16) * 16
    own, rows = 2 * block, 4 * block
    pad = ((0, 0), (0, block - local_len), (0, 0))

    keep = lax.dynamic_index_in_dim(key_mask, x, 0, keepdims=False).reshape(2, 2, local_len)
    keep = jnp.pad(keep.transpose(1, 0, 2), ((0, 0), (0, 0), pad[1])).reshape(2, own)
    kbias = jnp.broadcast_to(jnp.where(keep > 0, 0.0, -1e30).astype(F32).reshape(rows, 1), (rows, PAIR))
    p_exp = expand_weights
    if r % 128:
        p_exp = lax.dynamic_index_in_dim(expand_weights.reshape(r, dp_n, 4, r), place, 2, keepdims=False)
        p_exp = p_exp.reshape(r, 2, BLOCKS, PAIR).transpose(1, 2, 0, 3)
    vec_len = vector_params.shape[0]
    here = lax.dynamic_slice_in_dim(key_mask, place * local_len, local_len, 1)
    grad_out = jnp.where(here[:, :, None] > 0, cotangent, jnp.zeros_like(cotangent))
    vec_rows = -(-vec_len // 1024) * 8
    p_vec = jnp.pad(vector_params.astype(BF16).astype(F32), (0, vec_rows * 128 - vec_len)).reshape(vec_rows, 128)

    vmem = pl.BlockSpec(memory_space=pltpu.VMEM)
    hbm = pl.BlockSpec(memory_space=pl.ANY)
    padded = jax.ShapeDtypeStruct((2, block, width), BF16)
    o_blk, o_tok, o_att, o_exp, o_shr, o_vec = pl.pallas_call(
        functools.partial(layer_kernel, line, vec_len),
        out_shape=(
            padded,
            padded,
            jax.ShapeDtypeStruct((r, 4 * width), BF16),
            jax.ShapeDtypeStruct((2, 4, BLOCKS, r, PAIR) if r % 128 else (r, 4 * width), BF16),
            jax.ShapeDtypeStruct((4 * r, width), BF16),
            jax.ShapeDtypeStruct((16, width), F32),
        ),
        in_specs=[hbm, hbm, vmem, vmem, hbm, hbm, hbm],
        out_specs=(vmem, vmem, hbm, hbm, hbm, vmem),
        scratch_shapes=[
            pltpu.VMEM((UNITS, BLOCKS, line, 2, r, PAIR), BF16),
            pltpu.VMEM((4, line, 2, r, PAIR), BF16),
            pltpu.VMEM((UNITS, BLOCKS, line, 2, r, PAIR), BF16),
            pltpu.VMEM((4, line, 2, r, PAIR), BF16),
            pltpu.VMEM((FIRST_EDGE, HALF, line, r, PAIR), BF16),
            pltpu.VMEM((FIRST_EDGE, line - 1, HALF, r, PAIR), BF16),
            pltpu.VMEM((4, 1, line, r, PAIR), BF16),
            pltpu.VMEM((4, line - 1, 1, r, PAIR), BF16),
            pltpu.VMEM((4, HALF, r, PAIR), BF16),
            pltpu.VMEM((4, HALF, r, PAIR), BF16),
            pltpu.VMEM((UNITS, BLOCKS, r, PAIR), BF16),
            pltpu.VMEM((8, HALF, r, PAIR), BF16),
            pltpu.VMEM((dp_n, vec_rows, 128), F32),
            pltpu.VMEM((16, width), F32),
            pltpu.VMEM((1, width), F32),
            pltpu.VMEM((16, width), F32),
            pltpu.VMEM((3, 16, width), F32),
            pltpu.VMEM((line, 16, width), F32),
            pltpu.VMEM((8, width), F32),
            pltpu.VMEM((own, width), BF16),
            pltpu.VMEM((own, width), BF16),
            pltpu.VMEM((rows, width), BF16),
            pltpu.VMEM((2 * rows, width), BF16),
            pltpu.VMEM((rows, 3 * UNIT), BF16),
            pltpu.VMEM((rows, width), BF16),
            pltpu.VMEM(((rows // PAIR) * (UNIT // PAIR), 2 * PAIR), F32),
            pltpu.VMEM((own, width), F32),
            pltpu.VMEM((2 * rows, width), BF16),
            pltpu.VMEM((2 * rows, width), BF16),
            pltpu.VMEM((2 * rows, width), BF16),
        ]
        + [pltpu.VMEM((own, width), F32)] * 7
        + [
            pltpu.VMEM((own, width), BF16),
            pltpu.VMEM((rows, width), BF16),
            pltpu.VMEM((width, 2 * rows), BF16),
            pltpu.VMEM((rows, PAIR), F32),
            pltpu.VMEM((rows, PAIR), F32),
            pltpu.SemaphoreType.DMA((6, ITEMS)),
            pltpu.SemaphoreType.DMA((14, ITEMS)),
            pltpu.SemaphoreType.DMA((2, 12)),
            pltpu.SemaphoreType.DMA((2, 4)),
            pltpu.SemaphoreType.DMA((2, 10)),
            pltpu.SemaphoreType.DMA((2, 5)),
            pltpu.SemaphoreType.DMA((UNITS, 2)),
            pltpu.SemaphoreType.DMA((2,)),
        ],
        compiler_params=pltpu.CompilerParams(
            collective_id=0, has_side_effects=True, vmem_limit_bytes=VMEM_LIMIT
        ),
        name="layer",
    )(jnp.pad(tokens, pad), jnp.pad(grad_out, pad), kbias, p_vec, attention_weights, p_exp, shrink_weights)

    block_output = o_blk[:, :local_len]
    token_gradient = o_tok[:, :local_len]
    grad_attention, grad_shrink = o_att.astype(F32), o_shr.astype(F32)
    if r % 128:
        o_exp = o_exp.transpose(3, 1, 0, 2, 4).reshape(r, 4, dp_n, r).transpose(0, 2, 1, 3).reshape(r, 4 * width)
    grad_expand = o_exp.astype(F32)
    hidden_sums = o_vec[8:12].reshape(4, dp_n, r).transpose(1, 0, 2).reshape(4, width)
    grad_vector = jnp.concatenate([o_vec[0:8], hidden_sums], 0).reshape(dp_n, vec_len)
    grad_vector = lax.dynamic_index_in_dim(grad_vector, d, 0, keepdims=False)

    attention_out = adamw(
        grad_attention, attention_moment, attention_square, attention_weights, RATE_MATRIX, DECAY_MATRIX
    )
    expand_out = adamw(grad_expand, expand_moment, expand_square, expand_weights, RATE_MATRIX, DECAY_MATRIX)
    shrink_out = adamw(grad_shrink, shrink_moment, shrink_square, shrink_weights, RATE_MATRIX, DECAY_MATRIX)
    vector_out = adamw(grad_vector, vector_moment, vector_square, vector_params, RATE_VECTOR, 0.0)
    return (block_output, token_gradient, *attention_out, *expand_out, *shrink_out, *vector_out)


VMEM_LIMIT = 63 * 2**20

ORDER = (
    ("A", 12, 0), ("W", "cot", 0), ("C", "go", 0), ("W", "vec", 0), ("C", "vec", 0), ("A", 0, 0), ("A", 12, 1),
    ("A", 13, 0), ("A", 0, 1), ("A", 1, 0), ("W", "tok", 0), ("C", "ln1", 0), ("A", 13, 1), ("A", 14, 0),
    ("W", "n1", 0), ("A", 0, 2), ("A", 1, 1), ("A", 2, 0), ("A", 12, 2), ("A", 14, 1), ("A", 15, 0), ("A", 13, 2),
    ("A", 1, 2), ("A", 2, 1), ("A", 12, 3), ("C", "qkv", 0), ("A", 3, 0), ("C", "afa", 0), ("C", "afb", 0),
    ("A", 14, 2), ("A", 15, 1), ("A", 13, 3), ("C", "qkv", 1), ("C", "afa", 1), ("A", 2, 2), ("A", 4, 0),
    ("C", "afb", 1), ("A", 3, 1), ("W", "gox", 0), ("A", 15, 2), ("A", 14, 3), ("C", "qkv", 2), ("C", "afa", 2),
    ("A", 5, 0), ("C", "afb", 2), ("A", 4, 1), ("A", 3, 2), ("A", 15, 3), ("C", "qkv", 3), ("C", "afa", 3),
    ("A", 6, 0), ("C", "afb", 3), ("A", 5, 1), ("A", 4, 2), ("W", "att", 0), ("C", "out", 0), ("A", 7, 0),
    ("C", "ln2", 0), ("A", 6, 1), ("A", 5, 2), ("A", 8, 0), ("W", "n2", 0), ("C", "eo", 0), ("C", "eo", 1),
    ("A", 7, 1), ("A", 6, 2), ("C", "eo", 2), ("A", 9, 0), ("A", 8, 1), ("A", 7, 2), ("C", "eo", 3), ("A", 10, 0),
    ("W", "n2x", 0), ("A", 9, 1), ("W", "n2r", 0), ("C", "ex", 0), ("A", 8, 2), ("C", "ex", 1), ("A", 11, 0),
    ("C", "ex", 2), ("A", 10, 1), ("C", "ex", 3), ("C", "tra", 0), ("A", 9, 2), ("C", "gs", 0), ("C", "gs", 1),
    ("A", 11, 1), ("C", "gs", 2), ("A", 10, 2), ("C", "gs", 3), ("I", 8, 0), ("A", 11, 2), ("C", "hx", 0),
    ("C", "hx", 1), ("C", "hx", 2), ("C", "hx", 3), ("I", 9, 0), ("C", "bp0", 0), ("C", "bp1", 0), ("R", 8, 0),
    ("C", "hb", 0), ("C", "hb", 1), ("I", 10, 0), ("W", "b", 0), ("C", "tox", 0), ("C", "hb", 2), ("C", "hb", 3),
    ("R", 9, 0), ("C", "bp2", 0), ("I", 11, 0), ("C", "bp3", 0), ("C", "trn", 0), ("C", "gx", 0), ("R", 10, 0),
    ("I", 4, 0), ("C", "gx", 1), ("C", "gx", 2), ("C", "gx", 3), ("R", 8, 1), ("R", 11, 0), ("I", 5, 0),
    ("C", "trb", 0), ("R", 9, 1), ("C", "br0", 0), ("R", 8, 2), ("R", 10, 1), ("R", 4, 0), ("R", 9, 2), ("R", 8, 3),
    ("R", 11, 1), ("I", 6, 0), ("C", "br1", 0), ("R", 9, 3), ("R", 10, 2), ("W", "a", 0), ("W", "xb", 0),
    ("C", "ln2b", 0), ("R", 10, 3), ("R", 11, 2), ("R", 4, 1), ("R", 5, 0), ("I", 7, 0), ("W", "bm", 0),
    ("C", "tox2", 0), ("R", 11, 3), ("W", "gb", 0), ("C", "gat", 0), ("C", "gat", 1), ("C", "aba", 0), ("R", 4, 2),
    ("R", 6, 0), ("C", "abb", 0), ("R", 4, 3), ("C", "ga", 0), ("I", 0, 0), ("C", "aba", 1), ("R", 7, 0),
    ("C", "abb", 1), ("R", 5, 1), ("C", "ga", 1), ("R", 6, 1), ("I", 1, 0), ("C", "br2", 0), ("R", 5, 2), ("R", 0, 0),
    ("R", 6, 2), ("R", 5, 3), ("R", 7, 1), ("C", "br3", 0), ("I", 12, 0), ("R", 6, 3), ("C", "aba", 2), ("R", 7, 2),
    ("R", 1, 0), ("C", "abb", 2), ("R", 7, 3), ("R", 0, 1), ("C", "ga", 2), ("R", 12, 0), ("I", 13, 0),
    ("C", "aba", 3), ("R", 0, 2), ("I", 2, 0), ("C", "abb", 3), ("R", 12, 1), ("R", 0, 3), ("R", 1, 1),
    ("C", "ga", 3), ("I", 14, 0), ("W", "am", 0), ("C", "b1o", 0), ("R", 1, 2), ("R", 13, 0), ("R", 2, 0),
    ("C", "b1m", 0), ("R", 1, 3), ("R", 12, 2), ("I", 3, 0), ("I", 15, 0), ("W", "p1", 0), ("C", "ln1b", 0),
    ("R", 12, 3), ("R", 13, 1), ("C", "v0", 0), ("W", "xm", 0), ("C", "fin", 0), ("R", 14, 0), ("R", 12, 4),
    ("W", "v0", 0), ("C", "v1", 0), ("R", 3, 0), ("R", 14, 1), ("W", "v1", 0), ("C", "v2", 0), ("R", 15, 0),
    ("W", "v2", 0), ("C", "v3", 0), ("R", 15, 1), ("R", 13, 2), ("R", 2, 1), ("W", "v3", 0), ("C", "ov", 0),
    ("R", 14, 2), ("R", 13, 3), ("R", 3, 1), ("R", 2, 2), ("R", 13, 4), ("R", 14, 3), ("R", 15, 2), ("R", 3, 2),
    ("R", 2, 3), ("R", 14, 4), ("R", 15, 3), ("R", 3, 3), ("R", 15, 4),
)


def solution(mesh):
    split = P("dp", "seq", None)
    rows = P("dp", None)
    flat = P("dp")
    return jax.shard_map(
        body,
        mesh=mesh,
        in_specs=(split, split, rows, rows, rows, rows, flat) + (rows,) * 6 + (flat, flat),
        out_specs=(split, split) + (rows,) * 12 + (flat,) * 4,
        check_vma=False,
    )
```

```python
import functools

import jax
import jax.numpy as jnp
from jax import lax
from jax.experimental import pallas as pl
from jax.experimental.pallas import tpu as pltpu
from jax.sharding import PartitionSpec as P

HEAD_DIM = 64
STEP = 5
EPS_NORM = 1e-05
BETA_ONE = 0.5
BETA_TWO = 0.5
EPS_ADAM = 1e-08
RATE_MATRIX = 0.05
RATE_VECTOR = 0.2
DECAY_MATRIX = 0.1
SLOPE = 1.702

BF16 = jnp.bfloat16
F32 = jnp.float32
MESH = pl.DeviceIdType.MESH

UNIT = 512
BLOCKS = 4
EDGE = BLOCKS - 1
HALF = 2
UNITS = 8
ITEMS = 16
FIRST_EDGE = 12
PAIR = 128


def dot(a, b):
    return jnp.dot(a, b, preferred_element_type=F32)


def dot_rows(a, b):
    return lax.dot_general(a, b, (((0,), (0,)), ((), ())), preferred_element_type=F32)


def dot_cols(a, b):
    return lax.dot_general(a, b, (((1,), (1,)), ((), ())), preferred_element_type=F32)


def unit_rows(x):
    centred = x - jnp.mean(x, -1, keepdims=True)
    rstd = lax.rsqrt(jnp.mean(centred * centred, -1, keepdims=True) + EPS_NORM)
    return centred * rstd, rstd


def norm_back(grad_normed, unit, rstd, gain):
    g = grad_normed * gain
    return rstd * (g - jnp.mean(g, -1, keepdims=True) - unit * jnp.mean(g * unit, -1, keepdims=True))


def fold8(v):
    return jnp.sum(v.reshape(v.shape[0] // 8, 8, v.shape[1]), 0)


def layer_kernel(
    line, vec_len,
    tok, cot, kbias, p_vec, p_att, p_exp, p_shr,
    o_blk, o_tok, o_att, o_exp, o_shr, o_vec,
    w, w_oth, g, rx, ry, rz, ry_e, rz_e, s_own, s_oth, f_own, f_oth,
    vec_all, vec, bias_h, vg, vr, vz, hidden_sums,
    tok_own, cot_own,
    n1, go, qkv, att, lse, resid, n2, act, fac,
    part_a, part_b, recv_a, recv_b, recv_m, x_recv_m,
    gb, tr, dk_acc, dv_acc,
    ag, rs, sib, wo, xe, vs, fill, loc,
):
    dp_n = 2 * line
    r = w.shape[4]
    block = tok.shape[1]
    own = 2 * block
    rows = 2 * own
    width = tok.shape[2]
    half = UNIT
    d = lax.axis_index("dp")
    s = lax.axis_index("seq")
    zi, yi = d // 2, d % 2
    x, c = s // 2, s % 2
    sibling = (d, x * 2 + 1 - c)
    x_neigh = (d, (1 - x) * 2 + c)
    y_neigh = (zi * 2 + 1 - yi, s)

    def z_peer(o):
        return (lax.rem(zi + o, line) * 2 + yi, s)

    def own_rows(core):
        return pl.ds(pl.multiple_of(core * own, own), own)

    def ff_rows(chip, core):
        return pl.ds(pl.multiple_of(chip * rows + core * own, own), own)

    my_rows = own_rows(c)
    own_p, send_a = part_a.at[own_rows(c)], part_a.at[own_rows(1 - c)]
    keep_p, send_b = part_b.at[own_rows(c)], part_b.at[own_rows(1 - c)]
    my_half = pl.ds(pl.multiple_of(c * half, half), half)
    oth_half = pl.ds(pl.multiple_of((1 - c) * half, half), half)
    my_block = pl.ds(pl.multiple_of(x * block, block), block)
    oth_block = pl.ds(pl.multiple_of((1 - x) * block, block), block)

    mine, theirs = x * EDGE, (1 - x) * EDGE

    def blocks_of(i):
        if i < 4:
            return i, 1, HALF
        if i < FIRST_EDGE:
            return 4 + (i - 4) // 2, (i - 4) % 2 * HALF, HALF
        return i - FIRST_EDGE, mine, 1

    def item(ref, i):
        u, first, count = blocks_of(i)
        return ref.at[u, pl.ds(first, count)]

    def remote(src, dst, send, recv, to):
        return pltpu.make_async_remote_copy(
            src_ref=src, dst_ref=dst, send_sem=send, recv_sem=recv, device_id=to, device_id_type=MESH
        )

    def wait_bytes(ref, sem):
        pltpu.make_async_copy(ref, ref, sem).wait()

    wide = r % 128 == 0

    def unit_parts(u, place):
        if u < 4:
            core = place % 2
            return [
                (slice(None), pl.ds(pl.multiple_of(n * width + core * half + u * PAIR, PAIR), PAIR)) for n in range(BLOCKS)
            ]
        if u < 6:
            if not wide:
                return None
            parts = []
            for n in range((u - 4) * UNIT, (u - 3) * UNIT, PAIR):
                at = n // r * 4 * r + place * r + n % r
                parts.append((slice(None), pl.ds(pl.multiple_of(at, PAIR), PAIR)))
            return parts
        first = (u - 6) * UNIT
        held = pl.ds(pl.multiple_of(place * r, r), r)
        return [(held, slice(first + n * PAIR, first + (n + 1) * PAIR)) for n in range(BLOCKS)]

    def stage(u):
        n = u % 4 if u < 4 else u % 2
        hold, first = (part_a, 0) if u < 4 else (part_b, u // 6 * r)
        first = first + n // 2 * r
        return hold.at[first : first + r, (n % 2) * UNIT : (n % 2 + 1) * UNIT]

    def matrix(u, refs):
        return refs[0 if u < 4 else 1 if u < 6 else 2]

    for u in range(UNITS):
        parts = unit_parts(u, s)
        source = matrix(u, (p_att, p_exp, p_shr))
        for n in range(BLOCKS):
            part = source.at[parts[n]] if parts else source.at[u - 4, n]
            pltpu.make_async_copy(part, stage(u).at[:, n * PAIR : (n + 1) * PAIR], fill.at[u, n // HALF if u >= 4 else int(n in (0, EDGE))]).start()

    vec_all[d] = p_vec[...]
    tok_copy_in = pltpu.make_async_copy(tok.at[x], tok_own.at[my_block], loc.at[0])
    tok_copy_in.start()

    def go_rows(chip, place):
        return pl.ds(pl.multiple_of(chip * rows + place % 2 * own + place // 2 * block, block), block)

    go_local = [pltpu.make_async_copy(cot.at[n], go.at[go_rows(n, s)], loc.at[1]) for n in range(2)]
    for copy in go_local:
        copy.start()

    barrier = pltpu.get_barrier_semaphore()

    def greet(o, carry):
        pl.semaphore_signal(barrier, inc=1, device_id=(lax.rem(d + o, dp_n), s), device_id_type=MESH)
        return carry

    lax.fori_loop(1, dp_n, greet, 0)
    pl.semaphore_signal(barrier, inc=1, device_id=sibling, device_id_type=MESH)
    pl.semaphore_signal(barrier, inc=1, device_id=x_neigh, device_id_type=MESH)
    pl.semaphore_wait(barrier, dp_n + 1)

    def send_vec(o, carry):
        remote(p_vec, vec_all.at[d], vs.at[0, 0], vs.at[1, 0], (lax.rem(d + o, dp_n), s)).start()
        return carry

    lax.fori_loop(1, dp_n, send_vec, 0)
    tok_copy_x = remote(tok.at[1 - x], tok_own.at[my_block], xe.at[0, 0], xe.at[1, 0], x_neigh)
    tok_copy_x.start()
    other = (1 - x) * 2 + c
    go_copies = [
        [remote(cot.at[n], go.at[go_rows(n, s)], sib.at[0, 4], sib.at[1, 4], sibling) for n in range(2)],
        [remote(cot.at[n], go.at[go_rows(n, s)], xe.at[0, 4], xe.at[1, 4], x_neigh) for n in range(2)],
        [remote(go.at[go_rows(n, other)], go.at[go_rows(n, other)], sib.at[0, 5], sib.at[1, 5], sibling) for n in range(2)],
    ]
    go_bytes = go.at[:own]

    def ag_z(i):
        u, first, count = blocks_of(i)
        group = first // HALF if 4 <= i < FIRST_EDGE else int(i >= FIRST_EDGE)
        wait_bytes(stage(u).at[:, : HALF * PAIR], fill.at[u, group])
        for n in range(count):
            w[u, first + n, zi, yi] = stage(u)[:, pl.ds(pl.multiple_of((first + n) * PAIR, PAIR), PAIR)].astype(BF16)
        part = item(w, i).at[:, zi, yi]
        for o in range(1, line):
            remote(part, part, ag.at[0, i], ag.at[1, i], z_peer(o)).start()

    def ag_y_copy(i):
        part = item(w, i).at[:, :, yi]
        return remote(part, part, ag.at[2, i], ag.at[3, i], y_neigh)

    def ag_x_copy(i):
        return remote(item(w, i), item(w, i), ag.at[4, i], ag.at[5, i], x_neigh)

    def z_bytes(i):
        return item(w, i).at[:, pl.ds(0, line - 1), yi]

    def ag_y(i):
        wait_bytes(z_bytes(i), ag.at[1, i])
        ag_y_copy(i).start()

    def ag_x(i):
        ag_y_copy(i).wait_recv()
        if i >= FIRST_EDGE:
            ag_x_copy(i).start()

    def ag_end(i):
        ag_x_copy(i).wait_recv()

    gather_stages = [ag_z, ag_y, ag_x, ag_end]

    grain = 128 if vec_len % 128 == 0 else 64

    def vec_lanes(first):
        parts = []
        for e in range(first, first + 128, grain):
            o = e % vec_len
            parts.append(vec_all[e // vec_len, o // 128 : o // 128 + 1, o % 128 : o % 128 + grain])
        return parts[0] if len(parts) == 1 else jnp.concatenate(parts, 1)

    def hidden_bias(place):
        parts = []
        for shard in range(dp_n):
            n = shard * 4 * r + place * r
            parts.append(vec[8 + n // width : 9 + n // width, n % width : n % width + r])
        return jnp.concatenate(parts, 1)

    def vector():
        for row in range(12):
            for lane in range(0, width, 128):
                vec[row : row + 1, lane : lane + 128] = vec_lanes(row * width + lane)
        low_half = jnp.where(s == 0, hidden_bias(0), hidden_bias(1))
        bias_h[...] = jnp.where(s < 2, low_half, jnp.where(s == 2, hidden_bias(2), hidden_bias(3)))

    def live(to):
        return jnp.where(kbias[to, 0:1] < 0, 0.0, 1.0)

    chunk = block // 2

    def chunks(first, i):
        return pl.ds(pl.multiple_of(first + i * chunk, chunk), chunk)

    def first_norm():
        def some(i, carry):
            unit, _ = unit_rows(tok_own[chunks(0, i), :].astype(F32))
            n1[chunks(c * own, i), :] = (unit * vec[0:1, :] + vec[1:2, :]).astype(BF16)
            return carry

        lax.fori_loop(0, own // chunk, some, 0)
        n1_copy.start()

    def grad_output():
        for copy in go_copies[1] + go_copies[0]:
            copy.start()

    def rows_copies(ref, n):
        here, there = ref.at[ff_rows(x, c)], ref.at[ff_rows(1 - x, c)]
        return (
            remote(here, here, sib.at[0, n], sib.at[1, n], sibling),
            remote(here, here, xe.at[0, n], xe.at[1, n], x_neigh),
            remote(there, there, sib.at[0, n + 1], sib.at[1, n + 1], sibling),
        )

    n1_copy = remote(n1.at[my_rows], n1.at[my_rows], sib.at[0, 0], sib.at[1, 0], sibling)
    att_copy = remote(att.at[:, my_half], att.at[:, my_half], sib.at[0, 1], sib.at[1, 1], sibling)
    gb_copy = remote(gb.at[my_rows], gb.at[my_rows], sib.at[0, 2], sib.at[1, 2], sibling)
    p1_copy = remote(send_b, recv_a, sib.at[0, 3], sib.at[1, 3], sibling)
    n2_copies = rows_copies(n2, 6)
    b_copy = remote(send_b, recv_b, sib.at[0, 8], sib.at[1, 8], sibling)
    a_copy = remote(send_a, recv_a, sib.at[0, 9], sib.at[1, 9], sibling)
    bm_copy = remote(send_b, recv_m, sib.at[0, 10], sib.at[1, 10], sibling)
    am_copy = remote(send_a, recv_b, sib.at[0, 11], sib.at[1, 11], sibling)
    x_back = [
        remote(cot_own.at[pl.ds(n * block, block)], o_blk.at[n], xe.at[0, 7 + n], xe.at[1, 7 + n], x_neigh) for n in range(2)
    ]
    xm_copy = remote(cot_own, x_recv_m, xe.at[0, 9], xe.at[1, 9], x_neigh)
    tok_copy = remote(tok_own.at[oth_block], o_tok.at[x], xe.at[0, 3], xe.at[1, 3], x_neigh)
    blk_copy = remote(cot_own.at[oth_block], o_blk.at[x], xe.at[0, 2], xe.at[1, 2], x_neigh)

    low_lane = lax.broadcasted_iota(jnp.int32, (PAIR, PAIR), 1) < HEAD_DIM
    low_row = lax.broadcasted_iota(jnp.int32, (PAIR, PAIR), 0) < HEAD_DIM
    q_chunks = rows // PAIR

    def two_heads(v):
        zero = jnp.zeros_like(v)
        return jnp.concatenate([jnp.where(low_lane, v, zero), jnp.where(low_lane, zero, v)], 0)

    qkv_lanes = 3 * PAIR

    def pair_lanes(p):
        return tuple(slice(p * qkv_lanes + n * PAIR, p * qkv_lanes + (n + 1) * PAIR) for n in range(3))

    def att_lanes(p):
        return pl.ds(pl.multiple_of(c * half + p * PAIR, PAIR), PAIR)

    def wo_copy(p):
        return remote(w.at[p, BLOCKS - 1], w_oth.at[p], wo.at[0, p], wo.at[1, p], sibling)

    def columns(blocks):
        return jnp.concatenate([v.reshape(-1, PAIR) for v in blocks], 1)

    def project(p):
        wo_copy(p).start()
        q_at, k_at, v_at = pair_lanes(p)
        out = dot(n1[...], columns([w[p, n] for n in range(3)]))
        queries = (out[:, :PAIR] + vec[4:5, att_lanes(p)]).astype(BF16)
        qkv[:, q_at] = queries * jnp.asarray(HEAD_DIM**-0.5, BF16)
        qkv[:, k_at] = out[:, PAIR : 2 * PAIR].astype(BF16)
        qkv[:, v_at] = (out[:, 2 * PAIR :] + vec[5:6, att_lanes(p)]).astype(BF16)

    def attend_forward(p, first, last):
        q_at, k_at, v_at = pair_lanes(p)

        def some(j, carry):
            at = pl.ds(pl.multiple_of(j * PAIR, PAIR), PAIR)
            mask = kbias[...]
            scores = dot_cols(qkv[:, k_at], two_heads(qkv[at, q_at])) + jnp.concatenate([mask, mask], 1)
            highest = jnp.max(scores, 0, keepdims=True)
            raised = jnp.exp(scores - highest)
            total = jnp.sum(raised, 0, keepdims=True)
            out = dot_rows(qkv[:, v_at], raised.astype(BF16)) / total
            out = jnp.where(low_row, out[:, :PAIR], out[:, PAIR:])
            att[at, att_lanes(p)] = out.T.astype(BF16)
            lse[pl.ds(p * q_chunks + j, 1), :] = highest + jnp.log(total)
            return carry

        lax.fori_loop(first, last, some, 0)
        if p == 3 and last == q_chunks:
            att_copy.start()

    def own_out(z):
        return columns([w[p, BLOCKS - 1, z] for p in range(4)])

    def oth_out(z):
        return columns([w_oth[p, z] for p in range(4)])

    def output_projection():
        mixed = att[my_rows, :]
        resid[:, my_half] = dot(mixed, own_out(slice(None)))
        resid[:, oth_half] = dot(mixed, oth_out(slice(None)))

    def second_norm():
        def some(i, carry):
            at = chunks(0, i)
            res = resid[at, :] + tok_own[at, :].astype(F32) + vec[6:7, :]
            resid[at, :] = res
            unit, _ = unit_rows(res)
            n2[chunks(x * rows + c * own, i), :] = (unit * vec[2:3, :] + vec[3:4, :]).astype(BF16)
            return carry

        lax.fori_loop(0, own // chunk, some, 0)
        n2_copies[1].start()
        n2_copies[0].start()

    tile = HALF * PAIR

    def expand(n, chip):
        u, first, _ = blocks_of(4 + n)
        at = pl.ds(pl.multiple_of(chip * rows, rows), rows)
        to = slice(n * tile, (n + 1) * tile)
        hidden = dot(n2[at, :], columns([w[u, first], w[u, first + 1]])) + bias_h[:, to]
        gate = jax.nn.sigmoid(SLOPE * hidden)
        act[at, to] = (hidden * gate).astype(BF16)
        fac[at, to] = (gate + SLOPE * hidden * gate * (1.0 - gate)).astype(BF16)

    def rs_x_copy(i):
        u = i - FIRST_EDGE
        return remote(g.at[u, theirs], rx.at[u], rs.at[0, i], rs.at[1, i], x_neigh)

    def y_place(i):
        return ry.at[i] if i < FIRST_EDGE else ry_e.at[i - FIRST_EDGE]

    def z_place(i):
        return rz.at[i] if i < FIRST_EDGE else rz_e.at[i - FIRST_EDGE]

    def rs_y_copy(i):
        return remote(item(g, i).at[:, :, 1 - yi], y_place(i), rs.at[2, i], rs.at[3, i], y_neigh)

    def done_blocks(i):
        u, first, count = blocks_of(i)
        return f_own.at[u, pl.ds(first, count)]

    def rs_2_copy(i):
        if i < 4:
            return remote(s_own.at[i], s_oth.at[i], rs.at[6, i], rs.at[7, i], x_neigh)
        to = f_oth.at[i - 4] if i < FIRST_EDGE else f_own.at[i - FIRST_EDGE, pl.ds(mine, 1)]
        return remote(done_blocks(i), to, rs.at[6, i], rs.at[7, i], x_neigh)

    def to_result(u, n, place):
        result = matrix(u, (o_att, o_exp, o_shr))
        if u < 4:
            first = n * width + place % 2 * half + u * PAIR
            return result.at[:, pl.ds(pl.multiple_of(first, PAIR), PAIR)]
        parts = unit_parts(u, place)
        return result.at[parts[n]] if parts else result.at[u - 4, place, n]

    def rs_share(i, source, first, count, place, sems):
        u = blocks_of(i)[0]
        for n in range(count):
            to = to_result(u, first + n, place)
            remote(source.at[n], to, rs.at[sems, i], rs.at[sems + 1, i], sibling).start()
            pltpu.make_async_copy(source.at[n], to, rs.at[sems + 2, i]).start()

    def rs_x_add(i):
        rs_x_copy(i).wait_recv()
        u = i - FIRST_EDGE

        def add(z, carry):
            g[u, mine, z] = (g[u, mine, z].astype(F32) + rx[u, z].astype(F32)).astype(BF16)
            return carry

        lax.fori_loop(0, line, add, 0)
        rs_y_copy(i).start()

    def rs_y_add(i):
        rs_y_copy(i).wait_recv()
        u, first, count = blocks_of(i)
        got = y_place(i)

        def add(z, carry):
            for n in range(count):
                g[u, first + n, z, yi] = (g[u, first + n, z, yi].astype(F32) + got[n, z].astype(F32)).astype(BF16)
            return carry

        lax.fori_loop(0, line, add, 0)
        for o in range(1, line):
            z = lax.rem(zi + o, line)
            remote(item(g, i).at[:, z, yi], z_place(i).at[o - 1], rs.at[4, i], rs.at[5, i], z_peer(o)).start()

    def rs_z_add(i):
        u, first, count = blocks_of(i)
        got = z_place(i)
        wait_bytes(got, rs.at[5, i])
        for n in range(count):
            total = g[u, first + n, zi, yi].astype(F32)
            for o in range(1, line):
                total = total + got[o - 1, n].astype(F32)
            if i < 4:
                s_own[i, n] = total.astype(BF16)
            else:
                f_own[u, first + n] = total.astype(BF16)
        rs_2_copy(i).start()
        if i >= 4:
            rs_share(i, done_blocks(i), first, count, s, 8)

    def rs_join(i):
        rs_2_copy(i).wait_recv()
        u, first, count = blocks_of(i)
        if i < 4:
            for n in range(count):
                f_own[u, first + n] = (s_own[i, n].astype(F32) + s_oth[i, n].astype(F32)).astype(BF16)
            rs_share(i, done_blocks(i), first, count, s, 8)
        elif i < FIRST_EDGE:
            rs_share(i, f_oth.at[i - 4], first, count, other, 11)
        else:
            rs_share(i, f_own.at[u, pl.ds(theirs, 1)], theirs, count, other, 11)

    def rs_end(i):
        if i >= FIRST_EDGE:
            rs_x_copy(i).wait_send()
        rs_y_copy(i).wait_send()
        wait_bytes(z_place(i), rs.at[4, i])
        rs_2_copy(i).wait_send()
        for n in range(8, 11 if i < 4 else 14):
            wait_bytes(done_blocks(i), rs.at[n, i])

    def put(u, first, value):
        for n in range(value.shape[1] // PAIR):
            part = value[:, n * PAIR : (n + 1) * PAIR].astype(BF16)
            g[u, first + n] = part.reshape(line, 2, r, PAIR)

    def rs_start(i):
        (rs_y_copy(i) if i < FIRST_EDGE else rs_x_copy(i)).start()

    def rs_stage(i, k):
        stages = [rs_x_add, rs_y_add, rs_z_add, rs_join, rs_end]
        (stages[1:] if i < FIRST_EDGE else stages)[k](i)

    def transpose_into(dst, first, src, size):
        def move(i, carry):
            at = pl.ds(pl.multiple_of(i * 128, 128), 128)
            dst[at, first : first + size] = src[:, at].T
            return carry

        lax.fori_loop(0, width // 128, move, 0)

    def shrink_grad(n):
        u, first, _ = blocks_of(8 + n)
        put(u, first, dot(tr[...], go[:, n * tile : (n + 1) * tile]))

    span = max(1, tile // (2 * r))
    part_rows = span * 2 * r

    def hidden_back(n, chip, clear):
        at = pl.ds(pl.multiple_of(chip * rows, rows), rows)
        if clear:
            hidden_sums[...] = jnp.zeros_like(hidden_sums)

        def some(m, carry):
            to = pl.ds(pl.multiple_of(m * part_rows, part_rows), part_rows)
            total = None
            for j in range(2):
                part = columns([w[6 + j, b, pl.ds(m * span, span)] for b in range(BLOCKS)])
                term = dot_cols(go[at, j * UNIT : (j + 1) * UNIT], part)
                total = term if total is None else total + term
            low = (total * fac[at, to].astype(F32)).astype(BF16)
            fac[at, to] = low
            hidden_sums[:, to] += fold8(low.astype(F32))
            return carry

        count = line // span // 4
        lax.fori_loop(n * count, (n + 1) * count, some, 0)

    def back_partial(src, rows_at, units, blocks, dst):
        lanes = blocks * PAIR

        def back(n, carry):
            total = None
            for k, u in enumerate(units):
                part = columns([w[u, b, pl.ds(n * span, span)] for b in range(blocks)])
                term = dot_cols(src[rows_at, k * lanes : (k + 1) * lanes], part)
                total = term if total is None else total + term
            dst[:, pl.ds(pl.multiple_of(n * part_rows, part_rows), part_rows)] = total
            return carry

        lax.fori_loop(0, line // span, back, 0)

    def expand_grad(n):
        u, first, _ = blocks_of(4 + n)
        put(u, first, dot(tr[...], fac[:, n * tile : (n + 1) * tile]))

    def to_x(came):
        def some(i, carry):
            at = chunks(0, i)
            cot_own[at, :] = (keep_p[at, :] + came[at, :]).astype(BF16)
            return carry

        lax.fori_loop(0, own // chunk, some, 0)

    ff = (4, 5)

    def hidden_partial(chip, dst):
        back_partial(fac, pl.ds(pl.multiple_of(chip * rows, rows), rows), ff, BLOCKS, dst)

    def hidden_partials(own_image):
        if own_image:
            hidden_partial(x, part_a)
            a_copy.start()
        else:
            hidden_partial(1 - x, part_b)
            b_copy.start()

    def partial_over_x():
        to_x(recv_b)
        for copy in x_back:
            copy.start()

    zeros8 = jnp.zeros((8, width), F32)

    def second_norm_back():
        def some(i, carry):
            at = chunks(0, i)
            unit, rstd = unit_rows(resid[at, :])
            came = o_blk[i // 2, pl.ds(pl.multiple_of(i % 2 * chunk, chunk), chunk)].astype(F32)
            gn = own_p[at, :] + recv_a[at, :] + came
            grad_out = go[chunks(x * rows + c * own, i), :].astype(F32)
            gr = grad_out + norm_back(gn, unit, rstd, vec[2:3, :])
            own_p[at, :] = gr
            low = gr.astype(BF16)
            gb[chunks(c * own, i), :] = low
            a, b, e, f = carry
            return (a + fold8(gn * unit), b + fold8(gn), e + fold8(low.astype(F32)), f + fold8(grad_out))

        vg[...] = jnp.zeros_like(vg)
        vg[pl.ds(8 + s, 1), :] = jnp.sum(hidden_sums[...], 0, keepdims=True)
        sums = lax.fori_loop(0, own // chunk, some, (zeros8,) * 4)
        for row, v in zip((2, 3, 6, 7), sums):
            vg[row : row + 1, :] = jnp.sum(v, 0, keepdims=True)
        gb_copy.start()

    def grad_attended(n):
        if n == 0:
            for copy in n2_copies:
                copy.wait_send()
        quarter = line // 4
        head_rows = pl.ds(c * (line // 2) + n * quarter, quarter)
        part = dot_cols(gb[:, my_half], own_out(head_rows)) + dot_cols(gb[:, oth_half], oth_out(head_rows))
        n2[:rows, n * tile : (n + 1) * tile] = part.astype(BF16)

    def attend_backward(p, first, last):
        q_at, k_at, v_at = pair_lanes(p)
        own_lanes = slice(p * PAIR, (p + 1) * PAIR)
        if first == 0:
            dk_acc[...] = jnp.zeros_like(dk_acc)
            dv_acc[...] = jnp.zeros_like(dv_acc)

        def some(j, carry):
            at = pl.ds(pl.multiple_of(j * PAIR, PAIR), PAIR)
            both = two_heads(qkv[at, q_at])
            grads = two_heads(n2[at, own_lanes])
            mask = kbias[...]
            scores = dot_cols(qkv[:, k_at], both) + jnp.concatenate([mask, mask], 1)
            chance = jnp.exp(scores - lse[pl.ds(p * q_chunks + j, 1), :])
            dv_acc[...] += dot(chance.astype(BF16), grads)
            grad_chance = dot_cols(qkv[:, v_at], grads)
            inner = jnp.sum(chance * grad_chance, 0, keepdims=True)
            grad_scores = (chance * (grad_chance - inner)).astype(BF16)
            dk_acc[...] += dot(grad_scores, both)
            out = dot_rows(qkv[:, k_at], grad_scores)
            out = jnp.where(low_row, out[:, :PAIR], out[:, PAIR:]) * HEAD_DIM**-0.5
            qkv[at, q_at] = out.T.astype(BF16)
            return carry

        lax.fori_loop(first, last, some, 0)
        if last < q_chunks:
            return
        qkv[:, k_at] = dk_acc[...].astype(BF16)
        qkv[:, v_at] = dv_acc[...].astype(BF16)
        vg[4:5, att_lanes(p)] = jnp.sum(fold8(qkv[:, q_at].astype(F32)), 0, keepdims=True)
        vg[5:6, att_lanes(p)] = jnp.sum(fold8(qkv[:, v_at].astype(F32)), 0, keepdims=True)

    def attention_grad(p):
        put(p, 0, dot(tr[:, :rows], qkv[:, p * qkv_lanes : (p + 1) * qkv_lanes]))
        put(p, BLOCKS - 1, dot(tr[:, rows:], gb[:, att_lanes(p)]))

    def input_partial():
        back_partial(qkv, slice(0, rows), (0, 1, 2, 3), 3, part_b)
        p1_copy.start()

    def first_norm_back():
        def some(i, carry):
            at = chunks(0, i)
            unit, rstd = unit_rows(tok_own[at, :].astype(F32))
            gn = keep_p[at, :] + recv_a[at, :]
            out = own_p[at, :] + norm_back(gn, unit, rstd, vec[0:1, :])
            tok_own[at, :] = out.astype(BF16)
            a, b = carry
            return (a + fold8(gn * unit), b + fold8(gn))

        sums = lax.fori_loop(0, own // chunk, some, (zeros8,) * 2)
        for row, v in zip((0, 1), sums):
            vg[row : row + 1, :] = jnp.sum(v, 0, keepdims=True)
        o_tok[x] = tok_own[my_block, :]
        tok_copy.start()

    def branch(dst, rows_at, add):
        def out(n, carry):
            for j in range(2):
                part = columns([w[6 + j, 2 * n], w[6 + j, 2 * n + 1]])
                to = pl.ds(pl.multiple_of(j * UNIT + n * tile, tile), tile)
                total = dot(act[rows_at, :], part)
                dst[:, to] = dst[:, to] + total if add else total
            return carry

        lax.fori_loop(0, UNIT // tile, out, 0)

    def output_partial(n):
        if n == 0:
            branch(part_b, pl.ds(pl.multiple_of((1 - x) * rows, rows), rows), False)
            bm_copy.start()
        elif n == 2:
            branch(send_a, ff_rows(x, 1 - c), False)
            am_copy.start()
        else:
            branch(resid, ff_rows(x, c), True)

    def output_over_x():
        to_x(recv_m)
        xm_copy.start()

    def finish_block():
        def some(i, carry):
            at = chunks(0, i)
            out = resid[at, :] + recv_b[at, :] + x_recv_m[at, :].astype(F32) + vec[7:8, :]
            cot_own[at, :] = (live(chunks(c * own, i)) * out).astype(BF16)
            return carry

        lax.fori_loop(0, own // chunk, some, 0)
        o_blk[x] = cot_own[my_block, :]
        blk_copy.start()

    v_copies = [
        remote(vg, vr.at[n], vs.at[0, 1 + n], vs.at[1, 1 + n], to) for n, to in enumerate((sibling, x_neigh, y_neigh))
    ]

    def vector_hop(n):
        if n < 3:
            v_copies[n].start()
            return

        def send(o, carry):
            remote(vg, vz.at[zi], vs.at[0, 4], vs.at[1, 4], (lax.rem(zi + o, line) * 2 + yi, s)).start()
            return carry

        lax.fori_loop(1, line, send, 0)
        vz[zi] = vg[...]

    def vector_add(n):
        if n < 3:
            v_copies[n].wait()
            vg[...] += vr[n]
            return
        wait_bytes(vz.at[pl.ds(0, line - 1)], vs.at[1, 4])
        wait_bytes(vz.at[pl.ds(0, line - 1)], vs.at[0, 4])

    def vector_out():
        o_vec[...] = lax.fori_loop(1, line, lambda i, t: t + vz[i], vz[0])

    def both(*copies):
        for copy in copies:
            copy.wait()

    def received(*copies):
        for copy in copies:
            copy.wait_recv()

    def relay(copies):
        copies[1].wait_recv()
        copies[2].start()

    def relay_go():
        wait_bytes(go_bytes, xe.at[1, 4])
        for copy in go_copies[2]:
            copy.start()

    def all_rows():
        received(n2_copies[2])
        wait_bytes(go_bytes, loc.at[1])
        wait_bytes(go_bytes, sib.at[1, 4])
        wait_bytes(go_bytes, sib.at[1, 5])

    waits = dict(
        vec=lambda: wait_bytes(vec_all.at[pl.ds(0, dp_n - 1)], vs.at[1, 0]),
        tok=lambda: both(tok_copy_x, tok_copy_in),
        cot=lambda: None,
        n1=lambda: received(n1_copy),
        gox=relay_go,
        att=lambda: received(*[wo_copy(p) for p in range(4)], att_copy),
        n2=lambda: received(n2_copies[0]),
        n2x=lambda: relay(n2_copies),
        n2r=all_rows,
        b=lambda: both(b_copy),
        a=lambda: both(a_copy),
        xb=lambda: both(*x_back),
        gb=lambda: received(gb_copy),
        p1=lambda: both(p1_copy),
        bm=lambda: both(bm_copy),
        am=lambda: both(am_copy),
        xm=lambda: both(xm_copy),
        v0=lambda: vector_add(0),
        v1=lambda: vector_add(1),
        v2=lambda: vector_add(2),
        v3=lambda: vector_add(3),
    )
    split = 3
    work = dict(
        vec=lambda n: vector(),
        ln1=lambda n: first_norm(),
        go=lambda n: grad_output(),
        qkv=project,
        afa=lambda p: attend_forward(p, 0, split),
        afb=lambda p: attend_forward(p, split, q_chunks),
        out=lambda n: output_projection(),
        ln2=lambda n: second_norm(),
        eo=lambda n: expand(n, x),
        ex=lambda n: expand(n, 1 - x),
        tra=lambda n: transpose_into(tr, 0, act, 2 * rows),
        gs=shrink_grad,
        hx=lambda n: hidden_back(n, 1 - x, n == 0),
        hb=lambda n: hidden_back(n, x, False),
        bpx=lambda n: hidden_partials(False),
        tox=lambda n: partial_over_x(),
        bpo=lambda n: hidden_partials(True),
        trn=lambda n: transpose_into(tr, 0, n2, 2 * rows),
        gx=expand_grad,
        ln2b=lambda n: second_norm_back(),
        trb=lambda n: (transpose_into(tr, 0, n1, rows), transpose_into(tr, rows, att, rows)),
        gat=grad_attended,
        aba=lambda p: attend_backward(p, 0, split),
        abb=lambda p: attend_backward(p, split, q_chunks),
        ga=attention_grad,
        b1=lambda n: input_partial(),
        ln1b=lambda n: first_norm_back(),
        brx=lambda n: output_partial(0),
        tox2=lambda n: output_over_x(),
        br2=lambda n: output_partial(2),
        br3=lambda n: output_partial(3),
        v0=lambda n: vector_hop(0),
        v1=lambda n: vector_hop(1),
        v2=lambda n: vector_hop(2),
        v3=lambda n: vector_hop(3),
        fin=lambda n: finish_block(),
        ov=lambda n: vector_out(),
    )
    for kind, name, n in ORDER:
        if kind == "C":
            work[name](n)
        elif kind == "W":
            waits[name]()
        elif kind == "A":
            gather_stages[n](name)
        elif kind == "I":
            rs_start(name)
        else:
            rs_stage(name, n)

    blk_copy.wait()
    tok_copy.wait()
    wait_bytes(vec_all.at[pl.ds(0, dp_n - 1)], vs.at[0, 0])
    for sem in (sib.at[0, 4], sib.at[0, 5], xe.at[0, 4]):
        wait_bytes(go_bytes, sem)
    for copy in [n1_copy, att_copy, gb_copy] + [wo_copy(p) for p in range(4)]:
        copy.wait_send()
    for i in range(ITEMS):
        wait_bytes(z_bytes(i), ag.at[0, i])
        ag_y_copy(i).wait_send()
        if i >= FIRST_EDGE:
            ag_x_copy(i).wait_send()


def adamw(grad, moment, square, weight, rate, decay):
    momentum = BETA_ONE * moment + (1.0 - BETA_ONE) * grad
    variance = BETA_TWO * square + (1.0 - BETA_TWO) * grad * grad
    first_fix = 1.0 - BETA_ONE**STEP
    second_fix = 1.0 - BETA_TWO**STEP
    direction = momentum / first_fix / (jnp.sqrt(variance / second_fix) + EPS_ADAM)
    updated = weight - rate * (direction + decay * weight)
    return (momentum, variance, updated, updated.astype(BF16))


def body(
    tokens, cotangent, key_mask,
    attention_weights, expand_weights, shrink_weights, vector_params,
    attention_moment, attention_square, expand_moment, expand_square,
    shrink_moment, shrink_square, vector_moment, vector_square,
):
    dp_n = lax.axis_size("dp")
    line = dp_n // 2
    d = lax.axis_index("dp")
    place = lax.axis_index("seq")
    x, c = place // 2, place % 2
    _, local_len, width = tokens.shape
    r = width // dp_n
    block = -(-local_len // 16) * 16
    own, rows = 2 * block, 4 * block
    pad = ((0, 0), (0, block - local_len), (0, 0))

    keep = lax.dynamic_index_in_dim(key_mask, x, 0, keepdims=False).reshape(2, 2, local_len)
    keep = jnp.pad(keep.transpose(1, 0, 2), ((0, 0), (0, 0), pad[1])).reshape(2, own)
    kbias = jnp.broadcast_to(jnp.where(keep > 0, 0.0, -1e30).astype(F32).reshape(rows, 1), (rows, PAIR))
    p_exp = expand_weights
    if r % 128:
        p_exp = lax.dynamic_index_in_dim(expand_weights.reshape(r, dp_n, 4, r), place, 2, keepdims=False)
        p_exp = p_exp.reshape(r, 2, BLOCKS, PAIR).transpose(1, 2, 0, 3)
    vec_len = vector_params.shape[0]
    here = lax.dynamic_slice_in_dim(key_mask, place * local_len, local_len, 1)
    grad_out = jnp.where(here[:, :, None] > 0, cotangent, jnp.zeros_like(cotangent))
    vec_rows = -(-vec_len // 1024) * 8
    p_vec = jnp.pad(vector_params.astype(BF16).astype(F32), (0, vec_rows * 128 - vec_len)).reshape(vec_rows, 128)

    vmem = pl.BlockSpec(memory_space=pltpu.VMEM)
    hbm = pl.BlockSpec(memory_space=pl.ANY)
    padded = jax.ShapeDtypeStruct((2, block, width), BF16)
    o_blk, o_tok, o_att, o_exp, o_shr, o_vec = pl.pallas_call(
        functools.partial(layer_kernel, line, vec_len),
        out_shape=(
            padded,
            padded,
            jax.ShapeDtypeStruct((r, 4 * width), BF16),
            jax.ShapeDtypeStruct((2, 4, BLOCKS, r, PAIR) if r % 128 else (r, 4 * width), BF16),
            jax.ShapeDtypeStruct((4 * r, width), BF16),
            jax.ShapeDtypeStruct((16, width), F32),
        ),
        in_specs=[hbm, hbm, vmem, vmem, hbm, hbm, hbm],
        out_specs=(vmem, vmem, hbm, hbm, hbm, vmem),
        scratch_shapes=[
            pltpu.VMEM((UNITS, BLOCKS, line, 2, r, PAIR), BF16),
            pltpu.VMEM((4, line, 2, r, PAIR), BF16),
            pltpu.VMEM((UNITS, BLOCKS, line, 2, r, PAIR), BF16),
            pltpu.VMEM((4, line, 2, r, PAIR), BF16),
            pltpu.VMEM((FIRST_EDGE, HALF, line, r, PAIR), BF16),
            pltpu.VMEM((FIRST_EDGE, line - 1, HALF, r, PAIR), BF16),
            pltpu.VMEM((4, 1, line, r, PAIR), BF16),
            pltpu.VMEM((4, line - 1, 1, r, PAIR), BF16),
            pltpu.VMEM((4, HALF, r, PAIR), BF16),
            pltpu.VMEM((4, HALF, r, PAIR), BF16),
            pltpu.VMEM((UNITS, BLOCKS, r, PAIR), BF16),
            pltpu.VMEM((8, HALF, r, PAIR), BF16),
            pltpu.VMEM((dp_n, vec_rows, 128), F32),
            pltpu.VMEM((16, width), F32),
            pltpu.VMEM((1, width), F32),
            pltpu.VMEM((16, width), F32),
            pltpu.VMEM((3, 16, width), F32),
            pltpu.VMEM((line, 16, width), F32),
            pltpu.VMEM((8, width), F32),
            pltpu.VMEM((own, width), BF16),
            pltpu.VMEM((own, width), BF16),
            pltpu.VMEM((rows, width), BF16),
            pltpu.VMEM((2 * rows, width), BF16),
            pltpu.VMEM((rows, 3 * UNIT), BF16),
            pltpu.VMEM((rows, width), BF16),
            pltpu.VMEM(((rows // PAIR) * (UNIT // PAIR), 2 * PAIR), F32),
            pltpu.VMEM((own, width), F32),
            pltpu.VMEM((2 * rows, width), BF16),
            pltpu.VMEM((2 * rows, width), BF16),
            pltpu.VMEM((2 * rows, width), BF16),
        ]
        + [pltpu.VMEM((rows, width), F32)] * 2
        + [pltpu.VMEM((own, width), F32)] * 3
        + [
            pltpu.VMEM((own, width), BF16),
            pltpu.VMEM((rows, width), BF16),
            pltpu.VMEM((width, 2 * rows), BF16),
            pltpu.VMEM((rows, PAIR), F32),
            pltpu.VMEM((rows, PAIR), F32),
            pltpu.SemaphoreType.DMA((6, ITEMS)),
            pltpu.SemaphoreType.DMA((14, ITEMS)),
            pltpu.SemaphoreType.DMA((2, 12)),
            pltpu.SemaphoreType.DMA((2, 4)),
            pltpu.SemaphoreType.DMA((2, 10)),
            pltpu.SemaphoreType.DMA((2, 5)),
            pltpu.SemaphoreType.DMA((UNITS, 2)),
            pltpu.SemaphoreType.DMA((2,)),
        ],
        compiler_params=pltpu.CompilerParams(
            collective_id=0, has_side_effects=True, vmem_limit_bytes=VMEM_LIMIT
        ),
        name="layer",
    )(jnp.pad(tokens, pad), jnp.pad(grad_out, pad), kbias, p_vec, attention_weights, p_exp, shrink_weights)

    block_output = jnp.where(here[:, :, None] > 0, o_blk[:, :local_len], jnp.zeros_like(tokens))
    token_gradient = jnp.where(here[:, :, None] > 0, o_tok[:, :local_len], jnp.zeros_like(tokens))
    grad_attention, grad_shrink = o_att.astype(F32), o_shr.astype(F32)
    if r % 128:
        o_exp = o_exp.transpose(3, 1, 0, 2, 4).reshape(r, 4, dp_n, r).transpose(0, 2, 1, 3).reshape(r, 4 * width)
    grad_expand = o_exp.astype(F32)
    hidden_sums = o_vec[8:12].reshape(4, dp_n, r).transpose(1, 0, 2).reshape(4, width)
    grad_vector = jnp.concatenate([o_vec[0:8], hidden_sums], 0).reshape(dp_n, vec_len)
    grad_vector = lax.dynamic_index_in_dim(grad_vector, d, 0, keepdims=False)

    attention_out = adamw(
        grad_attention, attention_moment, attention_square, attention_weights, RATE_MATRIX, DECAY_MATRIX
    )
    expand_out = adamw(grad_expand, expand_moment, expand_square, expand_weights, RATE_MATRIX, DECAY_MATRIX)
    shrink_out = adamw(grad_shrink, shrink_moment, shrink_square, shrink_weights, RATE_MATRIX, DECAY_MATRIX)
    vector_out = adamw(grad_vector, vector_moment, vector_square, vector_params, RATE_VECTOR, 0.0)
    return (block_output, token_gradient, *attention_out, *expand_out, *shrink_out, *vector_out)


VMEM_LIMIT = 63 * 2**20

ORDER = (
    ("A", 12, 0), ("A", 0, 0), ("A", 13, 0), ("A", 1, 0), ("A", 14, 0), ("A", 2, 0), ("C", "go", 0), ("W", "vec", 0),
    ("C", "vec", 0), ("A", 12, 1), ("W", "tok", 0), ("C", "ln1", 0), ("A", 12, 2), ("A", 0, 1), ("A", 15, 0),
    ("A", 3, 0), ("A", 13, 1), ("A", 0, 2), ("A", 1, 1), ("A", 4, 0), ("A", 13, 2), ("A", 14, 1), ("A", 5, 0),
    ("W", "gox", 0), ("A", 1, 2), ("A", 2, 1), ("A", 6, 0), ("A", 12, 3), ("W", "n1", 0), ("C", "qkv", 0),
    ("A", 14, 2), ("C", "afa", 0), ("A", 15, 1), ("C", "afb", 0), ("A", 13, 3), ("C", "qkv", 1), ("A", 2, 2),
    ("C", "afa", 1), ("A", 3, 1), ("A", 7, 0), ("C", "afb", 1), ("A", 15, 2), ("A", 14, 3), ("C", "qkv", 2),
    ("C", "afa", 2), ("A", 4, 1), ("A", 8, 0), ("C", "afb", 2), ("A", 3, 2), ("A", 15, 3), ("C", "qkv", 3),
    ("C", "afa", 3), ("A", 5, 1), ("A", 9, 0), ("C", "afb", 3), ("A", 4, 2), ("W", "att", 0), ("C", "out", 0),
    ("A", 6, 1), ("A", 10, 0), ("C", "ln2", 0), ("A", 5, 2), ("A", 7, 1), ("A", 11, 0), ("W", "n2", 0),
    ("C", "eo", 0), ("C", "eo", 1), ("A", 6, 2), ("C", "eo", 2), ("A", 8, 1), ("A", 7, 2), ("C", "eo", 3),
    ("A", 9, 1), ("W", "n2x", 0), ("A", 8, 2), ("W", "n2r", 0), ("C", "ex", 0), ("A", 10, 1), ("C", "ex", 1),
    ("C", "ex", 2), ("A", 9, 2), ("C", "ex", 3), ("C", "tra", 0), ("A", 11, 1), ("C", "gs", 0), ("I", 8, 0),
    ("C", "gs", 1), ("A", 10, 2), ("I", 9, 0), ("C", "gs", 2), ("I", 10, 0), ("C", "gs", 3), ("C", "trn", 0),
    ("A", 11, 2), ("C", "hx", 0), ("C", "hb", 1), ("C", "hx", 1), ("C", "hx", 2), ("C", "hx", 3), ("R", 8, 0),
    ("I", 11, 0), ("C", "bpx", 0), ("C", "hb", 0), ("C", "hb", 2), ("R", 9, 0), ("C", "hb", 3), ("C", "gx", 0),
    ("R", 8, 1), ("I", 4, 0), ("W", "b", 0), ("C", "tox", 0), ("C", "gx", 2), ("R", 10, 0), ("R", 8, 2), ("I", 6, 0),
    ("C", "gx", 3), ("R", 8, 3), ("R", 9, 1), ("C", "bpo", 0), ("R", 11, 0), ("I", 7, 0), ("C", "gx", 1),
    ("R", 10, 1), ("C", "trb", 0), ("R", 4, 0), ("I", 5, 0), ("C", "brx", 0), ("R", 11, 1), ("W", "a", 0),
    ("W", "xb", 0), ("C", "ln2b", 0), ("R", 9, 2), ("R", 10, 2), ("R", 6, 0), ("R", 11, 2), ("W", "bm", 0),
    ("C", "tox2", 0), ("R", 4, 1), ("W", "gb", 0), ("C", "gat", 0), ("R", 9, 3), ("R", 10, 3), ("R", 11, 3),
    ("C", "gat", 1), ("R", 7, 0), ("C", "aba", 0), ("C", "abb", 0), ("R", 6, 1), ("R", 5, 0), ("C", "ga", 0),
    ("I", 12, 0), ("I", 0, 0), ("C", "aba", 1), ("R", 7, 1), ("C", "abb", 1), ("C", "ga", 1), ("I", 13, 0),
    ("I", 1, 0), ("C", "aba", 2), ("R", 4, 2), ("R", 6, 2), ("R", 5, 1), ("R", 0, 0), ("C", "abb", 2), ("R", 4, 3),
    ("R", 6, 3), ("C", "ga", 2), ("R", 12, 0), ("R", 1, 0), ("I", 14, 0), ("R", 7, 2), ("I", 2, 0), ("C", "aba", 3),
    ("R", 7, 3), ("R", 0, 1), ("C", "abb", 3), ("R", 12, 1), ("C", "b1", 0), ("R", 5, 2), ("R", 13, 0), ("R", 12, 2),
    ("R", 1, 1), ("R", 2, 0), ("C", "ga", 3), ("R", 14, 0), ("R", 0, 2), ("R", 5, 3), ("R", 12, 3), ("R", 13, 1),
    ("I", 15, 0), ("I", 3, 0), ("W", "p1", 0), ("C", "ln1b", 0), ("R", 12, 4), ("R", 0, 3), ("R", 1, 2),
    ("C", "v0", 0), ("R", 14, 1), ("C", "br2", 0), ("R", 1, 3), ("R", 2, 1), ("W", "v0", 0), ("C", "v1", 0),
    ("C", "br3", 0), ("R", 13, 2), ("R", 15, 0), ("R", 3, 0), ("R", 14, 2), ("W", "am", 0), ("W", "xm", 0),
    ("C", "fin", 0), ("W", "v1", 0), ("C", "v2", 0), ("R", 15, 1), ("W", "v2", 0), ("C", "v3", 0), ("R", 2, 2),
    ("R", 3, 1), ("R", 13, 3), ("R", 14, 3), ("R", 2, 3), ("R", 13, 4), ("R", 14, 4), ("R", 15, 2), ("R", 3, 2),
    ("R", 15, 3), ("W", "v3", 0), ("C", "ov", 0), ("R", 3, 3), ("R", 15, 4),
)


def solution(mesh):
    split = P("dp", "seq", None)
    rows = P("dp", None)
    flat = P("dp")
    return jax.shard_map(
        body,
        mesh=mesh,
        in_specs=(split, split, rows, rows, rows, rows, flat) + (rows,) * 6 + (flat, flat),
        out_specs=(split, split) + (rows,) * 12 + (flat,) * 4,
        check_vma=False,
    )
```

```python
import functools

import jax
import jax.numpy as jnp
from jax import lax
from jax.experimental import pallas as pl
from jax.experimental.pallas import tpu as pltpu
from jax.sharding import PartitionSpec as P

HEAD_DIM = 64
STEP = 5
EPS_NORM = 1e-05
BETA_ONE = 0.5
BETA_TWO = 0.5
EPS_ADAM = 1e-08
RATE_MATRIX = 0.05
RATE_VECTOR = 0.2
DECAY_MATRIX = 0.1
SLOPE = 1.702

BF16 = jnp.bfloat16
F32 = jnp.float32
MESH = pl.DeviceIdType.MESH

UNIT = 512
BLOCKS = 4
EDGE = BLOCKS - 1
HALF = 2
UNITS = 8
ITEMS = 16
FIRST_EDGE = 12
PAIR = 128


def dot(a, b):
    return jnp.dot(a, b, preferred_element_type=F32)


def dot_rows(a, b):
    return lax.dot_general(a, b, (((0,), (0,)), ((), ())), preferred_element_type=F32)


def dot_cols(a, b):
    return lax.dot_general(a, b, (((1,), (1,)), ((), ())), preferred_element_type=F32)


def unit_rows(x):
    centred = x - jnp.mean(x, -1, keepdims=True)
    rstd = lax.rsqrt(jnp.mean(centred * centred, -1, keepdims=True) + EPS_NORM)
    return centred * rstd, rstd


def norm_back(grad_normed, unit, rstd, gain):
    g = grad_normed * gain
    return rstd * (g - jnp.mean(g, -1, keepdims=True) - unit * jnp.mean(g * unit, -1, keepdims=True))


def fold8(v):
    return jnp.sum(v.reshape(v.shape[0] // 8, 8, v.shape[1]), 0)


def layer_kernel(
    line, vec_len,
    tok, cot, kbias, p_vec, p_att, p_exp, p_shr,
    o_blk, o_tok, o_att, o_exp, o_shr, o_vec,
    w, w_oth, g, rx, ry, rz, ry_e, rz_e, s_own, s_oth, f_own, f_oth,
    vec_all, vec, bias_h, vg, vr, vz, hidden_sums,
    tok_own, cot_own,
    n1, go, qkv, att, lse, resid, n2, act, fac,
    part_a, part_b, recv_a, recv_b, recv_m, x_recv_m,
    gb, tr, dk_acc, dv_acc,
    ag, rs, sib, wo, xe, vs, fill, loc,
):
    dp_n = 2 * line
    r = w.shape[4]
    block = tok.shape[1]
    own = 2 * block
    rows = 2 * own
    width = tok.shape[2]
    half = UNIT
    d = lax.axis_index("dp")
    s = lax.axis_index("seq")
    zi, yi = d // 2, d % 2
    x, c = s // 2, s % 2
    sibling = (d, x * 2 + 1 - c)
    x_neigh = (d, (1 - x) * 2 + c)
    y_neigh = (zi * 2 + 1 - yi, s)

    def z_peer(o):
        return (lax.rem(zi + o, line) * 2 + yi, s)

    def own_rows(core):
        return pl.ds(pl.multiple_of(core * own, own), own)

    def ff_rows(chip, core):
        return pl.ds(pl.multiple_of(chip * rows + core * own, own), own)

    my_rows = own_rows(c)
    own_p, send_a = part_a.at[own_rows(c)], part_a.at[own_rows(1 - c)]
    keep_p, send_b = part_b.at[own_rows(c)], part_b.at[own_rows(1 - c)]
    my_half = pl.ds(pl.multiple_of(c * half, half), half)
    oth_half = pl.ds(pl.multiple_of((1 - c) * half, half), half)
    my_block = pl.ds(pl.multiple_of(x * block, block), block)
    oth_block = pl.ds(pl.multiple_of((1 - x) * block, block), block)

    mine, theirs = x * EDGE, (1 - x) * EDGE

    def blocks_of(i):
        if i < 4:
            return i, 1, HALF
        if i < FIRST_EDGE:
            return 4 + (i - 4) // 2, (i - 4) % 2 * HALF, HALF
        return i - FIRST_EDGE, mine, 1

    def item(ref, i):
        u, first, count = blocks_of(i)
        return ref.at[u, pl.ds(first, count)]

    def remote(src, dst, send, recv, to):
        return pltpu.make_async_remote_copy(
            src_ref=src, dst_ref=dst, send_sem=send, recv_sem=recv, device_id=to, device_id_type=MESH
        )

    def wait_bytes(ref, sem):
        pltpu.make_async_copy(ref, ref, sem).wait()

    wide = r % 128 == 0

    def unit_parts(u, place):
        if u < 4:
            core = place % 2
            return [
                (slice(None), pl.ds(pl.multiple_of(n * width + core * half + u * PAIR, PAIR), PAIR)) for n in range(BLOCKS)
            ]
        if u < 6:
            if not wide:
                return None
            parts = []
            for n in range((u - 4) * UNIT, (u - 3) * UNIT, PAIR):
                at = n // r * 4 * r + place * r + n % r
                parts.append((slice(None), pl.ds(pl.multiple_of(at, PAIR), PAIR)))
            return parts
        first = (u - 6) * UNIT
        held = pl.ds(pl.multiple_of(place * r, r), r)
        return [(held, slice(first + n * PAIR, first + (n + 1) * PAIR)) for n in range(BLOCKS)]

    def stage(u):
        n = u % 4 if u < 4 else u % 2
        hold, first = (part_a, 0) if u < 4 else (part_b, u // 6 * r)
        first = first + n // 2 * r
        return hold.at[first : first + r, (n % 2) * UNIT : (n % 2 + 1) * UNIT]

    def matrix(u, refs):
        return refs[0 if u < 4 else 1 if u < 6 else 2]

    for u in range(UNITS):
        parts = unit_parts(u, s)
        source = matrix(u, (p_att, p_exp, p_shr))
        for n in range(BLOCKS):
            part = source.at[parts[n]] if parts else source.at[u - 4, n]
            pltpu.make_async_copy(part, stage(u).at[:, n * PAIR : (n + 1) * PAIR], fill.at[u, n // HALF if u >= 4 else int(n in (0, EDGE))]).start()

    vec_all[d] = p_vec[...]
    tok_copy_in = pltpu.make_async_copy(tok.at[x], tok_own.at[my_block], loc.at[0])
    tok_copy_in.start()

    def go_rows(chip, place):
        return pl.ds(pl.multiple_of(chip * rows + place % 2 * own + place // 2 * block, block), block)

    go_local = [pltpu.make_async_copy(cot.at[n], go.at[go_rows(n, s)], loc.at[1]) for n in range(2)]
    for copy in go_local:
        copy.start()

    barrier = pltpu.get_barrier_semaphore()

    def greet(o, carry):
        pl.semaphore_signal(barrier, inc=1, device_id=(lax.rem(d + o, dp_n), s), device_id_type=MESH)
        return carry

    lax.fori_loop(1, dp_n, greet, 0)
    pl.semaphore_signal(barrier, inc=1, device_id=sibling, device_id_type=MESH)
    pl.semaphore_signal(barrier, inc=1, device_id=x_neigh, device_id_type=MESH)
    pl.semaphore_wait(barrier, dp_n + 1)

    def send_vec(o, carry):
        remote(p_vec, vec_all.at[d], vs.at[0, 0], vs.at[1, 0], (lax.rem(d + o, dp_n), s)).start()
        return carry

    lax.fori_loop(1, dp_n, send_vec, 0)
    tok_copy_x = remote(tok.at[1 - x], tok_own.at[my_block], xe.at[0, 0], xe.at[1, 0], x_neigh)
    tok_copy_x.start()
    other = (1 - x) * 2 + c
    go_copies = [
        [remote(cot.at[n], go.at[go_rows(n, s)], sib.at[0, 4], sib.at[1, 4], sibling) for n in range(2)],
        [remote(cot.at[n], go.at[go_rows(n, s)], xe.at[0, 4], xe.at[1, 4], x_neigh) for n in range(2)],
        [remote(go.at[go_rows(n, other)], go.at[go_rows(n, other)], sib.at[0, 5], sib.at[1, 5], sibling) for n in range(2)],
    ]
    go_bytes = go.at[:own]

    def ag_z(i):
        u, first, count = blocks_of(i)
        group = first // HALF if 4 <= i < FIRST_EDGE else int(i >= FIRST_EDGE)
        wait_bytes(stage(u).at[:, : HALF * PAIR], fill.at[u, group])
        for n in range(count):
            w[u, first + n, zi, yi] = stage(u)[:, pl.ds(pl.multiple_of((first + n) * PAIR, PAIR), PAIR)].astype(BF16)
        part = item(w, i).at[:, zi, yi]
        for o in range(1, line):
            remote(part, part, ag.at[0, i], ag.at[1, i], z_peer(o)).start()

    def ag_y_copy(i):
        part = item(w, i).at[:, :, yi]
        return remote(part, part, ag.at[2, i], ag.at[3, i], y_neigh)

    def ag_x_copy(i):
        return remote(item(w, i), item(w, i), ag.at[4, i], ag.at[5, i], x_neigh)

    def z_bytes(i):
        return item(w, i).at[:, pl.ds(0, line - 1), yi]

    def ag_y(i):
        wait_bytes(z_bytes(i), ag.at[1, i])
        ag_y_copy(i).start()

    def ag_x(i):
        ag_y_copy(i).wait_recv()
        if i >= FIRST_EDGE:
            ag_x_copy(i).start()

    def ag_end(i):
        ag_x_copy(i).wait_recv()

    gather_stages = [ag_z, ag_y, ag_x, ag_end]

    grain = 128 if vec_len % 128 == 0 else 64

    def vec_lanes(first):
        parts = []
        for e in range(first, first + 128, grain):
            o = e % vec_len
            parts.append(vec_all[e // vec_len, o // 128 : o // 128 + 1, o % 128 : o % 128 + grain])
        return parts[0] if len(parts) == 1 else jnp.concatenate(parts, 1)

    def hidden_bias(place):
        parts = []
        for shard in range(dp_n):
            n = shard * 4 * r + place * r
            parts.append(vec[8 + n // width : 9 + n // width, n % width : n % width + r])
        return jnp.concatenate(parts, 1)

    def vector():
        for row in range(12):
            for lane in range(0, width, 128):
                vec[row : row + 1, lane : lane + 128] = vec_lanes(row * width + lane)
        low_half = jnp.where(s == 0, hidden_bias(0), hidden_bias(1))
        bias_h[...] = jnp.where(s < 2, low_half, jnp.where(s == 2, hidden_bias(2), hidden_bias(3)))

    def live(to):
        return jnp.where(kbias[to, 0:1] < 0, 0.0, 1.0)

    chunk = block // 2

    def chunks(first, i):
        return pl.ds(pl.multiple_of(first + i * chunk, chunk), chunk)

    def first_norm():
        def some(i, carry):
            unit, _ = unit_rows(tok_own[chunks(0, i), :].astype(F32))
            n1[chunks(c * own, i), :] = (unit * vec[0:1, :] + vec[1:2, :]).astype(BF16)
            return carry

        lax.fori_loop(0, own // chunk, some, 0)
        n1_copy.start()

    def grad_output():
        for copy in go_copies[1] + go_copies[0]:
            copy.start()

    def rows_copies(ref, n):
        here, there = ref.at[ff_rows(x, c)], ref.at[ff_rows(1 - x, c)]
        return (
            remote(here, here, sib.at[0, n], sib.at[1, n], sibling),
            remote(here, here, xe.at[0, n], xe.at[1, n], x_neigh),
            remote(there, there, sib.at[0, n + 1], sib.at[1, n + 1], sibling),
        )

    n1_copy = remote(n1.at[my_rows], n1.at[my_rows], sib.at[0, 0], sib.at[1, 0], sibling)
    att_copy = remote(att.at[:, my_half], att.at[:, my_half], sib.at[0, 1], sib.at[1, 1], sibling)
    gb_copy = remote(gb.at[my_rows], gb.at[my_rows], sib.at[0, 2], sib.at[1, 2], sibling)
    p1_copy = remote(send_b, recv_a, sib.at[0, 3], sib.at[1, 3], sibling)
    n2_copies = rows_copies(n2, 6)
    b_copy = remote(send_b, recv_b, sib.at[0, 8], sib.at[1, 8], sibling)
    a_copy = remote(send_a, recv_a, sib.at[0, 9], sib.at[1, 9], sibling)
    bm_copy = remote(send_b, recv_m, sib.at[0, 10], sib.at[1, 10], sibling)
    am_copy = remote(send_a, recv_b, sib.at[0, 11], sib.at[1, 11], sibling)
    x_back = [
        remote(cot_own.at[pl.ds(n * block, block)], o_blk.at[n], xe.at[0, 7 + n], xe.at[1, 7 + n], x_neigh) for n in range(2)
    ]
    xm_copy = remote(cot_own, x_recv_m, xe.at[0, 9], xe.at[1, 9], x_neigh)
    tok_copy = remote(tok_own.at[oth_block], o_tok.at[x], xe.at[0, 3], xe.at[1, 3], x_neigh)
    blk_copy = remote(cot_own.at[oth_block], o_blk.at[x], xe.at[0, 2], xe.at[1, 2], x_neigh)

    low_lane = lax.broadcasted_iota(jnp.int32, (PAIR, PAIR), 1) < HEAD_DIM
    low_row = lax.broadcasted_iota(jnp.int32, (PAIR, PAIR), 0) < HEAD_DIM
    q_chunks = rows // PAIR

    def two_heads(v):
        zero = jnp.zeros_like(v)
        return jnp.concatenate([jnp.where(low_lane, v, zero), jnp.where(low_lane, zero, v)], 0)

    qkv_lanes = 3 * PAIR

    def pair_lanes(p):
        return tuple(slice(p * qkv_lanes + n * PAIR, p * qkv_lanes + (n + 1) * PAIR) for n in range(3))

    def att_lanes(p):
        return pl.ds(pl.multiple_of(c * half + p * PAIR, PAIR), PAIR)

    def wo_copy(p):
        return remote(w.at[p, BLOCKS - 1], w_oth.at[p], wo.at[0, p], wo.at[1, p], sibling)

    def columns(blocks):
        return jnp.concatenate([v.reshape(-1, PAIR) for v in blocks], 1)

    def project(p):
        wo_copy(p).start()
        q_at, k_at, v_at = pair_lanes(p)
        out = dot(n1[...], columns([w[p, n] for n in range(3)]))
        queries = (out[:, :PAIR] + vec[4:5, att_lanes(p)]).astype(BF16)
        qkv[:, q_at] = queries * jnp.asarray(HEAD_DIM**-0.5, BF16)
        qkv[:, k_at] = out[:, PAIR : 2 * PAIR].astype(BF16)
        qkv[:, v_at] = (out[:, 2 * PAIR :] + vec[5:6, att_lanes(p)]).astype(BF16)

    def attend_forward(p, first, last):
        q_at, k_at, v_at = pair_lanes(p)

        def some(j, carry):
            at = pl.ds(pl.multiple_of(j * PAIR, PAIR), PAIR)
            mask = kbias[...]
            scores = dot_cols(qkv[:, k_at], two_heads(qkv[at, q_at])) + jnp.concatenate([mask, mask], 1)
            highest = jnp.max(scores, 0, keepdims=True)
            raised = jnp.exp(scores - highest)
            total = jnp.sum(raised, 0, keepdims=True)
            out = dot_rows(qkv[:, v_at], raised.astype(BF16)) / total
            out = jnp.where(low_row, out[:, :PAIR], out[:, PAIR:])
            att[at, att_lanes(p)] = out.T.astype(BF16)
            lse[pl.ds(p * q_chunks + j, 1), :] = highest + jnp.log(total)
            return carry

        lax.fori_loop(first, last, some, 0)
        if p == 3 and last == q_chunks:
            att_copy.start()

    def own_out(z):
        return columns([w[p, BLOCKS - 1, z] for p in range(4)])

    def oth_out(z):
        return columns([w_oth[p, z] for p in range(4)])

    def output_projection():
        mixed = att[my_rows, :]
        resid[:, my_half] = dot(mixed, own_out(slice(None)))
        resid[:, oth_half] = dot(mixed, oth_out(slice(None)))

    def second_norm():
        def some(i, carry):
            at = chunks(0, i)
            res = resid[at, :] + tok_own[at, :].astype(F32) + vec[6:7, :]
            resid[at, :] = res
            unit, _ = unit_rows(res)
            n2[chunks(x * rows + c * own, i), :] = (unit * vec[2:3, :] + vec[3:4, :]).astype(BF16)
            return carry

        lax.fori_loop(0, own // chunk, some, 0)
        n2_copies[1].start()
        n2_copies[0].start()

    tile = HALF * PAIR

    def expand(n, chip):
        u, first, _ = blocks_of(4 + n)
        at = pl.ds(pl.multiple_of(chip * rows, rows), rows)
        to = slice(n * tile, (n + 1) * tile)
        hidden = dot(n2[at, :], columns([w[u, first], w[u, first + 1]])) + bias_h[:, to]
        gate = jax.nn.sigmoid(SLOPE * hidden)
        act[at, to] = (hidden * gate).astype(BF16)
        fac[at, to] = (gate + SLOPE * hidden * gate * (1.0 - gate)).astype(BF16)

    def rs_x_copy(i):
        u = i - FIRST_EDGE
        return remote(g.at[u, theirs], rx.at[u], rs.at[0, i], rs.at[1, i], x_neigh)

    def y_place(i):
        return ry.at[i] if i < FIRST_EDGE else ry_e.at[i - FIRST_EDGE]

    def z_place(i):
        return rz.at[i] if i < FIRST_EDGE else rz_e.at[i - FIRST_EDGE]

    def rs_y_copy(i):
        return remote(item(g, i).at[:, :, 1 - yi], y_place(i), rs.at[2, i], rs.at[3, i], y_neigh)

    def done_blocks(i):
        u, first, count = blocks_of(i)
        return f_own.at[u, pl.ds(first, count)]

    def rs_2_copy(i):
        if i < 4:
            return remote(s_own.at[i], s_oth.at[i], rs.at[6, i], rs.at[7, i], x_neigh)
        to = f_oth.at[i - 4] if i < FIRST_EDGE else f_own.at[i - FIRST_EDGE, pl.ds(mine, 1)]
        return remote(done_blocks(i), to, rs.at[6, i], rs.at[7, i], x_neigh)

    def to_result(u, n, place):
        result = matrix(u, (o_att, o_exp, o_shr))
        if u < 4:
            first = n * width + place % 2 * half + u * PAIR
            return result.at[:, pl.ds(pl.multiple_of(first, PAIR), PAIR)]
        parts = unit_parts(u, place)
        return result.at[parts[n]] if parts else result.at[u - 4, place, n]

    def rs_share(i, source, first, count, place, sems):
        u = blocks_of(i)[0]
        for n in range(count):
            to = to_result(u, first + n, place)
            remote(source.at[n], to, rs.at[sems, i], rs.at[sems + 1, i], sibling).start()
            pltpu.make_async_copy(source.at[n], to, rs.at[sems + 2, i]).start()

    def rs_x_add(i):
        rs_x_copy(i).wait_recv()
        u = i - FIRST_EDGE
        g[u, mine] = g[u, mine] + rx[u]
        rs_y_copy(i).start()

    def rs_y_add(i):
        rs_y_copy(i).wait_recv()
        u, first, count = blocks_of(i)
        got = y_place(i)
        for n in range(count):
            for z in range(line):
                g[u, first + n, z, yi] = g[u, first + n, z, yi] + got[n, z]
        for o in range(1, line):
            z = lax.rem(zi + o, line)
            remote(item(g, i).at[:, z, yi], z_place(i).at[o - 1], rs.at[4, i], rs.at[5, i], z_peer(o)).start()

    def rs_z_add(i):
        u, first, count = blocks_of(i)
        got = z_place(i)
        wait_bytes(got, rs.at[5, i])
        for n in range(count):
            total = g[u, first + n, zi, yi].astype(F32)
            for o in range(1, line):
                total = total + got[o - 1, n].astype(F32)
            if i < 4:
                s_own[i, n] = total.astype(BF16)
            else:
                f_own[u, first + n] = total.astype(BF16)
        rs_2_copy(i).start()
        if i >= 4:
            rs_share(i, done_blocks(i), first, count, s, 8)

    def rs_join(i):
        rs_2_copy(i).wait_recv()
        u, first, count = blocks_of(i)
        if i < 4:
            for n in range(count):
                f_own[u, first + n] = s_own[i, n] + s_oth[i, n]
            rs_share(i, done_blocks(i), first, count, s, 8)
        elif i < FIRST_EDGE:
            rs_share(i, f_oth.at[i - 4], first, count, other, 11)
        else:
            rs_share(i, f_own.at[u, pl.ds(theirs, 1)], theirs, count, other, 11)

    def rs_end(i):
        if i >= FIRST_EDGE:
            rs_x_copy(i).wait_send()
        rs_y_copy(i).wait_send()
        wait_bytes(z_place(i), rs.at[4, i])
        rs_2_copy(i).wait_send()
        for n in range(8, 11 if i < 4 else 14):
            wait_bytes(done_blocks(i), rs.at[n, i])

    def put(u, first, value):
        for n in range(value.shape[1] // PAIR):
            part = value[:, n * PAIR : (n + 1) * PAIR].astype(BF16)
            g[u, first + n] = part.reshape(line, 2, r, PAIR)

    def rs_start(i):
        (rs_y_copy(i) if i < FIRST_EDGE else rs_x_copy(i)).start()

    def rs_stage(i, k):
        stages = [rs_x_add, rs_y_add, rs_z_add, rs_join, rs_end]
        (stages[1:] if i < FIRST_EDGE else stages)[k](i)

    def transpose_into(dst, first, src, size):
        def move(i, carry):
            at = pl.ds(pl.multiple_of(i * 128, 128), 128)
            dst[at, first : first + size] = src[:, at].T
            return carry

        lax.fori_loop(0, width // 128, move, 0)

    def shrink_grad(n):
        u, first, _ = blocks_of(8 + n)
        put(u, first, dot(tr[...], go[:, n * tile : (n + 1) * tile]))

    span = max(1, tile // (2 * r))
    part_rows = span * 2 * r

    def hidden_back(n, chip, clear):
        at = pl.ds(pl.multiple_of(chip * rows, rows), rows)
        if clear:
            hidden_sums[...] = jnp.zeros_like(hidden_sums)

        def some(m, carry):
            to = pl.ds(pl.multiple_of(m * part_rows, part_rows), part_rows)
            part = columns([w[6 + j, b, pl.ds(m * span, span)] for j in range(2) for b in range(BLOCKS)])
            total = dot_cols(go[at, :], part)
            low = (total * fac[at, to].astype(F32)).astype(BF16)
            fac[at, to] = low
            hidden_sums[:, to] += fold8(low.astype(F32))
            return carry

        count = line // span // 4
        lax.fori_loop(n * count, (n + 1) * count, some, 0)

    def back_partial(src, rows_at, groups, blocks, dst):
        lanes = len(groups[0]) * blocks * PAIR

        def back(n, carry):
            total = None
            for k, group in enumerate(groups):
                part = columns([w[u, b, pl.ds(n * span, span)] for u in group for b in range(blocks)])
                term = dot_cols(src[rows_at, k * lanes : (k + 1) * lanes], part)
                total = term if total is None else total + term
            dst[:, pl.ds(pl.multiple_of(n * part_rows, part_rows), part_rows)] = total
            return carry

        lax.fori_loop(0, line // span, back, 0)

    def expand_grad(n):
        u, first, _ = blocks_of(4 + n)
        put(u, first, dot(tr[...], fac[:, n * tile : (n + 1) * tile]))

    def to_x(came):
        def some(i, carry):
            at = chunks(0, i)
            cot_own[at, :] = (keep_p[at, :] + came[at, :]).astype(BF16)
            return carry

        lax.fori_loop(0, own // chunk, some, 0)

    ff = ((4, 5),)

    def hidden_partial(chip, dst):
        back_partial(fac, pl.ds(pl.multiple_of(chip * rows, rows), rows), ff, BLOCKS, dst)

    def hidden_partials(own_image):
        if own_image:
            hidden_partial(x, part_a)
            a_copy.start()
        else:
            hidden_partial(1 - x, part_b)
            b_copy.start()

    def partial_over_x():
        to_x(recv_b)
        for copy in x_back:
            copy.start()

    zeros8 = jnp.zeros((8, width), F32)

    def second_norm_back():
        def some(i, carry):
            at = chunks(0, i)
            unit, rstd = unit_rows(resid[at, :])
            came = o_blk[i // 2, pl.ds(pl.multiple_of(i % 2 * chunk, chunk), chunk)].astype(F32)
            gn = own_p[at, :] + recv_a[at, :] + came
            grad_out = go[chunks(x * rows + c * own, i), :].astype(F32)
            gr = grad_out + norm_back(gn, unit, rstd, vec[2:3, :])
            own_p[at, :] = gr
            low = gr.astype(BF16)
            gb[chunks(c * own, i), :] = low
            a, b, e, f = carry
            return (a + fold8(gn * unit), b + fold8(gn), e + fold8(low.astype(F32)), f + fold8(grad_out))

        vg[...] = jnp.zeros_like(vg)
        vg[pl.ds(8 + s, 1), :] = jnp.sum(hidden_sums[...], 0, keepdims=True)
        sums = lax.fori_loop(0, own // chunk, some, (zeros8,) * 4)
        for row, v in zip((2, 3, 6, 7), sums):
            vg[row : row + 1, :] = jnp.sum(v, 0, keepdims=True)
        gb_copy.start()

    def grad_attended(n):
        if n == 0:
            for copy in n2_copies:
                copy.wait_send()
        quarter = line // 4
        head_rows = pl.ds(c * (line // 2) + n * quarter, quarter)
        part = dot_cols(gb[:, my_half], own_out(head_rows)) + dot_cols(gb[:, oth_half], oth_out(head_rows))
        n2[:rows, n * tile : (n + 1) * tile] = part.astype(BF16)

    def attend_backward(p, first, last):
        q_at, k_at, v_at = pair_lanes(p)
        own_lanes = slice(p * PAIR, (p + 1) * PAIR)
        if first == 0:
            dk_acc[...] = jnp.zeros_like(dk_acc)
            dv_acc[...] = jnp.zeros_like(dv_acc)

        def some(j, carry):
            at = pl.ds(pl.multiple_of(j * PAIR, PAIR), PAIR)
            both = two_heads(qkv[at, q_at])
            grads = two_heads(n2[at, own_lanes])
            mask = kbias[...]
            scores = dot_cols(qkv[:, k_at], both) + jnp.concatenate([mask, mask], 1)
            chance = jnp.exp(scores - lse[pl.ds(p * q_chunks + j, 1), :])
            dv_acc[...] += dot(chance.astype(BF16), grads)
            grad_chance = dot_cols(qkv[:, v_at], grads)
            inner = jnp.sum(chance * grad_chance, 0, keepdims=True)
            grad_scores = (chance * (grad_chance - inner)).astype(BF16)
            dk_acc[...] += dot(grad_scores, both)
            out = dot_rows(qkv[:, k_at], grad_scores)
            out = jnp.where(low_row, out[:, :PAIR], out[:, PAIR:]) * HEAD_DIM**-0.5
            qkv[at, q_at] = out.T.astype(BF16)
            return carry

        lax.fori_loop(first, last, some, 0)
        if last < q_chunks:
            return
        qkv[:, k_at] = dk_acc[...].astype(BF16)
        qkv[:, v_at] = dv_acc[...].astype(BF16)
        vg[4:5, att_lanes(p)] = jnp.sum(fold8(qkv[:, q_at].astype(F32)), 0, keepdims=True)
        vg[5:6, att_lanes(p)] = jnp.sum(fold8(qkv[:, v_at].astype(F32)), 0, keepdims=True)

    def attention_grad(p):
        put(p, 0, dot(tr[:, :rows], qkv[:, p * qkv_lanes : (p + 1) * qkv_lanes]))
        put(p, BLOCKS - 1, dot(tr[:, rows:], gb[:, att_lanes(p)]))

    def input_partial():
        back_partial(qkv, slice(0, rows), ((0, 1), (2, 3)), 3, part_b)
        p1_copy.start()

    def first_norm_back():
        def some(i, carry):
            at = chunks(0, i)
            unit, rstd = unit_rows(tok_own[at, :].astype(F32))
            gn = keep_p[at, :] + recv_a[at, :]
            out = own_p[at, :] + norm_back(gn, unit, rstd, vec[0:1, :])
            tok_own[at, :] = out.astype(BF16)
            a, b = carry
            return (a + fold8(gn * unit), b + fold8(gn))

        sums = lax.fori_loop(0, own // chunk, some, (zeros8,) * 2)
        for row, v in zip((0, 1), sums):
            vg[row : row + 1, :] = jnp.sum(v, 0, keepdims=True)
        o_tok[x] = tok_own[my_block, :]
        tok_copy.start()

    def branch(dst, rows_at, add):
        def out(n, carry):
            for j in range(2):
                part = columns([w[6 + j, 2 * n], w[6 + j, 2 * n + 1]])
                to = pl.ds(pl.multiple_of(j * UNIT + n * tile, tile), tile)
                total = dot(act[rows_at, :], part)
                dst[:, to] = dst[:, to] + total if add else total
            return carry

        lax.fori_loop(0, UNIT // tile, out, 0)

    def output_partial(n):
        if n == 0:
            branch(part_b, pl.ds(pl.multiple_of((1 - x) * rows, rows), rows), False)
            bm_copy.start()
        elif n == 2:
            branch(send_a, ff_rows(x, 1 - c), False)
            am_copy.start()
        else:
            branch(resid, ff_rows(x, c), True)

    def output_over_x():
        to_x(recv_m)
        xm_copy.start()

    def finish_block():
        def some(i, carry):
            at = chunks(0, i)
            out = resid[at, :] + recv_b[at, :] + x_recv_m[at, :].astype(F32) + vec[7:8, :]
            cot_own[at, :] = (live(chunks(c * own, i)) * out).astype(BF16)
            return carry

        lax.fori_loop(0, own // chunk, some, 0)
        o_blk[x] = cot_own[my_block, :]
        blk_copy.start()

    v_copies = [
        remote(vg, vr.at[n], vs.at[0, 1 + n], vs.at[1, 1 + n], to) for n, to in enumerate((sibling, x_neigh, y_neigh))
    ]

    def vector_hop(n):
        if n < 3:
            v_copies[n].start()
            return

        def send(o, carry):
            remote(vg, vz.at[zi], vs.at[0, 4], vs.at[1, 4], (lax.rem(zi + o, line) * 2 + yi, s)).start()
            return carry

        lax.fori_loop(1, line, send, 0)
        vz[zi] = vg[...]

    def vector_add(n):
        if n < 3:
            v_copies[n].wait()
            vg[...] += vr[n]
            return
        wait_bytes(vz.at[pl.ds(0, line - 1)], vs.at[1, 4])
        wait_bytes(vz.at[pl.ds(0, line - 1)], vs.at[0, 4])

    def vector_out():
        o_vec[...] = lax.fori_loop(1, line, lambda i, t: t + vz[i], vz[0])

    def both(*copies):
        for copy in copies:
            copy.wait()

    def received(*copies):
        for copy in copies:
            copy.wait_recv()

    def relay(copies):
        copies[1].wait_recv()
        copies[2].start()

    def relay_go():
        wait_bytes(go_bytes, xe.at[1, 4])
        for copy in go_copies[2]:
            copy.start()

    def all_rows():
        received(n2_copies[2])
        wait_bytes(go_bytes, loc.at[1])
        wait_bytes(go_bytes, sib.at[1, 4])
        wait_bytes(go_bytes, sib.at[1, 5])

    waits = dict(
        vec=lambda: wait_bytes(vec_all.at[pl.ds(0, dp_n - 1)], vs.at[1, 0]),
        tok=lambda: both(tok_copy_x, tok_copy_in),
        cot=lambda: None,
        n1=lambda: received(n1_copy),
        gox=relay_go,
        att=lambda: received(*[wo_copy(p) for p in range(4)], att_copy),
        n2=lambda: received(n2_copies[0]),
        n2x=lambda: relay(n2_copies),
        n2r=all_rows,
        b=lambda: both(b_copy),
        a=lambda: both(a_copy),
        xb=lambda: both(*x_back),
        gb=lambda: received(gb_copy),
        p1=lambda: both(p1_copy),
        bm=lambda: both(bm_copy),
        am=lambda: both(am_copy),
        xm=lambda: both(xm_copy),
        v0=lambda: vector_add(0),
        v1=lambda: vector_add(1),
        v2=lambda: vector_add(2),
        v3=lambda: vector_add(3),
    )
    split = 3
    work = dict(
        vec=lambda n: vector(),
        ln1=lambda n: first_norm(),
        go=lambda n: grad_output(),
        qkv=project,
        afa=lambda p: attend_forward(p, 0, split),
        afb=lambda p: attend_forward(p, split, q_chunks),
        out=lambda n: output_projection(),
        ln2=lambda n: second_norm(),
        eo=lambda n: expand(n, x),
        ex=lambda n: expand(n, 1 - x),
        tra=lambda n: transpose_into(tr, 0, act, 2 * rows),
        gs=shrink_grad,
        hx=lambda n: hidden_back(n, 1 - x, n == 0),
        hb=lambda n: hidden_back(n, x, False),
        bpx=lambda n: hidden_partials(False),
        tox=lambda n: partial_over_x(),
        bpo=lambda n: hidden_partials(True),
        trn=lambda n: transpose_into(tr, 0, n2, 2 * rows),
        gx=expand_grad,
        ln2b=lambda n: second_norm_back(),
        trb=lambda n: (transpose_into(tr, 0, n1, rows), transpose_into(tr, rows, att, rows)),
        gat=grad_attended,
        aba=lambda p: attend_backward(p, 0, split),
        abb=lambda p: attend_backward(p, split, q_chunks),
        ga=attention_grad,
        b1=lambda n: input_partial(),
        ln1b=lambda n: first_norm_back(),
        brx=lambda n: output_partial(0),
        tox2=lambda n: output_over_x(),
        br2=lambda n: output_partial(2),
        br3=lambda n: output_partial(3),
        v0=lambda n: vector_hop(0),
        v1=lambda n: vector_hop(1),
        v2=lambda n: vector_hop(2),
        v3=lambda n: vector_hop(3),
        fin=lambda n: finish_block(),
        ov=lambda n: vector_out(),
    )
    for kind, name, n in ORDER:
        if kind == "C":
            work[name](n)
        elif kind == "W":
            waits[name]()
        elif kind == "A":
            gather_stages[n](name)
        elif kind == "I":
            rs_start(name)
        else:
            rs_stage(name, n)

    blk_copy.wait()
    tok_copy.wait()
    wait_bytes(vec_all.at[pl.ds(0, dp_n - 1)], vs.at[0, 0])
    for sem in (sib.at[0, 4], sib.at[0, 5], xe.at[0, 4]):
        wait_bytes(go_bytes, sem)
    for copy in [n1_copy, att_copy, gb_copy] + [wo_copy(p) for p in range(4)]:
        copy.wait_send()
    for i in range(ITEMS):
        wait_bytes(z_bytes(i), ag.at[0, i])
        ag_y_copy(i).wait_send()
        if i >= FIRST_EDGE:
            ag_x_copy(i).wait_send()


def adamw(grad, moment, square, weight, rate, decay):
    momentum = BETA_ONE * moment + (1.0 - BETA_ONE) * grad
    variance = BETA_TWO * square + (1.0 - BETA_TWO) * grad * grad
    first_fix = 1.0 - BETA_ONE**STEP
    second_fix = 1.0 - BETA_TWO**STEP
    direction = momentum / first_fix / (jnp.sqrt(variance / second_fix) + EPS_ADAM)
    updated = weight - rate * (direction + decay * weight)
    return (momentum, variance, updated, updated.astype(BF16))


def body(
    tokens, cotangent, key_mask,
    attention_weights, expand_weights, shrink_weights, vector_params,
    attention_moment, attention_square, expand_moment, expand_square,
    shrink_moment, shrink_square, vector_moment, vector_square,
):
    dp_n = lax.axis_size("dp")
    line = dp_n // 2
    d = lax.axis_index("dp")
    place = lax.axis_index("seq")
    x, c = place // 2, place % 2
    _, local_len, width = tokens.shape
    r = width // dp_n
    block = -(-local_len // 16) * 16
    own, rows = 2 * block, 4 * block
    pad = ((0, 0), (0, block - local_len), (0, 0))

    keep = lax.dynamic_index_in_dim(key_mask, x, 0, keepdims=False).reshape(2, 2, local_len)
    keep = jnp.pad(keep.transpose(1, 0, 2), ((0, 0), (0, 0), pad[1])).reshape(2, own)
    kbias = jnp.broadcast_to(jnp.where(keep > 0, 0.0, -1e30).astype(F32).reshape(rows, 1), (rows, PAIR))
    p_exp = expand_weights
    if r % 128:
        p_exp = lax.dynamic_index_in_dim(expand_weights.reshape(r, dp_n, 4, r), place, 2, keepdims=False)
        p_exp = p_exp.reshape(r, 2, BLOCKS, PAIR).transpose(1, 2, 0, 3)
    vec_len = vector_params.shape[0]
    here = lax.dynamic_slice_in_dim(key_mask, place * local_len, local_len, 1)
    grad_out = jnp.where(here[:, :, None] > 0, cotangent, jnp.zeros_like(cotangent))
    vec_rows = -(-vec_len // 1024) * 8
    p_vec = jnp.pad(vector_params.astype(BF16).astype(F32), (0, vec_rows * 128 - vec_len)).reshape(vec_rows, 128)

    vmem = pl.BlockSpec(memory_space=pltpu.VMEM)
    hbm = pl.BlockSpec(memory_space=pl.ANY)
    padded = jax.ShapeDtypeStruct((2, block, width), BF16)
    o_blk, o_tok, o_att, o_exp, o_shr, o_vec = pl.pallas_call(
        functools.partial(layer_kernel, line, vec_len),
        out_shape=(
            padded,
            padded,
            jax.ShapeDtypeStruct((r, 4 * width), BF16),
            jax.ShapeDtypeStruct((2, 4, BLOCKS, r, PAIR) if r % 128 else (r, 4 * width), BF16),
            jax.ShapeDtypeStruct((4 * r, width), BF16),
            jax.ShapeDtypeStruct((16, width), F32),
        ),
        in_specs=[hbm, hbm, vmem, vmem, hbm, hbm, hbm],
        out_specs=(vmem, vmem, hbm, hbm, hbm, vmem),
        scratch_shapes=[
            pltpu.VMEM((UNITS, BLOCKS, line, 2, r, PAIR), BF16),
            pltpu.VMEM((4, line, 2, r, PAIR), BF16),
            pltpu.VMEM((UNITS, BLOCKS, line, 2, r, PAIR), BF16),
            pltpu.VMEM((4, line, 2, r, PAIR), BF16),
            pltpu.VMEM((FIRST_EDGE, HALF, line, r, PAIR), BF16),
            pltpu.VMEM((FIRST_EDGE, line - 1, HALF, r, PAIR), BF16),
            pltpu.VMEM((4, 1, line, r, PAIR), BF16),
            pltpu.VMEM((4, line - 1, 1, r, PAIR), BF16),
            pltpu.VMEM((4, HALF, r, PAIR), BF16),
            pltpu.VMEM((4, HALF, r, PAIR), BF16),
            pltpu.VMEM((UNITS, BLOCKS, r, PAIR), BF16),
            pltpu.VMEM((8, HALF, r, PAIR), BF16),
            pltpu.VMEM((dp_n, vec_rows, 128), F32),
            pltpu.VMEM((16, width), F32),
            pltpu.VMEM((1, width), F32),
            pltpu.VMEM((16, width), F32),
            pltpu.VMEM((3, 16, width), F32),
            pltpu.VMEM((line, 16, width), F32),
            pltpu.VMEM((8, width), F32),
            pltpu.VMEM((own, width), BF16),
            pltpu.VMEM((own, width), BF16),
            pltpu.VMEM((rows, width), BF16),
            pltpu.VMEM((2 * rows, width), BF16),
            pltpu.VMEM((rows, 3 * UNIT), BF16),
            pltpu.VMEM((rows, width), BF16),
            pltpu.VMEM(((rows // PAIR) * (UNIT // PAIR), 2 * PAIR), F32),
            pltpu.VMEM((own, width), F32),
            pltpu.VMEM((2 * rows, width), BF16),
            pltpu.VMEM((2 * rows, width), BF16),
            pltpu.VMEM((2 * rows, width), BF16),
        ]
        + [pltpu.VMEM((rows, width), F32)] * 2
        + [pltpu.VMEM((own, width), F32)] * 3
        + [
            pltpu.VMEM((own, width), BF16),
            pltpu.VMEM((rows, width), BF16),
            pltpu.VMEM((width, 2 * rows), BF16),
            pltpu.VMEM((rows, PAIR), F32),
            pltpu.VMEM((rows, PAIR), F32),
            pltpu.SemaphoreType.DMA((6, ITEMS)),
            pltpu.SemaphoreType.DMA((14, ITEMS)),
            pltpu.SemaphoreType.DMA((2, 12)),
            pltpu.SemaphoreType.DMA((2, 4)),
            pltpu.SemaphoreType.DMA((2, 10)),
            pltpu.SemaphoreType.DMA((2, 5)),
            pltpu.SemaphoreType.DMA((UNITS, 2)),
            pltpu.SemaphoreType.DMA((2,)),
        ],
        compiler_params=pltpu.CompilerParams(
            collective_id=0, has_side_effects=True, vmem_limit_bytes=VMEM_LIMIT
        ),
        name="layer",
    )(jnp.pad(tokens, pad), jnp.pad(grad_out, pad), kbias, p_vec, attention_weights, p_exp, shrink_weights)

    block_output = jnp.where(here[:, :, None] > 0, o_blk[:, :local_len], jnp.zeros_like(tokens))
    token_gradient = jnp.where(here[:, :, None] > 0, o_tok[:, :local_len], jnp.zeros_like(tokens))
    grad_attention, grad_shrink = o_att.astype(F32), o_shr.astype(F32)
    if r % 128:
        o_exp = o_exp.transpose(3, 1, 0, 2, 4).reshape(r, 4, dp_n, r).transpose(0, 2, 1, 3).reshape(r, 4 * width)
    grad_expand = o_exp.astype(F32)
    hidden_sums = o_vec[8:12].reshape(4, dp_n, r).transpose(1, 0, 2).reshape(4, width)
    grad_vector = jnp.concatenate([o_vec[0:8], hidden_sums], 0).reshape(dp_n, vec_len)
    grad_vector = lax.dynamic_index_in_dim(grad_vector, d, 0, keepdims=False)

    attention_out = adamw(
        grad_attention, attention_moment, attention_square, attention_weights, RATE_MATRIX, DECAY_MATRIX
    )
    expand_out = adamw(grad_expand, expand_moment, expand_square, expand_weights, RATE_MATRIX, DECAY_MATRIX)
    shrink_out = adamw(grad_shrink, shrink_moment, shrink_square, shrink_weights, RATE_MATRIX, DECAY_MATRIX)
    vector_out = adamw(grad_vector, vector_moment, vector_square, vector_params, RATE_VECTOR, 0.0)
    return (block_output, token_gradient, *attention_out, *expand_out, *shrink_out, *vector_out)


VMEM_LIMIT = 63 * 2**20

ORDER = (
    ("A", 12, 0), ("A", 0, 0), ("A", 13, 0), ("A", 1, 0), ("A", 14, 0), ("A", 2, 0), ("C", "go", 0), ("W", "vec", 0),
    ("C", "vec", 0), ("A", 12, 1), ("W", "tok", 0), ("C", "ln1", 0), ("A", 12, 2), ("A", 0, 1), ("A", 15, 0),
    ("A", 3, 0), ("A", 13, 1), ("A", 0, 2), ("A", 1, 1), ("A", 4, 0), ("A", 13, 2), ("A", 14, 1), ("A", 5, 0),
    ("W", "gox", 0), ("A", 1, 2), ("A", 2, 1), ("A", 6, 0), ("A", 12, 3), ("W", "n1", 0), ("C", "qkv", 0),
    ("A", 14, 2), ("A", 15, 1), ("C", "afa", 0), ("C", "afb", 0), ("A", 13, 3), ("C", "qkv", 1), ("A", 2, 2),
    ("C", "afa", 1), ("A", 3, 1), ("A", 7, 0), ("C", "afb", 1), ("A", 15, 2), ("A", 14, 3), ("C", "qkv", 2),
    ("C", "afa", 2), ("A", 4, 1), ("A", 8, 0), ("C", "afb", 2), ("A", 3, 2), ("A", 15, 3), ("C", "qkv", 3),
    ("C", "afa", 3), ("A", 5, 1), ("A", 9, 0), ("C", "afb", 3), ("A", 4, 2), ("W", "att", 0), ("C", "out", 0),
    ("A", 6, 1), ("A", 10, 0), ("C", "ln2", 0), ("A", 5, 2), ("A", 7, 1), ("A", 11, 0), ("W", "n2", 0),
    ("C", "eo", 0), ("C", "eo", 1), ("A", 6, 2), ("C", "eo", 2), ("A", 8, 1), ("A", 7, 2), ("C", "eo", 3),
    ("A", 9, 1), ("W", "n2x", 0), ("A", 8, 2), ("W", "n2r", 0), ("C", "ex", 0), ("A", 10, 1), ("C", "ex", 1),
    ("C", "ex", 2), ("A", 9, 2), ("C", "ex", 3), ("C", "tra", 0), ("A", 11, 1), ("C", "gs", 3), ("I", 11, 0),
    ("A", 10, 2), ("C", "gs", 0), ("I", 8, 0), ("C", "gs", 1), ("I", 9, 0), ("C", "gs", 2), ("A", 11, 2),
    ("C", "hx", 0), ("C", "hx", 1), ("C", "hx", 2), ("C", "hx", 3), ("C", "bpx", 0), ("R", 11, 0), ("I", 10, 0),
    ("C", "hb", 0), ("C", "hb", 1), ("C", "hb", 2), ("C", "hb", 3), ("R", 8, 0), ("C", "bpo", 0), ("R", 11, 1),
    ("W", "b", 0), ("C", "tox", 0), ("C", "trn", 0), ("R", 9, 0), ("C", "gx", 0), ("R", 11, 2), ("R", 8, 1),
    ("I", 4, 0), ("C", "gx", 1), ("R", 11, 3), ("R", 10, 0), ("I", 5, 0), ("C", "gx", 2), ("I", 6, 0), ("C", "gx", 3),
    ("R", 9, 1), ("C", "trb", 0), ("R", 4, 0), ("I", 7, 0), ("C", "brx", 0), ("R", 10, 1), ("W", "a", 0),
    ("W", "xb", 0), ("C", "ln2b", 0), ("R", 8, 2), ("R", 9, 2), ("R", 10, 2), ("R", 4, 1), ("R", 5, 0),
    ("W", "bm", 0), ("C", "tox2", 0), ("W", "gb", 0), ("C", "gat", 0), ("R", 8, 3), ("R", 9, 3), ("R", 6, 0),
    ("R", 10, 3), ("C", "gat", 1), ("R", 4, 2), ("C", "aba", 0), ("R", 4, 3), ("C", "abb", 0), ("R", 5, 1),
    ("R", 7, 0), ("C", "aba", 1), ("C", "abb", 1), ("C", "aba", 2), ("R", 6, 1), ("C", "ga", 0), ("I", 12, 0),
    ("I", 0, 0), ("C", "ga", 1), ("R", 5, 2), ("R", 6, 2), ("R", 7, 1), ("I", 13, 0), ("I", 1, 0), ("C", "abb", 2),
    ("R", 5, 3), ("R", 6, 3), ("C", "aba", 3), ("R", 12, 0), ("R", 0, 0), ("C", "ga", 2), ("R", 7, 2), ("I", 14, 0),
    ("I", 2, 0), ("C", "abb", 3), ("R", 7, 3), ("R", 1, 0), ("C", "b1", 0), ("R", 12, 1), ("R", 0, 1), ("R", 13, 0),
    ("C", "ga", 3), ("I", 15, 0), ("I", 3, 0), ("R", 14, 0), ("C", "br2", 0), ("R", 0, 2), ("R", 1, 1), ("R", 2, 0),
    ("W", "p1", 0), ("C", "ln1b", 0), ("R", 12, 2), ("R", 13, 1), ("C", "v0", 0), ("C", "br3", 0), ("R", 0, 3),
    ("R", 15, 0), ("W", "v0", 0), ("C", "v1", 0), ("W", "am", 0), ("W", "xm", 0), ("C", "fin", 0), ("R", 1, 2),
    ("R", 3, 0), ("R", 2, 1), ("R", 1, 3), ("R", 14, 1), ("W", "v1", 0), ("C", "v2", 0), ("R", 13, 2), ("R", 15, 1),
    ("R", 12, 3), ("W", "v2", 0), ("C", "v3", 0), ("R", 12, 4), ("R", 3, 1), ("R", 14, 2), ("R", 15, 2), ("R", 2, 2),
    ("R", 13, 3), ("R", 3, 2), ("R", 2, 3), ("R", 13, 4), ("R", 14, 3), ("R", 15, 3), ("W", "v3", 0), ("C", "ov", 0),
    ("R", 3, 3), ("R", 14, 4), ("R", 15, 4),
)


def solution(mesh):
    split = P("dp", "seq", None)
    rows = P("dp", None)
    flat = P("dp")
    return jax.shard_map(
        body,
        mesh=mesh,
        in_specs=(split, split, rows, rows, rows, rows, flat) + (rows,) * 6 + (flat, flat),
        out_specs=(split, split) + (rows,) * 12 + (flat,) * 4,
        check_vma=False,
    )
```

```python
import functools

import jax
import jax.numpy as jnp
from jax import lax
from jax.experimental import pallas as pl
from jax.experimental.pallas import tpu as pltpu
from jax.sharding import PartitionSpec as P

HEAD_DIM = 64
STEP = 5
EPS_NORM = 1e-05
BETA_ONE = 0.5
BETA_TWO = 0.5
EPS_ADAM = 1e-08
RATE_MATRIX = 0.05
RATE_VECTOR = 0.2
DECAY_MATRIX = 0.1
SLOPE = 1.702

BF16 = jnp.bfloat16
F32 = jnp.float32
MESH = pl.DeviceIdType.MESH

UNIT = 512
BLOCKS = 4
EDGE = BLOCKS - 1
HALF = 2
UNITS = 8
ITEMS = 16
FIRST_EDGE = 12
PAIR = 128


def dot(a, b):
    return jnp.dot(a, b, preferred_element_type=F32)


def dot_rows(a, b):
    return lax.dot_general(a, b, (((0,), (0,)), ((), ())), preferred_element_type=F32)


def dot_cols(a, b):
    return lax.dot_general(a, b, (((1,), (1,)), ((), ())), preferred_element_type=F32)


def unit_rows(x):
    centred = x - jnp.mean(x, -1, keepdims=True)
    rstd = lax.rsqrt(jnp.mean(centred * centred, -1, keepdims=True) + EPS_NORM)
    return centred * rstd, rstd


def norm_back(grad_normed, unit, rstd, gain):
    g = grad_normed * gain
    return rstd * (g - jnp.mean(g, -1, keepdims=True) - unit * jnp.mean(g * unit, -1, keepdims=True))


def fold8(v):
    return jnp.sum(v.reshape(v.shape[0] // 8, 8, v.shape[1]), 0)


def layer_kernel(
    line, vec_len,
    tok, cot, mask_row, p_vec, p_att, p_exp, p_shr,
    o_blk, o_tok, o_att, o_exp, o_shr, o_vec,
    w, w_oth, g, rx, ry, rz, ry_e, rz_e, s_own, s_oth, f_own, f_oth,
    vec_all, vec, bias_h, vg, vr, vz, hidden_sums,
    tok_own, cot_own,
    n1, go, qkv, att, lse, resid, n2, act, fac,
    part_a, part_b, recv_a, recv_b, recv_m, x_recv_m,
    gb, tr, dk_acc, dv_acc, flipped, kbias,
    ag, rs, sib, wo, xe, vs, fill, loc,
):
    dp_n = 2 * line
    r = w.shape[4]
    block = tok.shape[1]
    own = 2 * block
    rows = 2 * own
    width = tok.shape[2]
    half = UNIT
    d = lax.axis_index("dp")
    s = lax.axis_index("seq")
    zi, yi = d // 2, d % 2
    x, c = s // 2, s % 2
    sibling = (d, x * 2 + 1 - c)
    x_neigh = (d, (1 - x) * 2 + c)
    y_neigh = (zi * 2 + 1 - yi, s)

    def z_peer(o):
        return (lax.rem(zi + o, line) * 2 + yi, s)

    def own_rows(core):
        return pl.ds(pl.multiple_of(core * own, own), own)

    def ff_rows(chip, core):
        return pl.ds(pl.multiple_of(chip * rows + core * own, own), own)

    my_rows = own_rows(c)
    own_p, send_a = part_a.at[own_rows(c)], part_a.at[own_rows(1 - c)]
    keep_p, send_b = part_b.at[own_rows(c)], part_b.at[own_rows(1 - c)]
    my_half = pl.ds(pl.multiple_of(c * half, half), half)
    oth_half = pl.ds(pl.multiple_of((1 - c) * half, half), half)
    my_block = pl.ds(pl.multiple_of(x * block, block), block)
    oth_block = pl.ds(pl.multiple_of((1 - x) * block, block), block)

    mine, theirs = x * EDGE, (1 - x) * EDGE

    def blocks_of(i):
        if i < 4:
            return i, 1, HALF
        if i < FIRST_EDGE:
            return 4 + (i - 4) // 2, (i - 4) % 2 * HALF, HALF
        return i - FIRST_EDGE, mine, 1

    def item(ref, i):
        u, first, count = blocks_of(i)
        return ref.at[u, pl.ds(first, count)]

    def remote(src, dst, send, recv, to):
        return pltpu.make_async_remote_copy(
            src_ref=src, dst_ref=dst, send_sem=send, recv_sem=recv, device_id=to, device_id_type=MESH
        )

    def wait_bytes(ref, sem):
        pltpu.make_async_copy(ref, ref, sem).wait()

    wide = r % 128 == 0

    def unit_parts(u, place):
        if u < 4:
            core = place % 2
            return [
                (slice(None), pl.ds(pl.multiple_of(n * width + core * half + u * PAIR, PAIR), PAIR)) for n in range(BLOCKS)
            ]
        if u < 6:
            if not wide:
                return None
            parts = []
            for n in range((u - 4) * UNIT, (u - 3) * UNIT, PAIR):
                at = n // r * 4 * r + place * r + n % r
                parts.append((slice(None), pl.ds(pl.multiple_of(at, PAIR), PAIR)))
            return parts
        first = (u - 6) * UNIT
        held = pl.ds(pl.multiple_of(place * r, r), r)
        return [(held, slice(first + n * PAIR, first + (n + 1) * PAIR)) for n in range(BLOCKS)]

    def stage(u):
        n = u % 4 if u < 4 else u % 2
        hold, first = (part_a, 0) if u < 4 else (part_b, u // 6 * r)
        first = first + n // 2 * r
        return hold.at[first : first + r, (n % 2) * UNIT : (n % 2 + 1) * UNIT]

    def matrix(u, refs):
        return refs[0 if u < 4 else 1 if u < 6 else 2]

    for u in range(UNITS):
        parts = unit_parts(u, s)
        source = matrix(u, (p_att, p_exp, p_shr))
        for n in range(BLOCKS):
            part = source.at[parts[n]] if parts else source.at[u - 4, n]
            pltpu.make_async_copy(part, stage(u).at[:, n * PAIR : (n + 1) * PAIR], fill.at[u, n // HALF if u >= 4 else int(n in (0, EDGE))]).start()

    vec_all[d] = p_vec[...]
    tok_copy_in = pltpu.make_async_copy(tok.at[x], tok_own.at[my_block], loc.at[0])
    tok_copy_in.start()

    def go_rows(chip, place):
        return pl.ds(pl.multiple_of(chip * rows + place % 2 * own + place // 2 * block, block), block)

    go_local = [pltpu.make_async_copy(cot.at[n], go.at[go_rows(n, s)], loc.at[1]) for n in range(2)]
    for copy in go_local:
        copy.start()

    barrier = pltpu.get_barrier_semaphore()

    def greet(o, carry):
        pl.semaphore_signal(barrier, inc=1, device_id=(lax.rem(d + o, dp_n), s), device_id_type=MESH)
        return carry

    lax.fori_loop(1, dp_n, greet, 0)
    pl.semaphore_signal(barrier, inc=1, device_id=sibling, device_id_type=MESH)
    pl.semaphore_signal(barrier, inc=1, device_id=x_neigh, device_id_type=MESH)
    pl.semaphore_wait(barrier, dp_n + 1)

    def send_vec(o, carry):
        remote(p_vec, vec_all.at[d], vs.at[0, 0], vs.at[1, 0], (lax.rem(d + o, dp_n), s)).start()
        return carry

    lax.fori_loop(1, dp_n, send_vec, 0)
    tok_copy_x = remote(tok.at[1 - x], tok_own.at[my_block], xe.at[0, 0], xe.at[1, 0], x_neigh)
    tok_copy_x.start()
    other = (1 - x) * 2 + c
    go_copies = [
        [remote(cot.at[n], go.at[go_rows(n, s)], sib.at[0, 4], sib.at[1, 4], sibling) for n in range(2)],
        [remote(cot.at[n], go.at[go_rows(n, s)], xe.at[0, 4], xe.at[1, 4], x_neigh) for n in range(2)],
        [remote(go.at[go_rows(n, other)], go.at[go_rows(n, other)], sib.at[0, 5], sib.at[1, 5], sibling) for n in range(2)],
    ]
    go_bytes = go.at[:own]

    def ag_z(i):
        u, first, count = blocks_of(i)
        group = first // HALF if 4 <= i < FIRST_EDGE else int(i >= FIRST_EDGE)
        wait_bytes(stage(u).at[:, : HALF * PAIR], fill.at[u, group])
        for n in range(count):
            w[u, first + n, zi, yi] = stage(u)[:, pl.ds(pl.multiple_of((first + n) * PAIR, PAIR), PAIR)].astype(BF16)
        part = item(w, i).at[:, zi, yi]
        for o in range(1, line):
            remote(part, part, ag.at[0, i], ag.at[1, i], z_peer(o)).start()

    def ag_y_copy(i):
        part = item(w, i).at[:, :, yi]
        return remote(part, part, ag.at[2, i], ag.at[3, i], y_neigh)

    def ag_x_copy(i):
        return remote(item(w, i), item(w, i), ag.at[4, i], ag.at[5, i], x_neigh)

    def z_bytes(i):
        return item(w, i).at[:, pl.ds(0, line - 1), yi]

    def ag_y(i):
        wait_bytes(z_bytes(i), ag.at[1, i])
        ag_y_copy(i).start()

    def ag_x(i):
        ag_y_copy(i).wait_recv()
        if i >= FIRST_EDGE:
            ag_x_copy(i).start()

    def ag_end(i):
        ag_x_copy(i).wait_recv()

    gather_stages = [ag_z, ag_y, ag_x, ag_end]

    grain = 128 if vec_len % 128 == 0 else 64

    def vec_lanes(first):
        parts = []
        for e in range(first, first + 128, grain):
            o = e % vec_len
            parts.append(vec_all[e // vec_len, o // 128 : o // 128 + 1, o % 128 : o % 128 + grain])
        return parts[0] if len(parts) == 1 else jnp.concatenate(parts, 1)

    def hidden_bias(place):
        parts = []
        for shard in range(dp_n):
            n = shard * 4 * r + place * r
            parts.append(vec[8 + n // width : 9 + n // width, n % width : n % width + r])
        return jnp.concatenate(parts, 1)

    def vector():
        kbias[...] = jnp.broadcast_to(mask_row[...], (PAIR, rows)).T
        for row in range(12):
            for lane in range(0, width, 128):
                vec[row : row + 1, lane : lane + 128] = vec_lanes(row * width + lane)
        low_half = jnp.where(s == 0, hidden_bias(0), hidden_bias(1))
        bias_h[...] = jnp.where(s < 2, low_half, jnp.where(s == 2, hidden_bias(2), hidden_bias(3)))

    def live(to):
        return jnp.where(kbias[to, 0:1] < 0, 0.0, 1.0)

    chunk = block // 2

    def chunks(first, i):
        return pl.ds(pl.multiple_of(first + i * chunk, chunk), chunk)

    def first_norm():
        def some(i, carry):
            unit, _ = unit_rows(tok_own[chunks(0, i), :].astype(F32))
            n1[chunks(c * own, i), :] = (unit * vec[0:1, :] + vec[1:2, :]).astype(BF16)
            return carry

        lax.fori_loop(0, own // chunk, some, 0)
        n1_copy.start()

    def grad_output():
        for copy in go_copies[1] + go_copies[0]:
            copy.start()

    def rows_copies(ref, n):
        here, there = ref.at[ff_rows(x, c)], ref.at[ff_rows(1 - x, c)]
        return (
            remote(here, here, sib.at[0, n], sib.at[1, n], sibling),
            remote(here, here, xe.at[0, n], xe.at[1, n], x_neigh),
            remote(there, there, sib.at[0, n + 1], sib.at[1, n + 1], sibling),
        )

    n1_copy = remote(n1.at[my_rows], n1.at[my_rows], sib.at[0, 0], sib.at[1, 0], sibling)
    att_copy = remote(att.at[:, my_half], att.at[:, my_half], sib.at[0, 1], sib.at[1, 1], sibling)
    gb_copy = remote(gb.at[my_rows], gb.at[my_rows], sib.at[0, 2], sib.at[1, 2], sibling)
    p1_copy = remote(send_b, recv_a, sib.at[0, 3], sib.at[1, 3], sibling)
    n2_copies = rows_copies(n2, 6)
    b_copy = remote(send_b, recv_b, sib.at[0, 8], sib.at[1, 8], sibling)
    a_copy = remote(send_a, recv_a, sib.at[0, 9], sib.at[1, 9], sibling)
    bm_copy = remote(send_b, recv_m, sib.at[0, 10], sib.at[1, 10], sibling)
    am_copy = remote(send_a, recv_b, sib.at[0, 11], sib.at[1, 11], sibling)
    x_back = [
        remote(cot_own.at[pl.ds(n * block, block)], o_blk.at[n], xe.at[0, 7 + n], xe.at[1, 7 + n], x_neigh) for n in range(2)
    ]
    xm_copy = remote(cot_own, x_recv_m, xe.at[0, 9], xe.at[1, 9], x_neigh)
    tok_copy = remote(tok_own.at[oth_block], o_tok.at[x], xe.at[0, 3], xe.at[1, 3], x_neigh)
    blk_copy = remote(cot_own.at[oth_block], o_blk.at[x], xe.at[0, 2], xe.at[1, 2], x_neigh)

    low_lane = lax.broadcasted_iota(jnp.int32, (PAIR, PAIR), 1) < HEAD_DIM
    low_row = lax.broadcasted_iota(jnp.int32, (PAIR, PAIR), 0) < HEAD_DIM
    q_chunks = rows // PAIR

    def two_heads(v):
        zero = jnp.zeros_like(v)
        return jnp.concatenate([jnp.where(low_lane, v, zero), jnp.where(low_lane, zero, v)], 0)

    qkv_lanes = 3 * PAIR

    def pair_lanes(p):
        return tuple(slice(p * qkv_lanes + n * PAIR, p * qkv_lanes + (n + 1) * PAIR) for n in range(3))

    def att_lanes(p):
        return pl.ds(pl.multiple_of(c * half + p * PAIR, PAIR), PAIR)

    def wo_copy(p):
        return remote(w.at[p, BLOCKS - 1], w_oth.at[p], wo.at[0, p], wo.at[1, p], sibling)

    def columns(blocks):
        return jnp.concatenate([v.reshape(-1, PAIR) for v in blocks], 1)

    def project(p):
        wo_copy(p).start()
        q_at, k_at, v_at = pair_lanes(p)
        out = dot(n1[...], columns([w[p, n] for n in range(3)]))
        queries = (out[:, :PAIR] + vec[4:5, att_lanes(p)]).astype(BF16)
        qkv[:, q_at] = queries * jnp.asarray(HEAD_DIM**-0.5, BF16)
        qkv[:, k_at] = out[:, PAIR : 2 * PAIR].astype(BF16)
        qkv[:, v_at] = (out[:, 2 * PAIR :] + vec[5:6, att_lanes(p)]).astype(BF16)

    def attend_forward(p, first, last):
        q_at, k_at, v_at = pair_lanes(p)
        if first == 0:
            flipped[...] = qkv[:, v_at].T

        def some(j, carry):
            at = pl.ds(pl.multiple_of(j * PAIR, PAIR), PAIR)
            mask = kbias[...]
            scores = dot_cols(qkv[:, k_at], two_heads(qkv[at, q_at])) + jnp.concatenate([mask, mask], 1)
            highest = jnp.max(scores, 0, keepdims=True)
            raised = jnp.exp(scores - highest)
            total = jnp.sum(raised, 0, keepdims=True)
            out = dot(flipped[...], raised.astype(BF16)) / total
            out = jnp.where(low_row, out[:, :PAIR], out[:, PAIR:])
            att[at, att_lanes(p)] = out.T.astype(BF16)
            lse[pl.ds(p * q_chunks + j, 1), :] = highest + jnp.log(total)
            return carry

        lax.fori_loop(first, last, some, 0)
        if p == 3 and last == q_chunks:
            att_copy.start()

    def own_out(z):
        return columns([w[p, BLOCKS - 1, z] for p in range(4)])

    def oth_out(z):
        return columns([w_oth[p, z] for p in range(4)])

    def output_projection():
        mixed = att[my_rows, :]
        resid[:, my_half] = dot(mixed, own_out(slice(None)))
        resid[:, oth_half] = dot(mixed, oth_out(slice(None)))

    def second_norm():
        def some(i, carry):
            at = chunks(0, i)
            res = resid[at, :] + tok_own[at, :].astype(F32) + vec[6:7, :]
            resid[at, :] = res
            unit, _ = unit_rows(res)
            n2[chunks(x * rows + c * own, i), :] = (unit * vec[2:3, :] + vec[3:4, :]).astype(BF16)
            return carry

        lax.fori_loop(0, own // chunk, some, 0)
        n2_copies[1].start()
        n2_copies[0].start()

    tile = HALF * PAIR

    def expand(n, chip):
        u, first, _ = blocks_of(4 + n)
        at = pl.ds(pl.multiple_of(chip * rows, rows), rows)
        to = slice(n * tile, (n + 1) * tile)
        hidden = dot(n2[at, :], columns([w[u, first], w[u, first + 1]])) + bias_h[:, to]
        gate = jax.nn.sigmoid(SLOPE * hidden)
        act[at, to] = (hidden * gate).astype(BF16)
        fac[at, to] = (gate + SLOPE * hidden * gate * (1.0 - gate)).astype(BF16)

    def rs_x_copy(i):
        u = i - FIRST_EDGE
        return remote(g.at[u, theirs], rx.at[u], rs.at[0, i], rs.at[1, i], x_neigh)

    def y_place(i):
        return ry.at[i] if i < FIRST_EDGE else ry_e.at[i - FIRST_EDGE]

    def z_place(i):
        return rz.at[i] if i < FIRST_EDGE else rz_e.at[i - FIRST_EDGE]

    def rs_y_copy(i):
        return remote(item(g, i).at[:, :, 1 - yi], y_place(i), rs.at[2, i], rs.at[3, i], y_neigh)

    def done_blocks(i):
        u, first, count = blocks_of(i)
        return f_own.at[u, pl.ds(first, count)]

    def rs_2_copy(i):
        if i < 4:
            return remote(s_own.at[i], s_oth.at[i], rs.at[6, i], rs.at[7, i], x_neigh)
        to = f_oth.at[i - 4] if i < FIRST_EDGE else f_own.at[i - FIRST_EDGE, pl.ds(mine, 1)]
        return remote(done_blocks(i), to, rs.at[6, i], rs.at[7, i], x_neigh)

    def to_result(u, n, place):
        result = matrix(u, (o_att, o_exp, o_shr))
        if u < 4:
            first = n * width + place % 2 * half + u * PAIR
            return result.at[:, pl.ds(pl.multiple_of(first, PAIR), PAIR)]
        parts = unit_parts(u, place)
        return result.at[parts[n]] if parts else result.at[u - 4, place, n]

    def rs_share(i, source, first, count, place, sems):
        u = blocks_of(i)[0]
        for n in range(count):
            to = to_result(u, first + n, place)
            remote(source.at[n], to, rs.at[sems, i], rs.at[sems + 1, i], sibling).start()
            pltpu.make_async_copy(source.at[n], to, rs.at[sems + 2, i]).start()

    def rs_x_add(i):
        rs_x_copy(i).wait_recv()
        u = i - FIRST_EDGE
        g[u, mine] = g[u, mine] + rx[u]
        rs_y_copy(i).start()

    def rs_y_add(i):
        rs_y_copy(i).wait_recv()
        u, first, count = blocks_of(i)
        got = y_place(i)
        for n in range(count):
            for z in range(line):
                g[u, first + n, z, yi] = g[u, first + n, z, yi] + got[n, z]
        for o in range(1, line):
            z = lax.rem(zi + o, line)
            remote(item(g, i).at[:, z, yi], z_place(i).at[o - 1], rs.at[4, i], rs.at[5, i], z_peer(o)).start()

    def rs_z_add(i):
        u, first, count = blocks_of(i)
        got = z_place(i)
        wait_bytes(got, rs.at[5, i])
        for n in range(count):
            total = g[u, first + n, zi, yi].astype(F32)
            for o in range(1, line):
                total = total + got[o - 1, n].astype(F32)
            if i < 4:
                s_own[i, n] = total.astype(BF16)
            else:
                f_own[u, first + n] = total.astype(BF16)
        rs_2_copy(i).start()
        if i >= 4:
            rs_share(i, done_blocks(i), first, count, s, 8)

    def rs_join(i):
        rs_2_copy(i).wait_recv()
        u, first, count = blocks_of(i)
        if i < 4:
            for n in range(count):
                f_own[u, first + n] = s_own[i, n] + s_oth[i, n]
            rs_share(i, done_blocks(i), first, count, s, 8)
        elif i < FIRST_EDGE:
            rs_share(i, f_oth.at[i - 4], first, count, other, 11)
        else:
            rs_share(i, f_own.at[u, pl.ds(theirs, 1)], theirs, count, other, 11)

    def rs_end(i):
        if i >= FIRST_EDGE:
            rs_x_copy(i).wait_send()
        rs_y_copy(i).wait_send()
        wait_bytes(z_place(i), rs.at[4, i])
        rs_2_copy(i).wait_send()
        for n in range(8, 11 if i < 4 else 14):
            wait_bytes(done_blocks(i), rs.at[n, i])

    def put(u, first, value):
        for n in range(value.shape[1] // PAIR):
            part = value[:, n * PAIR : (n + 1) * PAIR].astype(BF16)
            g[u, first + n] = part.reshape(line, 2, r, PAIR)

    def rs_start(i):
        (rs_y_copy(i) if i < FIRST_EDGE else rs_x_copy(i)).start()

    def rs_stage(i, k):
        stages = [rs_x_add, rs_y_add, rs_z_add, rs_join, rs_end]
        (stages[1:] if i < FIRST_EDGE else stages)[k](i)

    def transpose_into(dst, first, src, size):
        def move(i, carry):
            at = pl.ds(pl.multiple_of(i * 128, 128), 128)
            dst[at, first : first + size] = src[:, at].T
            return carry

        lax.fori_loop(0, width // 128, move, 0)

    def shrink_grad(n):
        u, first, _ = blocks_of(8 + n)
        put(u, first, dot(tr[...], go[:, n * tile : (n + 1) * tile]))

    span = max(1, tile // (2 * r))
    part_rows = span * 2 * r

    def hidden_back(n, chip, clear):
        at = pl.ds(pl.multiple_of(chip * rows, rows), rows)
        if clear:
            hidden_sums[...] = jnp.zeros_like(hidden_sums)

        def some(m, carry):
            to = pl.ds(pl.multiple_of(m * part_rows, part_rows), part_rows)
            part = columns([w[6 + j, b, pl.ds(m * span, span)] for j in range(2) for b in range(BLOCKS)])
            total = dot_cols(go[at, :], part)
            low = (total * fac[at, to].astype(F32)).astype(BF16)
            fac[at, to] = low
            hidden_sums[:, to] += fold8(low.astype(F32))
            return carry

        count = line // span // 4
        lax.fori_loop(n * count, (n + 1) * count, some, 0)

    def back_partial(src, rows_at, groups, blocks, dst):
        lanes = len(groups[0]) * blocks * PAIR

        def back(n, carry):
            total = None
            for k, group in enumerate(groups):
                part = columns([w[u, b, pl.ds(n * span, span)] for u in group for b in range(blocks)])
                term = dot_cols(src[rows_at, k * lanes : (k + 1) * lanes], part)
                total = term if total is None else total + term
            dst[:, pl.ds(pl.multiple_of(n * part_rows, part_rows), part_rows)] = total
            return carry

        lax.fori_loop(0, line // span, back, 0)

    def expand_grad(n):
        u, first, _ = blocks_of(4 + n)
        put(u, first, dot(tr[...], fac[:, n * tile : (n + 1) * tile]))

    def to_x(came):
        def some(i, carry):
            at = chunks(0, i)
            cot_own[at, :] = (keep_p[at, :] + came[at, :]).astype(BF16)
            return carry

        lax.fori_loop(0, own // chunk, some, 0)

    ff = ((4, 5),)

    def hidden_partial(chip, dst):
        back_partial(fac, pl.ds(pl.multiple_of(chip * rows, rows), rows), ff, BLOCKS, dst)

    def hidden_partials(own_image):
        if own_image:
            hidden_partial(x, part_a)
            a_copy.start()
        else:
            hidden_partial(1 - x, part_b)
            b_copy.start()

    def partial_over_x():
        to_x(recv_b)
        for copy in x_back:
            copy.start()

    zeros8 = jnp.zeros((8, width), F32)

    def second_norm_back():
        def some(i, carry):
            at = chunks(0, i)
            unit, rstd = unit_rows(resid[at, :])
            came = o_blk[i // 2, pl.ds(pl.multiple_of(i % 2 * chunk, chunk), chunk)].astype(F32)
            gn = own_p[at, :] + recv_a[at, :] + came
            grad_out = go[chunks(x * rows + c * own, i), :].astype(F32)
            gr = grad_out + norm_back(gn, unit, rstd, vec[2:3, :])
            own_p[at, :] = gr
            low = gr.astype(BF16)
            gb[chunks(c * own, i), :] = low
            a, b, e, f = carry
            return (a + fold8(gn * unit), b + fold8(gn), e + fold8(low.astype(F32)), f + fold8(grad_out))

        vg[...] = jnp.zeros_like(vg)
        vg[pl.ds(8 + s, 1), :] = jnp.sum(hidden_sums[...], 0, keepdims=True)
        sums = lax.fori_loop(0, own // chunk, some, (zeros8,) * 4)
        for row, v in zip((2, 3, 6, 7), sums):
            vg[row : row + 1, :] = jnp.sum(v, 0, keepdims=True)
        gb_copy.start()

    def grad_attended(n):
        if n == 0:
            for copy in n2_copies:
                copy.wait_send()
        quarter = line // 4
        head_rows = pl.ds(c * (line // 2) + n * quarter, quarter)
        part = dot_cols(gb[:, my_half], own_out(head_rows)) + dot_cols(gb[:, oth_half], oth_out(head_rows))
        n2[:rows, n * tile : (n + 1) * tile] = part.astype(BF16)

    def attend_backward(p, first, last):
        q_at, k_at, v_at = pair_lanes(p)
        own_lanes = slice(p * PAIR, (p + 1) * PAIR)
        if first == 0:
            flipped[...] = qkv[:, k_at].T
            dk_acc[...] = jnp.zeros_like(dk_acc)
            dv_acc[...] = jnp.zeros_like(dv_acc)

        def some(j, carry):
            at = pl.ds(pl.multiple_of(j * PAIR, PAIR), PAIR)
            both = two_heads(qkv[at, q_at])
            grads = two_heads(n2[at, own_lanes])
            mask = kbias[...]
            scores = dot_cols(qkv[:, k_at], both) + jnp.concatenate([mask, mask], 1)
            chance = jnp.exp(scores - lse[pl.ds(p * q_chunks + j, 1), :])
            dv_acc[...] += dot(chance.astype(BF16), grads)
            grad_chance = dot_cols(qkv[:, v_at], grads)
            inner = jnp.sum(chance * grad_chance, 0, keepdims=True)
            grad_scores = (chance * (grad_chance - inner)).astype(BF16)
            dk_acc[...] += dot(grad_scores, both)
            out = dot(flipped[...], grad_scores)
            out = jnp.where(low_row, out[:, :PAIR], out[:, PAIR:]) * HEAD_DIM**-0.5
            qkv[at, q_at] = out.T.astype(BF16)
            return carry

        lax.fori_loop(first, last, some, 0)
        if last < q_chunks:
            return
        qkv[:, k_at] = dk_acc[...].astype(BF16)
        qkv[:, v_at] = dv_acc[...].astype(BF16)
        vg[4:5, att_lanes(p)] = jnp.sum(fold8(qkv[:, q_at].astype(F32)), 0, keepdims=True)
        vg[5:6, att_lanes(p)] = jnp.sum(fold8(qkv[:, v_at].astype(F32)), 0, keepdims=True)

    def attention_grad(p):
        put(p, 0, dot(tr[:, :rows], qkv[:, p * qkv_lanes : (p + 1) * qkv_lanes]))
        put(p, BLOCKS - 1, dot(tr[:, rows:], gb[:, att_lanes(p)]))

    def input_partial():
        back_partial(qkv, slice(0, rows), ((0, 1), (2, 3)), 3, part_b)
        p1_copy.start()

    def first_norm_back():
        def some(i, carry):
            at = chunks(0, i)
            unit, rstd = unit_rows(tok_own[at, :].astype(F32))
            gn = keep_p[at, :] + recv_a[at, :]
            out = own_p[at, :] + norm_back(gn, unit, rstd, vec[0:1, :])
            tok_own[at, :] = out.astype(BF16)
            a, b = carry
            return (a + fold8(gn * unit), b + fold8(gn))

        sums = lax.fori_loop(0, own // chunk, some, (zeros8,) * 2)
        for row, v in zip((0, 1), sums):
            vg[row : row + 1, :] = jnp.sum(v, 0, keepdims=True)
        o_tok[x] = tok_own[my_block, :]
        tok_copy.start()

    def branch(dst, rows_at, add):
        def out(n, carry):
            for j in range(2):
                part = columns([w[6 + j, 2 * n], w[6 + j, 2 * n + 1]])
                to = pl.ds(pl.multiple_of(j * UNIT + n * tile, tile), tile)
                total = dot(act[rows_at, :], part)
                dst[:, to] = dst[:, to] + total if add else total
            return carry

        lax.fori_loop(0, UNIT // tile, out, 0)

    def output_partial(n):
        if n == 0:
            branch(part_b, pl.ds(pl.multiple_of((1 - x) * rows, rows), rows), False)
            bm_copy.start()
        elif n == 2:
            branch(send_a, ff_rows(x, 1 - c), False)
            am_copy.start()
        else:
            branch(resid, ff_rows(x, c), True)

    def output_over_x():
        to_x(recv_m)
        xm_copy.start()

    def finish_block():
        def some(i, carry):
            at = chunks(0, i)
            out = resid[at, :] + recv_b[at, :] + x_recv_m[at, :].astype(F32) + vec[7:8, :]
            cot_own[at, :] = (live(chunks(c * own, i)) * out).astype(BF16)
            return carry

        lax.fori_loop(0, own // chunk, some, 0)
        o_blk[x] = cot_own[my_block, :]
        blk_copy.start()

    v_copies = [
        remote(vg, vr.at[n], vs.at[0, 1 + n], vs.at[1, 1 + n], to) for n, to in enumerate((sibling, x_neigh, y_neigh))
    ]

    def vector_hop(n):
        if n < 3:
            v_copies[n].start()
            return

        def send(o, carry):
            remote(vg, vz.at[zi], vs.at[0, 4], vs.at[1, 4], (lax.rem(zi + o, line) * 2 + yi, s)).start()
            return carry

        lax.fori_loop(1, line, send, 0)
        vz[zi] = vg[...]

    def vector_add(n):
        if n < 3:
            v_copies[n].wait()
            vg[...] += vr[n]
            return
        wait_bytes(vz.at[pl.ds(0, line - 1)], vs.at[1, 4])
        wait_bytes(vz.at[pl.ds(0, line - 1)], vs.at[0, 4])

    def vector_out():
        o_vec[...] = lax.fori_loop(1, line, lambda i, t: t + vz[i], vz[0])

    def both(*copies):
        for copy in copies:
            copy.wait()

    def received(*copies):
        for copy in copies:
            copy.wait_recv()

    def relay(copies):
        copies[1].wait_recv()
        copies[2].start()

    def relay_go():
        wait_bytes(go_bytes, xe.at[1, 4])
        for copy in go_copies[2]:
            copy.start()

    def all_rows():
        received(n2_copies[2])
        wait_bytes(go_bytes, loc.at[1])
        wait_bytes(go_bytes, sib.at[1, 4])
        wait_bytes(go_bytes, sib.at[1, 5])

    waits = dict(
        vec=lambda: wait_bytes(vec_all.at[pl.ds(0, dp_n - 1)], vs.at[1, 0]),
        tok=lambda: both(tok_copy_x, tok_copy_in),
        cot=lambda: None,
        n1=lambda: received(n1_copy),
        gox=relay_go,
        att=lambda: received(*[wo_copy(p) for p in range(4)], att_copy),
        n2=lambda: received(n2_copies[0]),
        n2x=lambda: relay(n2_copies),
        n2r=all_rows,
        b=lambda: both(b_copy),
        a=lambda: both(a_copy),
        xb=lambda: both(*x_back),
        gb=lambda: received(gb_copy),
        p1=lambda: both(p1_copy),
        bm=lambda: both(bm_copy),
        am=lambda: both(am_copy),
        xm=lambda: both(xm_copy),
        v0=lambda: vector_add(0),
        v1=lambda: vector_add(1),
        v2=lambda: vector_add(2),
        v3=lambda: vector_add(3),
    )
    split = 3
    work = dict(
        vec=lambda n: vector(),
        ln1=lambda n: first_norm(),
        go=lambda n: grad_output(),
        qkv=project,
        afa=lambda p: attend_forward(p, 0, split),
        afb=lambda p: attend_forward(p, split, q_chunks),
        out=lambda n: output_projection(),
        ln2=lambda n: second_norm(),
        eo=lambda n: expand(n, x),
        ex=lambda n: expand(n, 1 - x),
        tra=lambda n: transpose_into(tr, 0, act, 2 * rows),
        gs=shrink_grad,
        hx=lambda n: hidden_back(n, 1 - x, n == 0),
        hb=lambda n: hidden_back(n, x, False),
        bpx=lambda n: hidden_partials(False),
        tox=lambda n: partial_over_x(),
        bpo=lambda n: hidden_partials(True),
        trn=lambda n: transpose_into(tr, 0, n2, 2 * rows),
        gx=expand_grad,
        ln2b=lambda n: second_norm_back(),
        trb=lambda n: (transpose_into(tr, 0, n1, rows), transpose_into(tr, rows, att, rows)),
        gat=grad_attended,
        aba=lambda p: attend_backward(p, 0, split),
        abb=lambda p: attend_backward(p, split, q_chunks),
        ga=attention_grad,
        b1=lambda n: input_partial(),
        ln1b=lambda n: first_norm_back(),
        brx=lambda n: output_partial(0),
        tox2=lambda n: output_over_x(),
        br2=lambda n: output_partial(2),
        br3=lambda n: output_partial(3),
        v0=lambda n: vector_hop(0),
        v1=lambda n: vector_hop(1),
        v2=lambda n: vector_hop(2),
        v3=lambda n: vector_hop(3),
        fin=lambda n: finish_block(),
        ov=lambda n: vector_out(),
    )
    for kind, name, n in ORDER:
        if kind == "C":
            work[name](n)
        elif kind == "W":
            waits[name]()
        elif kind == "A":
            gather_stages[n](name)
        elif kind == "I":
            rs_start(name)
        else:
            rs_stage(name, n)

    blk_copy.wait()
    tok_copy.wait()
    wait_bytes(vec_all.at[pl.ds(0, dp_n - 1)], vs.at[0, 0])
    for sem in (sib.at[0, 4], sib.at[0, 5], xe.at[0, 4]):
        wait_bytes(go_bytes, sem)
    for copy in [n1_copy, att_copy, gb_copy] + [wo_copy(p) for p in range(4)]:
        copy.wait_send()
    for i in range(ITEMS):
        wait_bytes(z_bytes(i), ag.at[0, i])
        ag_y_copy(i).wait_send()
        if i >= FIRST_EDGE:
            ag_x_copy(i).wait_send()


def adamw(grad, moment, square, weight, rate, decay):
    momentum = BETA_ONE * moment + (1.0 - BETA_ONE) * grad
    variance = BETA_TWO * square + (1.0 - BETA_TWO) * grad * grad
    first_fix = 1.0 - BETA_ONE**STEP
    second_fix = 1.0 - BETA_TWO**STEP
    direction = momentum / first_fix / (jnp.sqrt(variance / second_fix) + EPS_ADAM)
    updated = weight - rate * (direction + decay * weight)
    return (momentum, variance, updated, updated.astype(BF16))


def body(
    tokens, cotangent, key_mask,
    attention_weights, expand_weights, shrink_weights, vector_params,
    attention_moment, attention_square, expand_moment, expand_square,
    shrink_moment, shrink_square, vector_moment, vector_square,
):
    dp_n = lax.axis_size("dp")
    line = dp_n // 2
    d = lax.axis_index("dp")
    place = lax.axis_index("seq")
    x, c = place // 2, place % 2
    _, local_len, width = tokens.shape
    r = width // dp_n
    block = -(-local_len // 16) * 16
    own, rows = 2 * block, 4 * block
    pad = ((0, 0), (0, block - local_len), (0, 0))

    keep = lax.dynamic_index_in_dim(key_mask, x, 0, keepdims=False).reshape(2, 2, local_len)
    keep = jnp.pad(keep.transpose(1, 0, 2), ((0, 0), (0, 0), pad[1])).reshape(2, own)
    mask_row = jnp.where(keep > 0, 0.0, -1e30).astype(F32).reshape(1, rows)
    p_exp = expand_weights
    if r % 128:
        p_exp = lax.dynamic_index_in_dim(expand_weights.reshape(r, dp_n, 4, r), place, 2, keepdims=False)
        p_exp = p_exp.reshape(r, 2, BLOCKS, PAIR).transpose(1, 2, 0, 3)
    vec_len = vector_params.shape[0]
    here = lax.dynamic_slice_in_dim(key_mask, place * local_len, local_len, 1)
    grad_out = jnp.where(here[:, :, None] > 0, cotangent, jnp.zeros_like(cotangent))
    vec_rows = -(-vec_len // 1024) * 8
    p_vec = jnp.pad(vector_params.astype(BF16).astype(F32), (0, vec_rows * 128 - vec_len)).reshape(vec_rows, 128)

    vmem = pl.BlockSpec(memory_space=pltpu.VMEM)
    hbm = pl.BlockSpec(memory_space=pl.ANY)
    padded = jax.ShapeDtypeStruct((2, block, width), BF16)
    o_blk, o_tok, o_att, o_exp, o_shr, o_vec = pl.pallas_call(
        functools.partial(layer_kernel, line, vec_len),
        out_shape=(
            padded,
            padded,
            jax.ShapeDtypeStruct((r, 4 * width), BF16),
            jax.ShapeDtypeStruct((2, 4, BLOCKS, r, PAIR) if r % 128 else (r, 4 * width), BF16),
            jax.ShapeDtypeStruct((4 * r, width), BF16),
            jax.ShapeDtypeStruct((16, width), F32),
        ),
        in_specs=[hbm, hbm, vmem, vmem, hbm, hbm, hbm],
        out_specs=(vmem, vmem, hbm, hbm, hbm, vmem),
        scratch_shapes=[
            pltpu.VMEM((UNITS, BLOCKS, line, 2, r, PAIR), BF16),
            pltpu.VMEM((4, line, 2, r, PAIR), BF16),
            pltpu.VMEM((UNITS, BLOCKS, line, 2, r, PAIR), BF16),
            pltpu.VMEM((4, line, 2, r, PAIR), BF16),
            pltpu.VMEM((FIRST_EDGE, HALF, line, r, PAIR), BF16),
            pltpu.VMEM((FIRST_EDGE, line - 1, HALF, r, PAIR), BF16),
            pltpu.VMEM((4, 1, line, r, PAIR), BF16),
            pltpu.VMEM((4, line - 1, 1, r, PAIR), BF16),
            pltpu.VMEM((4, HALF, r, PAIR), BF16),
            pltpu.VMEM((4, HALF, r, PAIR), BF16),
            pltpu.VMEM((UNITS, BLOCKS, r, PAIR), BF16),
            pltpu.VMEM((8, HALF, r, PAIR), BF16),
            pltpu.VMEM((dp_n, vec_rows, 128), F32),
            pltpu.VMEM((16, width), F32),
            pltpu.VMEM((1, width), F32),
            pltpu.VMEM((16, width), F32),
            pltpu.VMEM((3, 16, width), F32),
            pltpu.VMEM((line, 16, width), F32),
            pltpu.VMEM((8, width), F32),
            pltpu.VMEM((own, width), BF16),
            pltpu.VMEM((own, width), BF16),
            pltpu.VMEM((rows, width), BF16),
            pltpu.VMEM((2 * rows, width), BF16),
            pltpu.VMEM((rows, 3 * UNIT), BF16),
            pltpu.VMEM((rows, width), BF16),
            pltpu.VMEM(((rows // PAIR) * (UNIT // PAIR), 2 * PAIR), F32),
            pltpu.VMEM((own, width), F32),
            pltpu.VMEM((2 * rows, width), BF16),
            pltpu.VMEM((2 * rows, width), BF16),
            pltpu.VMEM((2 * rows, width), BF16),
        ]
        + [pltpu.VMEM((rows, width), F32)] * 2
        + [pltpu.VMEM((own, width), F32)] * 3
        + [
            pltpu.VMEM((own, width), BF16),
            pltpu.VMEM((rows, width), BF16),
            pltpu.VMEM((width, 2 * rows), BF16),
            pltpu.VMEM((rows, PAIR), F32),
            pltpu.VMEM((rows, PAIR), F32),
            pltpu.VMEM((PAIR, rows), BF16),
            pltpu.VMEM((rows, PAIR), F32),
            pltpu.SemaphoreType.DMA((6, ITEMS)),
            pltpu.SemaphoreType.DMA((14, ITEMS)),
            pltpu.SemaphoreType.DMA((2, 12)),
            pltpu.SemaphoreType.DMA((2, 4)),
            pltpu.SemaphoreType.DMA((2, 10)),
            pltpu.SemaphoreType.DMA((2, 5)),
            pltpu.SemaphoreType.DMA((UNITS, 2)),
            pltpu.SemaphoreType.DMA((2,)),
        ],
        compiler_params=pltpu.CompilerParams(
            collective_id=0, has_side_effects=True, vmem_limit_bytes=VMEM_LIMIT
        ),
        name="layer",
    )(jnp.pad(tokens, pad), jnp.pad(grad_out, pad), mask_row, p_vec, attention_weights, p_exp, shrink_weights)

    block_output = jnp.where(here[:, :, None] > 0, o_blk[:, :local_len], jnp.zeros_like(tokens))
    token_gradient = jnp.where(here[:, :, None] > 0, o_tok[:, :local_len], jnp.zeros_like(tokens))
    grad_attention, grad_shrink = o_att.astype(F32), o_shr.astype(F32)
    if r % 128:
        o_exp = o_exp.transpose(3, 1, 0, 2, 4).reshape(r, 4, dp_n, r).transpose(0, 2, 1, 3).reshape(r, 4 * width)
    grad_expand = o_exp.astype(F32)
    hidden_sums = o_vec[8:12].reshape(4, dp_n, r).transpose(1, 0, 2).reshape(4, width)
    grad_vector = jnp.concatenate([o_vec[0:8], hidden_sums], 0).reshape(dp_n, vec_len)
    grad_vector = lax.dynamic_index_in_dim(grad_vector, d, 0, keepdims=False)

    attention_out = adamw(
        grad_attention, attention_moment, attention_square, attention_weights, RATE_MATRIX, DECAY_MATRIX
    )
    expand_out = adamw(grad_expand, expand_moment, expand_square, expand_weights, RATE_MATRIX, DECAY_MATRIX)
    shrink_out = adamw(grad_shrink, shrink_moment, shrink_square, shrink_weights, RATE_MATRIX, DECAY_MATRIX)
    vector_out = adamw(grad_vector, vector_moment, vector_square, vector_params, RATE_VECTOR, 0.0)
    return (block_output, token_gradient, *attention_out, *expand_out, *shrink_out, *vector_out)


VMEM_LIMIT = 63 * 2**20

ORDER = (
    ("A", 12, 0), ("A", 0, 0), ("A", 13, 0), ("A", 1, 0), ("A", 14, 0), ("A", 2, 0), ("C", "go", 0), ("W", "vec", 0),
    ("C", "vec", 0), ("A", 12, 1), ("W", "tok", 0), ("C", "ln1", 0), ("A", 12, 2), ("A", 0, 1), ("A", 15, 0),
    ("A", 3, 0), ("A", 13, 1), ("A", 0, 2), ("A", 1, 1), ("A", 4, 0), ("A", 13, 2), ("A", 14, 1), ("A", 5, 0),
    ("W", "gox", 0), ("A", 1, 2), ("A", 2, 1), ("A", 6, 0), ("A", 12, 3), ("W", "n1", 0), ("C", "qkv", 0),
    ("A", 14, 2), ("C", "afa", 0), ("A", 15, 1), ("C", "afb", 0), ("A", 13, 3), ("C", "qkv", 1), ("A", 2, 2),
    ("C", "afa", 1), ("A", 3, 1), ("A", 7, 0), ("C", "afb", 1), ("A", 15, 2), ("A", 14, 3), ("C", "qkv", 2),
    ("C", "afa", 2), ("A", 4, 1), ("A", 8, 0), ("C", "afb", 2), ("A", 3, 2), ("A", 15, 3), ("C", "qkv", 3),
    ("C", "afa", 3), ("A", 5, 1), ("A", 9, 0), ("C", "afb", 3), ("A", 4, 2), ("W", "att", 0), ("C", "out", 0),
    ("A", 6, 1), ("A", 10, 0), ("C", "ln2", 0), ("A", 5, 2), ("A", 7, 1), ("A", 11, 0), ("W", "n2", 0),
    ("C", "eo", 0), ("C", "eo", 1), ("A", 6, 2), ("C", "eo", 2), ("A", 8, 1), ("A", 7, 2), ("C", "eo", 3),
    ("A", 9, 1), ("W", "n2x", 0), ("A", 8, 2), ("W", "n2r", 0), ("C", "ex", 0), ("A", 10, 1), ("C", "ex", 1),
    ("C", "ex", 2), ("A", 9, 2), ("C", "ex", 3), ("C", "tra", 0), ("A", 11, 1), ("C", "gs", 0), ("I", 8, 0),
    ("C", "gs", 1), ("A", 10, 2), ("I", 9, 0), ("C", "gs", 2), ("I", 10, 0), ("C", "gs", 3), ("C", "trn", 0),
    ("A", 11, 2), ("C", "hx", 0), ("C", "hb", 1), ("C", "hx", 1), ("C", "hx", 2), ("C", "hx", 3), ("R", 8, 0),
    ("I", 11, 0), ("C", "bpx", 0), ("C", "hb", 0), ("C", "hb", 2), ("R", 9, 0), ("C", "hb", 3), ("C", "gx", 0),
    ("R", 8, 1), ("I", 4, 0), ("W", "b", 0), ("C", "tox", 0), ("C", "gx", 2), ("R", 10, 0), ("R", 8, 2), ("I", 6, 0),
    ("C", "gx", 3), ("R", 8, 3), ("R", 9, 1), ("C", "bpo", 0), ("R", 11, 0), ("I", 7, 0), ("C", "gx", 1),
    ("R", 10, 1), ("C", "trb", 0), ("R", 4, 0), ("I", 5, 0), ("C", "brx", 0), ("R", 11, 1), ("W", "a", 0),
    ("W", "xb", 0), ("C", "ln2b", 0), ("R", 9, 2), ("R", 10, 2), ("R", 6, 0), ("R", 11, 2), ("W", "bm", 0),
    ("C", "tox2", 0), ("R", 4, 1), ("W", "gb", 0), ("C", "gat", 0), ("R", 9, 3), ("R", 10, 3), ("R", 11, 3),
    ("C", "gat", 1), ("R", 7, 0), ("C", "aba", 0), ("C", "abb", 0), ("R", 6, 1), ("R", 5, 0), ("C", "ga", 0),
    ("I", 12, 0), ("I", 0, 0), ("C", "aba", 1), ("R", 7, 1), ("C", "abb", 1), ("C", "ga", 1), ("I", 13, 0),
    ("I", 1, 0), ("C", "aba", 2), ("R", 4, 2), ("R", 6, 2), ("R", 5, 1), ("R", 0, 0), ("C", "abb", 2), ("R", 4, 3),
    ("R", 6, 3), ("C", "ga", 2), ("R", 12, 0), ("R", 1, 0), ("I", 14, 0), ("R", 7, 2), ("I", 2, 0), ("C", "aba", 3),
    ("R", 7, 3), ("R", 0, 1), ("C", "abb", 3), ("R", 12, 1), ("C", "b1", 0), ("R", 5, 2), ("R", 13, 0), ("R", 12, 2),
    ("R", 1, 1), ("R", 2, 0), ("C", "ga", 3), ("R", 14, 0), ("R", 0, 2), ("R", 5, 3), ("R", 12, 3), ("R", 13, 1),
    ("I", 15, 0), ("I", 3, 0), ("W", "p1", 0), ("C", "ln1b", 0), ("R", 12, 4), ("R", 0, 3), ("R", 1, 2),
    ("C", "v0", 0), ("R", 14, 1), ("C", "br2", 0), ("R", 1, 3), ("R", 2, 1), ("W", "v0", 0), ("C", "v1", 0),
    ("C", "br3", 0), ("R", 13, 2), ("R", 15, 0), ("R", 3, 0), ("R", 14, 2), ("W", "am", 0), ("W", "xm", 0),
    ("C", "fin", 0), ("W", "v1", 0), ("C", "v2", 0), ("R", 15, 1), ("W", "v2", 0), ("C", "v3", 0), ("R", 2, 2),
    ("R", 3, 1), ("R", 13, 3), ("R", 14, 3), ("R", 2, 3), ("R", 13, 4), ("R", 14, 4), ("R", 15, 2), ("R", 3, 2),
    ("R", 15, 3), ("W", "v3", 0), ("C", "ov", 0), ("R", 3, 3), ("R", 15, 4),
)


def solution(mesh):
    split = P("dp", "seq", None)
    rows = P("dp", None)
    flat = P("dp")
    return jax.shard_map(
        body,
        mesh=mesh,
        in_specs=(split, split, rows, rows, rows, rows, flat) + (rows,) * 6 + (flat, flat),
        out_specs=(split, split) + (rows,) * 12 + (flat,) * 4,
        check_vma=False,
    )
```

```python
import functools

import jax
import jax.numpy as jnp
from jax import lax
from jax.experimental import pallas as pl
from jax.experimental.pallas import tpu as pltpu
from jax.sharding import PartitionSpec as P

HEAD_DIM = 64
STEP = 5
EPS_NORM = 1e-05
BETA_ONE = 0.5
BETA_TWO = 0.5
EPS_ADAM = 1e-08
RATE_MATRIX = 0.05
RATE_VECTOR = 0.2
DECAY_MATRIX = 0.1
SLOPE = 1.702

BF16 = jnp.bfloat16
F32 = jnp.float32
MESH = pl.DeviceIdType.MESH

UNIT = 512
BLOCKS = 4
EDGE = BLOCKS - 1
HALF = 2
UNITS = 8
ITEMS = 16
FIRST_EDGE = 12
PAIR = 128


def dot(a, b):
    return jnp.dot(a, b, preferred_element_type=F32)


def dot_rows(a, b):
    return lax.dot_general(a, b, (((0,), (0,)), ((), ())), preferred_element_type=F32)


def dot_cols(a, b):
    return lax.dot_general(a, b, (((1,), (1,)), ((), ())), preferred_element_type=F32)


def unit_rows(x):
    centred = x - jnp.mean(x, -1, keepdims=True)
    rstd = lax.rsqrt(jnp.mean(centred * centred, -1, keepdims=True) + EPS_NORM)
    return centred * rstd, rstd


def norm_back(grad_normed, unit, rstd, gain):
    g = grad_normed * gain
    return rstd * (g - jnp.mean(g, -1, keepdims=True) - unit * jnp.mean(g * unit, -1, keepdims=True))


def fold8(v):
    return jnp.sum(v.reshape(v.shape[0] // 8, 8, v.shape[1]), 0)


def layer_kernel(
    line, vec_len,
    tok, cot, mask_row, p_vec, p_att, p_exp, p_shr,
    o_blk, o_tok, o_att, o_exp, o_shr, o_vec,
    w, w_oth, g, rx, ry, rz, ry_e, rz_e, s_own, s_oth, f_own, f_oth,
    vec_all, vec, bias_h, vg, vr, vz, hidden_sums,
    tok_own, cot_own,
    n1, go, qkv, att, lse, resid, n2, act, fac,
    part_a, part_b, recv_a, recv_b, recv_m, x_recv_m,
    gb, tr, dk_acc, dv_acc, flipped, kbias,
    ag, rs, sib, wo, xe, vs, fill, loc,
):
    dp_n = 2 * line
    r = w.shape[4]
    block = tok.shape[1]
    own = 2 * block
    rows = 2 * own
    width = tok.shape[2]
    half = UNIT
    d = lax.axis_index("dp")
    s = lax.axis_index("seq")
    zi, yi = d // 2, d % 2
    x, c = s // 2, s % 2
    sibling = (d, x * 2 + 1 - c)
    x_neigh = (d, (1 - x) * 2 + c)
    y_neigh = (zi * 2 + 1 - yi, s)

    def z_peer(o):
        return (lax.rem(zi + o, line) * 2 + yi, s)

    def own_rows(core):
        return pl.ds(pl.multiple_of(core * own, own), own)

    def ff_rows(chip, core):
        return pl.ds(pl.multiple_of(chip * rows + core * own, own), own)

    my_rows = own_rows(c)
    own_p, send_a = part_a.at[own_rows(c)], part_a.at[own_rows(1 - c)]
    keep_p, send_b = part_b.at[own_rows(c)], part_b.at[own_rows(1 - c)]
    my_half = pl.ds(pl.multiple_of(c * half, half), half)
    oth_half = pl.ds(pl.multiple_of((1 - c) * half, half), half)
    my_block = pl.ds(pl.multiple_of(x * block, block), block)
    oth_block = pl.ds(pl.multiple_of((1 - x) * block, block), block)

    mine, theirs = x * EDGE, (1 - x) * EDGE

    def blocks_of(i):
        if i < 4:
            return i, 1, HALF
        if i < FIRST_EDGE:
            return 4 + (i - 4) // 2, (i - 4) % 2 * HALF, HALF
        return i - FIRST_EDGE, mine, 1

    def item(ref, i):
        u, first, count = blocks_of(i)
        return ref.at[u, pl.ds(first, count)]

    def remote(src, dst, send, recv, to):
        return pltpu.make_async_remote_copy(
            src_ref=src, dst_ref=dst, send_sem=send, recv_sem=recv, device_id=to, device_id_type=MESH
        )

    def wait_bytes(ref, sem):
        pltpu.make_async_copy(ref, ref, sem).wait()

    wide = r % 128 == 0

    def unit_parts(u, place):
        if u < 4:
            core = place % 2
            return [
                (slice(None), pl.ds(pl.multiple_of(n * width + core * half + u * PAIR, PAIR), PAIR)) for n in range(BLOCKS)
            ]
        if u < 6:
            if not wide:
                return None
            parts = []
            for n in range((u - 4) * UNIT, (u - 3) * UNIT, PAIR):
                at = n // r * 4 * r + place * r + n % r
                parts.append((slice(None), pl.ds(pl.multiple_of(at, PAIR), PAIR)))
            return parts
        first = (u - 6) * UNIT
        held = pl.ds(pl.multiple_of(place * r, r), r)
        return [(held, slice(first + n * PAIR, first + (n + 1) * PAIR)) for n in range(BLOCKS)]

    def stage(u):
        n = u % 4 if u < 4 else u % 2
        hold, first = (part_a, 0) if u < 4 else (part_b, u // 6 * r)
        first = first + n // 2 * r
        return hold.at[first : first + r, (n % 2) * UNIT : (n % 2 + 1) * UNIT]

    def matrix(u, refs):
        return refs[0 if u < 4 else 1 if u < 6 else 2]

    for u in range(UNITS):
        parts = unit_parts(u, s)
        source = matrix(u, (p_att, p_exp, p_shr))
        for n in range(BLOCKS):
            part = source.at[parts[n]] if parts else source.at[u - 4, n]
            pltpu.make_async_copy(part, stage(u).at[:, n * PAIR : (n + 1) * PAIR], fill.at[u, n // HALF if u >= 4 else int(n in (0, EDGE))]).start()

    vec_all[d] = p_vec[...]
    tok_copy_in = pltpu.make_async_copy(tok.at[x], tok_own.at[my_block], loc.at[0])
    tok_copy_in.start()

    def go_rows(chip, place):
        return pl.ds(pl.multiple_of(chip * rows + place % 2 * own + place // 2 * block, block), block)

    go_local = [pltpu.make_async_copy(cot.at[n], go.at[go_rows(n, s)], loc.at[1]) for n in range(2)]
    for copy in go_local:
        copy.start()

    barrier = pltpu.get_barrier_semaphore()

    def greet(o, carry):
        pl.semaphore_signal(barrier, inc=1, device_id=(lax.rem(d + o, dp_n), s), device_id_type=MESH)
        return carry

    lax.fori_loop(1, dp_n, greet, 0)
    pl.semaphore_signal(barrier, inc=1, device_id=sibling, device_id_type=MESH)
    pl.semaphore_signal(barrier, inc=1, device_id=x_neigh, device_id_type=MESH)
    pl.semaphore_wait(barrier, dp_n + 1)

    def send_vec(o, carry):
        remote(p_vec, vec_all.at[d], vs.at[0, 0], vs.at[1, 0], (lax.rem(d + o, dp_n), s)).start()
        return carry

    lax.fori_loop(1, dp_n, send_vec, 0)
    tok_copy_x = remote(tok.at[1 - x], tok_own.at[my_block], xe.at[0, 0], xe.at[1, 0], x_neigh)
    tok_copy_x.start()
    other = (1 - x) * 2 + c
    go_copies = [
        [remote(cot.at[n], go.at[go_rows(n, s)], sib.at[0, 4], sib.at[1, 4], sibling) for n in range(2)],
        [remote(cot.at[n], go.at[go_rows(n, s)], xe.at[0, 4], xe.at[1, 4], x_neigh) for n in range(2)],
        [remote(go.at[go_rows(n, other)], go.at[go_rows(n, other)], sib.at[0, 5], sib.at[1, 5], sibling) for n in range(2)],
    ]
    go_bytes = go.at[:own]

    def ag_z(i):
        u, first, count = blocks_of(i)
        group = first // HALF if 4 <= i < FIRST_EDGE else int(i >= FIRST_EDGE)
        wait_bytes(stage(u).at[:, : HALF * PAIR], fill.at[u, group])
        for n in range(count):
            w[u, first + n, zi, yi] = stage(u)[:, pl.ds(pl.multiple_of((first + n) * PAIR, PAIR), PAIR)].astype(BF16)
        part = item(w, i).at[:, zi, yi]
        for o in range(1, line):
            remote(part, part, ag.at[0, i], ag.at[1, i], z_peer(o)).start()

    def ag_y_copy(i):
        part = item(w, i).at[:, :, yi]
        return remote(part, part, ag.at[2, i], ag.at[3, i], y_neigh)

    def ag_x_copy(i):
        return remote(item(w, i), item(w, i), ag.at[4, i], ag.at[5, i], x_neigh)

    def z_bytes(i):
        return item(w, i).at[:, pl.ds(0, line - 1), yi]

    def ag_y(i):
        wait_bytes(z_bytes(i), ag.at[1, i])
        ag_y_copy(i).start()

    def ag_x(i):
        ag_y_copy(i).wait_recv()
        if i >= FIRST_EDGE:
            ag_x_copy(i).start()

    def ag_end(i):
        ag_x_copy(i).wait_recv()

    gather_stages = [ag_z, ag_y, ag_x, ag_end]

    grain = 128 if vec_len % 128 == 0 else 64

    def vec_lanes(first):
        parts = []
        for e in range(first, first + 128, grain):
            o = e % vec_len
            parts.append(vec_all[e // vec_len, o // 128 : o // 128 + 1, o % 128 : o % 128 + grain])
        return parts[0] if len(parts) == 1 else jnp.concatenate(parts, 1)

    def hidden_bias(place):
        parts = []
        for shard in range(dp_n):
            n = shard * 4 * r + place * r
            parts.append(vec[8 + n // width : 9 + n // width, n % width : n % width + r])
        return jnp.concatenate(parts, 1)

    def vector():
        kbias[...] = jnp.broadcast_to(mask_row[...], (PAIR, rows)).T
        for row in range(12):
            for lane in range(0, width, 128):
                vec[row : row + 1, lane : lane + 128] = vec_lanes(row * width + lane)
        low_half = jnp.where(s == 0, hidden_bias(0), hidden_bias(1))
        bias_h[...] = jnp.where(s < 2, low_half, jnp.where(s == 2, hidden_bias(2), hidden_bias(3)))

    def live(to):
        return jnp.where(kbias[to, 0:1] < 0, 0.0, 1.0)

    chunk = block // 2

    def chunks(first, i):
        return pl.ds(pl.multiple_of(first + i * chunk, chunk), chunk)

    def first_norm():
        def some(i, carry):
            unit, _ = unit_rows(tok_own[chunks(0, i), :].astype(F32))
            n1[chunks(c * own, i), :] = (unit * vec[0:1, :] + vec[1:2, :]).astype(BF16)
            return carry

        lax.fori_loop(0, own // chunk, some, 0)
        n1_copy.start()

    def grad_output():
        for copy in go_copies[1] + go_copies[0]:
            copy.start()

    def rows_copies(ref, n):
        here, there = ref.at[ff_rows(x, c)], ref.at[ff_rows(1 - x, c)]
        return (
            remote(here, here, sib.at[0, n], sib.at[1, n], sibling),
            remote(here, here, xe.at[0, n], xe.at[1, n], x_neigh),
            remote(there, there, sib.at[0, n + 1], sib.at[1, n + 1], sibling),
        )

    n1_copy = remote(n1.at[my_rows], n1.at[my_rows], sib.at[0, 0], sib.at[1, 0], sibling)
    att_copy = remote(att.at[:, my_half], att.at[:, my_half], sib.at[0, 1], sib.at[1, 1], sibling)
    gb_copy = remote(gb.at[my_rows], gb.at[my_rows], sib.at[0, 2], sib.at[1, 2], sibling)
    p1_copy = remote(send_b, recv_a, sib.at[0, 3], sib.at[1, 3], sibling)
    n2_copies = rows_copies(n2, 6)
    b_copy = remote(send_b, recv_b, sib.at[0, 8], sib.at[1, 8], sibling)
    a_copy = remote(send_a, recv_a, sib.at[0, 9], sib.at[1, 9], sibling)
    bm_copy = remote(send_b, recv_m, sib.at[0, 10], sib.at[1, 10], sibling)
    am_copy = remote(send_a, recv_b, sib.at[0, 11], sib.at[1, 11], sibling)
    x_back = [
        remote(cot_own.at[pl.ds(n * block, block)], o_blk.at[n], xe.at[0, 7 + n], xe.at[1, 7 + n], x_neigh) for n in range(2)
    ]
    xm_copy = remote(cot_own, x_recv_m, xe.at[0, 9], xe.at[1, 9], x_neigh)
    tok_copy = remote(tok_own.at[oth_block], o_tok.at[x], xe.at[0, 3], xe.at[1, 3], x_neigh)
    blk_copy = remote(cot_own.at[oth_block], o_blk.at[x], xe.at[0, 2], xe.at[1, 2], x_neigh)

    low_lane = lax.broadcasted_iota(jnp.int32, (PAIR, PAIR), 1) < HEAD_DIM
    low_row = lax.broadcasted_iota(jnp.int32, (PAIR, PAIR), 0) < HEAD_DIM
    q_chunks = rows // PAIR

    def two_heads(v):
        zero = jnp.zeros_like(v)
        return jnp.concatenate([jnp.where(low_lane, v, zero), jnp.where(low_lane, zero, v)], 0)

    qkv_lanes = 3 * PAIR

    def pair_lanes(p):
        return tuple(slice(p * qkv_lanes + n * PAIR, p * qkv_lanes + (n + 1) * PAIR) for n in range(3))

    def att_lanes(p):
        return pl.ds(pl.multiple_of(c * half + p * PAIR, PAIR), PAIR)

    def wo_copy(p):
        return remote(w.at[p, BLOCKS - 1], w_oth.at[p], wo.at[0, p], wo.at[1, p], sibling)

    def columns(blocks):
        return jnp.concatenate([v.reshape(-1, PAIR) for v in blocks], 1)

    def project(p):
        wo_copy(p).start()
        q_at, k_at, v_at = pair_lanes(p)
        out = dot(n1[...], columns([w[p, n] for n in range(3)]))
        queries = (out[:, :PAIR] + vec[4:5, att_lanes(p)]).astype(BF16)
        qkv[:, q_at] = queries * jnp.asarray(HEAD_DIM**-0.5, BF16)
        qkv[:, k_at] = out[:, PAIR : 2 * PAIR].astype(BF16)
        qkv[:, v_at] = (out[:, 2 * PAIR :] + vec[5:6, att_lanes(p)]).astype(BF16)

    def attend_forward(p, first, last):
        q_at, k_at, v_at = pair_lanes(p)
        if first == 0:
            flipped[...] = qkv[:, v_at].T

        def some(j, carry):
            at = pl.ds(pl.multiple_of(j * PAIR, PAIR), PAIR)
            mask = kbias[...]
            scores = dot_cols(qkv[:, k_at], two_heads(qkv[at, q_at])) + jnp.concatenate([mask, mask], 1)
            highest = jnp.max(scores, 0, keepdims=True)
            raised = jnp.exp(scores - highest)
            total = jnp.sum(raised, 0, keepdims=True)
            out = dot(flipped[...], raised.astype(BF16)) / total
            out = jnp.where(low_row, out[:, :PAIR], out[:, PAIR:])
            att[at, att_lanes(p)] = out.T.astype(BF16)
            lse[pl.ds(p * q_chunks + j, 1), :] = highest + jnp.log(total)
            return carry

        lax.fori_loop(first, last, some, 0)
        if p == 3 and last == q_chunks:
            att_copy.start()

    def own_out(z):
        return columns([w[p, BLOCKS - 1, z] for p in range(4)])

    def oth_out(z):
        return columns([w_oth[p, z] for p in range(4)])

    def output_projection():
        mixed = att[my_rows, :]
        resid[:, my_half] = dot(mixed, own_out(slice(None)))
        resid[:, oth_half] = dot(mixed, oth_out(slice(None)))

    def second_norm():
        def some(i, carry):
            at = chunks(0, i)
            res = resid[at, :] + tok_own[at, :].astype(F32) + vec[6:7, :]
            resid[at, :] = res
            unit, _ = unit_rows(res)
            n2[chunks(x * rows + c * own, i), :] = (unit * vec[2:3, :] + vec[3:4, :]).astype(BF16)
            return carry

        lax.fori_loop(0, own // chunk, some, 0)
        n2_copies[1].start()
        n2_copies[0].start()

    tile = HALF * PAIR

    def expand(n, chip):
        u, first, _ = blocks_of(4 + n)
        at = pl.ds(pl.multiple_of(chip * rows, rows), rows)
        to = slice(n * tile, (n + 1) * tile)
        hidden = dot(n2[at, :], columns([w[u, first], w[u, first + 1]])) + bias_h[:, to]
        gate = jax.nn.sigmoid(SLOPE * hidden)
        act[at, to] = (hidden * gate).astype(BF16)
        fac[at, to] = (gate + SLOPE * hidden * gate * (1.0 - gate)).astype(BF16)

    def rs_x_copy(i):
        u = i - FIRST_EDGE
        return remote(g.at[u, theirs], rx.at[u], rs.at[0, i], rs.at[1, i], x_neigh)

    def y_place(i):
        return ry.at[i] if i < FIRST_EDGE else ry_e.at[i - FIRST_EDGE]

    def z_place(i):
        return rz.at[i] if i < FIRST_EDGE else rz_e.at[i - FIRST_EDGE]

    def rs_y_copy(i):
        return remote(item(g, i).at[:, :, 1 - yi], y_place(i), rs.at[2, i], rs.at[3, i], y_neigh)

    def done_blocks(i):
        u, first, count = blocks_of(i)
        return f_own.at[u, pl.ds(first, count)]

    def rs_2_copy(i):
        if i < 4:
            return remote(s_own.at[i], s_oth.at[i], rs.at[6, i], rs.at[7, i], x_neigh)
        to = f_oth.at[i - 4] if i < FIRST_EDGE else f_own.at[i - FIRST_EDGE, pl.ds(mine, 1)]
        return remote(done_blocks(i), to, rs.at[6, i], rs.at[7, i], x_neigh)

    def to_result(u, n, place):
        result = matrix(u, (o_att, o_exp, o_shr))
        if u < 4:
            first = n * width + place % 2 * half + u * PAIR
            return result.at[:, pl.ds(pl.multiple_of(first, PAIR), PAIR)]
        parts = unit_parts(u, place)
        return result.at[parts[n]] if parts else result.at[u - 4, place, n]

    def rs_share(i, source, first, count, place, sems):
        u = blocks_of(i)[0]
        for n in range(count):
            to = to_result(u, first + n, place)
            remote(source.at[n], to, rs.at[sems, i], rs.at[sems + 1, i], sibling).start()
            pltpu.make_async_copy(source.at[n], to, rs.at[sems + 2, i]).start()

    def rs_x_add(i):
        rs_x_copy(i).wait_recv()
        u = i - FIRST_EDGE
        g[u, mine] = g[u, mine] + rx[u]
        rs_y_copy(i).start()

    def rs_y_add(i):
        rs_y_copy(i).wait_recv()
        u, first, count = blocks_of(i)
        got = y_place(i)
        for n in range(count):
            for z in range(line):
                g[u, first + n, z, yi] = g[u, first + n, z, yi] + got[n, z]
        for o in range(1, line):
            z = lax.rem(zi + o, line)
            remote(item(g, i).at[:, z, yi], z_place(i).at[o - 1], rs.at[4, i], rs.at[5, i], z_peer(o)).start()

    def rs_z_add(i):
        u, first, count = blocks_of(i)
        got = z_place(i)
        wait_bytes(got, rs.at[5, i])
        for n in range(count):
            total = g[u, first + n, zi, yi].astype(F32)
            for o in range(1, line):
                total = total + got[o - 1, n].astype(F32)
            if i < 4:
                s_own[i, n] = total.astype(BF16)
            else:
                f_own[u, first + n] = total.astype(BF16)
        rs_2_copy(i).start()
        if i >= 4:
            rs_share(i, done_blocks(i), first, count, s, 8)

    def rs_join(i):
        rs_2_copy(i).wait_recv()
        u, first, count = blocks_of(i)
        if i < 4:
            for n in range(count):
                f_own[u, first + n] = s_own[i, n] + s_oth[i, n]
            rs_share(i, done_blocks(i), first, count, s, 8)
        elif i < FIRST_EDGE:
            rs_share(i, f_oth.at[i - 4], first, count, other, 11)
        else:
            rs_share(i, f_own.at[u, pl.ds(theirs, 1)], theirs, count, other, 11)

    def rs_end(i):
        if i >= FIRST_EDGE:
            rs_x_copy(i).wait_send()
        rs_y_copy(i).wait_send()
        wait_bytes(z_place(i), rs.at[4, i])
        rs_2_copy(i).wait_send()
        for n in range(8, 11 if i < 4 else 14):
            wait_bytes(done_blocks(i), rs.at[n, i])

    def put(u, first, value):
        for n in range(value.shape[1] // PAIR):
            part = value[:, n * PAIR : (n + 1) * PAIR].astype(BF16)
            g[u, first + n] = part.reshape(line, 2, r, PAIR)

    def rs_start(i):
        (rs_y_copy(i) if i < FIRST_EDGE else rs_x_copy(i)).start()

    def rs_stage(i, k):
        stages = [rs_x_add, rs_y_add, rs_z_add, rs_join, rs_end]
        (stages[1:] if i < FIRST_EDGE else stages)[k](i)

    def transpose_into(dst, first, src, size):
        def move(i, carry):
            at = pl.ds(pl.multiple_of(i * 128, 128), 128)
            dst[at, first : first + size] = src[:, at].T
            return carry

        lax.fori_loop(0, width // 128, move, 0)

    def shrink_grad(n):
        u, first, _ = blocks_of(8 + n)
        put(u, first, dot(tr[...], go[:, n * tile : (n + 1) * tile]))

    span = max(1, tile // (2 * r))
    part_rows = span * 2 * r

    def hidden_back(n, chip, clear):
        at = pl.ds(pl.multiple_of(chip * rows, rows), rows)
        if clear:
            hidden_sums[...] = jnp.zeros_like(hidden_sums)

        def some(m, carry):
            to = pl.ds(pl.multiple_of(m * part_rows, part_rows), part_rows)
            part = columns([w[6 + j, b, pl.ds(m * span, span)] for j in range(2) for b in range(BLOCKS)])
            total = dot_cols(go[at, :], part)
            low = (total * fac[at, to].astype(F32)).astype(BF16)
            fac[at, to] = low
            hidden_sums[:, to] += fold8(low.astype(F32))
            return carry

        count = line // span // 4
        lax.fori_loop(n * count, (n + 1) * count, some, 0)

    def back_partial(src, rows_at, groups, blocks, dst):
        lanes = len(groups[0]) * blocks * PAIR

        def back(n, carry):
            total = None
            for k, group in enumerate(groups):
                part = columns([w[u, b, pl.ds(n * span, span)] for u in group for b in range(blocks)])
                term = dot_cols(src[rows_at, k * lanes : (k + 1) * lanes], part)
                total = term if total is None else total + term
            dst[:, pl.ds(pl.multiple_of(n * part_rows, part_rows), part_rows)] = total
            return carry

        lax.fori_loop(0, line // span, back, 0)

    def expand_grad(n):
        u, first, _ = blocks_of(4 + n)
        put(u, first, dot(tr[...], fac[:, n * tile : (n + 1) * tile]))

    def to_x(came):
        def some(i, carry):
            at = chunks(0, i)
            cot_own[at, :] = (keep_p[at, :] + came[at, :]).astype(BF16)
            return carry

        lax.fori_loop(0, own // chunk, some, 0)

    ff = ((4, 5),)

    def hidden_partial(chip, dst):
        back_partial(fac, pl.ds(pl.multiple_of(chip * rows, rows), rows), ff, BLOCKS, dst)

    def hidden_partials(own_image):
        if own_image:
            hidden_partial(x, part_a)
            a_copy.start()
        else:
            hidden_partial(1 - x, part_b)
            b_copy.start()

    def partial_over_x():
        to_x(recv_b)
        for copy in x_back:
            copy.start()

    zeros8 = jnp.zeros((8, width), F32)

    def second_norm_back():
        def some(i, carry):
            at = chunks(0, i)
            unit, rstd = unit_rows(resid[at, :])
            came = o_blk[i // 2, pl.ds(pl.multiple_of(i % 2 * chunk, chunk), chunk)].astype(F32)
            gn = own_p[at, :] + recv_a[at, :] + came
            grad_out = go[chunks(x * rows + c * own, i), :].astype(F32)
            gr = grad_out + norm_back(gn, unit, rstd, vec[2:3, :])
            own_p[at, :] = gr
            low = gr.astype(BF16)
            gb[chunks(c * own, i), :] = low
            a, b, e, f = carry
            return (a + fold8(gn * unit), b + fold8(gn), e + fold8(low.astype(F32)), f + fold8(grad_out))

        vg[...] = jnp.zeros_like(vg)
        vg[pl.ds(8 + s, 1), :] = jnp.sum(hidden_sums[...], 0, keepdims=True)
        sums = lax.fori_loop(0, own // chunk, some, (zeros8,) * 4)
        for row, v in zip((2, 3, 6, 7), sums):
            vg[row : row + 1, :] = jnp.sum(v, 0, keepdims=True)
        gb_copy.start()

    def grad_attended(n):
        if n == 0:
            for copy in n2_copies:
                copy.wait_send()
        quarter = line // 4
        head_rows = pl.ds(c * (line // 2) + n * quarter, quarter)
        part = dot_cols(gb[:, my_half], own_out(head_rows)) + dot_cols(gb[:, oth_half], oth_out(head_rows))
        n2[:rows, n * tile : (n + 1) * tile] = part.astype(BF16)

    def attend_backward(p, first, last):
        q_at, k_at, v_at = pair_lanes(p)
        own_lanes = slice(p * PAIR, (p + 1) * PAIR)
        if first == 0:
            flipped[...] = qkv[:, k_at].T
            dk_acc[...] = jnp.zeros_like(dk_acc)
            dv_acc[...] = jnp.zeros_like(dv_acc)

        def some(j, carry):
            at = pl.ds(pl.multiple_of(j * PAIR, PAIR), PAIR)
            both = two_heads(qkv[at, q_at])
            grads = two_heads(n2[at, own_lanes])
            mask = kbias[...]
            scores = dot_cols(qkv[:, k_at], both) + jnp.concatenate([mask, mask], 1)
            chance = jnp.exp(scores - lse[pl.ds(p * q_chunks + j, 1), :])
            dv_acc[...] += dot(chance.astype(BF16), grads)
            grad_chance = dot_cols(qkv[:, v_at], grads)
            inner = jnp.sum(chance * grad_chance, 0, keepdims=True)
            grad_scores = (chance * (grad_chance - inner)).astype(BF16)
            dk_acc[...] += dot(grad_scores, both)
            out = dot(flipped[...], grad_scores)
            out = jnp.where(low_row, out[:, :PAIR], out[:, PAIR:]) * HEAD_DIM**-0.5
            qkv[at, q_at] = out.T.astype(BF16)
            return carry

        lax.fori_loop(first, last, some, 0)
        if last < q_chunks:
            return
        qkv[:, k_at] = dk_acc[...].astype(BF16)
        qkv[:, v_at] = dv_acc[...].astype(BF16)
        vg[4:5, att_lanes(p)] = jnp.sum(fold8(qkv[:, q_at].astype(F32)), 0, keepdims=True)
        vg[5:6, att_lanes(p)] = jnp.sum(fold8(qkv[:, v_at].astype(F32)), 0, keepdims=True)

    def attention_grad(p):
        put(p, 0, dot(tr[:, :rows], qkv[:, p * qkv_lanes : (p + 1) * qkv_lanes]))
        put(p, BLOCKS - 1, dot(tr[:, rows:], gb[:, att_lanes(p)]))

    def input_partial():
        back_partial(qkv, slice(0, rows), ((0, 1), (2, 3)), 3, part_b)
        p1_copy.start()

    def first_norm_back():
        def some(i, carry):
            at = chunks(0, i)
            unit, rstd = unit_rows(tok_own[at, :].astype(F32))
            gn = keep_p[at, :] + recv_a[at, :]
            out = own_p[at, :] + norm_back(gn, unit, rstd, vec[0:1, :])
            tok_own[at, :] = out.astype(BF16)
            a, b = carry
            return (a + fold8(gn * unit), b + fold8(gn))

        sums = lax.fori_loop(0, own // chunk, some, (zeros8,) * 2)
        for row, v in zip((0, 1), sums):
            vg[row : row + 1, :] = jnp.sum(v, 0, keepdims=True)
        o_tok[x] = tok_own[my_block, :]
        tok_copy.start()

    def branch(dst, rows_at, add):
        def out(n, carry):
            for j in range(2):
                part = columns([w[6 + j, 2 * n], w[6 + j, 2 * n + 1]])
                to = pl.ds(pl.multiple_of(j * UNIT + n * tile, tile), tile)
                total = dot(act[rows_at, :], part)
                dst[:, to] = dst[:, to] + total if add else total
            return carry

        lax.fori_loop(0, UNIT // tile, out, 0)

    def output_partial(n):
        if n == 0:
            branch(part_b, pl.ds(pl.multiple_of((1 - x) * rows, rows), rows), False)
            bm_copy.start()
        elif n == 2:
            branch(send_a, ff_rows(x, 1 - c), False)
            am_copy.start()
        else:
            branch(resid, ff_rows(x, c), True)

    def output_over_x():
        to_x(recv_m)
        xm_copy.start()

    def finish_block():
        def some(i, carry):
            at = chunks(0, i)
            out = resid[at, :] + recv_b[at, :] + x_recv_m[at, :].astype(F32) + vec[7:8, :]
            cot_own[at, :] = (live(chunks(c * own, i)) * out).astype(BF16)
            return carry

        lax.fori_loop(0, own // chunk, some, 0)
        o_blk[x] = cot_own[my_block, :]
        blk_copy.start()

    v_copies = [
        remote(vg, vr.at[n], vs.at[0, 1 + n], vs.at[1, 1 + n], to) for n, to in enumerate((sibling, x_neigh, y_neigh))
    ]

    def vector_hop(n):
        if n < 3:
            v_copies[n].start()
            return

        def send(o, carry):
            remote(vg, vz.at[zi], vs.at[0, 4], vs.at[1, 4], (lax.rem(zi + o, line) * 2 + yi, s)).start()
            return carry

        lax.fori_loop(1, line, send, 0)
        vz[zi] = vg[...]

    def vector_add(n):
        if n < 3:
            v_copies[n].wait()
            vg[...] += vr[n]
            return
        wait_bytes(vz.at[pl.ds(0, line - 1)], vs.at[1, 4])
        wait_bytes(vz.at[pl.ds(0, line - 1)], vs.at[0, 4])

    def vector_out():
        o_vec[...] = lax.fori_loop(1, line, lambda i, t: t + vz[i], vz[0])

    def both(*copies):
        for copy in copies:
            copy.wait()

    def received(*copies):
        for copy in copies:
            copy.wait_recv()

    def relay(copies):
        copies[1].wait_recv()
        copies[2].start()

    def relay_go():
        wait_bytes(go_bytes, xe.at[1, 4])
        for copy in go_copies[2]:
            copy.start()

    def all_rows():
        received(n2_copies[2])
        wait_bytes(go_bytes, loc.at[1])
        wait_bytes(go_bytes, sib.at[1, 4])
        wait_bytes(go_bytes, sib.at[1, 5])

    waits = dict(
        vec=lambda: wait_bytes(vec_all.at[pl.ds(0, dp_n - 1)], vs.at[1, 0]),
        tok=lambda: both(tok_copy_x, tok_copy_in),
        cot=lambda: None,
        n1=lambda: received(n1_copy),
        gox=relay_go,
        att=lambda: received(*[wo_copy(p) for p in range(4)], att_copy),
        n2=lambda: received(n2_copies[0]),
        n2x=lambda: relay(n2_copies),
        n2r=all_rows,
        b=lambda: both(b_copy),
        a=lambda: both(a_copy),
        xb=lambda: both(*x_back),
        gb=lambda: received(gb_copy),
        p1=lambda: both(p1_copy),
        bm=lambda: both(bm_copy),
        am=lambda: both(am_copy),
        xm=lambda: both(xm_copy),
        v0=lambda: vector_add(0),
        v1=lambda: vector_add(1),
        v2=lambda: vector_add(2),
        v3=lambda: vector_add(3),
    )
    split = 3
    work = dict(
        vec=lambda n: vector(),
        ln1=lambda n: first_norm(),
        go=lambda n: grad_output(),
        qkv=project,
        afa=lambda p: attend_forward(p, 0, split),
        afb=lambda p: attend_forward(p, split, q_chunks),
        out=lambda n: output_projection(),
        ln2=lambda n: second_norm(),
        eo=lambda n: expand(n, x),
        ex=lambda n: expand(n, 1 - x),
        tra=lambda n: transpose_into(tr, 0, act, 2 * rows),
        gs=shrink_grad,
        hx=lambda n: hidden_back(n, 1 - x, n == 0),
        hb=lambda n: hidden_back(n, x, False),
        bpx=lambda n: hidden_partials(False),
        tox=lambda n: partial_over_x(),
        bpo=lambda n: hidden_partials(True),
        trn=lambda n: transpose_into(tr, 0, n2, 2 * rows),
        gx=expand_grad,
        ln2b=lambda n: second_norm_back(),
        trb=lambda n: (transpose_into(tr, 0, n1, rows), transpose_into(tr, rows, att, rows)),
        gat=grad_attended,
        aba=lambda p: attend_backward(p, 0, split),
        abb=lambda p: attend_backward(p, split, q_chunks),
        ga=attention_grad,
        b1=lambda n: input_partial(),
        ln1b=lambda n: first_norm_back(),
        brx=lambda n: output_partial(0),
        tox2=lambda n: output_over_x(),
        br2=lambda n: output_partial(2),
        br3=lambda n: output_partial(3),
        v0=lambda n: vector_hop(0),
        v1=lambda n: vector_hop(1),
        v2=lambda n: vector_hop(2),
        v3=lambda n: vector_hop(3),
        fin=lambda n: finish_block(),
        ov=lambda n: vector_out(),
    )
    for kind, name, n in ORDER:
        if kind == "C":
            work[name](n)
        elif kind == "W":
            waits[name]()
        elif kind == "A":
            gather_stages[n](name)
        elif kind == "I":
            rs_start(name)
        else:
            rs_stage(name, n)

    blk_copy.wait()
    tok_copy.wait()
    wait_bytes(vec_all.at[pl.ds(0, dp_n - 1)], vs.at[0, 0])
    for sem in (sib.at[0, 4], sib.at[0, 5], xe.at[0, 4]):
        wait_bytes(go_bytes, sem)
    for copy in [n1_copy, att_copy, gb_copy] + [wo_copy(p) for p in range(4)]:
        copy.wait_send()
    for i in range(ITEMS):
        wait_bytes(z_bytes(i), ag.at[0, i])
        ag_y_copy(i).wait_send()
        if i >= FIRST_EDGE:
            ag_x_copy(i).wait_send()


def adamw(grad, moment, square, weight, rate, decay):
    momentum = BETA_ONE * moment + (1.0 - BETA_ONE) * grad
    variance = BETA_TWO * square + (1.0 - BETA_TWO) * grad * grad
    first_fix = 1.0 - BETA_ONE**STEP
    second_fix = 1.0 - BETA_TWO**STEP
    direction = momentum / first_fix / (jnp.sqrt(variance / second_fix) + EPS_ADAM)
    updated = weight - rate * (direction + decay * weight)
    return (momentum, variance, updated, updated.astype(BF16))


def body(
    tokens, cotangent, key_mask,
    attention_weights, expand_weights, shrink_weights, vector_params,
    attention_moment, attention_square, expand_moment, expand_square,
    shrink_moment, shrink_square, vector_moment, vector_square,
):
    dp_n = lax.axis_size("dp")
    line = dp_n // 2
    d = lax.axis_index("dp")
    place = lax.axis_index("seq")
    x, c = place // 2, place % 2
    _, local_len, width = tokens.shape
    r = width // dp_n
    block = -(-local_len // 16) * 16
    own, rows = 2 * block, 4 * block
    pad = ((0, 0), (0, block - local_len), (0, 0))

    keep = lax.dynamic_index_in_dim(key_mask, x, 0, keepdims=False).reshape(2, 2, local_len)
    keep = jnp.pad(keep.transpose(1, 0, 2), ((0, 0), (0, 0), pad[1])).reshape(2, own)
    mask_row = jnp.where(keep > 0, 0.0, -1e30).astype(F32).reshape(1, rows)
    p_exp = expand_weights
    if r % 128:
        p_exp = lax.dynamic_index_in_dim(expand_weights.reshape(r, dp_n, 4, r), place, 2, keepdims=False)
        p_exp = p_exp.reshape(r, 2, BLOCKS, PAIR).transpose(1, 2, 0, 3)
    vec_len = vector_params.shape[0]
    here = lax.dynamic_slice_in_dim(key_mask, place * local_len, local_len, 1)
    grad_out = jnp.where(here[:, :, None] > 0, cotangent, jnp.zeros_like(cotangent))
    vec_rows = -(-vec_len // 1024) * 8
    p_vec = jnp.pad(vector_params.astype(BF16).astype(F32), (0, vec_rows * 128 - vec_len)).reshape(vec_rows, 128)

    vmem = pl.BlockSpec(memory_space=pltpu.VMEM)
    hbm = pl.BlockSpec(memory_space=pl.ANY)
    padded = jax.ShapeDtypeStruct((2, block, width), BF16)
    o_blk, o_tok, o_att, o_exp, o_shr, o_vec = pl.pallas_call(
        functools.partial(layer_kernel, line, vec_len),
        out_shape=(
            padded,
            padded,
            jax.ShapeDtypeStruct((r, 4 * width), BF16),
            jax.ShapeDtypeStruct((2, 4, BLOCKS, r, PAIR) if r % 128 else (r, 4 * width), BF16),
            jax.ShapeDtypeStruct((4 * r, width), BF16),
            jax.ShapeDtypeStruct((16, width), F32),
        ),
        in_specs=[hbm, hbm, vmem, vmem, hbm, hbm, hbm],
        out_specs=(vmem, vmem, hbm, hbm, hbm, vmem),
        scratch_shapes=[
            pltpu.VMEM((UNITS, BLOCKS, line, 2, r, PAIR), BF16),
            pltpu.VMEM((4, line, 2, r, PAIR), BF16),
            pltpu.VMEM((UNITS, BLOCKS, line, 2, r, PAIR), BF16),
            pltpu.VMEM((4, line, 2, r, PAIR), BF16),
            pltpu.VMEM((FIRST_EDGE, HALF, line, r, PAIR), BF16),
            pltpu.VMEM((FIRST_EDGE, line - 1, HALF, r, PAIR), BF16),
            pltpu.VMEM((4, 1, line, r, PAIR), BF16),
            pltpu.VMEM((4, line - 1, 1, r, PAIR), BF16),
            pltpu.VMEM((4, HALF, r, PAIR), BF16),
            pltpu.VMEM((4, HALF, r, PAIR), BF16),
            pltpu.VMEM((UNITS, BLOCKS, r, PAIR), BF16),
            pltpu.VMEM((8, HALF, r, PAIR), BF16),
            pltpu.VMEM((dp_n, vec_rows, 128), F32),
            pltpu.VMEM((16, width), F32),
            pltpu.VMEM((1, width), F32),
            pltpu.VMEM((16, width), F32),
            pltpu.VMEM((3, 16, width), F32),
            pltpu.VMEM((line, 16, width), F32),
            pltpu.VMEM((8, width), F32),
            pltpu.VMEM((own, width), BF16),
            pltpu.VMEM((own, width), BF16),
            pltpu.VMEM((rows, width), BF16),
            pltpu.VMEM((2 * rows, width), BF16),
            pltpu.VMEM((rows, 3 * UNIT), BF16),
            pltpu.VMEM((rows, width), BF16),
            pltpu.VMEM(((rows // PAIR) * (UNIT // PAIR), 2 * PAIR), F32),
            pltpu.VMEM((own, width), F32),
            pltpu.VMEM((2 * rows, width), BF16),
            pltpu.VMEM((2 * rows, width), BF16),
            pltpu.VMEM((2 * rows, width), BF16),
        ]
        + [pltpu.VMEM((rows, width), F32)] * 2
        + [pltpu.VMEM((own, width), F32)] * 3
        + [
            pltpu.VMEM((own, width), BF16),
            pltpu.VMEM((rows, width), BF16),
            pltpu.VMEM((width, 2 * rows), BF16),
            pltpu.VMEM((rows, PAIR), F32),
            pltpu.VMEM((rows, PAIR), F32),
            pltpu.VMEM((PAIR, rows), BF16),
            pltpu.VMEM((rows, PAIR), F32),
            pltpu.SemaphoreType.DMA((6, ITEMS)),
            pltpu.SemaphoreType.DMA((14, ITEMS)),
            pltpu.SemaphoreType.DMA((2, 12)),
            pltpu.SemaphoreType.DMA((2, 4)),
            pltpu.SemaphoreType.DMA((2, 10)),
            pltpu.SemaphoreType.DMA((2, 5)),
            pltpu.SemaphoreType.DMA((UNITS, 2)),
            pltpu.SemaphoreType.DMA((2,)),
        ],
        compiler_params=pltpu.CompilerParams(
            collective_id=0, has_side_effects=True, vmem_limit_bytes=VMEM_LIMIT
        ),
        name="layer",
    )(jnp.pad(tokens, pad), jnp.pad(grad_out, pad), mask_row, p_vec, attention_weights, p_exp, shrink_weights)

    block_output = jnp.where(here[:, :, None] > 0, o_blk[:, :local_len], jnp.zeros_like(tokens))
    token_gradient = jnp.where(here[:, :, None] > 0, o_tok[:, :local_len], jnp.zeros_like(tokens))
    grad_attention, grad_shrink = o_att.astype(F32), o_shr.astype(F32)
    if r % 128:
        o_exp = o_exp.transpose(3, 1, 0, 2, 4).reshape(r, 4, dp_n, r).transpose(0, 2, 1, 3).reshape(r, 4 * width)
    grad_expand = o_exp.astype(F32)
    hidden_sums = o_vec[8:12].reshape(4, dp_n, r).transpose(1, 0, 2).reshape(4, width)
    grad_vector = jnp.concatenate([o_vec[0:8], hidden_sums], 0).reshape(dp_n, vec_len)
    grad_vector = lax.dynamic_index_in_dim(grad_vector, d, 0, keepdims=False)

    attention_out = adamw(
        grad_attention, attention_moment, attention_square, attention_weights, RATE_MATRIX, DECAY_MATRIX
    )
    expand_out = adamw(grad_expand, expand_moment, expand_square, expand_weights, RATE_MATRIX, DECAY_MATRIX)
    shrink_out = adamw(grad_shrink, shrink_moment, shrink_square, shrink_weights, RATE_MATRIX, DECAY_MATRIX)
    vector_out = adamw(grad_vector, vector_moment, vector_square, vector_params, RATE_VECTOR, 0.0)
    return (block_output, token_gradient, *attention_out, *expand_out, *shrink_out, *vector_out)


VMEM_LIMIT = 63 * 2**20

ORDER = (
    ("A", 12, 0), ("A", 0, 0), ("A", 13, 0), ("A", 1, 0), ("A", 14, 0), ("A", 2, 0), ("C", "go", 0), ("W", "vec", 0),
    ("C", "vec", 0), ("A", 12, 1), ("W", "tok", 0), ("C", "ln1", 0), ("A", 12, 2), ("A", 0, 1), ("A", 15, 0),
    ("A", 3, 0), ("A", 13, 1), ("A", 0, 2), ("A", 1, 1), ("A", 4, 0), ("A", 13, 2), ("A", 14, 1), ("A", 5, 0),
    ("W", "gox", 0), ("A", 1, 2), ("A", 2, 1), ("A", 6, 0), ("A", 12, 3), ("W", "n1", 0), ("C", "qkv", 0),
    ("A", 14, 2), ("C", "afa", 0), ("A", 15, 1), ("C", "afb", 0), ("A", 13, 3), ("C", "qkv", 1), ("A", 2, 2),
    ("C", "afa", 1), ("A", 3, 1), ("A", 7, 0), ("C", "afb", 1), ("A", 15, 2), ("A", 14, 3), ("C", "qkv", 2),
    ("C", "afa", 2), ("A", 4, 1), ("A", 8, 0), ("C", "afb", 2), ("A", 3, 2), ("A", 15, 3), ("C", "qkv", 3),
    ("C", "afa", 3), ("A", 5, 1), ("A", 9, 0), ("C", "afb", 3), ("A", 4, 2), ("W", "att", 0), ("C", "out", 0),
    ("A", 6, 1), ("A", 10, 0), ("C", "ln2", 0), ("A", 5, 2), ("A", 7, 1), ("A", 11, 0), ("W", "n2", 0),
    ("C", "eo", 0), ("C", "eo", 1), ("A", 6, 2), ("C", "eo", 2), ("A", 8, 1), ("A", 7, 2), ("C", "eo", 3),
    ("A", 9, 1), ("W", "n2x", 0), ("A", 8, 2), ("W", "n2r", 0), ("C", "ex", 2), ("A", 10, 1), ("C", "ex", 0),
    ("C", "ex", 1), ("A", 9, 2), ("C", "ex", 3), ("C", "tra", 0), ("A", 11, 1), ("C", "gs", 2), ("I", 10, 0),
    ("A", 10, 2), ("C", "gs", 3), ("I", 11, 0), ("C", "gs", 1), ("I", 9, 0), ("C", "gs", 0), ("C", "trn", 0),
    ("A", 11, 2), ("C", "hx", 0), ("C", "hx", 3), ("C", "hx", 1), ("C", "hb", 0), ("C", "hx", 2), ("R", 10, 0),
    ("I", 8, 0), ("C", "bpx", 0), ("C", "hb", 1), ("C", "hb", 3), ("C", "hb", 2), ("R", 11, 0), ("C", "gx", 2),
    ("R", 10, 1), ("I", 6, 0), ("W", "b", 0), ("C", "tox", 0), ("C", "brx", 0), ("R", 10, 2), ("R", 9, 0),
    ("C", "gx", 0), ("R", 11, 1), ("I", 4, 0), ("C", "bpo", 0), ("R", 10, 3), ("R", 8, 0), ("C", "gx", 3),
    ("I", 7, 0), ("R", 9, 1), ("C", "gx", 1), ("C", "trb", 0), ("R", 6, 0), ("I", 5, 0), ("W", "a", 0),
    ("W", "xb", 0), ("C", "ln2b", 0), ("R", 11, 2), ("R", 9, 2), ("R", 8, 1), ("R", 4, 0), ("W", "bm", 0),
    ("C", "tox2", 0), ("W", "gb", 0), ("C", "gat", 0), ("R", 11, 3), ("R", 9, 3), ("C", "gat", 1), ("R", 6, 1),
    ("R", 8, 2), ("C", "aba", 0), ("R", 8, 3), ("R", 7, 0), ("C", "abb", 0), ("R", 4, 1), ("C", "aba", 1),
    ("R", 5, 0), ("C", "abb", 1), ("R", 7, 1), ("C", "aba", 2), ("C", "ga", 0), ("R", 6, 2), ("R", 4, 2), ("R", 5, 1),
    ("R", 7, 2), ("R", 6, 3), ("I", 12, 0), ("I", 0, 0), ("C", "ga", 1), ("R", 4, 3), ("R", 7, 3), ("I", 13, 0),
    ("R", 5, 2), ("I", 1, 0), ("C", "abb", 2), ("R", 5, 3), ("C", "ga", 2), ("I", 14, 0), ("I", 2, 0),
    ("C", "aba", 3), ("R", 12, 0), ("R", 0, 0), ("C", "abb", 3), ("C", "b1", 0), ("R", 13, 0), ("R", 1, 0),
    ("C", "ga", 3), ("R", 0, 1), ("R", 2, 0), ("R", 14, 0), ("I", 15, 0), ("I", 3, 0), ("C", "br2", 0),
    ("W", "p1", 0), ("C", "ln1b", 0), ("R", 12, 1), ("R", 0, 2), ("R", 13, 1), ("R", 1, 1), ("C", "v0", 0),
    ("C", "br3", 0), ("R", 0, 3), ("W", "am", 0), ("W", "xm", 0), ("C", "fin", 0), ("R", 14, 1), ("R", 15, 0),
    ("W", "v0", 0), ("C", "v1", 0), ("R", 2, 1), ("R", 12, 2), ("R", 3, 0), ("W", "v1", 0), ("C", "v2", 0),
    ("R", 13, 2), ("R", 15, 1), ("R", 1, 2), ("W", "v2", 0), ("C", "v3", 0), ("R", 14, 2), ("R", 1, 3), ("R", 3, 1),
    ("R", 2, 2), ("R", 12, 3), ("R", 13, 3), ("R", 15, 2), ("R", 14, 3), ("R", 12, 4), ("R", 2, 3), ("R", 13, 4),
    ("R", 3, 2), ("R", 14, 4), ("R", 15, 3), ("W", "v3", 0), ("C", "ov", 0), ("R", 3, 3), ("R", 15, 4),
)


def solution(mesh):
    split = P("dp", "seq", None)
    rows = P("dp", None)
    flat = P("dp")
    return jax.shard_map(
        body,
        mesh=mesh,
        in_specs=(split, split, rows, rows, rows, rows, flat) + (rows,) * 6 + (flat, flat),
        out_specs=(split, split) + (rows,) * 12 + (flat,) * 4,
        check_vma=False,
    )
```
